32 devices in a mesh: dp: 8 (over z, y), tensor: 4 (over x, core).
Axes of the slice: x: 2, y: 2, z: 4, core: 2. Of those that a mesh axis runs over, the one named last changes fastest.
Arguments:
- tokens: bfloat16 [8192, 768], P(('dp', 'tensor')), may hold values from -6 to 6
- cotangent: bfloat16 [8192, 768], P(('dp', 'tensor')), may hold values from -6 to 6
- lengths: int32 [8], P('dp'), may hold values from 128 to 1024, as said below
- attn_w: float32 [4, 768, 768], P('tensor', 'dp')
- up_w: float32 [768, 3072], P('dp', 'tensor'), may hold values from -0.21875 to 0.21875
- down_w: float32 [3072, 768], P('tensor', 'dp'), may hold values from -0.109375 to 0.109375
- norm_params: float32 [4, 768], replicated, may hold values from -2 to 2
- attn_mom: float32 [4, 768, 768], P('tensor', 'dp')
- up_mom: float32 [768, 3072], P('dp', 'tensor')
- down_mom: float32 [3072, 768], P('tensor', 'dp')
- norm_m1: float32 [4, 768], replicated
- norm_m2: float32 [4, 768], replicated, may hold values from 204 to 910
Outputs:
- mixed: bfloat16 [8192, 768], P(('dp', 'tensor'))
- input_grad: float32 [8192, 768], P(('dp', 'tensor'))
- attn_new: float32 [4, 768, 768], P('tensor', 'dp')
- attn_moment: float32 [4, 768, 768], P('tensor', 'dp')
- up_new: float32 [768, 3072], P('dp', 'tensor')
- up_moment: float32 [768, 3072], P('dp', 'tensor')
- down_new: float32 [3072, 768], P('tensor', 'dp')
- down_moment: float32 [3072, 768], P('tensor', 'dp')
- norm_moment1: float32 [4, 768], replicated
- norm_moment2: float32 [4, 768], replicated
- norm_new: float32 [4, 768], replicated
The draws below stay inside these ranges and needn't reach their ends.
Inputs may be any that keep to these rules, and one draw needn't show every extreme that they name: `lengths`: some sequence has exactly 1024 true positions.
All inputs are finite; a program needn't handle non-finite values.
Results may differ from the reference program's by a relative error of at most 0.017.
Values may be sent and summed in bfloat16 or wider, within the bound.
A program may use at most 192 MiB of HBM per device.

```python
import math
import jax
import jax.numpy as jnp
from jax import lax

D = 768
HEADS = 12
HDIM = 64
FF = 3072
LEN = 1024
MINLEN = 128
BLOCK = 64
NS_STEPS = 5
STEP = 10
SEQS = 8
TOKENS = 8192


def rising(count, spread):
    return 1.0 + spread * jnp.arange(count, dtype=jnp.float32) / max(count - 1, 1)


def signed_noise(key, shape):
    return jnp.clip(jax.random.normal(key, shape, jnp.float32), -5.0, 5.0)


def growth():
    return 2.0


def draw_lengths(key, part):
    key = jax.random.fold_in(key, 3)
    first, second = jax.random.split(key)
    values = jax.random.randint(first, (SEQS,), MINLEN, LEN + 1)
    chosen = jax.random.randint(second, (), 0, SEQS)
    return jnp.where(jnp.arange(SEQS) == chosen, LEN, values).astype(jnp.int32)


def draw_attn_w(key, part):
    key = jax.random.fold_in(key, 5)
    scales = jnp.array([1.0, 1.0, 1.0, math.sqrt(8.0)], jnp.float32) / math.sqrt(D)
    return signed_noise(key, (4, D, D)) * scales[:, None, None]


def draw_attn_mom(key, part):
    key = jax.random.fold_in(key, 7)
    base = math.sqrt(TOKENS / 2.0) * jnp.array([0.1, 0.1, 0.3, 0.06], jnp.float32)
    return signed_noise(key, (4, D, D)) * base[:, None, None] * rising(D, growth())[None, :, None]


def draw_up_mom(key, part):
    key = jax.random.fold_in(key, 11)
    base = 0.3 * math.sqrt(TOKENS / 2.0)
    return signed_noise(key, (D, FF)) * base * rising(D, growth())[:, None] * rising(FF, growth())[None, :]


def draw_down_mom(key, part):
    key = jax.random.fold_in(key, 13)
    base = 0.6 * math.sqrt(TOKENS / 2.0)
    return signed_noise(key, (FF, D)) * base * rising(FF, growth())[:, None] * rising(D, growth())[None, :]


def draw_norm_params(key, part):
    key = jax.random.fold_in(key, 17)
    first, second = jax.random.split(key)
    gains = jax.random.uniform(first, (4, D), jnp.float32, 0.6, 1.4)
    biases = 0.3 * jnp.clip(jax.random.normal(second, (4, D), jnp.float32), -4.0, 4.0)
    pick = (jnp.arange(4) % 2 == 0)[:, None]
    return jnp.where(pick, gains, biases)


def draw_norm_m1(key, part):
    key = jax.random.fold_in(key, 19)
    return signed_noise(key, (4, D)) * math.sqrt(TOKENS / 2.0)


def draw_norm_m2(key, part):
    key = jax.random.fold_in(key, 23)
    factor = jnp.exp(jax.random.uniform(key, (4, D), jnp.float32, 0.0, math.log(4.0)))
    return TOKENS / 2.0 * (0.05 / 0.95) * factor


def block_scale(key, extent, cuts, low, largest):
    level = 1.0
    for axis_at, parts in cuts:
        draws = jax.random.uniform(jax.random.fold_in(jax.random.fold_in(key, 6), axis_at), (parts,), jnp.float32, low / len(cuts), largest / len(cuts))
        level = level * jnp.repeat(jnp.exp(draws), extent[axis_at] // parts).reshape((-1,) + (1,) * (len(extent) - 1 - axis_at))
    return level


def noise(own_key, shape, scale, reach, shards=(), held_as=jnp.bfloat16):
    values = jax.random.normal(own_key, shape, jnp.float32) * scale
    if len(shards) > 0:
        values = block_scale(own_key, shape, shards, -0.22, 0.18) * values
    return jnp.clip(values, min=-reach, max=reach).astype(held_as)


def setup_inputs(seed: int = 0) -> dict:
    key_list = jax.random.split(jax.random.key(seed), 13)
    return {
        "tokens": noise(key_list[0], (TOKENS, D), 1.0, 6.0, ((0, 32),)),
        "cotangent": noise(key_list[1], (TOKENS, D), 1.0, 6.0, ((0, 32),)),
        "lengths": draw_lengths(jax.random.fold_in(key_list[12], 71), 0),
        "attn_w": draw_attn_w(jax.random.fold_in(key_list[12], 71), 0),
        "up_w": noise(key_list[4], (D, FF), D ** -0.5, 0.21875, ((0, 8), (1, 4)), jnp.float32),
        "down_w": noise(key_list[5], (FF, D), FF ** -0.5, 0.109375, ((0, 4), (1, 8)), jnp.float32),
        "norm_params": draw_norm_params(jax.random.fold_in(key_list[12], 71), 0),
        "attn_mom": draw_attn_mom(jax.random.fold_in(key_list[12], 71), 0),
        "up_mom": draw_up_mom(jax.random.fold_in(key_list[12], 71), 0),
        "down_mom": draw_down_mom(jax.random.fold_in(key_list[12], 71), 0),
        "norm_m1": draw_norm_m1(jax.random.fold_in(key_list[12], 71), 0),
        "norm_m2": draw_norm_m2(jax.random.fold_in(key_list[12], 71), 0),
    }


@jax.custom_vjp
def low(v):
    return lax.optimization_barrier(v.astype(jnp.bfloat16)).astype(jnp.float32)

@jax.custom_vjp
def low_back(v):
    return v

def low_keep(v):
    return (low(v), None)

def low_pass(kept, grad):
    return (grad,)

def back_keep(v):
    return (v, None)

def back_low(kept, grad):
    return (low(grad),)
low.defvjp(low_keep, low_pass)
low_back.defvjp(back_keep, back_low)
HIGH = lax.Precision.HIGHEST
NORM_EPS = 1e-05
NS_EPS = 1e-07
COEF_A = 3.4445
COEF_B = -4.775
COEF_C = 2.0315
MUON_RATE = 0.15
MUON_DECAY = 0.1
ADAM_RATE = 0.2

def matmul(left, right):
    return jnp.dot(left, right, precision=HIGH, preferred_element_type=jnp.float32)

def layer_norm(resid, gain, bias):
    center = resid - lax.optimization_barrier(jnp.mean(resid, -1, keepdims=True))
    spread = lax.optimization_barrier(jnp.mean(center * center, -1, keepdims=True))
    return center * lax.rsqrt(spread + NORM_EPS) * gain + bias

def features(proj, cosine, sine, weight_rows):
    count = proj.shape[0]
    soft = jax.nn.softplus(proj).reshape(count, HEADS, HDIM)
    both = jnp.concatenate([soft * cosine[:, None, None], soft * sine[:, None, None]], -1)
    return both * weight_rows[:, None, None]

def attention(query, key_proj, value, length):
    count = query.shape[0]
    blocks = count // BLOCK
    where = jnp.arange(count)
    live = (where < length).astype(jnp.float32)
    place = jnp.minimum(where, length - 1).astype(jnp.float32)
    theta = 0.5 * math.pi * place / length.astype(jnp.float32)
    cosine = jnp.cos(theta)
    sine = jnp.sin(theta)
    every_row = jnp.ones((count,), jnp.float32)
    qfeat = low(features(query, cosine, sine, every_row)).reshape(blocks, BLOCK, HEADS, 2 * HDIM)
    kfeat = low(features(key_proj, cosine, sine, live)).reshape(blocks, BLOCK, HEADS, 2 * HDIM)
    values = low(value).reshape(blocks, BLOCK, HEADS, HDIM)
    lower = jnp.tril(jnp.ones((BLOCK, BLOCK), jnp.float32))
    scores = low_back(jnp.einsum('nihf,njhf->nhij', qfeat, kfeat, precision=HIGH) * lower)
    pairs = low_back(jnp.einsum('njhf,njhd->nhfd', kfeat, values, precision=HIGH))
    state = low(jnp.cumsum(pairs, 0) - pairs)
    key_sum = lax.optimization_barrier(jnp.sum(kfeat, 1))
    zsum = jnp.cumsum(key_sum, 0) - key_sum
    numer = jnp.einsum('nhij,njhd->nihd', low(scores), values, precision=HIGH)
    numer = low_back(numer + jnp.einsum('nihf,nhfd->nihd', qfeat, state, precision=HIGH))
    denom = jnp.transpose(lax.optimization_barrier(jnp.sum(scores, -1)), (0, 2, 1)) + jnp.einsum('nihf,nhf->nih', qfeat, zsum, precision=HIGH)
    return (numer / denom[..., None]).reshape(count, HEADS * HDIM)

def forward(inputs, w_query, w_key, w_value, w_out, w_up, w_down, norms, length):
    inputs_low = low(inputs)
    query = low_back(matmul(inputs_low, low(w_query)))
    key_proj = low_back(matmul(inputs_low, low(w_key)))
    value = low_back(matmul(inputs_low, low(w_value)))
    attn = attention(query, key_proj, value, length)
    branch = low_back(matmul(low(attn), low(w_out)))
    hidden_in = layer_norm(inputs + branch, norms[0], norms[1])
    pre = low_back(matmul(low(hidden_in), low(w_up)))
    ffn = low_back(matmul(low(jax.nn.gelu(pre, approximate=True)), low(w_down)))
    live = (jnp.arange(inputs.shape[0]) < length).astype(jnp.float32)
    return live[:, None] * layer_norm(hidden_in + ffn, norms[2], norms[3])

def orthogonalize(iterate):
    for step in range(NS_STEPS):
        gram = jnp.dot(iterate, iterate.T, preferred_element_type=jnp.float32).astype(jnp.bfloat16)
        poly = (COEF_B * gram.astype(jnp.float32) + COEF_C * jnp.dot(gram, gram, preferred_element_type=jnp.float32)).astype(jnp.bfloat16)
        iterate = (COEF_A * iterate.astype(jnp.float32) + jnp.dot(poly, iterate, preferred_element_type=jnp.float32)).astype(jnp.bfloat16)
    return iterate.astype(jnp.float32)

def muon(weight, moment, grad, flip):
    fresh = 0.5 * moment + grad
    matrix = fresh.T if flip else fresh
    start_x = (matrix / (jnp.sqrt(jnp.sum(matrix * matrix)) + NS_EPS)).astype(jnp.bfloat16)
    result = orthogonalize(start_x)
    if flip:
        result = result.T
    scale = 0.2 * math.sqrt(max(weight.shape))
    return (weight * (1.0 - MUON_RATE * MUON_DECAY) - MUON_RATE * scale * result, fresh)

def reference(tokens, cotangent, lengths, attn_w, up_w, down_w, norm_params, attn_mom, up_mom, down_mom, norm_m1, norm_m2):
    weights = (attn_w[0], attn_w[1], attn_w[2], attn_w[3], up_w, down_w, norm_params)
    seqs = tokens.astype(jnp.float32).reshape(SEQS, LEN, D)
    backs = cotangent.astype(jnp.float32).reshape(SEQS, LEN, D)

    def per_sequence(total, item):
        inputs, back, length = item

        def apply_layer(inputs_arg, *params):
            return forward(inputs_arg, *params, length)
        output, pull = jax.vjp(apply_layer, inputs, *weights)
        grads = pull(back)
        total = tuple((left + right for left, right in zip(total, grads[1:])))
        return (total, (output, grads[0]))
    start = tuple((jnp.zeros_like(weight) for weight in weights))
    totals, (outputs, input_grads) = lax.scan(per_sequence, start, (seqs, backs, lengths))
    mixed = outputs.reshape(TOKENS, D).astype(jnp.bfloat16)
    input_grad = input_grads.reshape(TOKENS, D)
    new_list = []
    moment_list = []
    for index in range(4):
        updated, fresh = muon(attn_w[index], attn_mom[index], totals[index], False)
        new_list.append(updated)
        moment_list.append(fresh)
    attn_new = jnp.stack(new_list)
    attn_moment = jnp.stack(moment_list)
    up_new, up_moment = muon(up_w, up_mom, totals[4], False)
    down_new, down_moment = muon(down_w, down_mom, totals[5], True)
    norm_grad = totals[6]
    norm_moment1 = 0.5 * norm_m1 + 0.5 * norm_grad
    norm_moment2 = 0.95 * norm_m2 + 0.05 * norm_grad * norm_grad
    first_hat = norm_moment1 / (1.0 - 0.5 ** STEP)
    second_hat = norm_moment2 / (1.0 - 0.95 ** STEP)
    norm_new = norm_params - ADAM_RATE * first_hat / (jnp.sqrt(second_hat) + 1e-08)
    return (mixed, input_grad, attn_new, attn_moment, up_new, up_moment, down_new, down_moment, norm_moment1, norm_moment2, norm_new)
```

```python
import functools
import math
import types

import jax
import jax.numpy as jnp
from jax import lax
from jax.experimental import pallas as pl
from jax.experimental.pallas import tpu as pltpu
from jax.sharding import PartitionSpec as P

HEADS = 12
HDIM = 64
BLOCK = 64
NS_STEPS = 5
STEP = 10


NORM_EPS = 1e-05
NS_EPS = 1e-07
COEF_A = 3.4445
COEF_B = -4.775
COEF_C = 2.0315
MUON_RATE = 0.15
MUON_DECAY = 0.1
ADAM_RATE = 0.2


def cut_along(array, dim, size):
    lengths = array.shape
    pieces = array.reshape(*lengths[:dim], size, lengths[dim] // size, *lengths[dim + 1 :])
    return jnp.moveaxis(pieces, dim, 0)


def sum_at_owner(array, axis, dim):
    size = lax.axis_size(axis)
    pieces = lax.all_to_all(cut_along(array, dim, size), axis, 0, 0, tiled=True)
    return jnp.sum(pieces.astype(jnp.float32), axis=0)


def sent_together(arrays, axis, dim, along):
    widths = [a.shape[along] for a in arrays]
    both = jnp.concatenate(arrays, axis=along)
    whole = sum_at_owner(both, axis, dim)
    return tuple(jnp.split(whole, [sum(widths[:k]) for k in range(1, len(widths))], axis=along))


def partner(array, axis, bit):
    return lax.ppermute(array, axis, [(i, i ^ 1 << bit) for i in range(lax.axis_size(axis))])


def contract_rows(left, right):
    return lax.dot_general(
        left, right, (((0,), (0,)), ((), ())), preferred_element_type=jnp.float32
    )


def contract_cols(left, right):
    return lax.dot_general(
        left, right, (((1,), (1,)), ((), ())), preferred_element_type=jnp.float32
    )


def norm_forward(resid, gain, bias):
    center = resid - jnp.mean(resid, -1, keepdims=True)
    spread = jnp.mean(center * center, -1, keepdims=True)
    scale_inv = lax.rsqrt(spread + NORM_EPS)
    normal_rows = center * scale_inv
    return (normal_rows, scale_inv, normal_rows * gain + bias)


def norm_back(normal_rows, scale_inv, grad_normed):
    return scale_inv * (
        grad_normed
        - jnp.mean(grad_normed, -1, keepdims=True)
        - normal_rows * jnp.mean(grad_normed * normal_rows, -1, keepdims=True)
    )


def smooth_gate(values):
    return jax.nn.gelu(values, approximate=True)


def features(proj, cosine, sine, weight_rows):
    count = proj.shape[0]
    soft = jax.nn.softplus(proj).reshape(count, HEADS, HDIM)
    both = jnp.concatenate([soft * cosine[:, None, None], soft * sine[:, None, None]], -1)
    return both * weight_rows[:, None, None]


def features_back(grad_feat, proj, cosine, sine, weight_rows):
    count = proj.shape[0]
    grad_soft = (
        grad_feat[..., :HDIM] * cosine[:, None, None] + grad_feat[..., HDIM:] * sine[:, None, None]
    )
    grad_soft = grad_soft * weight_rows[:, None, None]
    slope = jax.nn.sigmoid(proj).reshape(count, HEADS, HDIM)
    return (grad_soft * slope).reshape(count, HEADS * HDIM).astype(jnp.bfloat16)


def blocked(array):
    return array.reshape(array.shape[0] // BLOCK, BLOCK, array.shape[1], array.shape[2])


def attend_forward(qblock, kblock, vblock, lower):
    scores = (
        jnp.einsum("nihf,njhf->nhij", qblock, kblock, preferred_element_type=jnp.float32) * lower
    )
    scores_low = scores.astype(jnp.bfloat16)
    pairs = jnp.einsum("njhf,njhd->nhfd", kblock, vblock, preferred_element_type=jnp.float32)
    state = jnp.cumsum(pairs, 0) - pairs
    state_low = state.astype(jnp.bfloat16)
    key_sum = jnp.sum(kblock.astype(jnp.float32), 1)
    zsum = jnp.cumsum(key_sum, 0) - key_sum
    numer = jnp.einsum("nhij,njhd->nihd", scores_low, vblock, preferred_element_type=jnp.float32)
    numer = numer + jnp.einsum(
        "nihf,nhfd->nihd", qblock, state_low, preferred_element_type=jnp.float32
    )
    denom = jnp.transpose(jnp.sum(scores, -1), (0, 2, 1))
    denom = denom + jnp.einsum(
        "nihf,nhf->nih", qblock.astype(jnp.float32), zsum, precision=lax.Precision.HIGHEST
    )
    return (scores_low, state_low, zsum, denom, numer / denom[..., None])


def attend_backward(
    qblock, kblock, vblock, lower, scores_low, state_low, zsum, denom, result, grad_out
):
    grad_numer = (grad_out / denom[..., None]).astype(jnp.bfloat16)
    grad_denom = -jnp.sum(grad_out * result, -1) / denom
    grad_scores = jnp.einsum(
        "nihd,njhd->nhij", grad_numer, vblock, preferred_element_type=jnp.float32
    )
    grad_scores = ((grad_scores + jnp.transpose(grad_denom, (0, 2, 1))[..., None]) * lower).astype(
        jnp.bfloat16
    )
    grad_state = jnp.einsum(
        "nihf,nihd->nhfd", qblock, grad_numer, preferred_element_type=jnp.float32
    )
    grad_pairs = (jnp.cumsum(grad_state[::-1], 0)[::-1] - grad_state).astype(jnp.bfloat16)
    grad_z = jnp.einsum(
        "nih,nihf->nhf", grad_denom, qblock.astype(jnp.float32), precision=lax.Precision.HIGHEST
    )
    grad_ksum = jnp.cumsum(grad_z[::-1], 0)[::-1] - grad_z
    grad_qf = jnp.einsum("nhij,njhf->nihf", grad_scores, kblock, preferred_element_type=jnp.float32)
    grad_qf = grad_qf + jnp.einsum(
        "nihd,nhfd->nihf", grad_numer, state_low, preferred_element_type=jnp.float32
    )
    grad_qf = grad_qf + grad_denom[..., None] * zsum[:, None]
    grad_kf = jnp.einsum("nhij,nihf->njhf", grad_scores, qblock, preferred_element_type=jnp.float32)
    grad_kf = grad_kf + jnp.einsum(
        "njhd,nhfd->njhf", vblock, grad_pairs, preferred_element_type=jnp.float32
    )
    grad_kf = grad_kf + grad_ksum[:, None]
    grad_val = jnp.einsum(
        "nhij,nihd->njhd", scores_low, grad_numer, preferred_element_type=jnp.float32
    )
    grad_val = grad_val + jnp.einsum(
        "njhf,nhfd->njhd", kblock, grad_pairs, preferred_element_type=jnp.float32
    )
    return (grad_qf, grad_kf, grad_val.astype(jnp.bfloat16))


def newton_update(iterate, gram):
    poly = (
        COEF_B * gram.astype(jnp.float32)
        + COEF_C * jnp.dot(gram, gram, preferred_element_type=jnp.float32)
    ).astype(jnp.bfloat16)
    return (
        COEF_A * iterate.astype(jnp.float32)
        + jnp.dot(poly, iterate, preferred_element_type=jnp.float32)
    ).astype(jnp.bfloat16)


def orthogonalize(iterate):
    for step in range(NS_STEPS):
        gram = jnp.dot(iterate, iterate.T, preferred_element_type=jnp.float32).astype(jnp.bfloat16)
        iterate = newton_update(iterate, gram)
    return iterate


def on_device(
    tokens,
    cotangent,
    lengths,
    attn_w,
    up_w,
    down_w,
    norm_params,
    attn_mom,
    up_mom,
    down_mom,
    norm_m1,
    norm_m2,
):
    tensor_index = lax.axis_index("tensor")
    data_index = lax.axis_index("dp")
    tensor_count = lax.axis_size("tensor")
    length = lengths[0]
    rows_here = tokens.shape[0]
    wa_rows, up_block, down_block = (
        lax.all_gather(attn_w.astype(jnp.bfloat16), "dp", axis=1, tiled=True),
        lax.all_gather(up_w.astype(jnp.bfloat16), "dp", axis=0, tiled=True),
        lax.all_gather(down_w.astype(jnp.bfloat16), "dp", axis=1, tiled=True),
    )
    w_all = lax.all_gather(wa_rows, "tensor", axis=0, tiled=True)
    w_query = w_all[0]
    w_key = w_all[1]
    w_value = w_all[2]
    w_out = w_all[3]
    sequence = lax.all_gather(tokens, "tensor", axis=0, tiled=True)
    count = sequence.shape[0]
    width = sequence.shape[1]
    blocks = count // BLOCK
    start_row = tensor_index * rows_here

    def mine(array):
        return lax.dynamic_slice_in_dim(array, start_row, rows_here, 0)

    where = jnp.arange(count)
    live = (where < length).astype(jnp.float32)
    place = jnp.minimum(where, length - 1).astype(jnp.float32)
    theta = 0.5 * math.pi * place / length.astype(jnp.float32)
    cosine = jnp.cos(theta)
    sine = jnp.sin(theta)
    every_row = jnp.ones((count,), jnp.float32)
    query = jnp.dot(sequence, w_query, preferred_element_type=jnp.float32)
    key_proj = jnp.dot(sequence, w_key, preferred_element_type=jnp.float32)
    value = jnp.dot(sequence, w_value, preferred_element_type=jnp.float32)
    qblock = blocked(features(query, cosine, sine, every_row).astype(jnp.bfloat16))
    kblock = blocked(features(key_proj, cosine, sine, live).astype(jnp.bfloat16))
    vblock = value.astype(jnp.bfloat16).reshape(blocks, BLOCK, HEADS, HDIM)
    lower = jnp.tril(jnp.ones((BLOCK, BLOCK), jnp.float32))
    scores_low, state_low, zsum, denom, result = attend_forward(qblock, kblock, vblock, lower)
    attn_low = result.reshape(count, width).astype(jnp.bfloat16)
    branch = jnp.dot(attn_low, w_out, preferred_element_type=jnp.float32)
    normal_one, scale_one, hidden_in = norm_forward(
        sequence.astype(jnp.float32) + branch, norm_params[0], norm_params[1]
    )
    hidden_low = hidden_in.astype(jnp.bfloat16)
    pre = jnp.dot(hidden_low, up_block, preferred_element_type=jnp.float32)
    act_low = smooth_gate(pre).astype(jnp.bfloat16)
    ffn_rows = lax.psum_scatter(
        jnp.dot(act_low, down_block, preferred_element_type=jnp.float32).astype(jnp.bfloat16),
        "tensor",
        scatter_dimension=0,
        tiled=True,
    ).astype(jnp.float32)
    live_rows = mine(live)
    normal_two, scale_two, normed = norm_forward(
        mine(hidden_in) + ffn_rows, norm_params[2], norm_params[3]
    )
    mixed = (live_rows[:, None] * normed).astype(jnp.bfloat16)
    grad_y = cotangent.astype(jnp.float32) * live_rows[:, None]
    grad_g2 = jnp.sum(grad_y * normal_two, 0)
    grad_b2 = jnp.sum(grad_y, 0)
    grad_r2 = norm_back(normal_two, scale_two, grad_y * norm_params[2])
    grad_r2_all = lax.all_gather(grad_r2.astype(jnp.bfloat16), "tensor", axis=0, tiled=True)
    grad_down = contract_rows(act_low, grad_r2_all)
    grad_act = contract_cols(grad_r2_all, down_block)
    gate_out, gate_pull = jax.vjp(smooth_gate, pre)
    grad_pre = gate_pull(grad_act)[0].astype(jnp.bfloat16)
    grad_up = contract_rows(hidden_low, grad_pre)
    grad_hidden = (
        lax.psum_scatter(
            contract_cols(grad_pre, up_block).astype(jnp.bfloat16),
            "tensor",
            scatter_dimension=0,
            tiled=True,
        ).astype(jnp.float32)
        + grad_r2
    )
    normal_one_rows = mine(normal_one)
    grad_g1 = jnp.sum(grad_hidden * normal_one_rows, 0)
    grad_b1 = jnp.sum(grad_hidden, 0)
    grad_r1 = norm_back(normal_one_rows, mine(scale_one), grad_hidden * norm_params[0])
    grad_branch = lax.all_gather(grad_r1.astype(jnp.bfloat16), "tensor", axis=0, tiled=True)
    grad_attn = contract_cols(grad_branch, w_out).reshape(blocks, BLOCK, HEADS, HDIM)
    grad_qf, grad_kf, grad_val = attend_backward(
        qblock, kblock, vblock, lower, scores_low, state_low, zsum, denom, result, grad_attn
    )
    grad_query = features_back(
        grad_qf.reshape(count, HEADS, 2 * HDIM), query, cosine, sine, every_row
    )
    grad_key = features_back(grad_kf.reshape(count, HEADS, 2 * HDIM), key_proj, cosine, sine, live)
    grad_value = grad_val.reshape(count, width)
    input_grad = (
        grad_r1
        + contract_cols(mine(grad_query), w_query)
        + contract_cols(mine(grad_key), w_key)
        + contract_cols(mine(grad_value), w_value)
    )
    left_rows = jnp.where(tensor_index == 3, attn_low, sequence)
    right_all = jnp.stack((grad_query, grad_key, grad_value, grad_branch))
    right_rows = lax.dynamic_index_in_dim(right_all, tensor_index, 0, keepdims=False)
    grad_owned = contract_rows(left_rows, right_rows)
    norm_partial = jnp.stack((grad_g1, grad_b1, grad_g2, grad_b2))
    grad_a, grad_u, grad_d = (
        *sent_together((grad_owned.astype(jnp.bfloat16), grad_up.astype(jnp.bfloat16)), "dp", 0, 1),
        sum_at_owner(grad_down.astype(jnp.bfloat16), "dp", 1),
    )
    moment_a = 0.5 * attn_mom[0] + grad_a
    moment_u = 0.5 * up_mom + grad_u
    moment_d = 0.5 * down_mom + grad_d
    owner_pick = jax.nn.one_hot(tensor_index, 4, dtype=jnp.float32)
    squares = jnp.concatenate(
        (
            owner_pick * jnp.sum(moment_a * moment_a),
            jnp.stack((jnp.sum(moment_u * moment_u), jnp.sum(moment_d * moment_d))),
        )
    )
    totals, norm_grad = lax.psum((squares, norm_partial), ("dp", "tensor"))
    size_a = jnp.sqrt(jnp.sum(totals[:4] * owner_pick))
    size_u = jnp.sqrt(totals[4])
    size_d = jnp.sqrt(totals[5])
    start_a = (moment_a / (size_a + NS_EPS)).astype(jnp.bfloat16)
    start_u = (moment_u / (size_u + NS_EPS)).astype(jnp.bfloat16)
    start_d = (moment_d.T / (size_d + NS_EPS)).astype(jnp.bfloat16)
    whole_a, cols_u, cols_d = (
        lax.all_gather(start_a, "dp", axis=0, tiled=True),
        lax.all_gather(start_u, "dp", axis=0, tiled=True),
        lax.all_gather(start_d, "dp", axis=0, tiled=True),
    )
    orth_a = orthogonalize(whole_a)
    is_even = tensor_index % 2 == 0
    whole_u, whole_d = (
        lax.all_gather(cols_u, "tensor", axis=1, tiled=True),
        lax.all_gather(cols_d, "tensor", axis=1, tiled=True),
    )
    orth_whole = orthogonalize(jnp.where(is_even, whole_u, whole_d))
    block_cols = cols_u.shape[1]
    own_block = lax.dynamic_slice_in_dim(orth_whole, tensor_index * block_cols, block_cols, 1)
    partner_block = lax.dynamic_slice_in_dim(
        orth_whole, jnp.bitwise_xor(tensor_index, 1) * block_cols, block_cols, 1
    )
    fetched = partner(partner_block, "tensor", 0)
    orth_u = jnp.where(is_even, own_block, fetched)
    orth_d = jnp.where(is_even, fetched, own_block)
    span = moment_a.shape[0]

    def take_rows(array):
        return lax.dynamic_slice_in_dim(array, data_index * span, span, 0).astype(jnp.float32)

    ff_whole = up_block.shape[1] * tensor_count
    keep = 1.0 - MUON_RATE * MUON_DECAY
    new_a = attn_w[0] * keep - MUON_RATE * 0.2 * math.sqrt(width) * take_rows(orth_a)
    scale_ff = 0.2 * math.sqrt(max(width, ff_whole))
    new_u = up_w * keep - MUON_RATE * scale_ff * take_rows(orth_u)
    new_d = down_w * keep - MUON_RATE * scale_ff * take_rows(orth_d).T
    norm_moment1 = 0.5 * norm_m1 + 0.5 * norm_grad
    norm_moment2 = 0.95 * norm_m2 + 0.05 * norm_grad * norm_grad
    first_hat = norm_moment1 / (1.0 - 0.5**STEP)
    second_hat = norm_moment2 / (1.0 - 0.95**STEP)
    norm_new = norm_params - ADAM_RATE * first_hat / (jnp.sqrt(second_hat) + 1e-08)
    return (
        mixed,
        input_grad,
        new_a[None],
        moment_a[None],
        new_u,
        moment_u,
        new_d,
        moment_d,
        norm_moment1,
        norm_moment2,
        norm_new,
    )


BF = jnp.bfloat16
F32 = jnp.float32
MESH = pl.DeviceIdType.MESH
TENSOR = 4
QUARTER = 256
LANES = 128
VMEM_LIMIT = 62 << 20
GELU_C = math.sqrt(2.0 / math.pi)
GELU_A = 0.044715


def nn(left, right):
    return jnp.dot(left, right, preferred_element_type=F32)


def nt(left, right):
    return lax.dot_general(left, right, (((1,), (1,)), ((), ())), preferred_element_type=F32)


def tn(left, right):
    return lax.dot_general(left, right, (((0,), (0,)), ((), ())), preferred_element_type=F32)


def lanes_of(rows, cols=LANES):
    return lax.broadcasted_iota(jnp.int32, (rows, cols), 1)


def half_roll(array):
    return pltpu.roll(array, LANES // 2, 1)


def place():
    data = lax.axis_index("dp")
    tensor = lax.axis_index("tensor")
    return data, tensor


def greet(devices):
    barrier = pltpu.get_barrier_semaphore()
    for device in devices:
        pl.semaphore_signal(barrier, inc=1, device_id=device, device_id_type=MESH)
    pl.semaphore_wait(barrier, len(devices))


def send(src, dst, send_sem, recv_sem, device):
    copy = pltpu.make_async_remote_copy(
        src_ref=src,
        dst_ref=dst,
        send_sem=send_sem,
        recv_sem=recv_sem,
        device_id=device,
        device_id_type=MESH,
    )
    copy.start()
    return copy


def kernel_call(body, name, ins, outs, scratch, collective):
    in_names = list(ins)
    out_names = list(outs)
    scratch_names = list(scratch)

    def kernel(*refs):
        body(types.SimpleNamespace(**dict(zip(in_names + out_names + scratch_names, refs))))

    results = pl.pallas_call(
        kernel,
        name=name,
        out_shape=[outs[n] for n in out_names],
        in_specs=[pl.BlockSpec(memory_space=pltpu.VMEM)] * len(in_names),
        out_specs=[pl.BlockSpec(memory_space=pltpu.VMEM)] * len(out_names),
        scratch_shapes=[scratch[n] for n in scratch_names],
        compiler_params=pltpu.CompilerParams(
            collective_id=collective, has_side_effects=True, vmem_limit_bytes=VMEM_LIMIT
        ),
    )(*[ins[n] for n in in_names])
    return dict(zip(out_names, results))


def shape(*dims, dtype=BF):
    return jax.ShapeDtypeStruct(dims, dtype)


def dma(*dims):
    return pltpu.SemaphoreType.DMA(dims)


class GatherDp:
    def __init__(self, slot_of, sends, recvs, data, tensor, count):
        self.slot_of, self.sends, self.recvs = slot_of, sends, recvs
        self.data, self.tensor = data, tensor
        self.high_count = count // 2
        self.high, self.low = data // 2, data % 2
        self.partner = (self.high * 2 + 1 - self.low, tensor)
        self.copies = []

    def peer(self, step):
        return lax.rem(self.high + step, self.high_count) * 2 + self.low

    def start(self):
        mine = self.slot_of(self.data)
        n = self.high_count
        self.along = []
        for step in range(1, n):
            self.along.append(
                send(mine, mine, self.sends.at[step], self.recvs.at[step], (self.peer(step), self.tensor))
            )
        self.across = [send(mine, mine, self.sends.at[0], self.recvs.at[0], self.partner)]

    def forward(self):
        n = self.high_count
        for step in range(1, n):
            self.along[step - 1].wait_recv()
            slot = self.slot_of(self.peer(n - step))
            self.across.append(
                send(slot, slot, self.sends.at[n - 1 + step], self.recvs.at[n - 1 + step], self.partner)
            )

    def finish(self):
        for copy in self.across:
            copy.wait_recv()
        for copy in self.along + self.across:
            copy.wait_send()


def gather_body(count, r):
    data, tensor = place()
    core = tensor % 2
    high, low = data // 2, data % 2
    n = count // 2
    group = [(data, tensor ^ k) for k in (1, 2, 3)]
    along = [(lax.rem(high + k, n) * 2 + low, tensor) for k in range(1, n)]
    greet(group + along + [(high * 2 + 1 - low, tensor)])

    r.seq[tensor] = r.tokens[...]
    mine = r.seq.at[tensor]
    tok_core = send(mine, mine, r.tok_s.at[0], r.tok_r.at[0], group[0])
    tok_x = send(mine, mine, r.tok_s.at[1], r.tok_r.at[1], group[1])

    for k in (1, 2, 3):
        peer = tensor ^ k

        @pl.when(tensor < 3)
        def _():
            send(r.slabs.at[peer], r.wqkv.at[data, tensor], r.slab_s.at[k], r.slab_r.at[tensor], group[k - 1])

        @pl.when(tensor == 3)
        def _():
            send(r.halves.at[peer % 2], r.wo.at[data, peer % 2], r.slab_s.at[k], r.slab_r.at[3], group[k - 1])

    @pl.when(tensor < 3)
    def _():
        r.wqkv[data, tensor] = r.slabs[tensor]

    @pl.when(tensor == 3)
    def _():
        r.wo[data, core] = r.halves[core]

    for m in range(3):

        @pl.when(tensor != m)
        def _():
            pltpu.make_async_copy(r.wqkv.at[data, m], r.wqkv.at[data, m], r.slab_r.at[m]).wait()

    @pl.when(tensor != 3)
    def _():
        pltpu.make_async_copy(r.wo.at[data, core], r.wo.at[data, core], r.slab_r.at[3]).wait()

    r.wu[data] = r.up[...]
    r.wd[data] = r.down[...]
    gathers = [
        GatherDp(lambda d: r.wqkv.at[d], r.q_s, r.q_r, data, tensor, count),
        GatherDp(lambda d: r.wo.at[d, core], r.o_s, r.o_r, data, tensor, count),
        GatherDp(lambda d: r.wu.at[d], r.u_s, r.u_r, data, tensor, count),
        GatherDp(lambda d: r.wd.at[d], r.d_s, r.d_r, data, tensor, count),
    ]
    for g in gathers:
        g.start()
    tok_x.wait_recv()
    far = r.seq.at[tensor ^ 2]
    tok_f = send(far, far, r.tok_s.at[2], r.tok_r.at[2], group[0])
    for g in gathers:
        g.forward()
    for g in gathers:
        g.finish()
    share = []
    for d in range(count):
        part = r.wo.at[d, core]
        share.append(send(part, part, r.share_s.at[d], r.share_r.at[d], group[0]))
    for copy in share:
        copy.wait_send()
    for d in range(count):
        part = r.wo.at[d, 1 - core]
        pltpu.make_async_copy(part, part, r.share_r.at[d]).wait()
    tok_core.wait_recv()
    tok_f.wait_recv()
    for copy in (tok_core, tok_x, tok_f):
        copy.wait_send()
    for k in (1, 2, 3):

        @pl.when(tensor < 3)
        def _():
            pltpu.make_async_copy(r.slabs.at[0], r.slabs.at[0], r.slab_s.at[k]).wait()

        @pl.when(tensor == 3)
        def _():
            pltpu.make_async_copy(r.halves.at[0], r.halves.at[0], r.slab_s.at[k]).wait()


def gather_inputs(count, rows, tokens, slabs, halves, up, down):
    gather_sems = {}
    for key in "qoud":
        gather_sems[key + "_s"] = dma(count)
        gather_sems[key + "_r"] = dma(count)
    return kernel_call(
        functools.partial(gather_body, count),
        "gather_inputs",
        dict(tokens=tokens, slabs=slabs, halves=halves, up=up, down=down),
        dict(
            seq=shape(TENSOR, QUARTER, 768),
            wqkv=shape(count, 3, rows, 256),
            wo=shape(count, 2, rows // 2, 768),
            wu=shape(count, rows, 768),
            wd=shape(count, rows, 768),
        ),
        dict(
            tok_s=dma(3),
            tok_r=dma(3),
            slab_s=dma(4),
            slab_r=dma(4),
            share_s=dma(count),
            share_r=dma(count),
            **gather_sems,
        ),
        0,
    )


def softplus_and_slope(x):
    small = jnp.exp(-jnp.abs(x))
    soft = jnp.maximum(x, 0.0) + jnp.log1p(small)
    slope = jnp.where(x >= 0.0, 1.0, small) / (1.0 + small)
    return soft, slope


def spread_weights(r):
    low = lanes_of(768) < 64
    for m in range(3):
        w = r.wqkv[:, m].reshape(768, 256)
        first, second = w[:, :LANES].astype(F32), w[:, LANES:].astype(F32)
        turned = half_roll(first)
        if m < 2:
            parts = [
                jnp.where(low, first, turned),
                jnp.where(low, turned, first),
                jnp.where(low, second, half_roll(second)),
            ]
        else:
            parts = [jnp.where(low, p, 0.0) for p in (first, turned, second)]
        for h, part in enumerate(parts):
            r.wall[:, (3 * m + h) * LANES : (3 * m + h + 1) * LANES] = part.astype(BF)


def project(r):
    lane = lanes_of(QUARTER)

    def step(q, carry):
        both = nn(r.seq[q], r.wall[...])
        table, table_live = r.table[q], r.table_live[q]
        for h in range(3):
            soft, slope = softplus_and_slope(both[:, h * LANES : (h + 1) * LANES])
            r.qf[h, q] = (soft * table).astype(BF)
            r.qg[h, q] = slope * table
            soft, slope = softplus_and_slope(both[:, (3 + h) * LANES : (4 + h) * LANES])
            r.kf[h, q] = (soft * table_live).astype(BF)
            r.kg[h, q] = slope * table_live
            value = both[:, (6 + h) * LANES : (7 + h) * LANES]
            ones = jnp.where((lane == 64) | (lane == 65), 1.0, 0.0)
            r.va[h, q] = jnp.where(lane < 64, value, ones).astype(BF)
        return carry

    lax.fori_loop(0, TENSOR, step, 0)


def attend(r, q):
    lane = lanes_of(QUARTER)
    keep = lanes_of(QUARTER, QUARTER) <= lax.broadcasted_iota(jnp.int32, (QUARTER, QUARTER), 0)

    def head(h, carry):
        qf, kf, va = r.qf[h, q], r.kf[h, q], r.va[h, q]
        scores = jnp.where(keep, nt(qf, kf), 0.0).astype(BF)
        r.sb[h, q] = scores
        total = nn(scores, va)
        if q > 0:
            state = r.state[h].astype(BF)
            r.st[h, q] = state
            total = total + nn(qf, state)
        if q < TENSOR - 1:
            pairs = tn(kf, va)
            r.state[h] = pairs if q == 0 else r.state[h] + pairs
        inverse = 1.0 / total[:, 64:65]
        r.af[h, q] = jnp.where(lane < 64, total * inverse, inverse)
        return carry

    lax.fori_loop(0, 3, head, 0)
    zero, one, two = r.af[0, q], r.af[1, q], r.af[2, q]
    r.attn[q, :, :LANES] = jnp.where(lane < 64, zero, half_roll(one)).astype(BF)
    r.attn[q, :, LANES:] = jnp.where(lane < 64, two, 0.0).astype(BF)


def norm_rows(resid):
    center = resid - jnp.mean(resid, -1, keepdims=True)
    spread = jnp.mean(center * center, -1, keepdims=True)
    scale = lax.rsqrt(spread + NORM_EPS)
    return center * scale, scale


def norm_rows_back(normal, scale, grad):
    return scale * (
        grad
        - jnp.mean(grad, -1, keepdims=True)
        - normal * jnp.mean(grad * normal, -1, keepdims=True)
    )


class Group:
    def __init__(self):
        self.data, self.tensor = place()
        self.far, self.core = self.tensor // 2, self.tensor % 2

    def device(self, k):
        return (self.data, self.tensor ^ k)


def spread_quarter(r, g, buf, sends, recvs):
    own = buf.at[g.tensor]
    far = send(own, own, sends.at[0], recvs.at[0], g.device(2))
    near = send(own, own, sends.at[1], recvs.at[1], g.device(1))

    def arrived_near():
        near.wait_recv()

    def arrived_far():
        far.wait_recv()
        slot = buf.at[g.tensor ^ 2]
        passed = send(slot, slot, sends.at[2], recvs.at[2], g.device(1))
        passed.wait_recv()
        for copy in (far, near, passed):
            copy.wait_send()

    return arrived_near, arrived_far


class SumQuarters:
    def __init__(self, r, g, slot):
        self.r, self.g, self.slot = r, g, slot

    def near_out(self, j, value):
        r, k = self.r, self.slot * 2 + j
        r.near_send[k] = value.astype(BF)
        self.copy = send(r.near_send.at[k], r.near_recv.at[k], r.near_s.at[k], r.near_r.at[k], self.g.device(1))
        self.copies = getattr(self, "copies", []) + [self.copy]

    def near_in(self, j, value):
        self.copies[j].wait_recv()
        return value + self.r.near_recv[self.slot * 2 + j].astype(F32)

    def far_out(self, value):
        r, k = self.r, self.slot
        r.far_send[k] = value.astype(BF)
        self.far = send(r.far_send.at[k], r.far_recv.at[k], r.far_s.at[k], r.far_r.at[k], self.g.device(2))

    def far_in(self, value):
        self.far.wait_recv()
        value = value + self.r.far_recv[self.slot].astype(F32)
        for copy in self.copies + [self.far]:
            copy.wait_send()
        return value


def feed(r, q):
    pre = nn(r.hb[q], r.wu[...].reshape(768, 768))
    inner = jnp.tanh(GELU_C * (pre + GELU_A * pre * pre * pre))
    half = 0.5 * (1.0 + inner)
    r.gp[q] = half + 0.5 * pre * (1.0 - inner * inner) * (GELU_C * (1.0 + 3.0 * GELU_A * pre * pre))
    hid = (pre * half).astype(BF)
    r.hid[q] = hid
    return nt(hid, r.wd[...].reshape(768, 768))


def feed_back(r, q):
    grad_act = nn(r.dr2[q], r.wd[...].reshape(768, 768))
    grad_pre = (grad_act * r.gp[q]).astype(BF)
    r.du[q] = grad_pre
    return nt(grad_pre, r.wu[...].reshape(768, 768))


def attend_back(r, g, q):
    lane = lanes_of(QUARTER)
    keep = lanes_of(QUARTER, QUARTER) <= lax.broadcasted_iota(jnp.int32, (QUARTER, QUARTER), 0)
    dr1 = r.dr1[q]

    def head(h, carry):
        grad = nt(dr1, r.woh[h])
        af = r.af[h, q]
        inverse = af[:, 64:65]
        dden = -jnp.sum(grad * af, -1, keepdims=True) * inverse
        dden_low = dden.astype(BF).astype(F32)
        extra = jnp.where(lane == 64, dden_low, jnp.where(lane == 65, dden - dden_low, 0.0))
        dnum = jnp.where(lane < 64, grad * inverse, extra).astype(BF)
        qf, kf, va, sb = r.qf[h, q], r.kf[h, q], r.va[h, q], r.sb[h, q]
        ds = jnp.where(keep, nt(dnum, va), 0.0).astype(BF)
        dqf = nn(ds, kf)
        if q > 0:
            dqf = dqf + nt(dnum, r.st[h, q])
        dkf = tn(ds, qf)
        dv = tn(sb, dnum)
        if q < TENSOR - 1:
            dkv = r.state[h].astype(BF)
            dkf = dkf + nt(va, dkv)
            dv = dv + nn(kf, dkv)
        if q > 0:
            pairs = tn(qf, dnum)
            r.state[h] = pairs if q == TENSOR - 1 else r.state[h] + pairs
        dqf = dqf * r.qg[h, q]
        dkf = dkf * r.kg[h, q]
        r.fold[0, h] = dqf + half_roll(dqf)
        r.fold[1, h] = dkf + half_roll(dkf)
        r.fold[2, h] = dv
        return carry

    lax.fori_loop(0, 3, head, 0)
    for m in range(3):
        second = r.fold[m, 1] if m < 2 else half_roll(r.fold[m, 1])
        r.dqkv[q, :, 256 * m : 256 * m + LANES] = jnp.where(lane < 64, r.fold[m, 0], second).astype(BF)
        r.dqkv[q, :, 256 * m + LANES : 256 * (m + 1)] = jnp.where(lane < 64, r.fold[m, 2], 0.0).astype(BF)
    total = None
    for m in range(3):
        part = nt(r.dqkv[q, :, 256 * m : 256 * (m + 1)], r.wqkv[:, m].reshape(768, 256))
        total = part if total is None else total + part
    r.ig[q] = total


def layer_body(r):
    g = Group()
    tensor, far, core = g.tensor, g.far, g.core
    greet([g.device(k) for k in (1, 2, 3)])
    spread_weights(r)
    for t in range(TENSOR):
        r.wop[t, :192] = r.wo[192 * t : 192 * (t + 1)]
        r.wop[t, 192:] = jnp.zeros((64, 768), BF)
    for h in range(3):
        r.woh[h, :64] = r.wo[pl.ds(pl.multiple_of(192 * tensor + 64 * h, 64), 64)]
        r.woh[h, 64:] = jnp.zeros((64, 768), BF)
    project(r)

    copies = [[], []]
    for j in range(2):
        attend(r, 2 * j)
        attend(r, 2 * j + 1)
        mine, other = 2 * j + core, 2 * j + 1 - core
        for k in (2, 1, 3):
            quarter = mine if k == 2 else other
            copies[j].append(
                send(r.attn.at[quarter], r.aall.at[tensor, j], r.attn_s.at[j, k], r.attn_r.at[j, k], g.device(k))
            )
        r.aall[tensor, j] = r.attn[mine]

    gain1, bias1, gain2, bias2 = (r.norms[k : k + 1] for k in range(4))
    hs = []
    for own in (False, True):
        j = far if own else 1 - far
        for copy in copies[1] if False else []:
            copy.wait_recv()
        if not own:
            for group_copies in copies:
                for copy in group_copies:
                    copy.wait_recv()
        q = 2 * j + core
        branch = nn(r.aall[0, j], r.wop[0])
        for t in range(1, TENSOR):
            branch = branch + nn(r.aall[t, j], r.wop[t])
        normal, scale = norm_rows(r.seq[q].astype(F32) + branch)
        hidden = normal * gain1 + bias1
        r.hb[q] = hidden.astype(BF)
        if own:
            r.n1[...] = normal
            r.s1[...] = jnp.broadcast_to(scale, (QUARTER, LANES))
            r.h1[...] = hidden
        hs.append(send(r.hb.at[q], r.hb.at[q], r.h_s.at[int(own)], r.h_r.at[int(own)], g.device(1)))
    for group_copies in copies:
        for copy in group_copies:
            copy.wait_send()

    total = SumQuarters(r, g, 0)
    kept = feed(r, tensor ^ 2)
    hs[0].wait_recv()
    total.near_out(0, feed(r, tensor ^ 3))
    kept = total.near_in(0, kept)
    total.far_out(kept)
    hs[1].wait_recv()
    total.near_out(1, feed(r, tensor ^ 1))
    kept = feed(r, tensor)
    kept = total.far_in(total.near_in(1, kept))
    for copy in hs:
        copy.wait_send()

    n2, s2 = norm_rows(r.h1[...] + kept)
    live = r.live[...]
    r.mixed[...] = (live * (n2 * gain2 + bias2)).astype(BF)
    dy = live * r.cotangent[...].astype(F32)
    r.partial[2:3] = jnp.sum(dy * n2, 0, keepdims=True)
    r.partial[3:4] = jnp.sum(dy, 0, keepdims=True)
    dr2 = norm_rows_back(n2, s2, dy * gain2)
    r.dr2f[...] = dr2
    r.dr2[tensor] = dr2.astype(BF)
    near, distant = spread_quarter(r, g, r.dr2, r.dr2_s, r.dr2_r)

    total = SumQuarters(r, g, 1)
    kept_own = feed_back(r, tensor)
    near()
    total.near_out(0, feed_back(r, tensor ^ 1))
    distant()
    total.near_out(1, feed_back(r, tensor ^ 3))
    kept = feed_back(r, tensor ^ 2)
    total.far_out(total.near_in(1, kept))
    kept_own = total.near_in(0, kept_own)
    r.dh[...] = kept_own
    grad = tn(r.hb[...].reshape(1024, 768), r.du[...].reshape(1024, 768))
    r.gu[...] = grad.astype(BF).reshape(r.gu.shape)
    grad = tn(r.dr2[...].reshape(1024, 768), r.hid[...].reshape(1024, 768))
    r.gd[...] = grad.astype(BF).reshape(r.gd.shape)
    dh = total.far_in(r.dh[...]) + r.dr2f[...]

    n1 = r.n1[...]
    r.partial[0:1] = jnp.sum(dh * n1, 0, keepdims=True)
    r.partial[1:2] = jnp.sum(dh, 0, keepdims=True)
    dr1 = norm_rows_back(n1, r.s1[:, :1], dh * gain1)
    r.dr1f[...] = dr1
    r.dr1[tensor] = dr1.astype(BF)
    near, distant = spread_quarter(r, g, r.dr1, r.dr1_s, r.dr1_r)
    near()
    distant()

    for q in (3, 2, 1, 0):
        attend_back(r, g, q)
    total = SumQuarters(r, g, 2)
    total.near_out(0, r.ig[tensor ^ 3])
    total.near_out(1, r.ig[tensor ^ 1])
    total.far_out(total.near_in(0, r.ig[tensor ^ 2]))
    grad = tn(r.seq[...].reshape(1024, 768), r.dqkv[...].reshape(1024, 768)).astype(BF)
    for m in range(3):
        r.ga[:, m] = grad[:, 256 * m : 256 * (m + 1)].reshape(r.ga.shape[0], r.ga.shape[2], 256)
    grad = tn(r.attn[...].reshape(1024, 256), r.dr1[...].reshape(1024, 768)).astype(BF)
    r.go[...] = grad[:192].reshape(r.go.shape)
    r.input_grad[...] = total.far_in(total.near_in(1, r.ig[tensor])) + r.dr1f[...]


def layer(count, rows, gathered, wo, cotangent, norms, live, table, table_live):
    v = pltpu.VMEM
    return kernel_call(
        layer_body,
        "layer",
        dict(
            seq=gathered["seq"],
            wqkv=gathered["wqkv"],
            wo=wo,
            wu=gathered["wu"],
            wd=gathered["wd"],
            cotangent=cotangent,
            norms=norms,
            live=live,
            table=table,
            table_live=table_live,
        ),
        dict(
            mixed=shape(QUARTER, 768),
            input_grad=shape(QUARTER, 768, dtype=F32),
            gu=shape(count, rows, 768),
            gd=shape(count, rows, 768),
            ga=shape(count, 3, rows, 256),
            go=shape(2, rows, 768),
            partial=shape(4, 768, dtype=F32),
        ),
        dict(
            wall=v((768, 9 * LANES), BF),
            wop=v((TENSOR, 256, 768), BF),
            woh=v((3, LANES, 768), BF),
            qf=v((3, TENSOR, QUARTER, LANES), BF),
            kf=v((3, TENSOR, QUARTER, LANES), BF),
            va=v((3, TENSOR, QUARTER, LANES), BF),
            qg=v((3, TENSOR, QUARTER, LANES), F32),
            kg=v((3, TENSOR, QUARTER, LANES), F32),
            af=v((3, TENSOR, QUARTER, LANES), F32),
            sb=v((3, TENSOR, QUARTER, QUARTER), BF),
            st=v((3, TENSOR, LANES, LANES), BF),
            state=v((3, LANES, LANES), F32),
            attn=v((TENSOR, QUARTER, 256), BF),
            aall=v((TENSOR, 2, QUARTER, 256), BF),
            hb=v((TENSOR, QUARTER, 768), BF),
            n1=v((QUARTER, 768), F32),
            s1=v((QUARTER, LANES), F32),
            h1=v((QUARTER, 768), F32),
            hid=v((TENSOR, QUARTER, 768), BF),
            gp=v((TENSOR, QUARTER, 768), F32),
            du=v((TENSOR, QUARTER, 768), BF),
            dr2=v((TENSOR, QUARTER, 768), BF),
            dr2f=v((QUARTER, 768), F32),
            dr1=v((TENSOR, QUARTER, 768), BF),
            dr1f=v((QUARTER, 768), F32),
            dh=v((QUARTER, 768), F32),
            fold=v((3, 3, QUARTER, LANES), F32),
            dqkv=v((TENSOR, QUARTER, 768), BF),
            ig=v((TENSOR, QUARTER, 768), F32),
            near_send=v((6, QUARTER, 768), BF),
            near_recv=v((6, QUARTER, 768), BF),
            far_send=v((3, QUARTER, 768), BF),
            far_recv=v((3, QUARTER, 768), BF),
            near_s=dma(6),
            near_r=dma(6),
            far_s=dma(3),
            far_r=dma(3),
            attn_s=dma(2, 4),
            attn_r=dma(2, 4),
            h_s=dma(2),
            h_r=dma(2),
            dr2_s=dma(3),
            dr2_r=dma(3),
            dr1_s=dma(3),
            dr1_r=dma(3),
        ),
        1,
    )


def await_bytes(ref, sem):
    pltpu.make_async_copy(ref, ref, sem).wait()


class ReduceDp:
    def __init__(self, src, low_buf, high_send, high_buf, sems, data, tensor, count):
        self.src, self.low_buf, self.high_send, self.high_buf = src, low_buf, high_send, high_buf
        self.low_s, self.low_r, self.high_s, self.high_r = sems
        self.tensor, self.n = tensor, count // 2
        self.high, self.low = data // 2, data % 2

    def at(self, step):
        return lax.rem(self.high + step, self.n)

    def start(self):
        partner = (self.high * 2 + 1 - self.low, self.tensor)
        self.across = {}
        for step in list(range(1, self.n)) + [0]:
            h = self.at(step)
            self.across[step] = send(
                self.src.at[h * 2 + 1 - self.low],
                self.low_buf.at[h],
                self.low_s.at[step],
                self.low_r.at[step],
                partner,
            )

    def pair(self, step):
        self.across[step].wait_recv()
        h = self.at(step)
        return self.src[h * 2 + self.low].astype(F32) + self.low_buf[h].astype(F32)

    def forward(self):
        self.along = []
        for step in range(1, self.n):
            self.high_send[step] = self.pair(step).astype(BF)
            self.along.append(
                send(
                    self.high_send.at[step],
                    self.high_buf.at[step],
                    self.high_s.at[step],
                    self.high_r.at[step],
                    (self.at(step) * 2 + self.low, self.tensor),
                )
            )

    def finish(self):
        total = self.pair(0)
        for step in range(1, self.n):
            self.along[step - 1].wait_recv()
            total = total + self.high_buf[step].astype(F32)
        for copy in list(self.across.values()) + self.along:
            copy.wait_send()
        return total


def assemble(r, core_rows):
    low = lanes_of(core_rows) < 64
    for pair in range(2):
        even, odd = r.abuf[2 * pair].astype(F32), r.abuf[2 * pair + 1].astype(F32)
        turned = half_roll(odd[:, :LANES])
        base = 3 * LANES * pair
        r.grad_a[:, base : base + LANES] = even[:, :LANES]
        r.grad_a[:, base + LANES : base + 2 * LANES] = jnp.where(low, even[:, LANES:], turned)
        r.grad_a[:, base + 2 * LANES : base + 3 * LANES] = jnp.where(low, turned, half_roll(odd[:, LANES:]))


def sum_partials(r, data, tensor, count):
    r.pbuf[tensor] = r.partial[...]
    copies = []
    for k in (1, 2, 3):
        copies.append(send(r.partial, r.pbuf.at[tensor], r.pt_s.at[k], r.pt_r.at[k], (data, tensor ^ k)))
    for copy in copies:
        copy.wait()
    r.psum[...] = ((r.pbuf[0] + r.pbuf[1]) + r.pbuf[2]) + r.pbuf[3]
    r.qbuf[data] = r.psum[...]
    copies = []
    for k in range(1, count):
        copies.append(
            send(r.psum, r.qbuf.at[data], r.pd_s.at[k], r.pd_r.at[k], (lax.rem(data + k, count), tensor))
        )

    def finish():
        for copy in copies:
            copy.wait()
        total = r.qbuf[0]
        for d in range(1, count):
            total = total + r.qbuf[d]
        r.norm_grad[...] = total

    return finish


def reduce_body(count, rows, r):
    data, tensor = place()
    far, core = tensor // 2, tensor % 2
    high, low = data // 2, data % 2
    other = high * 2 + 1 - low
    n = count // 2
    greet(
        [(data, tensor ^ k) for k in (1, 2, 3)]
        + [(lax.rem(data + k, count), tensor) for k in range(1, count)]
        + [(other, tensor ^ 1)]
    )
    finish_partials = sum_partials(r, data, tensor, count)
    sums = {}
    for key in "dua":
        sums[key] = ReduceDp(
            *(getattr(r, name + key) for name in ("g", "low", "hs", "hb")),
            [getattr(r, name + key) for name in ("ls_", "lr_", "hs_", "hr_")],
            data,
            tensor,
            count,
        )
    for key in "dua":
        sums[key].start()
    out_low = send(r.go.at[1 - low], r.olow, r.o_s.at[0], r.o_r.at[0], (other, tensor))
    for key in "dua":
        sums[key].forward()

    out_low.wait_recv()
    out_part = r.go[low].astype(F32) + r.olow[...].astype(F32)
    r.osend[...] = out_part.astype(BF)
    for k in range(1, n):

        @pl.when(lax.rem(high + k, n) == tensor)
        def _():
            send(r.osend, r.ohigh.at[k], r.o_s.at[1], r.o_r.at[k], (tensor * 2 + low, tensor))

    wide = 768
    here = pl.ds(pl.multiple_of(data * rows, rows), rows)

    def cols(t):
        return pl.ds(pl.multiple_of(t * wide, wide), wide)

    moment = 0.5 * r.down_mom[...] + sums["d"].finish()
    r.mom_d[...] = moment
    r.xsd[...] = moment.astype(BF)
    moment = 0.5 * r.up_mom[...] + sums["u"].finish()
    r.mom_u[...] = moment
    r.xsu[...] = moment.astype(BF)
    own = r.xmat.at[here, cols(tensor)]
    mine = r.xmat.at[here, cols(tensor ^ 2)]

    @pl.when(far == 0)
    def _():
        r.xmat[here, cols(tensor)] = r.xsu[...]
        send(r.xsd, own, r.swap_s, r.swap_r, (data, tensor ^ 2))

    @pl.when(far == 1)
    def _():
        r.xmat[here, cols(tensor)] = r.xsd[...]
        send(r.xsu, own, r.swap_s, r.swap_r, (data, tensor ^ 2))

    gathers = [
        GatherDp(lambda d: r.xmat.at[pl.ds(pl.multiple_of(d * rows, rows), rows), cols(tensor)], r.x_s, r.x_r, data, tensor, count),
        GatherDp(lambda d: r.xmat.at[pl.ds(pl.multiple_of(d * rows, rows), rows), cols(tensor ^ 2)], r.y_s, r.y_r, data, tensor, count),
    ]
    gathers[0].start()
    await_bytes(mine, r.swap_r)
    gathers[1].start()

    total = sums["a"].finish()
    for m in range(3):
        r.asend[m] = total[m].astype(BF)
    for m in range(3):

        @pl.when(tensor != m)
        def _():
            send(r.asend.at[m], r.abuf.at[tensor], r.a_s.at[m], r.a_r.at[tensor], (data, m))

        @pl.when(tensor == m)
        def _():
            r.abuf[tensor] = r.asend[m]

    for k in range(1, n):

        @pl.when(high == tensor)
        def _():
            await_bytes(r.ohigh.at[k], r.o_r.at[k])

    @pl.when(high == tensor)
    def _():
        whole = out_part
        for k in range(1, n):
            whole = whole + r.ohigh[k].astype(F32)
        r.grad_a[...] = whole
        r.oout[...] = whole.astype(BF)

    @pl.when((high == tensor) & (tensor != 3))
    def _():
        send(r.oout, r.oin, r.o_s.at[2], r.oin_r, (data, 3))

    @pl.when((tensor == 3) & (high != 3))
    def _():
        await_bytes(r.oin, r.oin_r)
        r.grad_a[...] = r.oin[...].astype(F32)

    for t in range(TENSOR):

        @pl.when((tensor < 3) & (tensor != t))
        def _():
            await_bytes(r.abuf.at[t], r.a_r.at[t])

    @pl.when(tensor < 3)
    def _():
        assemble(r, rows)

    moment = 0.5 * r.attn_mom[...] + r.grad_a[...]
    r.mom_a[...] = moment
    r.xsa[...] = moment.astype(BF)

    slot = r.xa.at[here]
    there = (high * 2 + core, far * 2 + 1)

    @pl.when((core == 1) & (low == 1))
    def _():
        r.xa[here] = r.xsa[...]

    @pl.when((core == 0) | (low == 0))
    def _():
        send(r.xsa, slot, r.e_s.at[0], r.e_r.at[low], there)

    def rows_of(d):
        return r.xa.at[pl.ds(pl.multiple_of(d * rows, rows), rows)]

    for side in range(2):
        rows_from = high * 2 + side

        @pl.when((core == 1) & ((low == 0) | (side == 0)))
        def _():
            await_bytes(rows_of(rows_from), r.e_r.at[side])

        @pl.when(core == 1)
        def _():
            for k in range(1, n):
                part = rows_of(rows_from)
                send(part, part, r.f_s.at[side, k], r.f_r.at[side, k], (lax.rem(high + k, n) * 2 + low, tensor))

    for g in gathers:
        g.forward()
    for g in gathers:
        g.finish()

    @pl.when(core == 1)
    def _():
        for t, s in ((tensor, 0), (tensor ^ 2, 1)):
            block = r.xmat.at[:, cols(t)]
            send(block, block, r.j_s.at[s], r.j_r.at[s], (data, tensor ^ 1))

    @pl.when(core == 1)
    def _():
        for side in range(2):
            for k in range(1, n):
                part = rows_of(lax.rem(high + n - k, n) * 2 + side)
                await_bytes(part, r.f_r.at[side, k])
                await_bytes(part, r.f_s.at[side, k])
        for s in range(2):
            await_bytes(r.xmat.at[:, cols(0)], r.j_s.at[s])

    @pl.when(core == 0)
    def _():
        for s in range(2):
            await_bytes(r.xmat.at[:, cols(0)], r.j_r.at[s])

    await_bytes(r.xsd, r.swap_s)
    out_low.wait_send()

    @pl.when(high != tensor)
    def _():
        await_bytes(r.osend, r.o_s.at[1])

    @pl.when((high == tensor) & (tensor != 3))
    def _():
        await_bytes(r.oout, r.o_s.at[2])

    for m in range(3):

        @pl.when(tensor != m)
        def _():
            await_bytes(r.asend.at[m], r.a_s.at[m])

    @pl.when((core == 0) | (low == 0))
    def _():
        await_bytes(r.xsa, r.e_s.at[0])

    finish_partials()


def reduce_and_gather(count, rows, grads, attn_mom, up_mom, down_mom):
    v = pltpu.VMEM
    n = count // 2
    scratch = dict(
        pbuf=v((TENSOR, 4, 768), F32),
        psum=v((4, 768), F32),
        qbuf=v((count, 4, 768), F32),
        pt_s=dma(4),
        pt_r=dma(4),
        pd_s=dma(count),
        pd_r=dma(count),
        olow=v((rows, 768), BF),
        osend=v((rows, 768), BF),
        ohigh=v((n, rows, 768), BF),
        oout=v((rows, 768), BF),
        oin=v((rows, 768), BF),
        o_s=dma(3),
        o_r=dma(n),
        oin_r=pltpu.SemaphoreType.DMA,
        xsd=v((rows, 768), BF),
        xsu=v((rows, 768), BF),
        xsa=v((rows, 768), BF),
        swap_s=pltpu.SemaphoreType.DMA,
        swap_r=pltpu.SemaphoreType.DMA,
        x_s=dma(count),
        x_r=dma(count),
        y_s=dma(count),
        y_r=dma(count),
        asend=v((3, rows, 256), BF),
        abuf=v((TENSOR, rows, 256), BF),
        a_s=dma(3),
        a_r=dma(TENSOR),
        grad_a=v((rows, 768), F32),
        e_s=dma(1),
        e_r=dma(2),
        f_s=dma(2, n),
        f_r=dma(2, n),
        j_s=dma(2),
        j_r=dma(2),
    )
    for key in "dua":
        part = (3, rows, 256) if key == "a" else (rows, 768)
        for name in ("low", "hs", "hb"):
            scratch[name + key] = v((n,) + part, BF)
        for name in ("ls_", "lr_", "hs_", "hr_"):
            scratch[name + key] = dma(n)
    return kernel_call(
        functools.partial(reduce_body, count, rows),
        "reduce_and_gather",
        dict(
            gu=grads["gu"],
            gd=grads["gd"],
            ga=grads["ga"],
            go=grads["go"],
            partial=grads["partial"],
            attn_mom=attn_mom,
            up_mom=up_mom,
            down_mom=down_mom,
        ),
        dict(
            mom_a=shape(rows, 768, dtype=F32),
            mom_u=shape(rows, 768, dtype=F32),
            mom_d=shape(rows, 768, dtype=F32),
            norm_grad=shape(4, 768, dtype=F32),
            xmat=shape(768, TENSOR * 768),
            xa=shape(768, 768),
        ),
        scratch,
        2,
    )


def square_sum(ref, width):
    def step(k, total):
        part = ref[pl.ds(pl.multiple_of(k * 96, 96), 96)].astype(F32)
        return total + part * part

    total = lax.fori_loop(0, 8, step, jnp.zeros((96, width), F32))
    return jnp.sum(total)


def newton(x, gram, poly, chunk):
    width = x.shape[1]
    start = 1.0 / (jnp.sqrt(square_sum(x, width)) + NS_EPS)
    edges = [slice(k * 256, (k + 1) * 256) for k in range(3)]

    def step(k, first):
        scale = jnp.where(k == 0, first, 1.0)
        for a in range(3):
            for b in range(a, 3):
                block = (nt(x[edges[a], :], x[edges[b], :]) * (scale * scale)).astype(BF)
                gram[edges[a], edges[b]] = block
                if b > a:
                    gram[edges[b], edges[a]] = block.T
        for a in range(3):
            for b in range(a, 3):
                block = COEF_C * nt(gram[edges[a], :], gram[edges[b], :])
                block = (block + COEF_B * gram[edges[a], edges[b]].astype(F32)).astype(BF)
                poly[edges[a], edges[b]] = block
                if b > a:
                    poly[edges[b], edges[a]] = block.T

        def columns(c, carry):
            at = pl.ds(pl.multiple_of(c * chunk, chunk), chunk)
            old = x[:, at]
            x[:, at] = (scale * (COEF_A * old.astype(F32) + nn(poly[...], old))).astype(BF)
            return carry

        lax.fori_loop(0, width // chunk, columns, 0)
        return first

    lax.fori_loop(0, NS_STEPS, step, start)


def ortho_body(count, rows, r):
    data, tensor = place()
    far, core = tensor // 2, tensor % 2
    high, low = data // 2, data % 2
    other = high * 2 + 1 - low
    greet([(data, tensor ^ k) for k in (1, 2, 3)] + [(other, tensor), (other, tensor ^ 1)])
    here = pl.ds(pl.multiple_of(data * rows, rows), rows)
    there = pl.ds(pl.multiple_of(other * rows, rows), rows)

    def cols(t):
        return pl.ds(pl.multiple_of(t * 768, 768), 768)

    @pl.when(core == 0)
    def _():
        r.big[...] = r.xmat[...]
        newton(r.big, r.gram, r.poly, 512)

    @pl.when(core == 1)
    def _():
        r.small[...] = r.xa[...]
        newton(r.small, r.gram, r.poly, 768)

    for m, out, recv in ((0, r.o_u, 0), (1, r.o_d, 1)):

        @pl.when((core == 0) & (far == m))
        def _():
            for k in (1, 2, 3):
                send(r.big.at[here, cols(tensor ^ k)], out, r.w_s.at[k], r.w_r.at[recv], (data, tensor ^ k))
            out[...] = r.big[here, cols(tensor)]

        @pl.when((core == 1) | (far != m))
        def _():
            await_bytes(out, r.w_r.at[recv])

    owner = far * 2 + low

    @pl.when((core == 1) & (low == 1))
    def _():
        r.o_a[...] = r.small[here]
        send(r.small.at[there], r.o_a, r.v_s.at[0], r.v_r, (other, owner))

    @pl.when((core == 1) & (low == 0))
    def _():
        send(r.small.at[here], r.o_a, r.v_s.at[0], r.v_r, (data, owner))
        send(r.small.at[there], r.o_a, r.v_s.at[1], r.v_r, (other, owner))

    @pl.when((core == 0) | (low == 0))
    def _():
        await_bytes(r.o_a, r.v_r)

    @pl.when(core == 0)
    def _():
        for k in (1, 2, 3):
            await_bytes(r.o_u, r.w_s.at[k])

    @pl.when(core == 1)
    def _():
        await_bytes(r.o_a, r.v_s.at[0])

    @pl.when((core == 1) & (low == 0))
    def _():
        await_bytes(r.o_a, r.v_s.at[1])


def orthogonalize_all(count, rows, xmat, xa):
    v = pltpu.VMEM
    return kernel_call(
        functools.partial(ortho_body, count, rows),
        "orthogonalize",
        dict(xmat=xmat, xa=xa),
        dict(o_u=shape(rows, 768), o_d=shape(rows, 768), o_a=shape(rows, 768)),
        dict(
            big=v((768, TENSOR * 768), BF),
            small=v((768, 768), BF),
            gram=v((768, 768), BF),
            poly=v((768, 768), BF),
            w_s=dma(4),
            w_r=dma(2),
            v_s=dma(2),
            v_r=pltpu.SemaphoreType.DMA,
        ),
        3,
    )


def step_on_device(
    tokens,
    cotangent,
    lengths,
    attn_w,
    up_w,
    down_w,
    norm_params,
    attn_mom,
    up_mom,
    down_mom,
    norm_m1,
    norm_m2,
):
    count = lax.axis_size("dp")
    tensor = lax.axis_index("tensor")
    rows = attn_w.shape[1]
    length = lengths[0]
    where = jnp.arange(TENSOR * QUARTER)
    live = (where < length).astype(F32)
    theta = 0.5 * math.pi * jnp.minimum(where, length - 1).astype(F32) / length.astype(F32)
    table = jnp.where(
        jnp.arange(LANES)[None, :] < HDIM, jnp.cos(theta)[:, None], jnp.sin(theta)[:, None]
    )
    table_live = (table * live[:, None]).reshape(TENSOR, QUARTER, LANES)
    table = table.reshape(TENSOR, QUARTER, LANES)
    live_rows = lax.dynamic_slice_in_dim(live, tensor * QUARTER, QUARTER, 0)[:, None]
    shard = attn_w[0].astype(BF)
    slabs = jnp.transpose(shard.reshape(rows, TENSOR, 192), (1, 0, 2))
    slabs = jnp.pad(slabs, ((0, 0), (0, 0), (0, 64)))
    gathered = gather_inputs(
        count,
        rows,
        tokens,
        slabs,
        shard.reshape(2, rows // 2, 768),
        up_w.astype(BF),
        down_w.T.astype(BF),
    )
    grads = layer(
        count,
        rows,
        gathered,
        gathered["wo"].reshape(768, 768),
        cotangent,
        norm_params,
        live_rows,
        table,
        table_live,
    )
    sums = reduce_and_gather(count, rows, grads, attn_mom[0], up_mom, down_mom.T)
    orth = orthogonalize_all(count, rows, sums["xmat"], sums["xa"])
    keep = 1.0 - MUON_RATE * MUON_DECAY
    rate_a = MUON_RATE * 0.2 * math.sqrt(768)
    rate_ff = MUON_RATE * 0.2 * math.sqrt(TENSOR * 768)
    new_a = attn_w[0] * keep - rate_a * orth["o_a"].astype(F32)
    new_u = up_w * keep - rate_ff * orth["o_u"].astype(F32)
    new_d = down_w * keep - rate_ff * orth["o_d"].T.astype(F32)
    norm_grad = sums["norm_grad"]
    norm_moment1 = 0.5 * norm_m1 + 0.5 * norm_grad
    norm_moment2 = 0.95 * norm_m2 + 0.05 * norm_grad * norm_grad
    first_hat = norm_moment1 / (1.0 - 0.5**STEP)
    second_hat = norm_moment2 / (1.0 - 0.95**STEP)
    norm_new = norm_params - ADAM_RATE * first_hat / (jnp.sqrt(second_hat) + 1e-08)
    return (
        grads["mixed"],
        grads["input_grad"],
        new_a[None],
        sums["mom_a"][None],
        new_u,
        sums["mom_u"],
        new_d,
        sums["mom_d"].T,
        norm_moment1,
        norm_moment2,
        norm_new,
    )


def solution(mesh):
    placed = (
        P(("dp", "tensor"), None),
        P(("dp", "tensor"), None),
        P("dp"),
        P("tensor", "dp", None),
        P("dp", "tensor"),
        P("tensor", "dp"),
        P(),
        P("tensor", "dp", None),
        P("dp", "tensor"),
        P("tensor", "dp"),
        P(),
        P(),
    )
    whole_tiles = mesh.shape["dp"] == 8 and mesh.shape["tensor"] == TENSOR
    return jax.shard_map(
        step_on_device if whole_tiles else on_device,
        mesh=mesh,
        in_specs=placed,
        out_specs=(
            P(("dp", "tensor"), None),
            P(("dp", "tensor"), None),
            P("tensor", "dp", None),
            P("tensor", "dp", None),
            P("dp", "tensor"),
            P("dp", "tensor"),
            P("tensor", "dp"),
            P("tensor", "dp"),
            P(),
            P(),
            P(),
        ),
        check_vma=False,
    )
```

```python
import functools
import math
import types

import jax
import jax.numpy as jnp
from jax import lax
from jax.experimental import pallas as pl
from jax.experimental.pallas import tpu as pltpu
from jax.sharding import PartitionSpec as P

HEADS = 12
HDIM = 64
BLOCK = 64
NS_STEPS = 5
STEP = 10


NORM_EPS = 1e-05
NS_EPS = 1e-07
COEF_A = 3.4445
COEF_B = -4.775
COEF_C = 2.0315
MUON_RATE = 0.15
MUON_DECAY = 0.1
ADAM_RATE = 0.2


def cut_along(array, dim, size):
    lengths = array.shape
    pieces = array.reshape(*lengths[:dim], size, lengths[dim] // size, *lengths[dim + 1 :])
    return jnp.moveaxis(pieces, dim, 0)


def sum_at_owner(array, axis, dim):
    size = lax.axis_size(axis)
    pieces = lax.all_to_all(cut_along(array, dim, size), axis, 0, 0, tiled=True)
    return jnp.sum(pieces.astype(jnp.float32), axis=0)


def sent_together(arrays, axis, dim, along):
    widths = [a.shape[along] for a in arrays]
    both = jnp.concatenate(arrays, axis=along)
    whole = sum_at_owner(both, axis, dim)
    return tuple(jnp.split(whole, [sum(widths[:k]) for k in range(1, len(widths))], axis=along))


def partner(array, axis, bit):
    return lax.ppermute(array, axis, [(i, i ^ 1 << bit) for i in range(lax.axis_size(axis))])


def contract_rows(left, right):
    return lax.dot_general(
        left, right, (((0,), (0,)), ((), ())), preferred_element_type=jnp.float32
    )


def contract_cols(left, right):
    return lax.dot_general(
        left, right, (((1,), (1,)), ((), ())), preferred_element_type=jnp.float32
    )


def norm_forward(resid, gain, bias):
    center = resid - jnp.mean(resid, -1, keepdims=True)
    spread = jnp.mean(center * center, -1, keepdims=True)
    scale_inv = lax.rsqrt(spread + NORM_EPS)
    normal_rows = center * scale_inv
    return (normal_rows, scale_inv, normal_rows * gain + bias)


def norm_back(normal_rows, scale_inv, grad_normed):
    return scale_inv * (
        grad_normed
        - jnp.mean(grad_normed, -1, keepdims=True)
        - normal_rows * jnp.mean(grad_normed * normal_rows, -1, keepdims=True)
    )


def smooth_gate(values):
    return jax.nn.gelu(values, approximate=True)


def features(proj, cosine, sine, weight_rows):
    count = proj.shape[0]
    soft = jax.nn.softplus(proj).reshape(count, HEADS, HDIM)
    both = jnp.concatenate([soft * cosine[:, None, None], soft * sine[:, None, None]], -1)
    return both * weight_rows[:, None, None]


def features_back(grad_feat, proj, cosine, sine, weight_rows):
    count = proj.shape[0]
    grad_soft = (
        grad_feat[..., :HDIM] * cosine[:, None, None] + grad_feat[..., HDIM:] * sine[:, None, None]
    )
    grad_soft = grad_soft * weight_rows[:, None, None]
    slope = jax.nn.sigmoid(proj).reshape(count, HEADS, HDIM)
    return (grad_soft * slope).reshape(count, HEADS * HDIM).astype(jnp.bfloat16)


def blocked(array):
    return array.reshape(array.shape[0] // BLOCK, BLOCK, array.shape[1], array.shape[2])


def attend_forward(qblock, kblock, vblock, lower):
    scores = (
        jnp.einsum("nihf,njhf->nhij", qblock, kblock, preferred_element_type=jnp.float32) * lower
    )
    scores_low = scores.astype(jnp.bfloat16)
    pairs = jnp.einsum("njhf,njhd->nhfd", kblock, vblock, preferred_element_type=jnp.float32)
    state = jnp.cumsum(pairs, 0) - pairs
    state_low = state.astype(jnp.bfloat16)
    key_sum = jnp.sum(kblock.astype(jnp.float32), 1)
    zsum = jnp.cumsum(key_sum, 0) - key_sum
    numer = jnp.einsum("nhij,njhd->nihd", scores_low, vblock, preferred_element_type=jnp.float32)
    numer = numer + jnp.einsum(
        "nihf,nhfd->nihd", qblock, state_low, preferred_element_type=jnp.float32
    )
    denom = jnp.transpose(jnp.sum(scores, -1), (0, 2, 1))
    denom = denom + jnp.einsum(
        "nihf,nhf->nih", qblock.astype(jnp.float32), zsum, precision=lax.Precision.HIGHEST
    )
    return (scores_low, state_low, zsum, denom, numer / denom[..., None])


def attend_backward(
    qblock, kblock, vblock, lower, scores_low, state_low, zsum, denom, result, grad_out
):
    grad_numer = (grad_out / denom[..., None]).astype(jnp.bfloat16)
    grad_denom = -jnp.sum(grad_out * result, -1) / denom
    grad_scores = jnp.einsum(
        "nihd,njhd->nhij", grad_numer, vblock, preferred_element_type=jnp.float32
    )
    grad_scores = ((grad_scores + jnp.transpose(grad_denom, (0, 2, 1))[..., None]) * lower).astype(
        jnp.bfloat16
    )
    grad_state = jnp.einsum(
        "nihf,nihd->nhfd", qblock, grad_numer, preferred_element_type=jnp.float32
    )
    grad_pairs = (jnp.cumsum(grad_state[::-1], 0)[::-1] - grad_state).astype(jnp.bfloat16)
    grad_z = jnp.einsum(
        "nih,nihf->nhf", grad_denom, qblock.astype(jnp.float32), precision=lax.Precision.HIGHEST
    )
    grad_ksum = jnp.cumsum(grad_z[::-1], 0)[::-1] - grad_z
    grad_qf = jnp.einsum("nhij,njhf->nihf", grad_scores, kblock, preferred_element_type=jnp.float32)
    grad_qf = grad_qf + jnp.einsum(
        "nihd,nhfd->nihf", grad_numer, state_low, preferred_element_type=jnp.float32
    )
    grad_qf = grad_qf + grad_denom[..., None] * zsum[:, None]
    grad_kf = jnp.einsum("nhij,nihf->njhf", grad_scores, qblock, preferred_element_type=jnp.float32)
    grad_kf = grad_kf + jnp.einsum(
        "njhd,nhfd->njhf", vblock, grad_pairs, preferred_element_type=jnp.float32
    )
    grad_kf = grad_kf + grad_ksum[:, None]
    grad_val = jnp.einsum(
        "nhij,nihd->njhd", scores_low, grad_numer, preferred_element_type=jnp.float32
    )
    grad_val = grad_val + jnp.einsum(
        "njhf,nhfd->njhd", kblock, grad_pairs, preferred_element_type=jnp.float32
    )
    return (grad_qf, grad_kf, grad_val.astype(jnp.bfloat16))


def newton_update(iterate, gram):
    poly = (
        COEF_B * gram.astype(jnp.float32)
        + COEF_C * jnp.dot(gram, gram, preferred_element_type=jnp.float32)
    ).astype(jnp.bfloat16)
    return (
        COEF_A * iterate.astype(jnp.float32)
        + jnp.dot(poly, iterate, preferred_element_type=jnp.float32)
    ).astype(jnp.bfloat16)


def orthogonalize(iterate):
    for step in range(NS_STEPS):
        gram = jnp.dot(iterate, iterate.T, preferred_element_type=jnp.float32).astype(jnp.bfloat16)
        iterate = newton_update(iterate, gram)
    return iterate


def on_device(
    tokens,
    cotangent,
    lengths,
    attn_w,
    up_w,
    down_w,
    norm_params,
    attn_mom,
    up_mom,
    down_mom,
    norm_m1,
    norm_m2,
):
    tensor_index = lax.axis_index("tensor")
    data_index = lax.axis_index("dp")
    tensor_count = lax.axis_size("tensor")
    length = lengths[0]
    rows_here = tokens.shape[0]
    wa_rows, up_block, down_block = (
        lax.all_gather(attn_w.astype(jnp.bfloat16), "dp", axis=1, tiled=True),
        lax.all_gather(up_w.astype(jnp.bfloat16), "dp", axis=0, tiled=True),
        lax.all_gather(down_w.astype(jnp.bfloat16), "dp", axis=1, tiled=True),
    )
    w_all = lax.all_gather(wa_rows, "tensor", axis=0, tiled=True)
    w_query = w_all[0]
    w_key = w_all[1]
    w_value = w_all[2]
    w_out = w_all[3]
    sequence = lax.all_gather(tokens, "tensor", axis=0, tiled=True)
    count = sequence.shape[0]
    width = sequence.shape[1]
    blocks = count // BLOCK
    start_row = tensor_index * rows_here

    def mine(array):
        return lax.dynamic_slice_in_dim(array, start_row, rows_here, 0)

    where = jnp.arange(count)
    live = (where < length).astype(jnp.float32)
    place = jnp.minimum(where, length - 1).astype(jnp.float32)
    theta = 0.5 * math.pi * place / length.astype(jnp.float32)
    cosine = jnp.cos(theta)
    sine = jnp.sin(theta)
    every_row = jnp.ones((count,), jnp.float32)
    query = jnp.dot(sequence, w_query, preferred_element_type=jnp.float32)
    key_proj = jnp.dot(sequence, w_key, preferred_element_type=jnp.float32)
    value = jnp.dot(sequence, w_value, preferred_element_type=jnp.float32)
    qblock = blocked(features(query, cosine, sine, every_row).astype(jnp.bfloat16))
    kblock = blocked(features(key_proj, cosine, sine, live).astype(jnp.bfloat16))
    vblock = value.astype(jnp.bfloat16).reshape(blocks, BLOCK, HEADS, HDIM)
    lower = jnp.tril(jnp.ones((BLOCK, BLOCK), jnp.float32))
    scores_low, state_low, zsum, denom, result = attend_forward(qblock, kblock, vblock, lower)
    attn_low = result.reshape(count, width).astype(jnp.bfloat16)
    branch = jnp.dot(attn_low, w_out, preferred_element_type=jnp.float32)
    normal_one, scale_one, hidden_in = norm_forward(
        sequence.astype(jnp.float32) + branch, norm_params[0], norm_params[1]
    )
    hidden_low = hidden_in.astype(jnp.bfloat16)
    pre = jnp.dot(hidden_low, up_block, preferred_element_type=jnp.float32)
    act_low = smooth_gate(pre).astype(jnp.bfloat16)
    ffn_rows = lax.psum_scatter(
        jnp.dot(act_low, down_block, preferred_element_type=jnp.float32).astype(jnp.bfloat16),
        "tensor",
        scatter_dimension=0,
        tiled=True,
    ).astype(jnp.float32)
    live_rows = mine(live)
    normal_two, scale_two, normed = norm_forward(
        mine(hidden_in) + ffn_rows, norm_params[2], norm_params[3]
    )
    mixed = (live_rows[:, None] * normed).astype(jnp.bfloat16)
    grad_y = cotangent.astype(jnp.float32) * live_rows[:, None]
    grad_g2 = jnp.sum(grad_y * normal_two, 0)
    grad_b2 = jnp.sum(grad_y, 0)
    grad_r2 = norm_back(normal_two, scale_two, grad_y * norm_params[2])
    grad_r2_all = lax.all_gather(grad_r2.astype(jnp.bfloat16), "tensor", axis=0, tiled=True)
    grad_down = contract_rows(act_low, grad_r2_all)
    grad_act = contract_cols(grad_r2_all, down_block)
    gate_out, gate_pull = jax.vjp(smooth_gate, pre)
    grad_pre = gate_pull(grad_act)[0].astype(jnp.bfloat16)
    grad_up = contract_rows(hidden_low, grad_pre)
    grad_hidden = (
        lax.psum_scatter(
            contract_cols(grad_pre, up_block).astype(jnp.bfloat16),
            "tensor",
            scatter_dimension=0,
            tiled=True,
        ).astype(jnp.float32)
        + grad_r2
    )
    normal_one_rows = mine(normal_one)
    grad_g1 = jnp.sum(grad_hidden * normal_one_rows, 0)
    grad_b1 = jnp.sum(grad_hidden, 0)
    grad_r1 = norm_back(normal_one_rows, mine(scale_one), grad_hidden * norm_params[0])
    grad_branch = lax.all_gather(grad_r1.astype(jnp.bfloat16), "tensor", axis=0, tiled=True)
    grad_attn = contract_cols(grad_branch, w_out).reshape(blocks, BLOCK, HEADS, HDIM)
    grad_qf, grad_kf, grad_val = attend_backward(
        qblock, kblock, vblock, lower, scores_low, state_low, zsum, denom, result, grad_attn
    )
    grad_query = features_back(
        grad_qf.reshape(count, HEADS, 2 * HDIM), query, cosine, sine, every_row
    )
    grad_key = features_back(grad_kf.reshape(count, HEADS, 2 * HDIM), key_proj, cosine, sine, live)
    grad_value = grad_val.reshape(count, width)
    input_grad = (
        grad_r1
        + contract_cols(mine(grad_query), w_query)
        + contract_cols(mine(grad_key), w_key)
        + contract_cols(mine(grad_value), w_value)
    )
    left_rows = jnp.where(tensor_index == 3, attn_low, sequence)
    right_all = jnp.stack((grad_query, grad_key, grad_value, grad_branch))
    right_rows = lax.dynamic_index_in_dim(right_all, tensor_index, 0, keepdims=False)
    grad_owned = contract_rows(left_rows, right_rows)
    norm_partial = jnp.stack((grad_g1, grad_b1, grad_g2, grad_b2))
    grad_a, grad_u, grad_d = (
        *sent_together((grad_owned.astype(jnp.bfloat16), grad_up.astype(jnp.bfloat16)), "dp", 0, 1),
        sum_at_owner(grad_down.astype(jnp.bfloat16), "dp", 1),
    )
    moment_a = 0.5 * attn_mom[0] + grad_a
    moment_u = 0.5 * up_mom + grad_u
    moment_d = 0.5 * down_mom + grad_d
    owner_pick = jax.nn.one_hot(tensor_index, 4, dtype=jnp.float32)
    squares = jnp.concatenate(
        (
            owner_pick * jnp.sum(moment_a * moment_a),
            jnp.stack((jnp.sum(moment_u * moment_u), jnp.sum(moment_d * moment_d))),
        )
    )
    totals, norm_grad = lax.psum((squares, norm_partial), ("dp", "tensor"))
    size_a = jnp.sqrt(jnp.sum(totals[:4] * owner_pick))
    size_u = jnp.sqrt(totals[4])
    size_d = jnp.sqrt(totals[5])
    start_a = (moment_a / (size_a + NS_EPS)).astype(jnp.bfloat16)
    start_u = (moment_u / (size_u + NS_EPS)).astype(jnp.bfloat16)
    start_d = (moment_d.T / (size_d + NS_EPS)).astype(jnp.bfloat16)
    whole_a, cols_u, cols_d = (
        lax.all_gather(start_a, "dp", axis=0, tiled=True),
        lax.all_gather(start_u, "dp", axis=0, tiled=True),
        lax.all_gather(start_d, "dp", axis=0, tiled=True),
    )
    orth_a = orthogonalize(whole_a)
    is_even = tensor_index % 2 == 0
    whole_u, whole_d = (
        lax.all_gather(cols_u, "tensor", axis=1, tiled=True),
        lax.all_gather(cols_d, "tensor", axis=1, tiled=True),
    )
    orth_whole = orthogonalize(jnp.where(is_even, whole_u, whole_d))
    block_cols = cols_u.shape[1]
    own_block = lax.dynamic_slice_in_dim(orth_whole, tensor_index * block_cols, block_cols, 1)
    partner_block = lax.dynamic_slice_in_dim(
        orth_whole, jnp.bitwise_xor(tensor_index, 1) * block_cols, block_cols, 1
    )
    fetched = partner(partner_block, "tensor", 0)
    orth_u = jnp.where(is_even, own_block, fetched)
    orth_d = jnp.where(is_even, fetched, own_block)
    span = moment_a.shape[0]

    def take_rows(array):
        return lax.dynamic_slice_in_dim(array, data_index * span, span, 0).astype(jnp.float32)

    ff_whole = up_block.shape[1] * tensor_count
    keep = 1.0 - MUON_RATE * MUON_DECAY
    new_a = attn_w[0] * keep - MUON_RATE * 0.2 * math.sqrt(width) * take_rows(orth_a)
    scale_ff = 0.2 * math.sqrt(max(width, ff_whole))
    new_u = up_w * keep - MUON_RATE * scale_ff * take_rows(orth_u)
    new_d = down_w * keep - MUON_RATE * scale_ff * take_rows(orth_d).T
    norm_moment1 = 0.5 * norm_m1 + 0.5 * norm_grad
    norm_moment2 = 0.95 * norm_m2 + 0.05 * norm_grad * norm_grad
    first_hat = norm_moment1 / (1.0 - 0.5**STEP)
    second_hat = norm_moment2 / (1.0 - 0.95**STEP)
    norm_new = norm_params - ADAM_RATE * first_hat / (jnp.sqrt(second_hat) + 1e-08)
    return (
        mixed,
        input_grad,
        new_a[None],
        moment_a[None],
        new_u,
        moment_u,
        new_d,
        moment_d,
        norm_moment1,
        norm_moment2,
        norm_new,
    )


BF = jnp.bfloat16
F32 = jnp.float32
MESH = pl.DeviceIdType.MESH
TENSOR = 4
QUARTER = 256
LANES = 128
VMEM_LIMIT = 63 << 20
GELU_C = math.sqrt(2.0 / math.pi)
GELU_A = 0.044715


def nn(left, right):
    return jnp.dot(left, right, preferred_element_type=F32)


def nt(left, right):
    return lax.dot_general(left, right, (((1,), (1,)), ((), ())), preferred_element_type=F32)


def tn(left, right):
    return lax.dot_general(left, right, (((0,), (0,)), ((), ())), preferred_element_type=F32)


def lanes_of(rows, cols=LANES):
    return lax.broadcasted_iota(jnp.int32, (rows, cols), 1)


def half_roll(array):
    return pltpu.roll(array, LANES // 2, 1)


def place():
    data = lax.axis_index("dp")
    tensor = lax.axis_index("tensor")
    return data, tensor


def greet(devices):
    barrier = pltpu.get_barrier_semaphore()
    for device in devices:
        pl.semaphore_signal(barrier, inc=1, device_id=device, device_id_type=MESH)
    pl.semaphore_wait(barrier, len(devices))


def send(src, dst, send_sem, recv_sem, device):
    copy = pltpu.make_async_remote_copy(
        src_ref=src,
        dst_ref=dst,
        send_sem=send_sem,
        recv_sem=recv_sem,
        device_id=device,
        device_id_type=MESH,
    )
    copy.start()
    return copy


def kernel_call(body, name, ins, outs, scratch, collective, scalars=()):
    in_names = list(ins)
    out_names = list(outs)
    scratch_names = list(scratch)

    def kernel(*refs):
        body(types.SimpleNamespace(**dict(zip(in_names + out_names + scratch_names, refs))))

    results = pl.pallas_call(
        kernel,
        name=name,
        out_shape=[outs[n] for n in out_names],
        in_specs=[
            pl.BlockSpec(memory_space=pltpu.SMEM if n in scalars else pltpu.VMEM) for n in in_names
        ],
        out_specs=[pl.BlockSpec(memory_space=pltpu.VMEM)] * len(out_names),
        scratch_shapes=[scratch[n] for n in scratch_names],
        compiler_params=pltpu.CompilerParams(
            collective_id=collective,
            has_side_effects=collective is not None,
            vmem_limit_bytes=VMEM_LIMIT,
        ),
    )(*[ins[n] for n in in_names])
    return dict(zip(out_names, results))


def shape(*dims, dtype=BF):
    return jax.ShapeDtypeStruct(dims, dtype)


def dma(*dims):
    return pltpu.SemaphoreType.DMA(dims)


def await_bytes(ref, sem):
    pltpu.make_async_copy(ref, ref, sem).wait()


class GatherDp:
    def __init__(self, slot_of, sends, recvs, data, tensor, count):
        self.slot_of, self.sends, self.recvs = slot_of, sends, recvs
        self.data, self.tensor = data, tensor
        self.n = count // 2
        self.high, self.low = data // 2, data % 2
        self.partner = (self.high * 2 + 1 - self.low, tensor)

    def peer(self, step):
        return lax.rem(self.high + step, self.n) * 2 + self.low

    def start(self):
        mine = self.slot_of(self.data)
        self.along = []
        for step in range(1, self.n):
            to = (self.peer(step), self.tensor)
            self.along.append(send(mine, mine, self.sends.at[step], self.recvs.at[step], to))
        self.across = [send(mine, mine, self.sends.at[0], self.recvs.at[0], self.partner)]

    def forward(self):
        n = self.n
        for step in range(1, n):
            self.along[step - 1].wait_recv()
            slot = self.slot_of(self.peer(n - step))
            at = n - 1 + step
            self.across.append(send(slot, slot, self.sends.at[at], self.recvs.at[at], self.partner))

    def arrive(self):
        for copy in self.across:
            copy.wait_recv()

    def close(self):
        for copy in self.along + self.across:
            copy.wait_send()


def softplus_and_slope(x):
    small = jnp.exp(-jnp.abs(x))
    soft = jnp.maximum(x, 0.0) + jnp.log1p(small)
    slope = jnp.where(x >= 0.0, 1.0, small) / (1.0 + small)
    return soft, slope


def spread_weights(r, matrices):
    low = lanes_of(768) < 64
    for m in matrices:
        w = r.wqkv[:, m].reshape(768, 256)
        first, second = w[:, :LANES].astype(F32), w[:, LANES:].astype(F32)
        turned = half_roll(first)
        if m < 2:
            parts = [
                jnp.where(low, first, turned),
                jnp.where(low, turned, first),
                jnp.where(low, second, half_roll(second)),
            ]
        else:
            parts = [jnp.where(low, p, 0.0) for p in (first, turned, second)]
        for h, part in enumerate(parts):
            r.xmat[:, (3 * m + h) * LANES : (3 * m + h + 1) * LANES] = part.astype(BF)


def project(r):
    lane = lanes_of(QUARTER)

    def step(q, carry):
        both = nn(r.seq[q], r.xmat[:, : 9 * LANES])
        table, table_live = r.gp[q, :, :LANES], r.gp[q, :, LANES : 2 * LANES]
        for h in range(3):
            soft, slope = softplus_and_slope(both[:, h * LANES : (h + 1) * LANES])
            r.qf[h, q] = (soft * table).astype(BF)
            r.qg[h, q] = slope * table
            soft, slope = softplus_and_slope(both[:, (3 + h) * LANES : (4 + h) * LANES])
            r.kf[h, q] = (soft * table_live).astype(BF)
            r.kg[h, q] = slope * table_live
            value = both[:, (6 + h) * LANES : (7 + h) * LANES]
            ones = jnp.where((lane == 64) | (lane == 65), 1.0, 0.0)
            r.va[h, q] = jnp.where(lane < 64, value, ones).astype(BF)
        return carry

    lax.fori_loop(0, TENSOR, step, 0)


def attend(r, q):
    lane = lanes_of(QUARTER)
    keep = lanes_of(QUARTER, QUARTER) <= lax.broadcasted_iota(jnp.int32, (QUARTER, QUARTER), 0)

    def head(h, carry):
        qf, kf, va = r.qf[h, q], r.kf[h, q], r.va[h, q]
        scores = jnp.where(keep, nt(qf, kf), 0.0).astype(BF)
        r.sb[h, q] = scores
        total = nn(scores, va)
        if q > 0:
            state = r.state[h].astype(BF)
            r.st[h, q] = state
            total = total + nn(qf, state)
        if q < TENSOR - 1:
            pairs = tn(kf, va)
            r.state[h] = pairs if q == 0 else r.state[h] + pairs
        inverse = 1.0 / total[:, 64:65]
        r.af[h, q] = jnp.where(lane < 64, total * inverse, inverse)
        return carry

    lax.fori_loop(0, 3, head, 0)
    zero, one, two = r.af[0, q], r.af[1, q], r.af[2, q]
    r.attn[q, :, :LANES] = jnp.where(lane < 64, zero, half_roll(one)).astype(BF)
    r.attn[q, :, LANES:] = jnp.where(lane < 64, two, 0.0).astype(BF)


def norm_rows(resid):
    center = resid - jnp.mean(resid, -1, keepdims=True)
    spread = jnp.mean(center * center, -1, keepdims=True)
    scale = lax.rsqrt(spread + NORM_EPS)
    return center * scale, scale


def norm_rows_back(normal, scale, grad):
    return scale * (
        grad
        - jnp.mean(grad, -1, keepdims=True)
        - normal * jnp.mean(grad * normal, -1, keepdims=True)
    )


class Group:
    def __init__(self):
        self.data, self.tensor = place()
        self.far, self.core = self.tensor // 2, self.tensor % 2

    def device(self, k):
        return (self.data, self.tensor ^ k)


def spread_quarter(r, g, buf, sends, recvs):
    own = buf.at[g.tensor]
    far = send(own, own, sends.at[0], recvs.at[0], g.device(2))
    near = send(own, own, sends.at[1], recvs.at[1], g.device(1))

    def arrived_near():
        near.wait_recv()

    def arrived_far():
        far.wait_recv()
        slot = buf.at[g.tensor ^ 2]
        passed = send(slot, slot, sends.at[2], recvs.at[2], g.device(1))
        passed.wait_recv()
        for copy in (far, near, passed):
            copy.wait_send()

    return arrived_near, arrived_far


class SumQuarters:
    def __init__(self, r, g, slot):
        self.r, self.g, self.slot, self.copies = r, g, slot, []

    def near_out(self, j, value):
        r, k = self.r, self.slot * 2 + j
        r.near_send[j] = value.astype(BF)
        self.copies.append(
            send(r.near_send.at[j], r.near_recv.at[j], r.near_s.at[k], r.near_r.at[k], self.g.device(1))
        )

    def near_in(self, j, value):
        self.copies[j].wait_recv()
        return value + self.r.near_recv[j].astype(F32)

    def far_out(self, value):
        r, k = self.r, self.slot
        r.far_send[...] = value.astype(BF)
        self.far = send(r.far_send, r.far_recv, r.far_s.at[k], r.far_r.at[k], self.g.device(2))

    def far_in(self, value):
        self.far.wait_recv()
        value = value + self.r.far_recv[...].astype(F32)
        for copy in self.copies + [self.far]:
            copy.wait_send()
        return value


def feed(r, q):
    pre = nn(r.hb[q], r.wu[...].reshape(768, 768))
    inner = jnp.tanh(GELU_C * (pre + GELU_A * pre * pre * pre))
    half = 0.5 * (1.0 + inner)
    r.gp[q] = half + 0.5 * pre * (1.0 - inner * inner) * (GELU_C * (1.0 + 3.0 * GELU_A * pre * pre))
    hid = (pre * half).astype(BF)
    r.hid[q] = hid
    return nt(hid, r.wd[...].reshape(768, 768))


def feed_back(r, q):
    grad_act = nn(r.dr2[q], r.wd[...].reshape(768, 768))
    grad_pre = (grad_act * r.gp[q]).astype(BF)
    r.du[q] = grad_pre
    return nt(grad_pre, r.wu[...].reshape(768, 768))


def attend_back(r, g, q):
    lane = lanes_of(QUARTER)
    keep = lanes_of(QUARTER, QUARTER) <= lax.broadcasted_iota(jnp.int32, (QUARTER, QUARTER), 0)
    dr1 = r.dr1[q]

    def head(h, carry):
        grad = nt(dr1, r.woh[h])
        af = r.af[h, q]
        inverse = af[:, 64:65]
        dden = -jnp.sum(grad * af, -1, keepdims=True) * inverse
        dden_low = dden.astype(BF).astype(F32)
        extra = jnp.where(lane == 64, dden_low, jnp.where(lane == 65, dden - dden_low, 0.0))
        dnum = jnp.where(lane < 64, grad * inverse, extra).astype(BF)
        qf, kf, va, sb = r.qf[h, q], r.kf[h, q], r.va[h, q], r.sb[h, q]
        ds = jnp.where(keep, nt(dnum, va), 0.0).astype(BF)
        dqf = nn(ds, kf)
        if q > 0:
            dqf = dqf + nt(dnum, r.st[h, q])
        dkf = tn(ds, qf)
        dv = tn(sb, dnum)
        if q < TENSOR - 1:
            dkv = r.state[h].astype(BF)
            dkf = dkf + nt(va, dkv)
            dv = dv + nn(kf, dkv)
        if q > 0:
            pairs = tn(qf, dnum)
            r.state[h] = pairs if q == TENSOR - 1 else r.state[h] + pairs
        dqf = dqf * r.qg[h, q]
        dkf = dkf * r.kg[h, q]
        r.fold[0, h] = dqf + half_roll(dqf)
        r.fold[1, h] = dkf + half_roll(dkf)
        r.fold[2, h] = dv
        return carry

    lax.fori_loop(0, 3, head, 0)
    for m in range(3):
        second = r.fold[m, 1] if m < 2 else half_roll(r.fold[m, 1])
        r.hb[q, :, 256 * m : 256 * m + LANES] = jnp.where(lane < 64, r.fold[m, 0], second).astype(BF)
        r.hb[q, :, 256 * m + LANES : 256 * (m + 1)] = jnp.where(lane < 64, r.fold[m, 2], 0.0).astype(BF)
    total = None
    for m in range(3):
        part = nt(r.hb[q, :, 256 * m : 256 * (m + 1)], r.wqkv[:, m].reshape(768, 256))
        total = part if total is None else total + part
    r.gp[q] = total


class ReduceDp:
    def __init__(self, src, low_buf, high_send, high_buf, sems, data, tensor, count):
        self.src, self.low_buf, self.high_send, self.high_buf = src, low_buf, high_send, high_buf
        self.low_s, self.low_r, self.high_s, self.high_r = sems
        self.tensor, self.n = tensor, count // 2
        self.high, self.low = data // 2, data % 2

    def at(self, step):
        return lax.rem(self.high + step, self.n)

    def start(self):
        partner = (self.high * 2 + 1 - self.low, self.tensor)
        self.across = {}
        for step in list(range(1, self.n)) + [0]:
            h = self.at(step)
            self.across[step] = send(
                self.src.at[h * 2 + 1 - self.low],
                self.low_buf.at[h],
                self.low_s.at[step],
                self.low_r.at[step],
                partner,
            )

    def pair(self, step):
        self.across[step].wait_recv()
        h = self.at(step)
        return self.src[h * 2 + self.low].astype(F32) + self.low_buf[h].astype(F32)

    def forward(self):
        self.along = []
        for step in range(1, self.n):
            self.high_send[step] = self.pair(step).astype(BF)
            self.along.append(
                send(
                    self.high_send.at[step],
                    self.high_buf.at[step],
                    self.high_s.at[step],
                    self.high_r.at[step],
                    (self.at(step) * 2 + self.low, self.tensor),
                )
            )

    def finish(self):
        total = self.pair(0)
        for step in range(1, self.n):
            self.along[step - 1].wait_recv()
            total = total + self.high_buf[step].astype(F32)
        for copy in list(self.across.values()) + self.along:
            copy.wait_send()
        return total


def assemble(r, core_rows):
    low = lanes_of(core_rows) < 64
    for pair in range(2):
        even, odd = r.abuf[2 * pair].astype(F32), r.abuf[2 * pair + 1].astype(F32)
        turned = half_roll(odd[:, :LANES])
        base = 3 * LANES * pair
        r.grad_a[:, base : base + LANES] = even[:, :LANES]
        r.grad_a[:, base + LANES : base + 2 * LANES] = jnp.where(low, even[:, LANES:], turned)
        r.grad_a[:, base + 2 * LANES : base + 3 * LANES] = jnp.where(low, turned, half_roll(odd[:, LANES:]))


def square_sum(ref, width):
    def step(k, total):
        part = ref[pl.ds(pl.multiple_of(k * 96, 96), 96)].astype(F32)
        return total + part * part

    total = lax.fori_loop(0, 8, step, jnp.zeros((96, width), F32))
    return jnp.sum(total)


def newton(x, gram, poly, chunk):
    width = x.shape[1]
    start = 1.0 / (jnp.sqrt(square_sum(x, width)) + NS_EPS)
    edges = [slice(k * 256, (k + 1) * 256) for k in range(3)]

    def step(k, first):
        scale = jnp.where(k == 0, first, 1.0)
        for a in range(3):
            for b in range(a, 3):
                block = (nt(x[edges[a], :], x[edges[b], :]) * (scale * scale)).astype(BF)
                gram[a, :, edges[b]] = block
                if b > a:
                    gram[b, :, edges[a]] = block.T
        for a in range(3):
            for b in range(a, 3):
                block = COEF_C * nt(gram[a], gram[b])
                block = (block + COEF_B * gram[a, :, edges[b]].astype(F32)).astype(BF)
                poly[a, :, edges[b]] = block
                if b > a:
                    poly[b, :, edges[a]] = block.T

        def columns(c, carry):
            at = pl.ds(pl.multiple_of(c * chunk, chunk), chunk)
            old = x[:, at]
            x[:, at] = (scale * (COEF_A * old.astype(F32) + nn(poly[:3].reshape(768, 768), old))).astype(BF)
            return carry

        lax.fori_loop(0, width // chunk, columns, 0)
        return first

    lax.fori_loop(0, NS_STEPS, step, start)


def angles(r):
    rows = TENSOR * QUARTER
    length = r.lengths[0]
    where = lax.broadcasted_iota(jnp.int32, (rows, LANES), 0)
    theta = 0.5 * math.pi * jnp.minimum(where, length - 1).astype(F32) / length.astype(F32)
    table = jnp.where(lanes_of(rows) < 64, jnp.cos(theta), jnp.sin(theta))
    live = jnp.where(where < length, 1.0, 0.0)
    r.gp[:, :, :LANES] = table.reshape(TENSOR, QUARTER, LANES)
    r.gp[:, :, LANES : 2 * LANES] = (table * live).reshape(TENSOR, QUARTER, LANES)


def cut_heads(r, rows):
    low = lanes_of(rows) < 64
    tiles = [r.attn_w[0, :, k * LANES : (k + 1) * LANES] for k in range(6)]
    for pair in range(2):
        first, middle, last = tiles[3 * pair : 3 * pair + 3]
        turned, rest = half_roll(middle), half_roll(last)
        parts = [first, jnp.where(low, middle, 0.0), jnp.where(low, turned, rest), jnp.where(low, rest, 0.0)]
        for k, part in enumerate(parts):
            r.slabs[2 * pair + k // 2, :, (k % 2) * LANES : (k % 2 + 1) * LANES] = part.astype(BF)


def assemble(r, core_rows):
    low = lanes_of(core_rows) < 64
    for pair in range(2):
        even, odd = r.abuf[2 * pair].astype(F32), r.abuf[2 * pair + 1].astype(F32)
        turned = half_roll(odd[:, :LANES])
        base = 3 * LANES * pair
        r.grad_a[:, base : base + LANES] = even[:, :LANES]
        r.grad_a[:, base + LANES : base + 2 * LANES] = jnp.where(low, even[:, LANES:], turned)
        r.grad_a[:, base + 2 * LANES : base + 3 * LANES] = jnp.where(low, turned, half_roll(odd[:, LANES:]))


def step_body(count, rows, r):
    g = Group()
    data, tensor, far, core = g.data, g.tensor, g.far, g.core
    high, low = data // 2, data % 2
    other = high * 2 + 1 - low
    n = count // 2
    half = rows // 2
    near_dev, far_dev = g.device(1), g.device(2)

    cut_heads(r, rows)
    r.wo_own[...] = r.attn_w[0].astype(BF).reshape(2, half, 768)
    greet(
        [g.device(k) for k in (1, 2, 3)]
        + [(lax.rem(data + k, count), tensor) for k in range(1, count)]
        + [(other, tensor ^ 1)]
    )

    for k in (1, 2, 3):
        peer = tensor ^ k

        @pl.when(tensor < 3)
        def _():
            send(r.slabs.at[peer], r.wqkv.at[data, tensor], r.slab_s.at[k], r.slab_r.at[tensor], g.device(k))

        @pl.when(tensor == 3)
        def _():
            send(r.wo_own.at[peer % 2], r.wo.at[data, peer % 2], r.slab_s.at[k], r.slab_r.at[3], g.device(k))

    r.seq[tensor] = r.tokens[...]
    mine = r.seq.at[tensor]
    tok_near = send(mine, mine, r.tok_s.at[0], r.tok_r.at[0], near_dev)
    tok_far = send(mine, mine, r.tok_s.at[1], r.tok_r.at[1], far_dev)

    @pl.when(tensor < 3)
    def _():
        r.wqkv[data, tensor] = r.slabs[tensor]

    @pl.when(tensor == 3)
    def _():
        r.wo[data, core] = r.wo_own[core]

    r.wu[data] = r.up_w[...].astype(BF)
    r.wd[data] = r.down_w[...].astype(BF)

    def gather(slot_of, key):
        return GatherDp(slot_of, r.gather_s.at[key], r.gather_r.at[key], data, tensor, count)

    heads = [gather(lambda d, m=m: r.wqkv.at[d, m], m) for m in range(3)]
    outs = gather(lambda d: r.wo.at[d, core], 3)
    ups = [gather(lambda d, k=k: r.wu.at[d, pl.ds(k * half, half)], 4 + k) for k in range(2)]
    downs = [gather(lambda d, k=k: r.wd.at[d, pl.ds(k * half, half)], 6 + k) for k in range(2)]

    for m in range(3):

        @pl.when(tensor != m)
        def _():
            await_bytes(r.wqkv.at[data, m], r.slab_r.at[m])

        heads[m].start()
    angles(r)

    @pl.when(tensor != 3)
    def _():
        await_bytes(r.wo.at[data, core], r.slab_r.at[3])

    heads[0].forward()
    outs.start()
    tok_far.wait_recv()
    slot = r.seq.at[tensor ^ 2]
    tok_pass = send(slot, slot, r.tok_s.at[2], r.tok_r.at[2], near_dev)
    heads[1].forward()
    ups[0].start()
    heads[2].forward()
    ups[1].start()
    for m in range(3):
        heads[m].arrive()
        spread_weights(r, [m])
    tok_near.wait_recv()
    tok_pass.wait_recv()
    project(r)
    outs.forward()
    downs[0].start()
    downs[1].start()

    copies = [[], []]
    for j in range(2):
        attend(r, 2 * j)
        attend(r, 2 * j + 1)
        mine, rest = 2 * j + core, 2 * j + 1 - core
        for k in (2, 1, 3):
            quarter = mine if k == 2 else rest
            copies[j].append(
                send(r.attn.at[quarter], r.aall.at[tensor, j], r.attn_s.at[j, k], r.attn_r.at[j, k], g.device(k))
            )
        r.aall[tensor, j] = r.attn[mine]
        ups[j].forward()

    outs.arrive()
    share = []
    for d in range(count):
        part = r.wo.at[d, core]
        share.append(send(part, part, r.share_s.at[d], r.share_r.at[d], near_dev))
    downs[0].forward()
    for d in range(count):
        part = r.wo.at[d, 1 - core]
        await_bytes(part, r.share_r.at[d])
    whole_out = r.wo[...].reshape(768, 768)
    wop = [r.xmat.at[256 * t : 256 * (t + 1), 1536:2304] for t in range(3)] + [r.xmat.at[0:256, 2304:3072]]
    for t in range(TENSOR):
        wop[t][:192, :] = whole_out[192 * t : 192 * (t + 1)]
        wop[t][192:, :] = jnp.zeros((64, 768), BF)
    for t in range(TENSOR):

        @pl.when(tensor == t)
        def _():
            for h in range(3):
                r.woh[h, :64] = wop[t][64 * h : 64 * (h + 1), :]
                r.woh[h, 64:] = jnp.zeros((64, 768), BF)

    gain1, bias1, gain2, bias2 = (r.norms[k : k + 1] for k in range(4))
    hs = []
    for group_copies in copies:
        for copy in group_copies:
            copy.wait_recv()
    for own in (False, True):
        j = far if own else 1 - far
        q = 2 * j + core
        branch = nn(r.aall[0, j], wop[0][...])
        for t in range(1, TENSOR):
            branch = branch + nn(r.aall[t, j], wop[t][...])
        normal, scale = norm_rows(r.seq[q].astype(F32) + branch)
        hidden = normal * gain1 + bias1
        r.hb[q] = hidden.astype(BF)
        if own:
            r.n1[...] = normal
            r.s1[...] = jnp.broadcast_to(scale, (QUARTER, LANES))
            r.h1[...] = hidden
        hs.append(send(r.hb.at[q], r.hb.at[q], r.h_s.at[int(own)], r.h_r.at[int(own)], near_dev))
    downs[1].forward()
    for group_copies in copies:
        for copy in group_copies:
            copy.wait_send()

    for part in ups + downs:
        part.arrive()
    total = SumQuarters(r, g, 0)
    kept = feed(r, tensor ^ 2)
    hs[0].wait_recv()
    total.near_out(0, feed(r, tensor ^ 3))
    total.far_out(total.near_in(0, kept))
    hs[1].wait_recv()
    total.near_out(1, feed(r, tensor ^ 1))
    kept = feed(r, tensor)
    for part in heads + [outs] + ups + downs:
        part.close()
    for copy in hs + share + [tok_near, tok_far, tok_pass]:
        copy.wait_send()
    for k in (1, 2, 3):

        @pl.when(tensor < 3)
        def _():
            await_bytes(r.slabs.at[0], r.slab_s.at[k])

        @pl.when(tensor == 3)
        def _():
            await_bytes(r.wo_own.at[0], r.slab_s.at[k])

    kept = total.far_in(total.near_in(1, kept))

    n2, s2 = norm_rows(r.h1[...] + kept)
    row = lax.broadcasted_iota(jnp.int32, (QUARTER, 1), 0) + tensor * QUARTER
    live = jnp.where(row < r.lengths[0], 1.0, 0.0)
    r.mixed[...] = (live * (n2 * gain2 + bias2)).astype(BF)
    dy = live * r.cotangent[...].astype(F32)
    r.partial[2:3] = jnp.sum(dy * n2, 0, keepdims=True)
    r.partial[3:4] = jnp.sum(dy, 0, keepdims=True)
    dr2 = norm_rows_back(n2, s2, dy * gain2)
    r.dr2f[...] = dr2
    r.dr2[tensor] = dr2.astype(BF)
    near, distant = spread_quarter(r, g, r.dr2, r.dr2_s, r.dr2_r)

    sums = {}
    for key in "dua":
        sums[key] = ReduceDp(
            *(getattr(r, name + key) for name in ("g", "low", "hs", "hb")),
            [getattr(r, name + key) for name in ("ls_", "lr_", "hs_", "hr_")],
            data,
            tensor,
            count,
        )
    total = SumQuarters(r, g, 1)
    r.dh[...] = feed_back(r, tensor)
    near()
    total.near_out(0, feed_back(r, tensor ^ 1))
    distant()
    total.near_out(1, feed_back(r, tensor ^ 3))
    total.far_out(total.near_in(1, feed_back(r, tensor ^ 2)))
    grad = tn(r.dr2[...].reshape(1024, 768), r.hid[...].reshape(1024, 768))
    r.gd[...] = grad.astype(BF).reshape(r.gd.shape)
    sums["d"].start()
    grad = tn(r.hb[...].reshape(1024, 768), r.du[...].reshape(1024, 768))
    r.gu[...] = grad.astype(BF).reshape(r.gu.shape)
    sums["u"].start()
    r.dh[...] = total.near_in(0, r.dh[...]) + r.dr2f[...]
    sums["d"].forward()
    dh = total.far_in(r.dh[...])

    n1 = r.n1[...]
    r.partial[0:1] = jnp.sum(dh * n1, 0, keepdims=True)
    r.partial[1:2] = jnp.sum(dh, 0, keepdims=True)
    dr1 = norm_rows_back(n1, r.s1[:, :1], dh * gain1)
    r.dr1f[...] = dr1
    r.dr1[tensor] = dr1.astype(BF)
    near, distant = spread_quarter(r, g, r.dr1, r.dr1_s, r.dr1_r)
    r.pbuf[tensor] = r.partial[...]
    parts = []
    for k in (1, 2, 3):
        parts.append(send(r.partial, r.pbuf.at[tensor], r.pt_s.at[k], r.pt_r.at[k], g.device(k)))
    near()
    sums["u"].forward()
    distant()

    attend_back(r, g, 3)
    for copy in parts:
        copy.wait()
    r.psum[...] = ((r.pbuf[0] + r.pbuf[1]) + r.pbuf[2]) + r.pbuf[3]
    r.qbuf[data] = r.psum[...]
    parts = []
    for k in range(1, count):
        to = (lax.rem(data + k, count), tensor)
        parts.append(send(r.psum, r.qbuf.at[data], r.pd_s.at[k], r.pd_r.at[k], to))
    attend_back(r, g, 2)
    here = pl.ds(pl.multiple_of(data * rows, rows), rows)
    there = pl.ds(pl.multiple_of(other * rows, rows), rows)

    def rows_of(d):
        return pl.ds(pl.multiple_of(d * rows, rows), rows)

    def cols(t):
        return pl.ds(pl.multiple_of(t * 768, 768), 768)

    moment = 0.5 * r.down_mom[...] + sums["d"].finish()
    r.mom_d[...] = moment
    r.xsd[...] = moment.astype(BF)
    moment = 0.5 * r.up_mom[...] + sums["u"].finish()
    r.mom_u[...] = moment
    r.xsu[...] = moment.astype(BF)
    own = r.xmat.at[here, cols(tensor)]

    @pl.when(far == 0)
    def _():
        r.xmat[here, cols(tensor)] = r.xsu[...]
        send(r.xsd, own, r.swap_s, r.swap_r, far_dev)

    @pl.when(far == 1)
    def _():
        r.xmat[here, cols(tensor)] = r.xsd[...]
        send(r.xsu, own, r.swap_s, r.swap_r, far_dev)

    blocks = [
        GatherDp(lambda d: r.xmat.at[rows_of(d), cols(tensor)], r.x_s.at[0], r.x_r.at[0], data, tensor, count),
        GatherDp(lambda d: r.xmat.at[rows_of(d), cols(tensor ^ 2)], r.x_s.at[1], r.x_r.at[1], data, tensor, count),
    ]
    blocks[0].start()
    attend_back(r, g, 1)
    await_bytes(r.xmat.at[here, cols(tensor ^ 2)], r.swap_r)
    blocks[1].start()
    attend_back(r, g, 0)

    grad = tn(r.seq[...].reshape(1024, 768), r.hb[...].reshape(1024, 768)).astype(BF)
    for m in range(3):
        r.ga[:, m] = grad[:, 256 * m : 256 * (m + 1)].reshape(count, rows, 256)
    sums["a"].start()
    grad = tn(r.attn[...].reshape(1024, 256), r.dr1[...].reshape(1024, 768)).astype(BF)
    r.go[...] = grad[:192].reshape(r.go.shape)
    out_low = send(r.go.at[1 - low], r.olow, r.o_s.at[0], r.o_r.at[0], (other, tensor))
    total = SumQuarters(r, g, 2)
    total.near_out(0, r.gp[tensor ^ 3])
    total.near_out(1, r.gp[tensor ^ 1])
    total.far_out(total.near_in(0, r.gp[tensor ^ 2]))
    blocks[0].forward()
    sums["a"].forward()

    out_low.wait_recv()
    r.grad_a[...] = r.go[low].astype(F32) + r.olow[...].astype(F32)
    r.osend[...] = r.grad_a[...].astype(BF)
    for k in range(1, n):

        @pl.when(lax.rem(high + k, n) == tensor)
        def _():
            send(r.osend, r.ohigh.at[k], r.o_s.at[1], r.o_r.at[k], (tensor * 2 + low, tensor))

    blocks[1].forward()
    r.input_grad[...] = total.far_in(total.near_in(1, r.gp[tensor])) + r.dr1f[...]

    summed = sums["a"].finish()
    for m in range(3):
        r.asend[m] = summed[m].astype(BF)
    for m in range(3):

        @pl.when(tensor != m)
        def _():
            send(r.asend.at[m], r.abuf.at[tensor], r.a_s.at[m], r.a_r.at[tensor], (data, m))

        @pl.when(tensor == m)
        def _():
            r.abuf[tensor] = r.asend[m]

    @pl.when(high == tensor)
    def _():
        whole = r.grad_a[...]
        for k in range(1, n):
            await_bytes(r.ohigh.at[k], r.o_r.at[k])
            whole = whole + r.ohigh[k].astype(F32)
        r.grad_a[...] = whole
        r.oout[...] = whole.astype(BF)

    @pl.when((high == tensor) & (tensor != 3))
    def _():
        send(r.oout, r.oin, r.o_s.at[2], r.oin_r, (data, 3))

    @pl.when((tensor == 3) & (high != 3))
    def _():
        await_bytes(r.oin, r.oin_r)
        r.grad_a[...] = r.oin[...].astype(F32)

    for t in range(TENSOR):

        @pl.when((tensor < 3) & (tensor != t))
        def _():
            await_bytes(r.abuf.at[t], r.a_r.at[t])

    @pl.when(tensor < 3)
    def _():
        assemble(r, rows)

    moment = 0.5 * r.attn_mom[0] + r.grad_a[...]
    r.mom_a[...] = moment
    r.xsa[...] = moment.astype(BF)

    at_work = (high * 2 + core, far * 2 + 1)

    @pl.when((core == 1) & (low == 1))
    def _():
        r.xa[here] = r.xsa[...]

    @pl.when((core == 0) | (low == 0))
    def _():
        send(r.xsa, r.xa.at[here], r.e_s, r.e_r.at[low], at_work)

    for side in range(2):
        part = r.xa.at[rows_of(high * 2 + side)]

        @pl.when((core == 1) & ((low == 0) | (side == 0)))
        def _():
            await_bytes(part, r.e_r.at[side])

        @pl.when(core == 1)
        def _():
            for k in range(1, n):
                to = (lax.rem(high + k, n) * 2 + low, tensor)
                send(part, part, r.f_s.at[side, k], r.f_r.at[side, k], to)

    for block in blocks:
        block.arrive()
        block.close()

    @pl.when(core == 1)
    def _():
        for s, t in enumerate((tensor, tensor ^ 2)):
            block = r.xmat.at[:, cols(t)]
            send(block, block, r.j_s.at[s], r.j_r.at[s], near_dev)

    for copy in parts:
        copy.wait()
    r.norm_grad[...] = sum((r.qbuf[d] for d in range(1, count)), r.qbuf[0])

    @pl.when(core == 0)
    def _():
        for s in range(2):
            await_bytes(r.xmat.at[:, cols(0)], r.j_r.at[s])
        newton(r.xmat, r.du, r.hid, 512)

    @pl.when(core == 1)
    def _():
        for side in range(2):
            for k in range(1, n):
                await_bytes(r.xa.at[rows_of(lax.rem(high + n - k, n) * 2 + side)], r.f_r.at[side, k])
                await_bytes(r.xa.at[here], r.f_s.at[side, k])
        newton(r.xa, r.du, r.hid, 768)

    for m, out in enumerate((r.o_u, r.o_d)):

        @pl.when((core == 0) & (far == m))
        def _():
            for k in (1, 2, 3):
                send(r.xmat.at[here, cols(tensor ^ k)], out, r.w_s.at[k], r.w_r.at[m], g.device(k))
            out[...] = r.xmat[here, cols(tensor)]

    owner = far * 2 + low

    @pl.when((core == 1) & (low == 1))
    def _():
        r.o_a[...] = r.xa[here]
        send(r.xa.at[there], r.o_a, r.v_s.at[0], r.v_r, (other, owner))

    @pl.when((core == 1) & (low == 0))
    def _():
        send(r.xa.at[here], r.o_a, r.v_s.at[0], r.v_r, (data, owner))
        send(r.xa.at[there], r.o_a, r.v_s.at[1], r.v_r, (other, owner))

    @pl.when((core == 0) | (low == 0))
    def _():
        await_bytes(r.o_a, r.v_r)

    for m, out in enumerate((r.o_u, r.o_d)):

        @pl.when((core == 1) | (far != m))
        def _():
            await_bytes(out, r.w_r.at[m])

    await_bytes(r.xsd, r.swap_s)
    out_low.wait_send()

    @pl.when(high != tensor)
    def _():
        await_bytes(r.osend, r.o_s.at[1])

    @pl.when((high == tensor) & (tensor != 3))
    def _():
        await_bytes(r.oout, r.o_s.at[2])

    for m in range(3):

        @pl.when(tensor != m)
        def _():
            await_bytes(r.asend.at[m], r.a_s.at[m])

    @pl.when((core == 0) | (low == 0))
    def _():
        await_bytes(r.xsa, r.e_s)

    @pl.when(core == 0)
    def _():
        for k in (1, 2, 3):
            await_bytes(r.o_u, r.w_s.at[k])

    @pl.when(core == 1)
    def _():
        for s in range(2):
            await_bytes(r.xmat.at[:, cols(0)], r.j_s.at[s])
        await_bytes(r.o_a, r.v_s.at[0])

    @pl.when((core == 1) & (low == 0))
    def _():
        await_bytes(r.o_a, r.v_s.at[1])


def step_call(count, rows, ins):
    v = pltpu.VMEM
    n = count // 2
    one = pltpu.SemaphoreType.DMA
    outs = dict(
        mixed=shape(QUARTER, 768),
        input_grad=shape(QUARTER, 768, dtype=F32),
        mom_a=shape(rows, 768, dtype=F32),
        mom_u=shape(rows, 768, dtype=F32),
        mom_d=shape(rows, 768, dtype=F32),
        norm_grad=shape(4, 768, dtype=F32),
        o_u=shape(rows, 768),
        o_d=shape(rows, 768),
        o_a=shape(rows, 768),
    )
    per_head = (3, TENSOR, QUARTER, LANES)
    quarters = (TENSOR, QUARTER, 768)
    scratch = dict(
        slabs=v((TENSOR, rows, 256), BF),
        wo_own=v((2, rows // 2, 768), BF),
        seq=v(quarters, BF),
        wqkv=v((count, 3, rows, 256), BF),
        wo=v((count, 2, rows // 2, 768), BF),
        wu=v((count, rows, 768), BF),
        wd=v((count, rows, 768), BF),
        woh=v((3, LANES, 768), BF),
        slab_s=dma(4),
        slab_r=dma(4),
        tok_s=dma(3),
        tok_r=dma(3),
        share_s=dma(count),
        share_r=dma(count),
        gather_s=dma(8, count),
        gather_r=dma(8, count),
        qf=v(per_head, BF),
        kf=v(per_head, BF),
        va=v(per_head, BF),
        qg=v(per_head, F32),
        kg=v(per_head, F32),
        af=v(per_head, F32),
        sb=v((3, TENSOR, QUARTER, QUARTER), BF),
        st=v((3, TENSOR, LANES, LANES), BF),
        state=v((3, LANES, LANES), F32),
        attn=v((TENSOR, QUARTER, 256), BF),
        aall=v((TENSOR, 2, QUARTER, 256), BF),
        fold=v((3, 3, QUARTER, LANES), F32),
        attn_s=dma(2, 4),
        attn_r=dma(2, 4),
        hb=v(quarters, BF),
        n1=v((QUARTER, 768), F32),
        s1=v((QUARTER, LANES), F32),
        h1=v((QUARTER, 768), F32),
        hid=v(quarters, BF),
        gp=v(quarters, F32),
        du=v(quarters, BF),
        dr2=v(quarters, BF),
        dr2f=v((QUARTER, 768), F32),
        dr1=v(quarters, BF),
        dr1f=v((QUARTER, 768), F32),
        dh=v((QUARTER, 768), F32),
        near_send=v((2, QUARTER, 768), BF),
        near_recv=v((2, QUARTER, 768), BF),
        far_send=v((QUARTER, 768), BF),
        far_recv=v((QUARTER, 768), BF),
        near_s=dma(6),
        near_r=dma(6),
        far_s=dma(3),
        far_r=dma(3),
        h_s=dma(2),
        h_r=dma(2),
        dr2_s=dma(3),
        dr2_r=dma(3),
        dr1_s=dma(3),
        dr1_r=dma(3),
        gu=v((count, rows, 768), BF),
        gd=v((count, rows, 768), BF),
        ga=v((count, 3, rows, 256), BF),
        go=v((2, rows, 768), BF),
        partial=v((4, 768), F32),
        pbuf=v((TENSOR, 4, 768), F32),
        psum=v((4, 768), F32),
        qbuf=v((count, 4, 768), F32),
        pt_s=dma(4),
        pt_r=dma(4),
        pd_s=dma(count),
        pd_r=dma(count),
        olow=v((rows, 768), BF),
        osend=v((rows, 768), BF),
        ohigh=v((n, rows, 768), BF),
        oout=v((rows, 768), BF),
        oin=v((rows, 768), BF),
        o_s=dma(3),
        o_r=dma(n),
        oin_r=one,
        asend=v((3, rows, 256), BF),
        abuf=v((TENSOR, rows, 256), BF),
        a_s=dma(3),
        a_r=dma(TENSOR),
        grad_a=v((rows, 768), F32),
        xsd=v((rows, 768), BF),
        xsu=v((rows, 768), BF),
        xsa=v((rows, 768), BF),
        xmat=v((768, TENSOR * 768), BF),
        xa=v((768, 768), BF),
        swap_s=one,
        swap_r=one,
        x_s=dma(2, count),
        x_r=dma(2, count),
        e_s=one,
        e_r=dma(2),
        f_s=dma(2, n),
        f_r=dma(2, n),
        j_s=dma(2),
        j_r=dma(2),
        w_s=dma(4),
        w_r=dma(2),
        v_s=dma(2),
        v_r=one,
    )
    for key in "dua":
        part = (3, rows, 256) if key == "a" else (rows, 768)
        for name in ("low", "hs", "hb"):
            scratch[name + key] = v((n,) + part, BF)
        for name in ("ls_", "lr_", "hs_", "hr_"):
            scratch[name + key] = dma(n)
    body = functools.partial(step_body, count, rows)
    return kernel_call(body, "layer_step", ins, outs, scratch, 0, ("lengths",))


def step_on_device(
    tokens,
    cotangent,
    lengths,
    attn_w,
    up_w,
    down_w,
    norm_params,
    attn_mom,
    up_mom,
    down_mom,
    norm_m1,
    norm_m2,
):
    count = lax.axis_size("dp")
    rows = attn_w.shape[1]
    done = step_call(
        count,
        rows,
        dict(
            lengths=lengths,
            tokens=tokens,
            cotangent=cotangent,
            attn_w=attn_w,
            up_w=up_w,
            down_w=down_w.T,
            norms=norm_params,
            attn_mom=attn_mom,
            up_mom=up_mom,
            down_mom=down_mom.T,
        ),
    )
    keep = 1.0 - MUON_RATE * MUON_DECAY
    rate_a = MUON_RATE * 0.2 * math.sqrt(768)
    rate_ff = MUON_RATE * 0.2 * math.sqrt(TENSOR * 768)
    new_a = attn_w[0] * keep - rate_a * done["o_a"].astype(F32)
    new_u = up_w * keep - rate_ff * done["o_u"].astype(F32)
    new_d = down_w * keep - rate_ff * done["o_d"].T.astype(F32)
    norm_grad = done["norm_grad"]
    norm_moment1 = 0.5 * norm_m1 + 0.5 * norm_grad
    norm_moment2 = 0.95 * norm_m2 + 0.05 * norm_grad * norm_grad
    first_hat = norm_moment1 / (1.0 - 0.5**STEP)
    second_hat = norm_moment2 / (1.0 - 0.95**STEP)
    norm_new = norm_params - ADAM_RATE * first_hat / (jnp.sqrt(second_hat) + 1e-08)
    return (
        done["mixed"],
        done["input_grad"],
        new_a[None],
        done["mom_a"][None],
        new_u,
        done["mom_u"],
        new_d,
        done["mom_d"].T,
        norm_moment1,
        norm_moment2,
        norm_new,
    )


def solution(mesh):
    placed = (
        P(("dp", "tensor"), None),
        P(("dp", "tensor"), None),
        P("dp"),
        P("tensor", "dp", None),
        P("dp", "tensor"),
        P("tensor", "dp"),
        P(),
        P("tensor", "dp", None),
        P("dp", "tensor"),
        P("tensor", "dp"),
        P(),
        P(),
    )
    whole_tiles = mesh.shape["dp"] == 8 and mesh.shape["tensor"] == TENSOR
    return jax.shard_map(
        step_on_device if whole_tiles else on_device,
        mesh=mesh,
        in_specs=placed,
        out_specs=(
            P(("dp", "tensor"), None),
            P(("dp", "tensor"), None),
            P("tensor", "dp", None),
            P("tensor", "dp", None),
            P("dp", "tensor"),
            P("dp", "tensor"),
            P("tensor", "dp"),
            P("tensor", "dp"),
            P(),
            P(),
            P(),
        ),
        check_vma=False,
    )
```

```python
import functools
import math
import types

import jax
import jax.numpy as jnp
from jax import lax
from jax.experimental import pallas as pl
from jax.experimental.pallas import tpu as pltpu
from jax.sharding import PartitionSpec as P

HEADS = 12
HDIM = 64
BLOCK = 64
NS_STEPS = 5
STEP = 10


NORM_EPS = 1e-05
NS_EPS = 1e-07
COEF_A = 3.4445
COEF_B = -4.775
COEF_C = 2.0315
MUON_RATE = 0.15
MUON_DECAY = 0.1
ADAM_RATE = 0.2


def cut_along(array, dim, size):
    lengths = array.shape
    pieces = array.reshape(*lengths[:dim], size, lengths[dim] // size, *lengths[dim + 1 :])
    return jnp.moveaxis(pieces, dim, 0)


def sum_at_owner(array, axis, dim):
    size = lax.axis_size(axis)
    pieces = lax.all_to_all(cut_along(array, dim, size), axis, 0, 0, tiled=True)
    return jnp.sum(pieces.astype(jnp.float32), axis=0)


def sent_together(arrays, axis, dim, along):
    widths = [a.shape[along] for a in arrays]
    both = jnp.concatenate(arrays, axis=along)
    whole = sum_at_owner(both, axis, dim)
    return tuple(jnp.split(whole, [sum(widths[:k]) for k in range(1, len(widths))], axis=along))


def partner(array, axis, bit):
    return lax.ppermute(array, axis, [(i, i ^ 1 << bit) for i in range(lax.axis_size(axis))])


def contract_rows(left, right):
    return lax.dot_general(
        left, right, (((0,), (0,)), ((), ())), preferred_element_type=jnp.float32
    )


def contract_cols(left, right):
    return lax.dot_general(
        left, right, (((1,), (1,)), ((), ())), preferred_element_type=jnp.float32
    )


def norm_forward(resid, gain, bias):
    center = resid - jnp.mean(resid, -1, keepdims=True)
    spread = jnp.mean(center * center, -1, keepdims=True)
    scale_inv = lax.rsqrt(spread + NORM_EPS)
    normal_rows = center * scale_inv
    return (normal_rows, scale_inv, normal_rows * gain + bias)


def norm_back(normal_rows, scale_inv, grad_normed):
    return scale_inv * (
        grad_normed
        - jnp.mean(grad_normed, -1, keepdims=True)
        - normal_rows * jnp.mean(grad_normed * normal_rows, -1, keepdims=True)
    )


def smooth_gate(values):
    return jax.nn.gelu(values, approximate=True)


def features(proj, cosine, sine, weight_rows):
    count = proj.shape[0]
    soft = jax.nn.softplus(proj).reshape(count, HEADS, HDIM)
    both = jnp.concatenate([soft * cosine[:, None, None], soft * sine[:, None, None]], -1)
    return both * weight_rows[:, None, None]


def features_back(grad_feat, proj, cosine, sine, weight_rows):
    count = proj.shape[0]
    grad_soft = (
        grad_feat[..., :HDIM] * cosine[:, None, None] + grad_feat[..., HDIM:] * sine[:, None, None]
    )
    grad_soft = grad_soft * weight_rows[:, None, None]
    slope = jax.nn.sigmoid(proj).reshape(count, HEADS, HDIM)
    return (grad_soft * slope).reshape(count, HEADS * HDIM).astype(jnp.bfloat16)


def blocked(array):
    return array.reshape(array.shape[0] // BLOCK, BLOCK, array.shape[1], array.shape[2])


def attend_forward(qblock, kblock, vblock, lower):
    scores = (
        jnp.einsum("nihf,njhf->nhij", qblock, kblock, preferred_element_type=jnp.float32) * lower
    )
    scores_low = scores.astype(jnp.bfloat16)
    pairs = jnp.einsum("njhf,njhd->nhfd", kblock, vblock, preferred_element_type=jnp.float32)
    state = jnp.cumsum(pairs, 0) - pairs
    state_low = state.astype(jnp.bfloat16)
    key_sum = jnp.sum(kblock.astype(jnp.float32), 1)
    zsum = jnp.cumsum(key_sum, 0) - key_sum
    numer = jnp.einsum("nhij,njhd->nihd", scores_low, vblock, preferred_element_type=jnp.float32)
    numer = numer + jnp.einsum(
        "nihf,nhfd->nihd", qblock, state_low, preferred_element_type=jnp.float32
    )
    denom = jnp.transpose(jnp.sum(scores, -1), (0, 2, 1))
    denom = denom + jnp.einsum(
        "nihf,nhf->nih", qblock.astype(jnp.float32), zsum, precision=lax.Precision.HIGHEST
    )
    return (scores_low, state_low, zsum, denom, numer / denom[..., None])


def attend_backward(
    qblock, kblock, vblock, lower, scores_low, state_low, zsum, denom, result, grad_out
):
    grad_numer = (grad_out / denom[..., None]).astype(jnp.bfloat16)
    grad_denom = -jnp.sum(grad_out * result, -1) / denom
    grad_scores = jnp.einsum(
        "nihd,njhd->nhij", grad_numer, vblock, preferred_element_type=jnp.float32
    )
    grad_scores = ((grad_scores + jnp.transpose(grad_denom, (0, 2, 1))[..., None]) * lower).astype(
        jnp.bfloat16
    )
    grad_state = jnp.einsum(
        "nihf,nihd->nhfd", qblock, grad_numer, preferred_element_type=jnp.float32
    )
    grad_pairs = (jnp.cumsum(grad_state[::-1], 0)[::-1] - grad_state).astype(jnp.bfloat16)
    grad_z = jnp.einsum(
        "nih,nihf->nhf", grad_denom, qblock.astype(jnp.float32), precision=lax.Precision.HIGHEST
    )
    grad_ksum = jnp.cumsum(grad_z[::-1], 0)[::-1] - grad_z
    grad_qf = jnp.einsum("nhij,njhf->nihf", grad_scores, kblock, preferred_element_type=jnp.float32)
    grad_qf = grad_qf + jnp.einsum(
        "nihd,nhfd->nihf", grad_numer, state_low, preferred_element_type=jnp.float32
    )
    grad_qf = grad_qf + grad_denom[..., None] * zsum[:, None]
    grad_kf = jnp.einsum("nhij,nihf->njhf", grad_scores, qblock, preferred_element_type=jnp.float32)
    grad_kf = grad_kf + jnp.einsum(
        "njhd,nhfd->njhf", vblock, grad_pairs, preferred_element_type=jnp.float32
    )
    grad_kf = grad_kf + grad_ksum[:, None]
    grad_val = jnp.einsum(
        "nhij,nihd->njhd", scores_low, grad_numer, preferred_element_type=jnp.float32
    )
    grad_val = grad_val + jnp.einsum(
        "njhf,nhfd->njhd", kblock, grad_pairs, preferred_element_type=jnp.float32
    )
    return (grad_qf, grad_kf, grad_val.astype(jnp.bfloat16))


def newton_update(iterate, gram):
    poly = (
        COEF_B * gram.astype(jnp.float32)
        + COEF_C * jnp.dot(gram, gram, preferred_element_type=jnp.float32)
    ).astype(jnp.bfloat16)
    return (
        COEF_A * iterate.astype(jnp.float32)
        + jnp.dot(poly, iterate, preferred_element_type=jnp.float32)
    ).astype(jnp.bfloat16)


def orthogonalize(iterate):
    for step in range(NS_STEPS):
        gram = jnp.dot(iterate, iterate.T, preferred_element_type=jnp.float32).astype(jnp.bfloat16)
        iterate = newton_update(iterate, gram)
    return iterate


def on_device(
    tokens,
    cotangent,
    lengths,
    attn_w,
    up_w,
    down_w,
    norm_params,
    attn_mom,
    up_mom,
    down_mom,
    norm_m1,
    norm_m2,
):
    tensor_index = lax.axis_index("tensor")
    data_index = lax.axis_index("dp")
    tensor_count = lax.axis_size("tensor")
    length = lengths[0]
    rows_here = tokens.shape[0]
    wa_rows, up_block, down_block = (
        lax.all_gather(attn_w.astype(jnp.bfloat16), "dp", axis=1, tiled=True),
        lax.all_gather(up_w.astype(jnp.bfloat16), "dp", axis=0, tiled=True),
        lax.all_gather(down_w.astype(jnp.bfloat16), "dp", axis=1, tiled=True),
    )
    w_all = lax.all_gather(wa_rows, "tensor", axis=0, tiled=True)
    w_query = w_all[0]
    w_key = w_all[1]
    w_value = w_all[2]
    w_out = w_all[3]
    sequence = lax.all_gather(tokens, "tensor", axis=0, tiled=True)
    count = sequence.shape[0]
    width = sequence.shape[1]
    blocks = count // BLOCK
    start_row = tensor_index * rows_here

    def mine(array):
        return lax.dynamic_slice_in_dim(array, start_row, rows_here, 0)

    where = jnp.arange(count)
    live = (where < length).astype(jnp.float32)
    place = jnp.minimum(where, length - 1).astype(jnp.float32)
    theta = 0.5 * math.pi * place / length.astype(jnp.float32)
    cosine = jnp.cos(theta)
    sine = jnp.sin(theta)
    every_row = jnp.ones((count,), jnp.float32)
    query = jnp.dot(sequence, w_query, preferred_element_type=jnp.float32)
    key_proj = jnp.dot(sequence, w_key, preferred_element_type=jnp.float32)
    value = jnp.dot(sequence, w_value, preferred_element_type=jnp.float32)
    qblock = blocked(features(query, cosine, sine, every_row).astype(jnp.bfloat16))
    kblock = blocked(features(key_proj, cosine, sine, live).astype(jnp.bfloat16))
    vblock = value.astype(jnp.bfloat16).reshape(blocks, BLOCK, HEADS, HDIM)
    lower = jnp.tril(jnp.ones((BLOCK, BLOCK), jnp.float32))
    scores_low, state_low, zsum, denom, result = attend_forward(qblock, kblock, vblock, lower)
    attn_low = result.reshape(count, width).astype(jnp.bfloat16)
    branch = jnp.dot(attn_low, w_out, preferred_element_type=jnp.float32)
    normal_one, scale_one, hidden_in = norm_forward(
        sequence.astype(jnp.float32) + branch, norm_params[0], norm_params[1]
    )
    hidden_low = hidden_in.astype(jnp.bfloat16)
    pre = jnp.dot(hidden_low, up_block, preferred_element_type=jnp.float32)
    act_low = smooth_gate(pre).astype(jnp.bfloat16)
    ffn_rows = lax.psum_scatter(
        jnp.dot(act_low, down_block, preferred_element_type=jnp.float32).astype(jnp.bfloat16),
        "tensor",
        scatter_dimension=0,
        tiled=True,
    ).astype(jnp.float32)
    live_rows = mine(live)
    normal_two, scale_two, normed = norm_forward(
        mine(hidden_in) + ffn_rows, norm_params[2], norm_params[3]
    )
    mixed = (live_rows[:, None] * normed).astype(jnp.bfloat16)
    grad_y = cotangent.astype(jnp.float32) * live_rows[:, None]
    grad_g2 = jnp.sum(grad_y * normal_two, 0)
    grad_b2 = jnp.sum(grad_y, 0)
    grad_r2 = norm_back(normal_two, scale_two, grad_y * norm_params[2])
    grad_r2_all = lax.all_gather(grad_r2.astype(jnp.bfloat16), "tensor", axis=0, tiled=True)
    grad_down = contract_rows(act_low, grad_r2_all)
    grad_act = contract_cols(grad_r2_all, down_block)
    gate_out, gate_pull = jax.vjp(smooth_gate, pre)
    grad_pre = gate_pull(grad_act)[0].astype(jnp.bfloat16)
    grad_up = contract_rows(hidden_low, grad_pre)
    grad_hidden = (
        lax.psum_scatter(
            contract_cols(grad_pre, up_block).astype(jnp.bfloat16),
            "tensor",
            scatter_dimension=0,
            tiled=True,
        ).astype(jnp.float32)
        + grad_r2
    )
    normal_one_rows = mine(normal_one)
    grad_g1 = jnp.sum(grad_hidden * normal_one_rows, 0)
    grad_b1 = jnp.sum(grad_hidden, 0)
    grad_r1 = norm_back(normal_one_rows, mine(scale_one), grad_hidden * norm_params[0])
    grad_branch = lax.all_gather(grad_r1.astype(jnp.bfloat16), "tensor", axis=0, tiled=True)
    grad_attn = contract_cols(grad_branch, w_out).reshape(blocks, BLOCK, HEADS, HDIM)
    grad_qf, grad_kf, grad_val = attend_backward(
        qblock, kblock, vblock, lower, scores_low, state_low, zsum, denom, result, grad_attn
    )
    grad_query = features_back(
        grad_qf.reshape(count, HEADS, 2 * HDIM), query, cosine, sine, every_row
    )
    grad_key = features_back(grad_kf.reshape(count, HEADS, 2 * HDIM), key_proj, cosine, sine, live)
    grad_value = grad_val.reshape(count, width)
    input_grad = (
        grad_r1
        + contract_cols(mine(grad_query), w_query)
        + contract_cols(mine(grad_key), w_key)
        + contract_cols(mine(grad_value), w_value)
    )
    left_rows = jnp.where(tensor_index == 3, attn_low, sequence)
    right_all = jnp.stack((grad_query, grad_key, grad_value, grad_branch))
    right_rows = lax.dynamic_index_in_dim(right_all, tensor_index, 0, keepdims=False)
    grad_owned = contract_rows(left_rows, right_rows)
    norm_partial = jnp.stack((grad_g1, grad_b1, grad_g2, grad_b2))
    grad_a, grad_u, grad_d = (
        *sent_together((grad_owned.astype(jnp.bfloat16), grad_up.astype(jnp.bfloat16)), "dp", 0, 1),
        sum_at_owner(grad_down.astype(jnp.bfloat16), "dp", 1),
    )
    moment_a = 0.5 * attn_mom[0] + grad_a
    moment_u = 0.5 * up_mom + grad_u
    moment_d = 0.5 * down_mom + grad_d
    owner_pick = jax.nn.one_hot(tensor_index, 4, dtype=jnp.float32)
    squares = jnp.concatenate(
        (
            owner_pick * jnp.sum(moment_a * moment_a),
            jnp.stack((jnp.sum(moment_u * moment_u), jnp.sum(moment_d * moment_d))),
        )
    )
    totals, norm_grad = lax.psum((squares, norm_partial), ("dp", "tensor"))
    size_a = jnp.sqrt(jnp.sum(totals[:4] * owner_pick))
    size_u = jnp.sqrt(totals[4])
    size_d = jnp.sqrt(totals[5])
    start_a = (moment_a / (size_a + NS_EPS)).astype(jnp.bfloat16)
    start_u = (moment_u / (size_u + NS_EPS)).astype(jnp.bfloat16)
    start_d = (moment_d.T / (size_d + NS_EPS)).astype(jnp.bfloat16)
    whole_a, cols_u, cols_d = (
        lax.all_gather(start_a, "dp", axis=0, tiled=True),
        lax.all_gather(start_u, "dp", axis=0, tiled=True),
        lax.all_gather(start_d, "dp", axis=0, tiled=True),
    )
    orth_a = orthogonalize(whole_a)
    is_even = tensor_index % 2 == 0
    whole_u, whole_d = (
        lax.all_gather(cols_u, "tensor", axis=1, tiled=True),
        lax.all_gather(cols_d, "tensor", axis=1, tiled=True),
    )
    orth_whole = orthogonalize(jnp.where(is_even, whole_u, whole_d))
    block_cols = cols_u.shape[1]
    own_block = lax.dynamic_slice_in_dim(orth_whole, tensor_index * block_cols, block_cols, 1)
    partner_block = lax.dynamic_slice_in_dim(
        orth_whole, jnp.bitwise_xor(tensor_index, 1) * block_cols, block_cols, 1
    )
    fetched = partner(partner_block, "tensor", 0)
    orth_u = jnp.where(is_even, own_block, fetched)
    orth_d = jnp.where(is_even, fetched, own_block)
    span = moment_a.shape[0]

    def take_rows(array):
        return lax.dynamic_slice_in_dim(array, data_index * span, span, 0).astype(jnp.float32)

    ff_whole = up_block.shape[1] * tensor_count
    keep = 1.0 - MUON_RATE * MUON_DECAY
    new_a = attn_w[0] * keep - MUON_RATE * 0.2 * math.sqrt(width) * take_rows(orth_a)
    scale_ff = 0.2 * math.sqrt(max(width, ff_whole))
    new_u = up_w * keep - MUON_RATE * scale_ff * take_rows(orth_u)
    new_d = down_w * keep - MUON_RATE * scale_ff * take_rows(orth_d).T
    norm_moment1 = 0.5 * norm_m1 + 0.5 * norm_grad
    norm_moment2 = 0.95 * norm_m2 + 0.05 * norm_grad * norm_grad
    first_hat = norm_moment1 / (1.0 - 0.5**STEP)
    second_hat = norm_moment2 / (1.0 - 0.95**STEP)
    norm_new = norm_params - ADAM_RATE * first_hat / (jnp.sqrt(second_hat) + 1e-08)
    return (
        mixed,
        input_grad,
        new_a[None],
        moment_a[None],
        new_u,
        moment_u,
        new_d,
        moment_d,
        norm_moment1,
        norm_moment2,
        norm_new,
    )


BF = jnp.bfloat16
F32 = jnp.float32
MESH = pl.DeviceIdType.MESH
TENSOR = 4
QUARTER = 256
LANES = 128
VMEM_LIMIT = 63 << 20
GELU_C = math.sqrt(2.0 / math.pi)
GELU_A = 0.044715


def nn(left, right):
    return jnp.dot(left, right, preferred_element_type=F32)


def nt(left, right):
    return lax.dot_general(left, right, (((1,), (1,)), ((), ())), preferred_element_type=F32)


def tn(left, right):
    return lax.dot_general(left, right, (((0,), (0,)), ((), ())), preferred_element_type=F32)


def lanes_of(rows, cols=LANES):
    return lax.broadcasted_iota(jnp.int32, (rows, cols), 1)


def half_roll(array):
    return pltpu.roll(array, LANES // 2, 1)


def place():
    data = lax.axis_index("dp")
    tensor = lax.axis_index("tensor")
    return data, tensor


def greet(devices):
    barrier = pltpu.get_barrier_semaphore()
    for device in devices:
        pl.semaphore_signal(barrier, inc=1, device_id=device, device_id_type=MESH)
    pl.semaphore_wait(barrier, len(devices))


def send(src, dst, send_sem, recv_sem, device):
    copy = pltpu.make_async_remote_copy(
        src_ref=src,
        dst_ref=dst,
        send_sem=send_sem,
        recv_sem=recv_sem,
        device_id=device,
        device_id_type=MESH,
    )
    copy.start()
    return copy


def kernel_call(body, name, ins, outs, scratch, collective, scalars=()):
    in_names = list(ins)
    out_names = list(outs)
    scratch_names = list(scratch)

    def kernel(*refs):
        body(types.SimpleNamespace(**dict(zip(in_names + out_names + scratch_names, refs))))

    results = pl.pallas_call(
        kernel,
        name=name,
        out_shape=[outs[n] for n in out_names],
        in_specs=[
            pl.BlockSpec(memory_space=pltpu.SMEM if n in scalars else pltpu.VMEM) for n in in_names
        ],
        out_specs=[pl.BlockSpec(memory_space=pltpu.VMEM)] * len(out_names),
        scratch_shapes=[scratch[n] for n in scratch_names],
        compiler_params=pltpu.CompilerParams(
            collective_id=collective,
            has_side_effects=collective is not None,
            vmem_limit_bytes=VMEM_LIMIT,
        ),
    )(*[ins[n] for n in in_names])
    return dict(zip(out_names, results))


def shape(*dims, dtype=BF):
    return jax.ShapeDtypeStruct(dims, dtype)


def dma(*dims):
    return pltpu.SemaphoreType.DMA(dims)


def await_bytes(ref, sem):
    pltpu.make_async_copy(ref, ref, sem).wait()


class GatherDp:
    def __init__(self, slot_of, sends, recvs, data, tensor, count):
        self.slot_of, self.sends, self.recvs = slot_of, sends, recvs
        self.data, self.tensor = data, tensor
        self.n = count // 2
        self.high, self.low = data // 2, data % 2
        self.partner = (self.high * 2 + 1 - self.low, tensor)

    def peer(self, step):
        return lax.rem(self.high + step, self.n) * 2 + self.low

    def start(self):
        mine = self.slot_of(self.data)
        self.along = []
        for step in range(1, self.n):
            to = (self.peer(step), self.tensor)
            self.along.append(send(mine, mine, self.sends.at[step], self.recvs.at[step], to))
        self.across = [send(mine, mine, self.sends.at[0], self.recvs.at[0], self.partner)]

    def forward(self):
        n = self.n
        for step in range(1, n):
            self.along[step - 1].wait_recv()
            slot = self.slot_of(self.peer(n - step))
            at = n - 1 + step
            self.across.append(send(slot, slot, self.sends.at[at], self.recvs.at[at], self.partner))

    def arrive(self):
        for copy in self.across:
            copy.wait_recv()

    def close(self):
        for copy in self.along + self.across:
            copy.wait_send()


def softplus_and_slope(x):
    small = jnp.exp(-jnp.abs(x))
    soft = jnp.maximum(x, 0.0) + jnp.log1p(small)
    slope = jnp.where(x >= 0.0, 1.0, small) / (1.0 + small)
    return soft, slope


def spread_weights(r, matrices):
    low = lanes_of(768) < 64
    for m in matrices:
        w = r.wqkv[:, m].reshape(768, 256)
        first, second = w[:, :LANES].astype(F32), w[:, LANES:].astype(F32)
        turned = half_roll(first)
        if m < 2:
            parts = [
                jnp.where(low, first, turned),
                jnp.where(low, turned, first),
                jnp.where(low, second, half_roll(second)),
            ]
        else:
            parts = [jnp.where(low, p, 0.0) for p in (first, turned, second)]
        for h, part in enumerate(parts):
            r.xmat[:, (3 * m + h) * LANES : (3 * m + h + 1) * LANES] = part.astype(BF)


def project(r):
    lane = lanes_of(QUARTER)

    def step(q, carry):
        both = nn(r.seq[q], r.xmat[:, : 9 * LANES])
        table, table_live = r.gp[q, :, :LANES], r.gp[q, :, LANES : 2 * LANES]
        for h in range(3):
            soft, slope = softplus_and_slope(both[:, h * LANES : (h + 1) * LANES])
            r.qf[h, q] = (soft * table).astype(BF)
            r.qg[h, q] = slope * table
            soft, slope = softplus_and_slope(both[:, (3 + h) * LANES : (4 + h) * LANES])
            r.kf[h, q] = (soft * table_live).astype(BF)
            r.kg[h, q] = slope * table_live
            value = both[:, (6 + h) * LANES : (7 + h) * LANES]
            ones = jnp.where((lane == 64) | (lane == 65), 1.0, 0.0)
            r.va[h, q] = jnp.where(lane < 64, value, ones).astype(BF)
        return carry

    lax.fori_loop(0, TENSOR, step, 0)


def attend(r, q):
    lane = lanes_of(QUARTER)
    keep = lanes_of(QUARTER, QUARTER) <= lax.broadcasted_iota(jnp.int32, (QUARTER, QUARTER), 0)

    def head(h, carry):
        qf, kf, va = r.qf[h, q], r.kf[h, q], r.va[h, q]
        scores = jnp.where(keep, nt(qf, kf), 0.0).astype(BF)
        r.sb[h, q] = scores
        total = nn(scores, va)
        if q > 0:
            state = r.state[h].astype(BF)
            r.st[h, q] = state
            total = total + nn(qf, state)
        if q < TENSOR - 1:
            pairs = tn(kf, va)
            r.state[h] = pairs if q == 0 else r.state[h] + pairs
        inverse = 1.0 / total[:, 64:65]
        r.af[h, q] = jnp.where(lane < 64, total * inverse, inverse)
        return carry

    lax.fori_loop(0, 3, head, 0)
    zero, one, two = r.af[0, q], r.af[1, q], r.af[2, q]
    r.attn[q, :, :LANES] = jnp.where(lane < 64, zero, half_roll(one)).astype(BF)
    r.attn[q, :, LANES:] = jnp.where(lane < 64, two, 0.0).astype(BF)


def norm_rows(resid):
    center = resid - jnp.mean(resid, -1, keepdims=True)
    spread = jnp.mean(center * center, -1, keepdims=True)
    scale = lax.rsqrt(spread + NORM_EPS)
    return center * scale, scale


def norm_rows_back(normal, scale, grad):
    return scale * (
        grad
        - jnp.mean(grad, -1, keepdims=True)
        - normal * jnp.mean(grad * normal, -1, keepdims=True)
    )


class Group:
    def __init__(self):
        self.data, self.tensor = place()
        self.far, self.core = self.tensor // 2, self.tensor % 2

    def device(self, k):
        return (self.data, self.tensor ^ k)


def spread_quarter(r, g, buf, sends, recvs):
    own = buf.at[g.tensor]
    far = send(own, own, sends.at[0], recvs.at[0], g.device(2))
    near = send(own, own, sends.at[1], recvs.at[1], g.device(1))

    def arrived_near():
        near.wait_recv()

    def arrived_far():
        far.wait_recv()
        slot = buf.at[g.tensor ^ 2]
        passed = send(slot, slot, sends.at[2], recvs.at[2], g.device(1))
        passed.wait_recv()
        for copy in (far, near, passed):
            copy.wait_send()

    return arrived_near, arrived_far


class SumQuarters:
    def __init__(self, r, g, slot):
        self.r, self.g, self.slot, self.copies = r, g, slot, []

    def near_out(self, j, value):
        r, k = self.r, self.slot * 2 + j
        r.near_send[j] = value.astype(BF)
        self.copies.append(
            send(r.near_send.at[j], r.near_recv.at[j], r.near_s.at[k], r.near_r.at[k], self.g.device(1))
        )

    def near_in(self, j, value):
        self.copies[j].wait_recv()
        return value + self.r.near_recv[j].astype(F32)

    def far_out(self, value):
        r, k = self.r, self.slot
        r.far_send[...] = value.astype(BF)
        self.far = send(r.far_send, r.far_recv, r.far_s.at[k], r.far_r.at[k], self.g.device(2))

    def far_in(self, value):
        self.far.wait_recv()
        value = value + self.r.far_recv[...].astype(F32)
        for copy in self.copies + [self.far]:
            copy.wait_send()
        return value


def feed(r, q):
    pre = nn(r.hb[q], r.wu[...].reshape(768, 768))
    inner = jnp.tanh(GELU_C * (pre + GELU_A * pre * pre * pre))
    half = 0.5 * (1.0 + inner)
    r.gp[q] = half + 0.5 * pre * (1.0 - inner * inner) * (GELU_C * (1.0 + 3.0 * GELU_A * pre * pre))
    hid = (pre * half).astype(BF)
    r.hid[q] = hid
    return nt(hid, r.wd[...].reshape(768, 768))


def feed_back(r, q):
    grad_act = nn(r.dr2[q], r.wd[...].reshape(768, 768))
    grad_pre = (grad_act * r.gp[q]).astype(BF)
    r.du[q] = grad_pre
    return nt(grad_pre, r.wu[...].reshape(768, 768))


def attend_back(r, g, q):
    lane = lanes_of(QUARTER)
    keep = lanes_of(QUARTER, QUARTER) <= lax.broadcasted_iota(jnp.int32, (QUARTER, QUARTER), 0)
    dr1 = r.dr1[q]

    def head(h, carry):
        grad = nt(dr1, r.woh[h])
        af = r.af[h, q]
        inverse = af[:, 64:65]
        dden = -jnp.sum(grad * af, -1, keepdims=True) * inverse
        dden_low = dden.astype(BF).astype(F32)
        extra = jnp.where(lane == 64, dden_low, jnp.where(lane == 65, dden - dden_low, 0.0))
        dnum = jnp.where(lane < 64, grad * inverse, extra).astype(BF)
        qf, kf, va, sb = r.qf[h, q], r.kf[h, q], r.va[h, q], r.sb[h, q]
        ds = jnp.where(keep, nt(dnum, va), 0.0).astype(BF)
        dqf = nn(ds, kf)
        if q > 0:
            dqf = dqf + nt(dnum, r.st[h, q])
        dkf = tn(ds, qf)
        dv = tn(sb, dnum)
        if q < TENSOR - 1:
            dkv = r.state[h].astype(BF)
            dkf = dkf + nt(va, dkv)
            dv = dv + nn(kf, dkv)
        if q > 0:
            pairs = tn(qf, dnum)
            r.state[h] = pairs if q == TENSOR - 1 else r.state[h] + pairs
        dqf = dqf * r.qg[h, q]
        dkf = dkf * r.kg[h, q]
        r.fold[0, h] = dqf + half_roll(dqf)
        r.fold[1, h] = dkf + half_roll(dkf)
        r.fold[2, h] = dv
        return carry

    lax.fori_loop(0, 3, head, 0)
    for m in range(3):
        second = r.fold[m, 1] if m < 2 else half_roll(r.fold[m, 1])
        r.hb[q, :, 256 * m : 256 * m + LANES] = jnp.where(lane < 64, r.fold[m, 0], second).astype(BF)
        r.hb[q, :, 256 * m + LANES : 256 * (m + 1)] = jnp.where(lane < 64, r.fold[m, 2], 0.0).astype(BF)
    total = None
    for m in range(3):
        part = nt(r.hb[q, :, 256 * m : 256 * (m + 1)], r.wqkv[:, m].reshape(768, 256))
        total = part if total is None else total + part
    r.gp[q] = total


class ReduceDp:
    def __init__(self, src, low_buf, high_send, high_buf, sems, data, tensor, count):
        self.src, self.low_buf, self.high_send, self.high_buf = src, low_buf, high_send, high_buf
        self.low_s, self.low_r, self.high_s, self.high_r = sems
        self.tensor, self.n = tensor, count // 2
        self.high, self.low = data // 2, data % 2

    def at(self, step):
        return lax.rem(self.high + step, self.n)

    def start(self):
        partner = (self.high * 2 + 1 - self.low, self.tensor)
        self.across = {}
        for step in list(range(1, self.n)) + [0]:
            h = self.at(step)
            self.across[step] = send(
                self.src.at[h * 2 + 1 - self.low],
                self.low_buf.at[h],
                self.low_s.at[step],
                self.low_r.at[step],
                partner,
            )

    def pair(self, step):
        self.across[step].wait_recv()
        h = self.at(step)
        return self.src[h * 2 + self.low].astype(F32) + self.low_buf[h].astype(F32)

    def forward(self):
        self.along = []
        for step in range(1, self.n):
            self.high_send[step] = self.pair(step).astype(BF)
            self.along.append(
                send(
                    self.high_send.at[step],
                    self.high_buf.at[step],
                    self.high_s.at[step],
                    self.high_r.at[step],
                    (self.at(step) * 2 + self.low, self.tensor),
                )
            )

    def finish(self):
        total = self.pair(0)
        for step in range(1, self.n):
            self.along[step - 1].wait_recv()
            total = total + self.high_buf[step].astype(F32)
        for copy in list(self.across.values()) + self.along:
            copy.wait_send()
        return total


def assemble(r, core_rows):
    low = lanes_of(core_rows) < 64
    for pair in range(2):
        even, odd = r.abuf[2 * pair].astype(F32), r.abuf[2 * pair + 1].astype(F32)
        turned = half_roll(odd[:, :LANES])
        base = 3 * LANES * pair
        r.grad_a[:, base : base + LANES] = even[:, :LANES]
        r.grad_a[:, base + LANES : base + 2 * LANES] = jnp.where(low, even[:, LANES:], turned)
        r.grad_a[:, base + 2 * LANES : base + 3 * LANES] = jnp.where(low, turned, half_roll(odd[:, LANES:]))


def newton_scale(x):
    width = x.shape[1]

    def step(k, total):
        part = x[pl.ds(pl.multiple_of(k * 96, 96), 96)].astype(F32)
        return total + part * part

    total = lax.fori_loop(0, 8, step, jnp.zeros((96, width), F32))
    return 1.0 / (jnp.sqrt(jnp.sum(total)) + NS_EPS)


def newton_gram(x, gram, scale):
    edges = [slice(k * 256, (k + 1) * 256) for k in range(3)]
    for a in range(3):
        for b in range(a, 3):
            block = (nt(x[edges[a], :], x[edges[b], :]) * (scale * scale)).astype(BF)
            gram[a, :, edges[b]] = block
            if b > a:
                gram[b, :, edges[a]] = block.T


def newton(x, gram, poly, chunk, first, begin, end):
    edges = [slice(k * 256, (k + 1) * 256) for k in range(3)]

    def step(k, carry):
        scale = jnp.where(k == 0, first, 1.0)
        newton_gram(x, gram, scale)
        for a in range(3):
            for b in range(a, 3):
                block = COEF_C * nt(gram[a], gram[b])
                block = (block + COEF_B * gram[a, :, edges[b]].astype(F32)).astype(BF)
                poly[a, :, edges[b]] = block
                if b > a:
                    poly[b, :, edges[a]] = block.T

        def columns(c, inner):
            at = pl.ds(pl.multiple_of(c * chunk, chunk), chunk)
            old = x[:, at]
            x[:, at] = (scale * (COEF_A * old.astype(F32) + nn(poly[:3].reshape(768, 768), old))).astype(BF)
            return inner

        lax.fori_loop(0, x.shape[1] // chunk, columns, 0)
        return carry

    lax.fori_loop(begin, end, step, 0)


def newton_rows(x, gram, index, rows, chunk, out):
    own = newton_rows_gram(gram, index, rows)
    poly = (COEF_C * nn(own, gram[:3].reshape(768, 768)) + COEF_B * own.astype(F32)).astype(BF)
    here = pl.ds(pl.multiple_of(index * rows, rows), rows)
    for c in range(x.shape[1] // chunk):
        at = slice(c * chunk, (c + 1) * chunk)
        out[:, at] = (COEF_A * x[here, at].astype(F32) + nn(poly, x[:, at])).astype(BF)


def newton_rows_gram(gram, index, rows):
    parts = []
    for k in range(rows // 32):
        row = index * rows + 32 * k
        parts.append(gram[row // 256, pl.ds(pl.multiple_of(lax.rem(row, 256), 32), 32), :])
    return jnp.concatenate(parts, axis=0)


def angles(r):
    rows = TENSOR * QUARTER
    length = r.lengths[0]
    where = lax.broadcasted_iota(jnp.int32, (rows, LANES), 0)
    theta = 0.5 * math.pi * jnp.minimum(where, length - 1).astype(F32) / length.astype(F32)
    table = jnp.where(lanes_of(rows) < 64, jnp.cos(theta), jnp.sin(theta))
    live = jnp.where(where < length, 1.0, 0.0)
    r.gp[:, :, :LANES] = table.reshape(TENSOR, QUARTER, LANES)
    r.gp[:, :, LANES : 2 * LANES] = (table * live).reshape(TENSOR, QUARTER, LANES)


def cut_heads(r, rows):
    low = lanes_of(rows) < 64
    tiles = [r.attn_w[0, :, k * LANES : (k + 1) * LANES] for k in range(6)]
    for pair in range(2):
        first, middle, last = tiles[3 * pair : 3 * pair + 3]
        turned, rest = half_roll(middle), half_roll(last)
        parts = [first, jnp.where(low, middle, 0.0), jnp.where(low, turned, rest), jnp.where(low, rest, 0.0)]
        for k, part in enumerate(parts):
            r.slabs[2 * pair + k // 2, :, (k % 2) * LANES : (k % 2 + 1) * LANES] = part.astype(BF)


def assemble(r, core_rows):
    low = lanes_of(core_rows) < 64
    for pair in range(2):
        even, odd = r.abuf[2 * pair].astype(F32), r.abuf[2 * pair + 1].astype(F32)
        turned = half_roll(odd[:, :LANES])
        base = 3 * LANES * pair
        r.grad_a[:, base : base + LANES] = even[:, :LANES]
        r.grad_a[:, base + LANES : base + 2 * LANES] = jnp.where(low, even[:, LANES:], turned)
        r.grad_a[:, base + 2 * LANES : base + 3 * LANES] = jnp.where(low, turned, half_roll(odd[:, LANES:]))


def step_body(count, rows, r):
    g = Group()
    data, tensor, far, core = g.data, g.tensor, g.far, g.core
    high, low = data // 2, data % 2
    other = high * 2 + 1 - low
    n = count // 2
    half = rows // 2
    near_dev, far_dev = g.device(1), g.device(2)

    cut_heads(r, rows)
    r.wo_own[...] = r.attn_w[0].astype(BF).reshape(2, half, 768)
    greet(
        [g.device(k) for k in (1, 2, 3)]
        + [(lax.rem(data + k, count), tensor) for k in range(1, count)]
        + [(other, tensor ^ 1)]
    )

    for k in (1, 2, 3):
        peer = tensor ^ k

        @pl.when(tensor < 3)
        def _():
            send(r.slabs.at[peer], r.wqkv.at[data, tensor], r.slab_s.at[k], r.slab_r.at[tensor], g.device(k))

        @pl.when(tensor == 3)
        def _():
            send(r.wo_own.at[peer % 2], r.wo.at[data, peer % 2], r.slab_s.at[k], r.slab_r.at[3], g.device(k))

    r.seq[tensor] = r.tokens[...]
    mine = r.seq.at[tensor]
    tok_near = send(mine, mine, r.tok_s.at[0], r.tok_r.at[0], near_dev)
    tok_far = send(mine, mine, r.tok_s.at[1], r.tok_r.at[1], far_dev)

    @pl.when(tensor < 3)
    def _():
        r.wqkv[data, tensor] = r.slabs[tensor]

    @pl.when(tensor == 3)
    def _():
        r.wo[data, core] = r.wo_own[core]

    r.wu[data] = r.up_w[...].astype(BF)
    r.wd[data] = r.down_w[...].astype(BF)

    def gather(slot_of, key):
        return GatherDp(slot_of, r.gather_s.at[key], r.gather_r.at[key], data, tensor, count)

    heads = [gather(lambda d, m=m: r.wqkv.at[d, m], m) for m in range(3)]
    outs = gather(lambda d: r.wo.at[d, core], 3)
    ups = [gather(lambda d, k=k: r.wu.at[d, pl.ds(k * half, half)], 4 + k) for k in range(2)]
    downs = [gather(lambda d, k=k: r.wd.at[d, pl.ds(k * half, half)], 6 + k) for k in range(2)]

    for m in range(3):

        @pl.when(tensor != m)
        def _():
            await_bytes(r.wqkv.at[data, m], r.slab_r.at[m])

        heads[m].start()
    angles(r)

    @pl.when(tensor != 3)
    def _():
        await_bytes(r.wo.at[data, core], r.slab_r.at[3])

    heads[0].forward()
    outs.start()
    tok_far.wait_recv()
    slot = r.seq.at[tensor ^ 2]
    tok_pass = send(slot, slot, r.tok_s.at[2], r.tok_r.at[2], near_dev)
    heads[1].forward()
    ups[0].start()
    heads[2].forward()
    ups[1].start()
    for m in range(3):
        heads[m].arrive()
        spread_weights(r, [m])
    tok_near.wait_recv()
    tok_pass.wait_recv()
    project(r)
    outs.forward()
    downs[0].start()
    downs[1].start()

    copies = [[], []]
    for j in range(2):
        attend(r, 2 * j)
        attend(r, 2 * j + 1)
        mine, rest = 2 * j + core, 2 * j + 1 - core
        for k in (2, 1, 3):
            quarter = mine if k == 2 else rest
            copies[j].append(
                send(r.attn.at[quarter], r.aall.at[tensor, j], r.attn_s.at[j, k], r.attn_r.at[j, k], g.device(k))
            )
        r.aall[tensor, j] = r.attn[mine]
        ups[j].forward()

    outs.arrive()
    share = []
    for d in range(count):
        part = r.wo.at[d, core]
        share.append(send(part, part, r.share_s.at[d], r.share_r.at[d], near_dev))
    downs[0].forward()
    for d in range(count):
        part = r.wo.at[d, 1 - core]
        await_bytes(part, r.share_r.at[d])
    whole_out = r.wo[...].reshape(768, 768)
    wop = [r.xmat.at[256 * t : 256 * (t + 1), 1536:2304] for t in range(3)] + [r.xmat.at[0:256, 2304:3072]]
    for t in range(TENSOR):
        wop[t][:192, :] = whole_out[192 * t : 192 * (t + 1)]
        wop[t][192:, :] = jnp.zeros((64, 768), BF)
    for t in range(TENSOR):

        @pl.when(tensor == t)
        def _():
            for h in range(3):
                r.woh[h, :64] = wop[t][64 * h : 64 * (h + 1), :]
                r.woh[h, 64:] = jnp.zeros((64, 768), BF)

    gain1, bias1, gain2, bias2 = (r.norms[k : k + 1] for k in range(4))
    hs = []
    for group_copies in copies:
        for copy in group_copies:
            copy.wait_recv()
    for own in (False, True):
        j = far if own else 1 - far
        q = 2 * j + core
        branch = nn(r.aall[0, j], wop[0][...])
        for t in range(1, TENSOR):
            branch = branch + nn(r.aall[t, j], wop[t][...])
        normal, scale = norm_rows(r.seq[q].astype(F32) + branch)
        hidden = normal * gain1 + bias1
        r.hb[q] = hidden.astype(BF)
        if own:
            r.n1[...] = normal
            r.s1[...] = jnp.broadcast_to(scale, (QUARTER, LANES))
            r.h1[...] = hidden
        hs.append(send(r.hb.at[q], r.hb.at[q], r.h_s.at[int(own)], r.h_r.at[int(own)], near_dev))
    downs[1].forward()
    for group_copies in copies:
        for copy in group_copies:
            copy.wait_send()

    for part in ups + downs:
        part.arrive()
    total = SumQuarters(r, g, 0)
    kept = feed(r, tensor ^ 2)
    hs[0].wait_recv()
    total.near_out(0, feed(r, tensor ^ 3))
    total.far_out(total.near_in(0, kept))
    hs[1].wait_recv()
    total.near_out(1, feed(r, tensor ^ 1))
    kept = feed(r, tensor)
    for part in heads + [outs] + ups + downs:
        part.close()
    for copy in hs + share + [tok_near, tok_far, tok_pass]:
        copy.wait_send()
    for k in (1, 2, 3):

        @pl.when(tensor < 3)
        def _():
            await_bytes(r.slabs.at[0], r.slab_s.at[k])

        @pl.when(tensor == 3)
        def _():
            await_bytes(r.wo_own.at[0], r.slab_s.at[k])

    kept = total.far_in(total.near_in(1, kept))

    n2, s2 = norm_rows(r.h1[...] + kept)
    row = lax.broadcasted_iota(jnp.int32, (QUARTER, 1), 0) + tensor * QUARTER
    live = jnp.where(row < r.lengths[0], 1.0, 0.0)
    r.mixed[...] = (live * (n2 * gain2 + bias2)).astype(BF)
    dy = live * r.cotangent[...].astype(F32)
    r.partial[2:3] = jnp.sum(dy * n2, 0, keepdims=True)
    r.partial[3:4] = jnp.sum(dy, 0, keepdims=True)
    dr2 = norm_rows_back(n2, s2, dy * gain2)
    r.dr2f[...] = dr2
    r.dr2[tensor] = dr2.astype(BF)
    near, distant = spread_quarter(r, g, r.dr2, r.dr2_s, r.dr2_r)

    sums = {}
    for key in "dua":
        sums[key] = ReduceDp(
            *(getattr(r, name + key) for name in ("g", "low", "hs", "hb")),
            [getattr(r, name + key) for name in ("ls_", "lr_", "hs_", "hr_")],
            data,
            tensor,
            count,
        )
    total = SumQuarters(r, g, 1)
    r.dh[...] = feed_back(r, tensor)
    near()
    total.near_out(0, feed_back(r, tensor ^ 1))
    distant()
    total.near_out(1, feed_back(r, tensor ^ 3))
    total.far_out(total.near_in(1, feed_back(r, tensor ^ 2)))
    grad = tn(r.dr2[...].reshape(1024, 768), r.hid[...].reshape(1024, 768))
    r.gd[...] = grad.astype(BF).reshape(r.gd.shape)
    sums["d"].start()
    grad = tn(r.hb[...].reshape(1024, 768), r.du[...].reshape(1024, 768))
    r.gu[...] = grad.astype(BF).reshape(r.gu.shape)
    sums["u"].start()
    r.dh[...] = total.near_in(0, r.dh[...]) + r.dr2f[...]
    sums["d"].forward()
    dh = total.far_in(r.dh[...])

    n1 = r.n1[...]
    r.partial[0:1] = jnp.sum(dh * n1, 0, keepdims=True)
    r.partial[1:2] = jnp.sum(dh, 0, keepdims=True)
    dr1 = norm_rows_back(n1, r.s1[:, :1], dh * gain1)
    r.dr1f[...] = dr1
    r.dr1[tensor] = dr1.astype(BF)
    near, distant = spread_quarter(r, g, r.dr1, r.dr1_s, r.dr1_r)
    r.pbuf[tensor] = r.partial[...]
    parts = []
    for k in (1, 2, 3):
        parts.append(send(r.partial, r.pbuf.at[tensor], r.pt_s.at[k], r.pt_r.at[k], g.device(k)))
    near()
    sums["u"].forward()
    distant()

    attend_back(r, g, 3)
    for copy in parts:
        copy.wait()
    r.psum[...] = ((r.pbuf[0] + r.pbuf[1]) + r.pbuf[2]) + r.pbuf[3]
    r.qbuf[data] = r.psum[...]
    parts = []
    for k in range(1, count):
        to = (lax.rem(data + k, count), tensor)
        parts.append(send(r.psum, r.qbuf.at[data], r.pd_s.at[k], r.pd_r.at[k], to))
    attend_back(r, g, 2)
    here = pl.ds(pl.multiple_of(data * rows, rows), rows)
    there = pl.ds(pl.multiple_of(other * rows, rows), rows)

    def rows_of(d):
        return pl.ds(pl.multiple_of(d * rows, rows), rows)

    def cols(t):
        return pl.ds(pl.multiple_of(t * 768, 768), 768)

    moment = 0.5 * r.down_mom[...] + sums["d"].finish()
    r.mom_d[...] = moment
    r.xsd[...] = moment.astype(BF)
    moment = 0.5 * r.up_mom[...] + sums["u"].finish()
    r.mom_u[...] = moment
    r.xsu[...] = moment.astype(BF)
    own = r.xmat.at[here, cols(tensor)]

    @pl.when(far == 0)
    def _():
        r.xmat[here, cols(tensor)] = r.xsu[...]
        send(r.xsd, own, r.swap_s, r.swap_r, far_dev)

    @pl.when(far == 1)
    def _():
        r.xmat[here, cols(tensor)] = r.xsd[...]
        send(r.xsu, own, r.swap_s, r.swap_r, far_dev)

    blocks = [
        GatherDp(lambda d: r.xmat.at[rows_of(d), cols(tensor)], r.x_s.at[0], r.x_r.at[0], data, tensor, count),
        GatherDp(lambda d: r.xmat.at[rows_of(d), cols(tensor ^ 2)], r.x_s.at[1], r.x_r.at[1], data, tensor, count),
    ]

    def pass_on(b, d):
        @pl.when(core == 1)
        def _():
            slot = blocks[b].slot_of(d)
            send(slot, slot, r.j_s.at[b, d], r.j_r.at[b, d], near_dev)

    blocks[0].start()
    attend_back(r, g, 1)
    await_bytes(r.xmat.at[here, cols(tensor ^ 2)], r.swap_r)
    blocks[1].start()
    attend_back(r, g, 0)

    grad = tn(r.seq[...].reshape(1024, 768), r.hb[...].reshape(1024, 768)).astype(BF)
    for m in range(3):
        r.ga[:, m] = grad[:, 256 * m : 256 * (m + 1)].reshape(count, rows, 256)
    sums["a"].start()
    grad = tn(r.attn[...].reshape(1024, 256), r.dr1[...].reshape(1024, 768)).astype(BF)
    r.go[...] = grad[:192].reshape(r.go.shape)
    out_low = send(r.go.at[1 - low], r.olow, r.o_s.at[0], r.o_r.at[0], (other, tensor))
    total = SumQuarters(r, g, 2)
    total.near_out(0, r.gp[tensor ^ 3])
    total.near_out(1, r.gp[tensor ^ 1])
    total.far_out(total.near_in(0, r.gp[tensor ^ 2]))
    for b in range(2):
        blocks[b].forward()
        for step in range(n):
            pass_on(b, blocks[b].peer(step))
    sums["a"].forward()

    out_low.wait_recv()
    r.grad_a[...] = r.go[low].astype(F32) + r.olow[...].astype(F32)
    r.osend[...] = r.grad_a[...].astype(BF)
    for k in range(1, n):

        @pl.when(lax.rem(high + k, n) == tensor)
        def _():
            send(r.osend, r.ohigh.at[k], r.o_s.at[1], r.o_r.at[k], (tensor * 2 + low, tensor))

    r.input_grad[...] = total.far_in(total.near_in(1, r.gp[tensor])) + r.dr1f[...]

    for b in range(2):
        for step in range(n):
            blocks[b].across[step].wait_recv()
            pass_on(b, blocks[b].peer(n - step) + 1 - 2 * low if step else other)
        blocks[b].close()

    @pl.when(core == 0)
    def _():
        for b in range(2):
            for d in range(count):
                await_bytes(own, r.j_r.at[b, d])
        r.scale[0] = newton_scale(r.xmat)
        newton(r.xmat, r.du, r.hid, 512, r.scale[0], 0, 1)

    summed = sums["a"].finish()
    for m in range(3):
        r.asend[m] = summed[m].astype(BF)
    for m in range(3):

        @pl.when(tensor != m)
        def _():
            send(r.asend.at[m], r.abuf.at[tensor], r.a_s.at[m], r.a_r.at[tensor], (data, m))

        @pl.when(tensor == m)
        def _():
            r.abuf[tensor] = r.asend[m]

    @pl.when(high == tensor)
    def _():
        whole = r.grad_a[...]
        for k in range(1, n):
            await_bytes(r.ohigh.at[k], r.o_r.at[k])
            whole = whole + r.ohigh[k].astype(F32)
        r.grad_a[...] = whole
        r.oout[...] = whole.astype(BF)

    @pl.when((high == tensor) & (tensor != 3))
    def _():
        send(r.oout, r.oin, r.o_s.at[2], r.oin_r, (data, 3))

    @pl.when((tensor == 3) & (high != 3))
    def _():
        await_bytes(r.oin, r.oin_r)
        r.grad_a[...] = r.oin[...].astype(F32)

    for t in range(TENSOR):

        @pl.when((tensor < 3) & (tensor != t))
        def _():
            await_bytes(r.abuf.at[t], r.a_r.at[t])

    @pl.when(tensor < 3)
    def _():
        assemble(r, rows)

    moment = 0.5 * r.attn_mom[0] + r.grad_a[...]
    r.mom_a[...] = moment
    r.xsa[...] = moment.astype(BF)

    at_work = (high * 2 + core, far * 2 + 1)

    @pl.when((core == 1) & (low == 1))
    def _():
        r.xa[here] = r.xsa[...]

    @pl.when((core == 0) | (low == 0))
    def _():
        send(r.xsa, r.xa.at[here], r.e_s, r.e_r.at[low], at_work)

    for side in range(2):
        part = r.xa.at[rows_of(high * 2 + side)]

        @pl.when((core == 1) & ((low == 0) | (side == 0)))
        def _():
            await_bytes(part, r.e_r.at[side])

        @pl.when(core == 1)
        def _():
            for k in range(1, n):
                to = (lax.rem(high + k, n) * 2 + low, tensor)
                send(part, part, r.f_s.at[side, k], r.f_r.at[side, k], to)

    for copy in parts:
        copy.wait()
    r.norm_grad[...] = sum((r.qbuf[d] for d in range(1, count)), r.qbuf[0])

    @pl.when(core == 0)
    def _():
        newton(r.xmat, r.du, r.hid, 512, 1.0, 1, NS_STEPS - 1)
        newton_gram(r.xmat, r.du, 1.0)
        newton_rows(r.xmat, r.du, data, rows, 768, r.orow)

    for m, out in enumerate((r.o_u, r.o_d)):

        @pl.when((core == 0) & (far == m))
        def _():
            for k in (1, 2, 3):
                send(r.orow.at[:, cols(tensor ^ k)], out, r.w_s.at[k], r.w_r.at[m], g.device(k))
            out[...] = r.orow[:, cols(tensor)]

    owner = far * 2 + low

    @pl.when(core == 1)
    def _():
        for side in range(2):
            for k in range(1, n):
                await_bytes(r.xa.at[rows_of(lax.rem(high + n - k, n) * 2 + side)], r.f_r.at[side, k])
                await_bytes(r.xa.at[here], r.f_s.at[side, k])
        newton(r.xa, r.du, r.hid, 768, newton_scale(r.xa), 0, NS_STEPS - 1)
        newton_gram(r.xa, r.du, 1.0)
        newton_rows(r.xa, r.du, other, rows, 768, r.orow.at[:, 768:1536])
        send(r.orow.at[:, 768:1536], r.o_a, r.v_s.at[0], r.v_r, (other, owner))
        newton_rows(r.xa, r.du, data, rows, 768, r.orow.at[:, :768])

    @pl.when((core == 1) & (low == 1))
    def _():
        r.o_a[...] = r.orow[:, :768]

    @pl.when((core == 1) & (low == 0))
    def _():
        send(r.orow.at[:, :768], r.o_a, r.v_s.at[1], r.v_r, (data, owner))

    @pl.when((core == 0) | (low == 0))
    def _():
        await_bytes(r.o_a, r.v_r)

    for m, out in enumerate((r.o_u, r.o_d)):

        @pl.when((core == 1) | (far != m))
        def _():
            await_bytes(out, r.w_r.at[m])

    await_bytes(r.xsd, r.swap_s)
    out_low.wait_send()

    @pl.when(high != tensor)
    def _():
        await_bytes(r.osend, r.o_s.at[1])

    @pl.when((high == tensor) & (tensor != 3))
    def _():
        await_bytes(r.oout, r.o_s.at[2])

    for m in range(3):

        @pl.when(tensor != m)
        def _():
            await_bytes(r.asend.at[m], r.a_s.at[m])

    @pl.when((core == 0) | (low == 0))
    def _():
        await_bytes(r.xsa, r.e_s)

    @pl.when(core == 0)
    def _():
        for k in (1, 2, 3):
            await_bytes(r.o_u, r.w_s.at[k])

    @pl.when(core == 1)
    def _():
        for b in range(2):
            for d in range(count):
                await_bytes(own, r.j_s.at[b, d])
        await_bytes(r.o_a, r.v_s.at[0])

    @pl.when((core == 1) & (low == 0))
    def _():
        await_bytes(r.o_a, r.v_s.at[1])


def step_call(count, rows, ins):
    v = pltpu.VMEM
    n = count // 2
    one = pltpu.SemaphoreType.DMA
    outs = dict(
        mixed=shape(QUARTER, 768),
        input_grad=shape(QUARTER, 768, dtype=F32),
        mom_a=shape(rows, 768, dtype=F32),
        mom_u=shape(rows, 768, dtype=F32),
        mom_d=shape(rows, 768, dtype=F32),
        norm_grad=shape(4, 768, dtype=F32),
        o_u=shape(rows, 768),
        o_d=shape(rows, 768),
        o_a=shape(rows, 768),
    )
    per_head = (3, TENSOR, QUARTER, LANES)
    quarters = (TENSOR, QUARTER, 768)
    scratch = dict(
        slabs=v((TENSOR, rows, 256), BF),
        wo_own=v((2, rows // 2, 768), BF),
        seq=v(quarters, BF),
        wqkv=v((count, 3, rows, 256), BF),
        wo=v((count, 2, rows // 2, 768), BF),
        wu=v((count, rows, 768), BF),
        wd=v((count, rows, 768), BF),
        woh=v((3, LANES, 768), BF),
        slab_s=dma(4),
        slab_r=dma(4),
        tok_s=dma(3),
        tok_r=dma(3),
        share_s=dma(count),
        share_r=dma(count),
        gather_s=dma(8, count),
        gather_r=dma(8, count),
        qf=v(per_head, BF),
        kf=v(per_head, BF),
        va=v(per_head, BF),
        qg=v(per_head, F32),
        kg=v(per_head, F32),
        af=v(per_head, F32),
        sb=v((3, TENSOR, QUARTER, QUARTER), BF),
        st=v((3, TENSOR, LANES, LANES), BF),
        state=v((3, LANES, LANES), F32),
        attn=v((TENSOR, QUARTER, 256), BF),
        aall=v((TENSOR, 2, QUARTER, 256), BF),
        fold=v((3, 3, QUARTER, LANES), F32),
        attn_s=dma(2, 4),
        attn_r=dma(2, 4),
        hb=v(quarters, BF),
        n1=v((QUARTER, 768), F32),
        s1=v((QUARTER, LANES), F32),
        h1=v((QUARTER, 768), F32),
        hid=v(quarters, BF),
        gp=v(quarters, F32),
        du=v(quarters, BF),
        dr2=v(quarters, BF),
        dr2f=v((QUARTER, 768), F32),
        dr1=v(quarters, BF),
        dr1f=v((QUARTER, 768), F32),
        dh=v((QUARTER, 768), F32),
        near_send=v((2, QUARTER, 768), BF),
        near_recv=v((2, QUARTER, 768), BF),
        far_send=v((QUARTER, 768), BF),
        far_recv=v((QUARTER, 768), BF),
        near_s=dma(6),
        near_r=dma(6),
        far_s=dma(3),
        far_r=dma(3),
        h_s=dma(2),
        h_r=dma(2),
        dr2_s=dma(3),
        dr2_r=dma(3),
        dr1_s=dma(3),
        dr1_r=dma(3),
        gu=v((count, rows, 768), BF),
        gd=v((count, rows, 768), BF),
        ga=v((count, 3, rows, 256), BF),
        go=v((2, rows, 768), BF),
        partial=v((4, 768), F32),
        pbuf=v((TENSOR, 4, 768), F32),
        psum=v((4, 768), F32),
        qbuf=v((count, 4, 768), F32),
        pt_s=dma(4),
        pt_r=dma(4),
        pd_s=dma(count),
        pd_r=dma(count),
        olow=v((rows, 768), BF),
        osend=v((rows, 768), BF),
        ohigh=v((n, rows, 768), BF),
        oout=v((rows, 768), BF),
        oin=v((rows, 768), BF),
        o_s=dma(3),
        o_r=dma(n),
        oin_r=one,
        asend=v((3, rows, 256), BF),
        abuf=v((TENSOR, rows, 256), BF),
        a_s=dma(3),
        a_r=dma(TENSOR),
        grad_a=v((rows, 768), F32),
        xsd=v((rows, 768), BF),
        xsu=v((rows, 768), BF),
        xsa=v((rows, 768), BF),
        xmat=v((768, TENSOR * 768), BF),
        xa=v((768, 768), BF),
        swap_s=one,
        swap_r=one,
        x_s=dma(2, count),
        x_r=dma(2, count),
        e_s=one,
        e_r=dma(2),
        f_s=dma(2, n),
        f_r=dma(2, n),
        j_s=dma(2, count),
        j_r=dma(2, count),
        orow=v((rows, TENSOR * 768), BF),
        scale=pltpu.SMEM((1,), F32),
        w_s=dma(4),
        w_r=dma(2),
        v_s=dma(2),
        v_r=one,
    )
    for key in "dua":
        part = (3, rows, 256) if key == "a" else (rows, 768)
        for name in ("low", "hs", "hb"):
            scratch[name + key] = v((n,) + part, BF)
        for name in ("ls_", "lr_", "hs_", "hr_"):
            scratch[name + key] = dma(n)
    body = functools.partial(step_body, count, rows)
    return kernel_call(body, "layer_step", ins, outs, scratch, 0, ("lengths",))


def finish_body(r):
    keep = 1.0 - MUON_RATE * MUON_DECAY
    rate_a = MUON_RATE * 0.2 * math.sqrt(768)
    rate_ff = MUON_RATE * 0.2 * math.sqrt(TENSOR * 768)
    r.attn_new[0] = r.attn_w[0] * keep - rate_a * r.o_a[...].astype(F32)
    r.up_new[...] = r.up_w[...] * keep - rate_ff * r.o_u[...].astype(F32)
    r.down_new[...] = r.down_w[...] * keep - rate_ff * r.o_d[...].astype(F32)
    r.attn_moment[0] = r.mom_a[...]
    r.up_moment[...] = r.mom_u[...]
    r.down_moment[...] = r.mom_d[...]
    r.mixed_out[...] = r.mixed[...]
    r.input_grad_out[...] = r.input_grad[...]
    grad = r.norm_grad[...]
    moment1 = 0.5 * r.norm_m1[...] + 0.5 * grad
    moment2 = 0.95 * r.norm_m2[...] + 0.05 * grad * grad
    first_hat = moment1 / (1.0 - 0.5**STEP)
    second_hat = moment2 / (1.0 - 0.95**STEP)
    r.norm_moment1[...] = moment1
    r.norm_moment2[...] = moment2
    r.norm_new[...] = r.norms[...] - ADAM_RATE * first_hat / (jnp.sqrt(second_hat) + 1e-08)


def finish_call(ins):
    rows = ins["up_w"].shape[0]
    block = shape(rows, 768, dtype=F32)
    small = shape(4, 768, dtype=F32)
    outs = dict(
        mixed_out=shape(QUARTER, 768),
        input_grad_out=shape(QUARTER, 768, dtype=F32),
        attn_new=shape(1, rows, 768, dtype=F32),
        attn_moment=shape(1, rows, 768, dtype=F32),
        up_new=block,
        up_moment=block,
        down_new=block,
        down_moment=block,
        norm_moment1=small,
        norm_moment2=small,
        norm_new=small,
    )
    return kernel_call(finish_body, "finish", ins, outs, {}, None)


def step_on_device(
    tokens,
    cotangent,
    lengths,
    attn_w,
    up_w,
    down_w,
    norm_params,
    attn_mom,
    up_mom,
    down_mom,
    norm_m1,
    norm_m2,
):
    count = lax.axis_size("dp")
    rows = attn_w.shape[1]
    done = step_call(
        count,
        rows,
        dict(
            lengths=lengths,
            tokens=tokens,
            cotangent=cotangent,
            attn_w=attn_w,
            up_w=up_w,
            down_w=down_w.T,
            norms=norm_params,
            attn_mom=attn_mom,
            up_mom=up_mom,
            down_mom=down_mom.T,
        ),
    )
    last = finish_call(
        dict(
            attn_w=attn_w,
            up_w=up_w,
            down_w=down_w.T,
            norms=norm_params,
            norm_m1=norm_m1,
            norm_m2=norm_m2,
            **done,
        )
    )
    return (
        last["mixed_out"],
        last["input_grad_out"],
        last["attn_new"],
        last["attn_moment"],
        last["up_new"],
        last["up_moment"],
        last["down_new"].T,
        last["down_moment"].T,
        last["norm_moment1"],
        last["norm_moment2"],
        last["norm_new"],
    )


def solution(mesh):
    placed = (
        P(("dp", "tensor"), None),
        P(("dp", "tensor"), None),
        P("dp"),
        P("tensor", "dp", None),
        P("dp", "tensor"),
        P("tensor", "dp"),
        P(),
        P("tensor", "dp", None),
        P("dp", "tensor"),
        P("tensor", "dp"),
        P(),
        P(),
    )
    whole_tiles = mesh.shape["dp"] == 8 and mesh.shape["tensor"] == TENSOR
    return jax.shard_map(
        step_on_device if whole_tiles else on_device,
        mesh=mesh,
        in_specs=placed,
        out_specs=(
            P(("dp", "tensor"), None),
            P(("dp", "tensor"), None),
            P("tensor", "dp", None),
            P("tensor", "dp", None),
            P("dp", "tensor"),
            P("dp", "tensor"),
            P("tensor", "dp"),
            P("tensor", "dp"),
            P(),
            P(),
            P(),
        ),
        check_vma=False,
    )
```

```python
import functools
import math
import types

import jax
import jax.numpy as jnp
from jax import lax
from jax.experimental import pallas as pl
from jax.experimental.pallas import tpu as pltpu
from jax.sharding import PartitionSpec as P

HEADS = 12
HDIM = 64
BLOCK = 64
NS_STEPS = 5
STEP = 10


NORM_EPS = 1e-05
NS_EPS = 1e-07
COEF_A = 3.4445
COEF_B = -4.775
COEF_C = 2.0315
MUON_RATE = 0.15
MUON_DECAY = 0.1
ADAM_RATE = 0.2


def cut_along(array, dim, size):
    lengths = array.shape
    pieces = array.reshape(*lengths[:dim], size, lengths[dim] // size, *lengths[dim + 1 :])
    return jnp.moveaxis(pieces, dim, 0)


def sum_at_owner(array, axis, dim):
    size = lax.axis_size(axis)
    pieces = lax.all_to_all(cut_along(array, dim, size), axis, 0, 0, tiled=True)
    return jnp.sum(pieces.astype(jnp.float32), axis=0)


def sent_together(arrays, axis, dim, along):
    widths = [a.shape[along] for a in arrays]
    both = jnp.concatenate(arrays, axis=along)
    whole = sum_at_owner(both, axis, dim)
    return tuple(jnp.split(whole, [sum(widths[:k]) for k in range(1, len(widths))], axis=along))


def partner(array, axis, bit):
    return lax.ppermute(array, axis, [(i, i ^ 1 << bit) for i in range(lax.axis_size(axis))])


def contract_rows(left, right):
    return lax.dot_general(
        left, right, (((0,), (0,)), ((), ())), preferred_element_type=jnp.float32
    )


def contract_cols(left, right):
    return lax.dot_general(
        left, right, (((1,), (1,)), ((), ())), preferred_element_type=jnp.float32
    )


def norm_forward(resid, gain, bias):
    center = resid - jnp.mean(resid, -1, keepdims=True)
    spread = jnp.mean(center * center, -1, keepdims=True)
    scale_inv = lax.rsqrt(spread + NORM_EPS)
    normal_rows = center * scale_inv
    return (normal_rows, scale_inv, normal_rows * gain + bias)


def norm_back(normal_rows, scale_inv, grad_normed):
    return scale_inv * (
        grad_normed
        - jnp.mean(grad_normed, -1, keepdims=True)
        - normal_rows * jnp.mean(grad_normed * normal_rows, -1, keepdims=True)
    )


def smooth_gate(values):
    return jax.nn.gelu(values, approximate=True)


def features(proj, cosine, sine, weight_rows):
    count = proj.shape[0]
    soft = jax.nn.softplus(proj).reshape(count, HEADS, HDIM)
    both = jnp.concatenate([soft * cosine[:, None, None], soft * sine[:, None, None]], -1)
    return both * weight_rows[:, None, None]


def features_back(grad_feat, proj, cosine, sine, weight_rows):
    count = proj.shape[0]
    grad_soft = (
        grad_feat[..., :HDIM] * cosine[:, None, None] + grad_feat[..., HDIM:] * sine[:, None, None]
    )
    grad_soft = grad_soft * weight_rows[:, None, None]
    slope = jax.nn.sigmoid(proj).reshape(count, HEADS, HDIM)
    return (grad_soft * slope).reshape(count, HEADS * HDIM).astype(jnp.bfloat16)


def blocked(array):
    return array.reshape(array.shape[0] // BLOCK, BLOCK, array.shape[1], array.shape[2])


def attend_forward(qblock, kblock, vblock, lower):
    scores = (
        jnp.einsum("nihf,njhf->nhij", qblock, kblock, preferred_element_type=jnp.float32) * lower
    )
    scores_low = scores.astype(jnp.bfloat16)
    pairs = jnp.einsum("njhf,njhd->nhfd", kblock, vblock, preferred_element_type=jnp.float32)
    state = jnp.cumsum(pairs, 0) - pairs
    state_low = state.astype(jnp.bfloat16)
    key_sum = jnp.sum(kblock.astype(jnp.float32), 1)
    zsum = jnp.cumsum(key_sum, 0) - key_sum
    numer = jnp.einsum("nhij,njhd->nihd", scores_low, vblock, preferred_element_type=jnp.float32)
    numer = numer + jnp.einsum(
        "nihf,nhfd->nihd", qblock, state_low, preferred_element_type=jnp.float32
    )
    denom = jnp.transpose(jnp.sum(scores, -1), (0, 2, 1))
    denom = denom + jnp.einsum(
        "nihf,nhf->nih", qblock.astype(jnp.float32), zsum, precision=lax.Precision.HIGHEST
    )
    return (scores_low, state_low, zsum, denom, numer / denom[..., None])


def attend_backward(
    qblock, kblock, vblock, lower, scores_low, state_low, zsum, denom, result, grad_out
):
    grad_numer = (grad_out / denom[..., None]).astype(jnp.bfloat16)
    grad_denom = -jnp.sum(grad_out * result, -1) / denom
    grad_scores = jnp.einsum(
        "nihd,njhd->nhij", grad_numer, vblock, preferred_element_type=jnp.float32
    )
    grad_scores = ((grad_scores + jnp.transpose(grad_denom, (0, 2, 1))[..., None]) * lower).astype(
        jnp.bfloat16
    )
    grad_state = jnp.einsum(
        "nihf,nihd->nhfd", qblock, grad_numer, preferred_element_type=jnp.float32
    )
    grad_pairs = (jnp.cumsum(grad_state[::-1], 0)[::-1] - grad_state).astype(jnp.bfloat16)
    grad_z = jnp.einsum(
        "nih,nihf->nhf", grad_denom, qblock.astype(jnp.float32), precision=lax.Precision.HIGHEST
    )
    grad_ksum = jnp.cumsum(grad_z[::-1], 0)[::-1] - grad_z
    grad_qf = jnp.einsum("nhij,njhf->nihf", grad_scores, kblock, preferred_element_type=jnp.float32)
    grad_qf = grad_qf + jnp.einsum(
        "nihd,nhfd->nihf", grad_numer, state_low, preferred_element_type=jnp.float32
    )
    grad_qf = grad_qf + grad_denom[..., None] * zsum[:, None]
    grad_kf = jnp.einsum("nhij,nihf->njhf", grad_scores, qblock, preferred_element_type=jnp.float32)
    grad_kf = grad_kf + jnp.einsum(
        "njhd,nhfd->njhf", vblock, grad_pairs, preferred_element_type=jnp.float32
    )
    grad_kf = grad_kf + grad_ksum[:, None]
    grad_val = jnp.einsum(
        "nhij,nihd->njhd", scores_low, grad_numer, preferred_element_type=jnp.float32
    )
    grad_val = grad_val + jnp.einsum(
        "njhf,nhfd->njhd", kblock, grad_pairs, preferred_element_type=jnp.float32
    )
    return (grad_qf, grad_kf, grad_val.astype(jnp.bfloat16))


def newton_update(iterate, gram):
    poly = (
        COEF_B * gram.astype(jnp.float32)
        + COEF_C * jnp.dot(gram, gram, preferred_element_type=jnp.float32)
    ).astype(jnp.bfloat16)
    return (
        COEF_A * iterate.astype(jnp.float32)
        + jnp.dot(poly, iterate, preferred_element_type=jnp.float32)
    ).astype(jnp.bfloat16)


def orthogonalize(iterate):
    for step in range(NS_STEPS):
        gram = jnp.dot(iterate, iterate.T, preferred_element_type=jnp.float32).astype(jnp.bfloat16)
        iterate = newton_update(iterate, gram)
    return iterate


def on_device(
    tokens,
    cotangent,
    lengths,
    attn_w,
    up_w,
    down_w,
    norm_params,
    attn_mom,
    up_mom,
    down_mom,
    norm_m1,
    norm_m2,
):
    tensor_index = lax.axis_index("tensor")
    data_index = lax.axis_index("dp")
    tensor_count = lax.axis_size("tensor")
    length = lengths[0]
    rows_here = tokens.shape[0]
    wa_rows, up_block, down_block = (
        lax.all_gather(attn_w.astype(jnp.bfloat16), "dp", axis=1, tiled=True),
        lax.all_gather(up_w.astype(jnp.bfloat16), "dp", axis=0, tiled=True),
        lax.all_gather(down_w.astype(jnp.bfloat16), "dp", axis=1, tiled=True),
    )
    w_all = lax.all_gather(wa_rows, "tensor", axis=0, tiled=True)
    w_query = w_all[0]
    w_key = w_all[1]
    w_value = w_all[2]
    w_out = w_all[3]
    sequence = lax.all_gather(tokens, "tensor", axis=0, tiled=True)
    count = sequence.shape[0]
    width = sequence.shape[1]
    blocks = count // BLOCK
    start_row = tensor_index * rows_here

    def mine(array):
        return lax.dynamic_slice_in_dim(array, start_row, rows_here, 0)

    where = jnp.arange(count)
    live = (where < length).astype(jnp.float32)
    place = jnp.minimum(where, length - 1).astype(jnp.float32)
    theta = 0.5 * math.pi * place / length.astype(jnp.float32)
    cosine = jnp.cos(theta)
    sine = jnp.sin(theta)
    every_row = jnp.ones((count,), jnp.float32)
    query = jnp.dot(sequence, w_query, preferred_element_type=jnp.float32)
    key_proj = jnp.dot(sequence, w_key, preferred_element_type=jnp.float32)
    value = jnp.dot(sequence, w_value, preferred_element_type=jnp.float32)
    qblock = blocked(features(query, cosine, sine, every_row).astype(jnp.bfloat16))
    kblock = blocked(features(key_proj, cosine, sine, live).astype(jnp.bfloat16))
    vblock = value.astype(jnp.bfloat16).reshape(blocks, BLOCK, HEADS, HDIM)
    lower = jnp.tril(jnp.ones((BLOCK, BLOCK), jnp.float32))
    scores_low, state_low, zsum, denom, result = attend_forward(qblock, kblock, vblock, lower)
    attn_low = result.reshape(count, width).astype(jnp.bfloat16)
    branch = jnp.dot(attn_low, w_out, preferred_element_type=jnp.float32)
    normal_one, scale_one, hidden_in = norm_forward(
        sequence.astype(jnp.float32) + branch, norm_params[0], norm_params[1]
    )
    hidden_low = hidden_in.astype(jnp.bfloat16)
    pre = jnp.dot(hidden_low, up_block, preferred_element_type=jnp.float32)
    act_low = smooth_gate(pre).astype(jnp.bfloat16)
    ffn_rows = lax.psum_scatter(
        jnp.dot(act_low, down_block, preferred_element_type=jnp.float32).astype(jnp.bfloat16),
        "tensor",
        scatter_dimension=0,
        tiled=True,
    ).astype(jnp.float32)
    live_rows = mine(live)
    normal_two, scale_two, normed = norm_forward(
        mine(hidden_in) + ffn_rows, norm_params[2], norm_params[3]
    )
    mixed = (live_rows[:, None] * normed).astype(jnp.bfloat16)
    grad_y = cotangent.astype(jnp.float32) * live_rows[:, None]
    grad_g2 = jnp.sum(grad_y * normal_two, 0)
    grad_b2 = jnp.sum(grad_y, 0)
    grad_r2 = norm_back(normal_two, scale_two, grad_y * norm_params[2])
    grad_r2_all = lax.all_gather(grad_r2.astype(jnp.bfloat16), "tensor", axis=0, tiled=True)
    grad_down = contract_rows(act_low, grad_r2_all)
    grad_act = contract_cols(grad_r2_all, down_block)
    gate_out, gate_pull = jax.vjp(smooth_gate, pre)
    grad_pre = gate_pull(grad_act)[0].astype(jnp.bfloat16)
    grad_up = contract_rows(hidden_low, grad_pre)
    grad_hidden = (
        lax.psum_scatter(
            contract_cols(grad_pre, up_block).astype(jnp.bfloat16),
            "tensor",
            scatter_dimension=0,
            tiled=True,
        ).astype(jnp.float32)
        + grad_r2
    )
    normal_one_rows = mine(normal_one)
    grad_g1 = jnp.sum(grad_hidden * normal_one_rows, 0)
    grad_b1 = jnp.sum(grad_hidden, 0)
    grad_r1 = norm_back(normal_one_rows, mine(scale_one), grad_hidden * norm_params[0])
    grad_branch = lax.all_gather(grad_r1.astype(jnp.bfloat16), "tensor", axis=0, tiled=True)
    grad_attn = contract_cols(grad_branch, w_out).reshape(blocks, BLOCK, HEADS, HDIM)
    grad_qf, grad_kf, grad_val = attend_backward(
        qblock, kblock, vblock, lower, scores_low, state_low, zsum, denom, result, grad_attn
    )
    grad_query = features_back(
        grad_qf.reshape(count, HEADS, 2 * HDIM), query, cosine, sine, every_row
    )
    grad_key = features_back(grad_kf.reshape(count, HEADS, 2 * HDIM), key_proj, cosine, sine, live)
    grad_value = grad_val.reshape(count, width)
    input_grad = (
        grad_r1
        + contract_cols(mine(grad_query), w_query)
        + contract_cols(mine(grad_key), w_key)
        + contract_cols(mine(grad_value), w_value)
    )
    left_rows = jnp.where(tensor_index == 3, attn_low, sequence)
    right_all = jnp.stack((grad_query, grad_key, grad_value, grad_branch))
    right_rows = lax.dynamic_index_in_dim(right_all, tensor_index, 0, keepdims=False)
    grad_owned = contract_rows(left_rows, right_rows)
    norm_partial = jnp.stack((grad_g1, grad_b1, grad_g2, grad_b2))
    grad_a, grad_u, grad_d = (
        *sent_together((grad_owned.astype(jnp.bfloat16), grad_up.astype(jnp.bfloat16)), "dp", 0, 1),
        sum_at_owner(grad_down.astype(jnp.bfloat16), "dp", 1),
    )
    moment_a = 0.5 * attn_mom[0] + grad_a
    moment_u = 0.5 * up_mom + grad_u
    moment_d = 0.5 * down_mom + grad_d
    owner_pick = jax.nn.one_hot(tensor_index, 4, dtype=jnp.float32)
    squares = jnp.concatenate(
        (
            owner_pick * jnp.sum(moment_a * moment_a),
            jnp.stack((jnp.sum(moment_u * moment_u), jnp.sum(moment_d * moment_d))),
        )
    )
    totals, norm_grad = lax.psum((squares, norm_partial), ("dp", "tensor"))
    size_a = jnp.sqrt(jnp.sum(totals[:4] * owner_pick))
    size_u = jnp.sqrt(totals[4])
    size_d = jnp.sqrt(totals[5])
    start_a = (moment_a / (size_a + NS_EPS)).astype(jnp.bfloat16)
    start_u = (moment_u / (size_u + NS_EPS)).astype(jnp.bfloat16)
    start_d = (moment_d.T / (size_d + NS_EPS)).astype(jnp.bfloat16)
    whole_a, cols_u, cols_d = (
        lax.all_gather(start_a, "dp", axis=0, tiled=True),
        lax.all_gather(start_u, "dp", axis=0, tiled=True),
        lax.all_gather(start_d, "dp", axis=0, tiled=True),
    )
    orth_a = orthogonalize(whole_a)
    is_even = tensor_index % 2 == 0
    whole_u, whole_d = (
        lax.all_gather(cols_u, "tensor", axis=1, tiled=True),
        lax.all_gather(cols_d, "tensor", axis=1, tiled=True),
    )
    orth_whole = orthogonalize(jnp.where(is_even, whole_u, whole_d))
    block_cols = cols_u.shape[1]
    own_block = lax.dynamic_slice_in_dim(orth_whole, tensor_index * block_cols, block_cols, 1)
    partner_block = lax.dynamic_slice_in_dim(
        orth_whole, jnp.bitwise_xor(tensor_index, 1) * block_cols, block_cols, 1
    )
    fetched = partner(partner_block, "tensor", 0)
    orth_u = jnp.where(is_even, own_block, fetched)
    orth_d = jnp.where(is_even, fetched, own_block)
    span = moment_a.shape[0]

    def take_rows(array):
        return lax.dynamic_slice_in_dim(array, data_index * span, span, 0).astype(jnp.float32)

    ff_whole = up_block.shape[1] * tensor_count
    keep = 1.0 - MUON_RATE * MUON_DECAY
    new_a = attn_w[0] * keep - MUON_RATE * 0.2 * math.sqrt(width) * take_rows(orth_a)
    scale_ff = 0.2 * math.sqrt(max(width, ff_whole))
    new_u = up_w * keep - MUON_RATE * scale_ff * take_rows(orth_u)
    new_d = down_w * keep - MUON_RATE * scale_ff * take_rows(orth_d).T
    norm_moment1 = 0.5 * norm_m1 + 0.5 * norm_grad
    norm_moment2 = 0.95 * norm_m2 + 0.05 * norm_grad * norm_grad
    first_hat = norm_moment1 / (1.0 - 0.5**STEP)
    second_hat = norm_moment2 / (1.0 - 0.95**STEP)
    norm_new = norm_params - ADAM_RATE * first_hat / (jnp.sqrt(second_hat) + 1e-08)
    return (
        mixed,
        input_grad,
        new_a[None],
        moment_a[None],
        new_u,
        moment_u,
        new_d,
        moment_d,
        norm_moment1,
        norm_moment2,
        norm_new,
    )


BF = jnp.bfloat16
F32 = jnp.float32
MESH = pl.DeviceIdType.MESH
TENSOR = 4
QUARTER = 256
LANES = 128
HALF = 128
HIGH = 4
VMEM_LIMIT = 63 << 20
GELU_C = math.sqrt(2.0 / math.pi)
GELU_A = 0.044715


def nn(left, right):
    return jnp.dot(left, right, preferred_element_type=F32)


def nt(left, right):
    return lax.dot_general(left, right, (((1,), (1,)), ((), ())), preferred_element_type=F32)


def tn(left, right):
    return lax.dot_general(left, right, (((0,), (0,)), ((), ())), preferred_element_type=F32)


def lanes_of(rows, cols=LANES):
    return lax.broadcasted_iota(jnp.int32, (rows, cols), 1)


def half_roll(array):
    return pltpu.roll(array, LANES // 2, 1)


def place():
    data = lax.axis_index("dp")
    tensor = lax.axis_index("tensor")
    return data, tensor


def greet(devices):
    barrier = pltpu.get_barrier_semaphore()
    for device in devices:
        pl.semaphore_signal(barrier, inc=1, device_id=device, device_id_type=MESH)
    pl.semaphore_wait(barrier, len(devices))


def send(src, dst, send_sem, recv_sem, device):
    copy = pltpu.make_async_remote_copy(
        src_ref=src,
        dst_ref=dst,
        send_sem=send_sem,
        recv_sem=recv_sem,
        device_id=device,
        device_id_type=MESH,
    )
    copy.start()
    return copy


def kernel_call(body, name, ins, outs, scratch, collective, scalars=()):
    in_names = list(ins)
    out_names = list(outs)
    scratch_names = list(scratch)

    def kernel(*refs):
        body(types.SimpleNamespace(**dict(zip(in_names + out_names + scratch_names, refs))))

    results = pl.pallas_call(
        kernel,
        name=name,
        out_shape=[outs[n] for n in out_names],
        in_specs=[
            pl.BlockSpec(memory_space=pltpu.SMEM if n in scalars else pltpu.VMEM) for n in in_names
        ],
        out_specs=[pl.BlockSpec(memory_space=pltpu.VMEM)] * len(out_names),
        scratch_shapes=[scratch[n] for n in scratch_names],
        compiler_params=pltpu.CompilerParams(
            collective_id=collective,
            has_side_effects=collective is not None,
            vmem_limit_bytes=VMEM_LIMIT,
        ),
    )(*[ins[n] for n in in_names])
    return dict(zip(out_names, results))


def shape(*dims, dtype=BF):
    return jax.ShapeDtypeStruct(dims, dtype)


def dma(*dims):
    return pltpu.SemaphoreType.DMA(dims)


def await_bytes(ref, sem):
    pltpu.make_async_copy(ref, ref, sem).wait()


class GatherDp:
    def __init__(self, slot_of, sends, recvs, data, tensor):
        self.slot_of, self.sends, self.recvs = slot_of, sends, recvs
        self.data, self.tensor = data, tensor
        self.high, self.low = data // 2, data % 2
        self.partner = (self.high * 2 + 1 - self.low, tensor)
        self.relays = (self.high == 1) | (self.high == 2)
        first_end, last_end = self.high == 0, self.high == HIGH - 1
        self.order = (
            jnp.where(first_end, 3, 1),
            jnp.where(first_end | last_end, 2, 3),
            jnp.where(first_end, 1, jnp.where(last_end, 3, 2)),
        )

    def source(self, step):
        return lax.rem(self.high + HIGH - step, HIGH) * 2 + self.low

    def push(self, slot, at, to, there=None):
        send(slot, slot, self.sends.at[at], self.recvs.at[at if there is None else there], to)

    def start(self):
        mine = self.slot_of(self.data)
        for step, allowed in ((1, self.high != HIGH - 1), (2, None), (3, self.high != 0)):
            to = (lax.rem(self.high + step, HIGH) * 2 + self.low, self.tensor)
            if allowed is None:
                self.push(mine, step, to)
            else:
                pl.when(allowed)(functools.partial(self.push, mine, step, to))

    def cross(self):
        self.push(self.slot_of(self.data), 0, self.partner)

    def forward(self, cross=True):
        for position, step in enumerate(self.order):
            slot = self.slot_of(self.source(step))
            await_bytes(slot, self.recvs.at[step])
            if position == HIGH - 2:
                to = ((self.high ^ 1) * 2 + self.low, self.tensor)
                pl.when(self.relays)(functools.partial(self.push, slot, 7, to, jnp.where(self.high == 2, 3, 1)))
            if cross:
                self.push(slot, HIGH - 1 + step, self.partner)

    def partner_slot(self, step):
        return self.source(step) + 1 - 2 * self.low

    def arrive(self, *steps):
        for step in steps or range(HIGH):
            at = HIGH - 1 + step if step else 0
            await_bytes(self.slot_of(self.partner_slot(step)), self.recvs.at[at])

    def close(self, cross=True):
        mine = self.slot_of(self.data)
        for at in (0, 4, 5, 6) if cross else ():
            await_bytes(mine, self.sends.at[at])
        for at, allowed in ((1, self.high != HIGH - 1), (3, self.high != 0), (7, self.relays)):
            pl.when(allowed)(functools.partial(await_bytes, mine, self.sends.at[at]))
        await_bytes(mine, self.sends.at[2])


def softplus_and_slope(x):
    small = jnp.exp(-jnp.abs(x))
    soft = jnp.maximum(x, 0.0) + jnp.log1p(small)
    slope = jnp.where(x >= 0.0, 1.0, small) / (1.0 + small)
    return soft, slope


def spread_weights(r, tiles):
    low = lanes_of(768) < 64
    for k in tiles:
        tile = r.wp[:, k * LANES : (k + 1) * LANES].astype(F32)
        turned = half_roll(tile)
        left, right = jnp.where(low, tile, turned), jnp.where(low, turned, tile)
        if k == 0:
            parts = {0: left, 1: right}
        elif k == 1:
            parts = {3: left, 4: right}
        elif k == 2:
            parts = {2: left, 5: right}
        elif k == 3:
            parts = {6: jnp.where(low, tile, 0.0), 7: jnp.where(low, turned, 0.0)}
        else:
            parts = {8: tile}
        for at, part in parts.items():
            r.xmat[:, at * LANES : (at + 1) * LANES] = part.astype(BF)


def project(r):
    lane = lanes_of(QUARTER)

    def step(q, carry):
        both = nn(r.seq[q], r.xmat[:, : 9 * LANES])
        table, table_live = r.gp[q, :, :LANES], r.gp[q, :, LANES : 2 * LANES]
        for h in range(3):
            soft, slope = softplus_and_slope(both[:, h * LANES : (h + 1) * LANES])
            r.qf[h, q] = (soft * table).astype(BF)
            r.qg[h, q] = slope * table
            soft, slope = softplus_and_slope(both[:, (3 + h) * LANES : (4 + h) * LANES])
            r.kf[h, q] = (soft * table_live).astype(BF)
            r.kg[h, q] = slope * table_live
            value = both[:, (6 + h) * LANES : (7 + h) * LANES]
            ones = jnp.where((lane == 64) | (lane == 65), 1.0, 0.0)
            r.va[h, q] = jnp.where(lane < 64, value, ones).astype(BF)
        return carry

    lax.fori_loop(0, TENSOR, step, 0)


def attend(r, q):
    lane = lanes_of(QUARTER)
    keep = lanes_of(QUARTER, QUARTER) <= lax.broadcasted_iota(jnp.int32, (QUARTER, QUARTER), 0)

    def head(h, carry):
        qf, kf, va = r.qf[h, q], r.kf[h, q], r.va[h, q]
        scores = jnp.where(keep, nt(qf, kf), 0.0).astype(BF)
        r.sb[h, q] = scores
        total = nn(scores, va)
        if q > 0:
            state = r.state[h].astype(BF)
            r.st[h, q] = state
            total = total + nn(qf, state)
        if q < TENSOR - 1:
            pairs = tn(kf, va)
            r.state[h] = pairs if q == 0 else r.state[h] + pairs
        inverse = 1.0 / total[:, 64:65]
        r.af[h, q] = jnp.where(lane < 64, total * inverse, inverse)
        return carry

    lax.fori_loop(0, 3, head, 0)
    zero, one, two = r.af[0, q], r.af[1, q], r.af[2, q]
    r.attn[q, :, :LANES] = jnp.where(lane < 64, zero, half_roll(one)).astype(BF)
    r.attn[q, :, LANES:] = jnp.where(lane < 64, two, 0.0).astype(BF)


def norm_rows(resid):
    center = resid - jnp.mean(resid, -1, keepdims=True)
    spread = jnp.mean(center * center, -1, keepdims=True)
    scale = lax.rsqrt(spread + NORM_EPS)
    return center * scale, scale


def norm_rows_back(normal, scale, grad):
    return scale * (
        grad
        - jnp.mean(grad, -1, keepdims=True)
        - normal * jnp.mean(grad * normal, -1, keepdims=True)
    )


class Group:
    def __init__(self):
        self.data, self.tensor = place()
        self.far, self.core = self.tensor // 2, self.tensor % 2

    def device(self, k):
        return (self.data, self.tensor ^ k)


def half_of(ref, q, part):
    return ref.at[q, pl.ds(part * HALF, HALF)]


class Spread:
    def __init__(self, g, buf, sends, recvs, part):
        self.g, self.buf, self.sends, self.recvs, self.part = g, buf, sends, recvs, part
        own = half_of(buf, g.tensor, part)
        self.far = self.push(own, 0, g.device(2))
        self.near = self.push(own, 1, g.device(1))

    def push(self, ref, k, device):
        k = 3 * self.part + k
        return send(ref, ref, self.sends.at[k], self.recvs.at[k], device)

    def arrive_near(self):
        self.near.wait_recv()

    def pass_far(self):
        self.far.wait_recv()
        self.passed = self.push(half_of(self.buf, self.g.tensor ^ 2, self.part), 2, self.g.device(1))

    def arrive_far(self):
        self.passed.wait_recv()
        for copy in (self.far, self.near, self.passed):
            copy.wait_send()


class SumQuarters:
    def __init__(self, r, g, slot):
        self.r, self.g, self.slot = r, g, slot
        self.near, self.far = {}, {}

    def near_out(self, j, part, value):
        r, k = self.r, 2 * j + part
        r.near_send[k] = value.astype(BF)
        at = 4 * self.slot + k
        self.near[j, part] = send(
            r.near_send.at[k], r.near_recv.at[k], r.near_s.at[at], r.near_r.at[at], self.g.device(1)
        )

    def near_in(self, j, part, value):
        self.near[j, part].wait_recv()
        return value + self.r.near_recv[2 * j + part].astype(F32)

    def far_out(self, part, value):
        r = self.r
        r.far_send[part] = value.astype(BF)
        at = 2 * self.slot + part
        self.far[part] = send(
            r.far_send.at[part], r.far_recv.at[part], r.far_s.at[at], r.far_r.at[at], self.g.device(2)
        )

    def far_in(self, part, value):
        self.far[part].wait_recv()
        value = value + self.r.far_recv[part].astype(F32)
        for copy in (self.far[part], self.near[0, part], self.near[1, part]):
            copy.wait_send()
        return value


def pair_of(ref, quarters, part):
    return jnp.concatenate([ref[q, pl.ds(part * HALF, HALF)] for q in quarters], axis=0)


def put_pair(ref, quarters, part, value):
    for k, q in enumerate(quarters):
        ref[q, pl.ds(part * HALF, HALF)] = value[k * HALF : (k + 1) * HALF]


def feed_in(r, quarters, part):
    pre = nn(pair_of(r.hb, quarters, part), r.wu[...].reshape(768, 768))
    inner = jnp.tanh(GELU_C * (pre + GELU_A * pre * pre * pre))
    half = 0.5 * (1.0 + inner)
    slope = half + 0.5 * pre * (1.0 - inner * inner) * (GELU_C * (1.0 + 3.0 * GELU_A * pre * pre))
    put_pair(r.gp, quarters, part, slope)
    put_pair(r.hid, quarters, part, (pre * half).astype(BF))


def feed_out(r, quarters, part):
    out = nt(pair_of(r.hid, quarters, part), r.wd[...].reshape(768, 768))
    return out[:HALF], out[HALF:]


def feed_back(r, quarters, part):
    grad_act = nn(pair_of(r.dr2, quarters, part), r.wd[...].reshape(768, 768))
    grad_pre = (grad_act * pair_of(r.gp, quarters, part)).astype(BF)
    put_pair(r.du, quarters, part, grad_pre)
    out = nt(grad_pre, r.wu[...].reshape(768, 768))
    return out[:HALF], out[HALF:]


def attend_back(r, g, q):
    lane = lanes_of(QUARTER)
    keep = lanes_of(QUARTER, QUARTER) <= lax.broadcasted_iota(jnp.int32, (QUARTER, QUARTER), 0)
    dr1 = r.dr1[q]

    def head(h, carry):
        grad = nt(dr1, r.woh[h])
        af = r.af[h, q]
        inverse = af[:, 64:65]
        dden = -jnp.sum(grad * af, -1, keepdims=True) * inverse
        dden_low = dden.astype(BF).astype(F32)
        extra = jnp.where(lane == 64, dden_low, jnp.where(lane == 65, dden - dden_low, 0.0))
        dnum = jnp.where(lane < 64, grad * inverse, extra).astype(BF)
        qf, kf, va, sb = r.qf[h, q], r.kf[h, q], r.va[h, q], r.sb[h, q]
        ds = jnp.where(keep, nt(dnum, va), 0.0).astype(BF)
        dqf = nn(ds, kf)
        if q > 0:
            dqf = dqf + nt(dnum, r.st[h, q])
        dkf = tn(ds, qf)
        dv = tn(sb, dnum)
        if q < TENSOR - 1:
            dkv = r.state[h].astype(BF)
            dkf = dkf + nt(va, dkv)
            dv = dv + nn(kf, dkv)
        if q > 0:
            pairs = tn(qf, dnum)
            r.state[h] = pairs if q == TENSOR - 1 else r.state[h] + pairs
        dqf = dqf * r.qg[h, q]
        dkf = dkf * r.kg[h, q]
        r.fold[0, h] = dqf + half_roll(dqf)
        r.fold[1, h] = dkf + half_roll(dkf)
        r.fold[2, h] = dv
        return carry

    lax.fori_loop(0, 3, head, 0)
    fold = r.fold
    tiles = (
        jnp.where(lane < 64, fold[0, 0], fold[0, 1]),
        jnp.where(lane < 64, fold[1, 0], fold[1, 1]),
        jnp.where(lane < 64, fold[0, 2], fold[1, 2]),
        jnp.where(lane < 64, fold[2, 0], half_roll(fold[2, 1])),
        jnp.where(lane < 64, fold[2, 2], 0.0),
    )
    for k, tile in enumerate(tiles):
        r.hb[q, :, k * LANES : (k + 1) * LANES] = tile.astype(BF)
    r.gp[q] = nt(r.hb[q, :, : 5 * LANES], r.wp[...])


class ReduceDp:
    def __init__(self, src, low_buf, high_send, high_buf, sems, data, tensor, count):
        self.src, self.low_buf, self.high_send, self.high_buf = src, low_buf, high_send, high_buf
        self.low_s, self.low_r, self.high_s, self.high_r = sems
        self.tensor, self.n = tensor, count // 2
        self.high, self.low = data // 2, data % 2

    def at(self, step):
        return lax.rem(self.high + step, self.n)

    def start(self):
        partner = (self.high * 2 + 1 - self.low, self.tensor)
        self.across, self.along = {}, {}
        for step in list(range(1, self.n)) + [0]:
            h = self.at(step)
            self.across[step] = send(
                self.src.at[h * 2 + 1 - self.low],
                self.low_buf.at[h],
                self.low_s.at[step],
                self.low_r.at[step],
                partner,
            )

    def pair(self, step):
        self.across[step].wait_recv()
        h = self.at(step)
        return self.src[h * 2 + self.low].astype(F32) + self.low_buf[h].astype(F32)

    def forward(self, *steps):
        for step in steps:
            self.high_send[step] = self.pair(step).astype(BF)
            self.along[step] = send(
                self.high_send.at[step],
                self.high_buf.at[step],
                self.high_s.at[step],
                self.high_r.at[step],
                (self.at(step) * 2 + self.low, self.tensor),
            )

    def finish(self):
        total = self.pair(0)
        for step in range(1, self.n):
            self.along[step].wait_recv()
            total = total + self.high_buf[step].astype(F32)
        for copy in list(self.across.values()) + list(self.along.values()):
            copy.wait_send()
        return total


def assemble(r, core_rows):
    low = lanes_of(core_rows) < 64
    for pair in range(2):
        even, odd = r.abuf[2 * pair].astype(F32), r.abuf[2 * pair + 1].astype(F32)
        turned = half_roll(odd[:, :LANES])
        base = 3 * LANES * pair
        r.grad_a[:, base : base + LANES] = even[:, :LANES]
        r.grad_a[:, base + LANES : base + 2 * LANES] = jnp.where(low, even[:, LANES:], turned)
        r.grad_a[:, base + 2 * LANES : base + 3 * LANES] = jnp.where(low, turned, half_roll(odd[:, LANES:]))


def newton_scale(x):
    width = x.shape[1]

    def step(k, total):
        part = x[pl.ds(pl.multiple_of(k * 96, 96), 96)].astype(F32)
        return total + part * part

    total = lax.fori_loop(0, 8, step, jnp.zeros((96, width), F32))
    return 1.0 / (jnp.sqrt(jnp.sum(total)) + NS_EPS)


def newton_gram(x, gram, scale):
    edges = [slice(k * 256, (k + 1) * 256) for k in range(3)]
    for a in range(3):
        for b in range(a, 3):
            block = nt(x[edges[a], :], x[edges[b], :])
            block = (block if scale is None else block * (scale * scale)).astype(BF)
            gram[a, :, edges[b]] = block
            if b > a:
                gram[b, :, edges[a]] = block.T


def newton_poly(gram, poly):
    edges = [slice(k * 256, (k + 1) * 256) for k in range(3)]
    for a in range(3):
        for b in range(a, 3):
            block = COEF_C * nt(gram[a], gram[b])
            block = (block + COEF_B * gram[a, :, edges[b]].astype(F32)).astype(BF)
            poly[a, :, edges[b]] = block
            if b > a:
                poly[b, :, edges[a]] = block.T


def newton_apply(x, poly, chunk, scale):
    def columns(c, inner):
        at = pl.ds(pl.multiple_of(c * chunk, chunk), chunk)
        old = x[:, at]
        new = COEF_A * old.astype(F32) + nn(poly[:3].reshape(768, 768), old)
        if scale is not None:
            new = scale * new
        x[:, at] = new.astype(BF)
        return inner

    lax.fori_loop(0, x.shape[1] // chunk, columns, 0)


def newton(x, gram, poly, chunk, first, steps):
    def step(k, carry):
        newton_gram(x, gram, first)
        newton_poly(gram, poly)
        newton_apply(x, poly, chunk, first)
        return carry

    lax.fori_loop(0, steps, step, 0)


def newton_rows(x, gram, index, rows, chunk, out):
    own = newton_rows_gram(gram, index, rows)
    poly = (COEF_C * nn(own, gram[:3].reshape(768, 768)) + COEF_B * own.astype(F32)).astype(BF)
    here = pl.ds(pl.multiple_of(index * rows, rows), rows)
    for c in range(x.shape[1] // chunk):
        at = slice(c * chunk, (c + 1) * chunk)
        out[:, at] = (COEF_A * x[here, at].astype(F32) + nn(poly, x[:, at])).astype(BF)


def newton_rows_gram(gram, index, rows):
    parts = []
    for k in range(rows // 32):
        row = index * rows + 32 * k
        parts.append(gram[row // 256, pl.ds(pl.multiple_of(lax.rem(row, 256), 32), 32), :])
    return jnp.concatenate(parts, axis=0)


def angles(r):
    rows = TENSOR * QUARTER
    length = r.lengths[0]
    where = lax.broadcasted_iota(jnp.int32, (rows, LANES), 0)
    theta = 0.5 * math.pi * jnp.minimum(where, length - 1).astype(F32) / length.astype(F32)
    table = jnp.where(lanes_of(rows) < 64, jnp.cos(theta), jnp.sin(theta))
    live = jnp.where(where < length, 1.0, 0.0)
    r.gp[:, :, :LANES] = table.reshape(TENSOR, QUARTER, LANES)
    r.gp[:, :, LANES : 2 * LANES] = (table * live).reshape(TENSOR, QUARTER, LANES)


def cut_heads(r, rows):
    low = lanes_of(rows) < 64
    tiles = [r.attn_w[0, :, k * LANES : (k + 1) * LANES] for k in range(6)]
    for pair in range(2):
        first, middle, last = tiles[3 * pair : 3 * pair + 3]
        turned, rest = half_roll(middle), half_roll(last)
        parts = [first, jnp.where(low, middle, 0.0), jnp.where(low, turned, rest), jnp.where(low, rest, 0.0)]
        for k, part in enumerate(parts):
            r.slabs[2 * pair + k // 2, :, (k % 2) * LANES : (k % 2 + 1) * LANES] = part.astype(BF)


def assemble(r, core_rows):
    low = lanes_of(core_rows) < 64
    for pair in range(2):
        even, odd = r.abuf[2 * pair].astype(F32), r.abuf[2 * pair + 1].astype(F32)
        turned = half_roll(odd[:, :LANES])
        base = 3 * LANES * pair
        r.grad_a[:, base : base + LANES] = even[:, :LANES]
        r.grad_a[:, base + LANES : base + 2 * LANES] = jnp.where(low, even[:, LANES:], turned)
        r.grad_a[:, base + 2 * LANES : base + 3 * LANES] = jnp.where(low, turned, half_roll(odd[:, LANES:]))


def step_body(count, rows, r):
    g = Group()
    data, tensor, far, core = g.data, g.tensor, g.far, g.core
    high, low = data // 2, data % 2
    other = high * 2 + 1 - low
    n = count // 2
    half = rows // 2
    near_dev, far_dev = g.device(1), g.device(2)

    cut_heads(r, rows)
    r.wo_own[...] = r.attn_w[0].astype(BF).reshape(2, half, 768)
    greet(
        [g.device(k) for k in (1, 2, 3)]
        + [(lax.rem(data + k, count), tensor) for k in range(1, count)]
        + [(other, tensor ^ 1)]
    )

    def rows_of(d):
        return pl.ds(pl.multiple_of(d * rows, rows), rows)

    def cols(t):
        return pl.ds(pl.multiple_of(t * 768, 768), 768)

    here, there = rows_of(data), rows_of(other)

    for k in (1, 2, 3):
        peer = tensor ^ k

        @pl.when(tensor < 3)
        def _():
            send(r.slabs.at[peer], r.slab_in.at[tensor], r.slab_s.at[k], r.slab_r.at[tensor], g.device(k))

        @pl.when(tensor == 3)
        def _():
            send(r.wo_own.at[peer % 2], r.wo.at[data, peer % 2], r.slab_s.at[k], r.slab_r.at[3], g.device(k))

    r.seq[tensor] = r.tokens[...]
    mine = r.seq.at[tensor]
    tok_near = send(mine, mine, r.tok_s.at[0], r.tok_r.at[0], near_dev)
    tok_far = send(mine, mine, r.tok_s.at[1], r.tok_r.at[1], far_dev)

    @pl.when(tensor < 3)
    def _():
        r.slab_in[tensor] = r.slabs[tensor]

    @pl.when(tensor == 3)
    def _():
        r.wo[data, core] = r.wo_own[core]

    r.wu[data] = r.up_w[...].astype(BF)
    r.wd[data] = r.down_w[...].astype(BF)

    def gather(slot_of, key):
        return GatherDp(slot_of, r.gather_s.at[key], r.gather_r.at[key], data, tensor)

    spans = ((0, 2), (2, 5))
    heads = [
        gather(lambda d, a=a, b=b: r.wp.at[rows_of(d), a * LANES : b * LANES], k) for k, (a, b) in enumerate(spans)
    ]
    outs = gather(lambda d: r.wo.at[d, core], 2)
    ups = [gather(lambda d, k=k: r.wu.at[d, pl.ds(k * half, half)], 3 + k) for k in range(2)]
    downs = [gather(lambda d, k=k: r.wd.at[d, pl.ds(k * half, half)], 5 + k) for k in range(2)]
    first_half = lanes_of(rows) < 64

    def slab(m):
        @pl.when(tensor != m)
        def _():
            await_bytes(r.slab_in.at[m], r.slab_r.at[m])

        return r.slab_in[m, :, :LANES], r.slab_in[m, :, LANES:]

    query, query_last = slab(0)
    key, key_last = slab(1)
    r.wp[here, :LANES] = query
    r.wp[here, LANES : 2 * LANES] = key
    heads[0].start()
    heads[0].cross()
    both = jnp.where(first_half, query_last.astype(F32), half_roll(key_last.astype(F32)))
    r.wp[here, 2 * LANES : 3 * LANES] = both.astype(BF)
    value, value_last = slab(2)
    r.wp[here, 3 * LANES : 4 * LANES] = value
    r.wp[here, 4 * LANES :] = value_last
    heads[1].start()
    heads[1].cross()

    @pl.when(tensor != 3)
    def _():
        await_bytes(r.wo.at[data, core], r.slab_r.at[3])

    for part in [outs] + ups + downs:
        part.start()
    outs.cross()
    angles(r)
    heads[0].forward()
    tok_far.wait_recv()
    slot = r.seq.at[tensor ^ 2]
    tok_pass = send(slot, slot, r.tok_s.at[2], r.tok_r.at[2], near_dev)
    heads[1].forward()
    for part in ups + downs:
        part.cross()
    heads[0].arrive()
    spread_weights(r, (0, 1))
    heads[1].arrive()
    spread_weights(r, (2, 3, 4))
    tok_near.wait_recv()
    tok_pass.wait_recv()
    project(r)
    outs.forward()

    copies = [[], []]
    for j in range(2):
        attend(r, 2 * j)
        attend(r, 2 * j + 1)
        mine, rest = 2 * j + core, 2 * j + 1 - core
        for k in (2, 1, 3):
            quarter = mine if k == 2 else rest
            copies[j].append(
                send(r.attn.at[quarter], r.aall.at[tensor, j], r.attn_s.at[j, k], r.attn_r.at[j, k], g.device(k))
            )
        r.aall[tensor, j] = r.attn[mine]
        if j == 0:
            ups[0].forward()

    outs.arrive()
    share = []
    for d in range(count):
        part = r.wo.at[d, core]
        share.append(send(part, part, r.share_s.at[d], r.share_r.at[d], near_dev))
    for part in (ups[1], downs[0], downs[1]):
        part.forward()
    for d in range(count):
        part = r.wo.at[d, 1 - core]
        await_bytes(part, r.share_r.at[d])
    whole_out = r.wo[...].reshape(768, 768)
    wop = [r.xmat.at[256 * t : 256 * (t + 1), 1536:2304] for t in range(3)] + [r.xmat.at[0:256, 2304:3072]]
    for t in range(TENSOR):
        wop[t][:192, :] = whole_out[192 * t : 192 * (t + 1)]
        wop[t][192:, :] = jnp.zeros((64, 768), BF)
    for t in range(TENSOR):

        @pl.when(tensor == t)
        def _():
            for h in range(3):
                r.woh[h, :64] = wop[t][64 * h : 64 * (h + 1), :]
                r.woh[h, 64:] = jnp.zeros((64, 768), BF)

    gain1, bias1, gain2, bias2 = (r.norms[k : k + 1] for k in range(4))
    hs = []
    for group_copies in copies:
        for copy in group_copies:
            copy.wait_recv()
    for own in (False, True):
        j = far if own else 1 - far
        q = 2 * j + core
        branch = nn(r.aall[0, j], wop[0][...])
        for t in range(1, TENSOR):
            branch = branch + nn(r.aall[t, j], wop[t][...])
        normal, scale = norm_rows(r.seq[q].astype(F32) + branch)
        hidden = normal * gain1 + bias1
        r.hb[q] = hidden.astype(BF)
        if own:
            r.n1[...] = normal
            r.s1[...] = jnp.broadcast_to(scale, (QUARTER, LANES))
            r.h1[...] = hidden
        hs.append(send(r.hb.at[q], r.hb.at[q], r.h_s.at[int(own)], r.h_r.at[int(own)], near_dev))
    for part in ups:
        part.arrive()

    theirs, ours = (tensor ^ 2, tensor ^ 3), (tensor, tensor ^ 1)
    halves = (0, 1)
    total = SumQuarters(r, g, 0)
    hs[0].wait_recv()
    for part in halves:
        feed_in(r, theirs, part)
    hs[1].wait_recv()
    for part in downs:
        part.arrive()
    for part in halves:
        kept, other_half = feed_out(r, theirs, part)
        total.near_out(0, part, other_half)
        r.kept[part] = kept
    for part in halves:
        total.far_out(part, total.near_in(0, part, r.kept[part]))
    for part in halves:
        feed_in(r, ours, part)
        kept, other_half = feed_out(r, ours, part)
        total.near_out(1, part, other_half)
        r.kept[part] = kept
    for part in heads + [outs] + ups + downs:
        part.close()
    for group_copies in copies:
        for copy in group_copies:
            copy.wait_send()
    for copy in hs + share + [tok_near, tok_far, tok_pass]:
        copy.wait_send()
    for k in (1, 2, 3):

        @pl.when(tensor < 3)
        def _():
            await_bytes(r.slabs.at[0], r.slab_s.at[k])

        @pl.when(tensor == 3)
        def _():
            await_bytes(r.wo_own.at[0], r.slab_s.at[k])

    back = SumQuarters(r, g, 1)
    spread = []

    def second_norm(part):
        at = pl.ds(part * HALF, HALF)
        ffn = total.far_in(part, total.near_in(1, part, r.kept[part]))
        n2, s2 = norm_rows(r.h1[at] + ffn)
        row = lax.broadcasted_iota(jnp.int32, (HALF, 1), 0) + (tensor * QUARTER + part * HALF)
        live = jnp.where(row < r.lengths[0], 1.0, 0.0)
        r.mixed[at] = (live * (n2 * gain2 + bias2)).astype(BF)
        dy = live * r.cotangent[at].astype(F32)
        gain_grad, bias_grad = jnp.sum(dy * n2, 0, keepdims=True), jnp.sum(dy, 0, keepdims=True)
        r.partial[2:3] = gain_grad if part == 0 else r.partial[2:3] + gain_grad
        r.partial[3:4] = bias_grad if part == 0 else r.partial[3:4] + bias_grad
        dr2 = norm_rows_back(n2, s2, dy * gain2)
        r.dr2f[at] = dr2
        r.dr2[tensor, at] = dr2.astype(BF)
        spread.append(Spread(g, r.dr2, r.dr2_s, r.dr2_r, part))

    def own_back(part):
        spread[part].arrive_near()
        kept, other_half = feed_back(r, ours, part)
        back.near_out(0, part, other_half)
        r.kept[part] = kept

    def their_back(part):
        spread[part].arrive_far()
        kept, other_half = feed_back(r, theirs, part)
        back.near_out(1, part, other_half)
        back.far_out(part, back.near_in(1, part, kept))

    second_norm(0)
    own_back(0)
    second_norm(1)
    spread[0].pass_far()
    own_back(1)
    their_back(0)
    spread[1].pass_far()
    their_back(1)

    sums = {}
    for key in "dua":
        sums[key] = ReduceDp(
            *(getattr(r, name + key) for name in ("g", "low", "hs", "hb")),
            [getattr(r, name + key) for name in ("ls_", "lr_", "hs_", "hr_")],
            data,
            tensor,
            count,
        )
    spread = []

    def first_norm_back(part):
        at = pl.ds(part * HALF, HALF)
        dh = back.far_in(part, back.near_in(0, part, r.kept[part])) + r.dr2f[at]
        n1 = r.n1[at]
        gain_grad, bias_grad = jnp.sum(dh * n1, 0, keepdims=True), jnp.sum(dh, 0, keepdims=True)
        r.partial[0:1] = gain_grad if part == 0 else r.partial[0:1] + gain_grad
        r.partial[1:2] = bias_grad if part == 0 else r.partial[1:2] + bias_grad
        dr1 = norm_rows_back(n1, r.s1[at, :1], dh * gain1)
        r.dr1f[at] = dr1
        r.dr1[tensor, at] = dr1.astype(BF)
        spread.append(Spread(g, r.dr1, r.dr1_s, r.dr1_r, part))

    grad = tn(r.dr2[...].reshape(1024, 768), r.hid[...].reshape(1024, 768))
    r.gd[...] = grad.astype(BF).reshape(r.gd.shape)
    sums["d"].start()
    first_norm_back(0)
    grad = tn(r.hb[...].reshape(1024, 768), r.du[...].reshape(1024, 768))
    r.gu[...] = grad.astype(BF).reshape(r.gu.shape)
    sums["u"].start()
    first_norm_back(1)
    r.pbuf[tensor] = r.partial[...]
    parts = []
    for k in (1, 2, 3):
        parts.append(send(r.partial, r.pbuf.at[tensor], r.pt_s.at[k], r.pt_r.at[k], g.device(k)))
    sums["d"].forward(1, 2)
    spread[0].pass_far()
    sums["d"].forward(3)
    spread[1].pass_far()
    for part in halves:
        spread[part].arrive_near()
        spread[part].arrive_far()

    attend_back(r, g, 3)
    sums["u"].forward(1)
    for copy in parts:
        copy.wait()
    r.psum[...] = ((r.pbuf[0] + r.pbuf[1]) + r.pbuf[2]) + r.pbuf[3]
    r.qbuf[data] = r.psum[...]
    parts = []
    for k in range(1, count):
        to = (lax.rem(data + k, count), tensor)
        parts.append(send(r.psum, r.qbuf.at[data], r.pd_s.at[k], r.pd_r.at[k], to))
    attend_back(r, g, 2)
    sums["u"].forward(2, 3)
    moment = 0.5 * r.down_mom[...] + sums["d"].finish()
    r.mom_d[...] = moment
    r.xsd[...] = moment.astype(BF)
    attend_back(r, g, 1)
    moment = 0.5 * r.up_mom[...] + sums["u"].finish()
    r.mom_u[...] = moment
    r.xsu[...] = moment.astype(BF)
    own = r.xmat.at[here, cols(tensor)]

    @pl.when(far == 0)
    def _():
        r.xmat[here, cols(tensor)] = r.xsu[...]
        send(r.xsd, own, r.swap_s, r.swap_r, far_dev)

    @pl.when(far == 1)
    def _():
        r.xmat[here, cols(tensor)] = r.xsd[...]
        send(r.xsu, own, r.swap_s, r.swap_r, far_dev)

    blocks = [
        GatherDp(lambda d: r.xmat.at[rows_of(d), cols(tensor)], r.x_s.at[0], r.x_r.at[0], data, tensor),
        GatherDp(lambda d: r.xmat.at[rows_of(d), cols(tensor ^ 2)], r.x_s.at[1], r.x_r.at[1], data, tensor),
    ]

    def pass_on(b, d):
        @pl.when(core == 1)
        def _():
            slot = blocks[b].slot_of(d)
            send(slot, slot, r.j_s.at[b, d], r.j_r.at[b, d], near_dev)

    blocks[0].start()
    blocks[0].cross()
    attend_back(r, g, 0)
    await_bytes(r.xmat.at[here, cols(tensor ^ 2)], r.swap_r)
    blocks[1].start()
    blocks[1].cross()

    grad = tn(r.seq[...].reshape(1024, 768), r.hb[:, :, : 5 * LANES].reshape(1024, 5 * LANES))
    r.ga[...] = grad.astype(BF).reshape(r.ga.shape)
    grad = tn(r.attn[...].reshape(1024, 256), r.dr1[...].reshape(1024, 768)).astype(BF)
    r.go[...] = grad[:192].reshape(r.go.shape)
    out_low = send(r.go.at[1 - low], r.olow, r.o_s.at[0], r.o_r.at[0], (other, tensor))
    total = SumQuarters(r, g, 2)
    for part in halves:
        total.near_out(0, part, half_of(r.gp, tensor ^ 3, part)[...])
        total.near_out(1, part, half_of(r.gp, tensor ^ 1, part)[...])
    for part in halves:
        total.far_out(part, total.near_in(0, part, half_of(r.gp, tensor ^ 2, part)[...]))
    def pass_far_rows(b):
        blocks[b].forward()
        for step in range(n):
            pass_on(b, blocks[b].source(step))

    out_low.wait_recv()
    r.grad_a[...] = r.go[low].astype(F32) + r.olow[...].astype(F32)
    r.osend[...] = r.grad_a[...].astype(BF)
    for k in range(1, n):

        @pl.when(lax.rem(high + k, n) == tensor)
        def _():
            send(r.osend, r.ohigh.at[k], r.o_s.at[1], r.o_r.at[k], (tensor * 2 + low, tensor))

    pass_far_rows(0)
    for part in halves:
        at = pl.ds(part * HALF, HALF)
        value = total.near_in(1, part, half_of(r.gp, tensor, part)[...])
        r.input_grad[at] = total.far_in(part, value) + r.dr1f[at]
    pass_far_rows(1)
    sums["a"].start()
    sums["a"].forward(1, 2, 3)
    for b in range(2):
        for step in range(n):
            blocks[b].arrive(step)
            pass_on(b, blocks[b].partner_slot(step))
        blocks[b].close()

    @pl.when(core == 0)
    def _():
        for b in range(2):
            for d in range(count):
                await_bytes(own, r.j_r.at[b, d])
        r.scale[0] = newton_scale(r.xmat)
        newton_gram(r.xmat, r.du, r.scale[0])
        newton_poly(r.du, r.hid)

    summed = sums["a"].finish()
    tiles = [summed[:, k * LANES : (k + 1) * LANES] for k in range(5)]
    for m, (first, last) in enumerate(((0, tiles[2]), (1, half_roll(tiles[2])), (3, tiles[4]))):
        r.asend[m, :, :LANES] = tiles[first].astype(BF)
        r.asend[m, :, LANES:] = last.astype(BF)
    for m in range(3):

        @pl.when(tensor != m)
        def _():
            send(r.asend.at[m], r.abuf.at[tensor], r.a_s.at[m], r.a_r.at[tensor], (data, m))

        @pl.when(tensor == m)
        def _():
            r.abuf[tensor] = r.asend[m]

    @pl.when(high == tensor)
    def _():
        whole = r.grad_a[...]
        for k in range(1, n):
            await_bytes(r.ohigh.at[k], r.o_r.at[k])
            whole = whole + r.ohigh[k].astype(F32)
        r.grad_a[...] = whole
        r.oout[...] = whole.astype(BF)

    @pl.when((high == tensor) & (tensor != 3))
    def _():
        send(r.oout, r.oin, r.o_s.at[2], r.oin_r, (data, 3))

    @pl.when((tensor == 3) & (high != 3))
    def _():
        await_bytes(r.oin, r.oin_r)
        r.grad_a[...] = r.oin[...].astype(F32)

    @pl.when(core == 0)
    def _():
        newton_apply(r.xmat, r.hid, 1536, r.scale[0])

    for t in range(TENSOR):

        @pl.when((tensor < 3) & (tensor != t))
        def _():
            await_bytes(r.abuf.at[t], r.a_r.at[t])

    @pl.when(tensor < 3)
    def _():
        assemble(r, rows)

    moment = 0.5 * r.attn_mom[0] + r.grad_a[...]
    r.mom_a[...] = moment
    r.xsa[...] = moment.astype(BF)

    at_work = (high * 2 + core, far * 2 + 1)

    @pl.when((core == 1) & (low == 1))
    def _():
        r.xa[here] = r.xsa[...]

    @pl.when((core == 0) | (low == 0))
    def _():
        send(r.xsa, r.xa.at[here], r.e_s, r.e_r.at[low], at_work)

    sides = [
        GatherDp(lambda d, side=side: r.xa.at[rows_of(d // 2 * 2 + side)], r.f_s.at[side], r.f_r.at[side], data, tensor)
        for side in range(2)
    ]
    for side in range(2):

        @pl.when((core == 1) & ((low == 0) | (side == 0)))
        def _():
            await_bytes(sides[side].slot_of(data), r.e_r.at[side])

        pl.when(core == 1)(sides[side].start)

    for copy in parts:
        copy.wait()
    r.norm_grad[...] = sum((r.qbuf[d] for d in range(1, count)), r.qbuf[0])

    @pl.when(core == 0)
    def _():
        newton(r.xmat, r.du, r.hid, 3072, None, NS_STEPS - 2)
        newton_gram(r.xmat, r.du, None)
        newton_rows(r.xmat, r.du, data, rows, 768, r.orow)

    for m, out in enumerate((r.o_u, r.o_d)):

        @pl.when((core == 0) & (far == m))
        def _():
            for k in (1, 2, 3):
                send(r.orow.at[:, cols(tensor ^ k)], out, r.w_s.at[k], r.w_r.at[m], g.device(k))
            out[...] = r.orow[:, cols(tensor)]

    owner = far * 2 + low

    @pl.when(core == 1)
    def _():
        for side in range(2):
            sides[side].forward(cross=False)
        for side in range(2):
            sides[side].close(cross=False)
        newton(r.xa, r.du, r.hid, 768, newton_scale(r.xa), 1)
        newton(r.xa, r.du, r.hid, 768, None, NS_STEPS - 2)
        newton_gram(r.xa, r.du, None)
        newton_rows(r.xa, r.du, other, rows, 768, r.orow.at[:, 768:1536])
        send(r.orow.at[:, 768:1536], r.o_a, r.v_s.at[0], r.v_r, (other, owner))
        newton_rows(r.xa, r.du, data, rows, 768, r.orow.at[:, :768])

    @pl.when((core == 1) & (low == 1))
    def _():
        r.o_a[...] = r.orow[:, :768]

    @pl.when((core == 1) & (low == 0))
    def _():
        send(r.orow.at[:, :768], r.o_a, r.v_s.at[1], r.v_r, (data, owner))

    @pl.when((core == 0) | (low == 0))
    def _():
        await_bytes(r.o_a, r.v_r)

    for m, out in enumerate((r.o_u, r.o_d)):

        @pl.when((core == 1) | (far != m))
        def _():
            await_bytes(out, r.w_r.at[m])

    await_bytes(r.xsd, r.swap_s)
    out_low.wait_send()

    @pl.when(high != tensor)
    def _():
        await_bytes(r.osend, r.o_s.at[1])

    @pl.when((high == tensor) & (tensor != 3))
    def _():
        await_bytes(r.oout, r.o_s.at[2])

    for m in range(3):

        @pl.when(tensor != m)
        def _():
            await_bytes(r.asend.at[m], r.a_s.at[m])

    @pl.when((core == 0) | (low == 0))
    def _():
        await_bytes(r.xsa, r.e_s)

    @pl.when(core == 0)
    def _():
        for k in (1, 2, 3):
            await_bytes(r.o_u, r.w_s.at[k])

    @pl.when(core == 1)
    def _():
        for b in range(2):
            for d in range(count):
                await_bytes(own, r.j_s.at[b, d])
        await_bytes(r.o_a, r.v_s.at[0])

    @pl.when((core == 1) & (low == 0))
    def _():
        await_bytes(r.o_a, r.v_s.at[1])


def step_call(count, rows, ins):
    v = pltpu.VMEM
    n = count // 2
    one = pltpu.SemaphoreType.DMA
    outs = dict(
        mixed=shape(QUARTER, 768),
        input_grad=shape(QUARTER, 768, dtype=F32),
        mom_a=shape(rows, 768, dtype=F32),
        mom_u=shape(rows, 768, dtype=F32),
        mom_d=shape(rows, 768, dtype=F32),
        norm_grad=shape(4, 768, dtype=F32),
        o_u=shape(rows, 768),
        o_d=shape(rows, 768),
        o_a=shape(rows, 768),
    )
    per_head = (3, TENSOR, QUARTER, LANES)
    quarters = (TENSOR, QUARTER, 768)
    scratch = dict(
        slabs=v((TENSOR, rows, 256), BF),
        wo_own=v((2, rows // 2, 768), BF),
        seq=v(quarters, BF),
        slab_in=v((3, rows, 256), BF),
        wp=v((768, 5 * LANES), BF),
        wo=v((count, 2, rows // 2, 768), BF),
        wu=v((count, rows, 768), BF),
        wd=v((count, rows, 768), BF),
        woh=v((3, LANES, 768), BF),
        slab_s=dma(4),
        slab_r=dma(4),
        tok_s=dma(3),
        tok_r=dma(3),
        share_s=dma(count),
        share_r=dma(count),
        gather_s=dma(7, 8),
        gather_r=dma(7, 8),
        qf=v(per_head, BF),
        kf=v(per_head, BF),
        va=v(per_head, BF),
        qg=v(per_head, F32),
        kg=v(per_head, F32),
        af=v(per_head, F32),
        sb=v((3, TENSOR, QUARTER, QUARTER), BF),
        st=v((3, TENSOR, LANES, LANES), BF),
        state=v((3, LANES, LANES), F32),
        attn=v((TENSOR, QUARTER, 256), BF),
        aall=v((TENSOR, 2, QUARTER, 256), BF),
        fold=v((3, 3, QUARTER, LANES), F32),
        attn_s=dma(2, 4),
        attn_r=dma(2, 4),
        hb=v(quarters, BF),
        n1=v((QUARTER, 768), F32),
        s1=v((QUARTER, LANES), F32),
        h1=v((QUARTER, 768), F32),
        hid=v(quarters, BF),
        gp=v(quarters, F32),
        du=v(quarters, BF),
        dr2=v(quarters, BF),
        dr2f=v((QUARTER, 768), F32),
        dr1=v(quarters, BF),
        dr1f=v((QUARTER, 768), F32),
        kept=v((2, HALF, 768), F32),
        near_send=v((4, HALF, 768), BF),
        near_recv=v((4, HALF, 768), BF),
        far_send=v((2, HALF, 768), BF),
        far_recv=v((2, HALF, 768), BF),
        near_s=dma(12),
        near_r=dma(12),
        far_s=dma(6),
        far_r=dma(6),
        h_s=dma(2),
        h_r=dma(2),
        dr2_s=dma(6),
        dr2_r=dma(6),
        dr1_s=dma(6),
        dr1_r=dma(6),
        gu=v((count, rows, 768), BF),
        gd=v((count, rows, 768), BF),
        ga=v((count, rows, 5 * LANES), BF),
        go=v((2, rows, 768), BF),
        partial=v((4, 768), F32),
        pbuf=v((TENSOR, 4, 768), F32),
        psum=v((4, 768), F32),
        qbuf=v((count, 4, 768), F32),
        pt_s=dma(4),
        pt_r=dma(4),
        pd_s=dma(count),
        pd_r=dma(count),
        olow=v((rows, 768), BF),
        osend=v((rows, 768), BF),
        ohigh=v((n, rows, 768), BF),
        oout=v((rows, 768), BF),
        oin=v((rows, 768), BF),
        o_s=dma(3),
        o_r=dma(n),
        oin_r=one,
        asend=v((3, rows, 256), BF),
        abuf=v((TENSOR, rows, 256), BF),
        a_s=dma(3),
        a_r=dma(TENSOR),
        grad_a=v((rows, 768), F32),
        xsd=v((rows, 768), BF),
        xsu=v((rows, 768), BF),
        xsa=v((rows, 768), BF),
        xmat=v((768, TENSOR * 768), BF),
        xa=v((768, 768), BF),
        scale=pltpu.SMEM((1,), F32),
        swap_s=one,
        swap_r=one,
        x_s=dma(2, 8),
        x_r=dma(2, 8),
        e_s=one,
        e_r=dma(2),
        f_s=dma(2, 8),
        f_r=dma(2, 8),
        j_s=dma(2, count),
        j_r=dma(2, count),
        orow=v((rows, TENSOR * 768), BF),
        w_s=dma(4),
        w_r=dma(2),
        v_s=dma(2),
        v_r=one,
    )
    for key in "dua":
        part = (rows, 5 * LANES if key == "a" else 768)
        for name in ("low", "hs", "hb"):
            scratch[name + key] = v((n,) + part, BF)
        for name in ("ls_", "lr_", "hs_", "hr_"):
            scratch[name + key] = dma(n)
    body = functools.partial(step_body, count, rows)
    return kernel_call(body, "layer_step", ins, outs, scratch, 0, ("lengths",))


def finish_body(r):
    keep = 1.0 - MUON_RATE * MUON_DECAY
    rate_a = MUON_RATE * 0.2 * math.sqrt(768)
    rate_ff = MUON_RATE * 0.2 * math.sqrt(TENSOR * 768)
    r.attn_new[0] = r.attn_w[0] * keep - rate_a * r.o_a[...].astype(F32)
    r.up_new[...] = r.up_w[...] * keep - rate_ff * r.o_u[...].astype(F32)
    r.down_new[...] = r.down_w[...] * keep - rate_ff * r.o_d[...].astype(F32)
    r.attn_moment[0] = r.mom_a[...]
    r.up_moment[...] = r.mom_u[...]
    r.down_moment[...] = r.mom_d[...]
    r.mixed_out[...] = r.mixed[...]
    r.input_grad_out[...] = r.input_grad[...]
    grad = r.norm_grad[...]
    moment1 = 0.5 * r.norm_m1[...] + 0.5 * grad
    moment2 = 0.95 * r.norm_m2[...] + 0.05 * grad * grad
    first_hat = moment1 / (1.0 - 0.5**STEP)
    second_hat = moment2 / (1.0 - 0.95**STEP)
    r.norm_moment1[...] = moment1
    r.norm_moment2[...] = moment2
    r.norm_new[...] = r.norms[...] - ADAM_RATE * first_hat / (jnp.sqrt(second_hat) + 1e-08)


def finish_call(ins):
    rows = ins["up_w"].shape[0]
    block = shape(rows, 768, dtype=F32)
    small = shape(4, 768, dtype=F32)
    outs = dict(
        mixed_out=shape(QUARTER, 768),
        input_grad_out=shape(QUARTER, 768, dtype=F32),
        attn_new=shape(1, rows, 768, dtype=F32),
        attn_moment=shape(1, rows, 768, dtype=F32),
        up_new=block,
        up_moment=block,
        down_new=block,
        down_moment=block,
        norm_moment1=small,
        norm_moment2=small,
        norm_new=small,
    )
    return kernel_call(finish_body, "finish", ins, outs, {}, None)


def step_on_device(
    tokens,
    cotangent,
    lengths,
    attn_w,
    up_w,
    down_w,
    norm_params,
    attn_mom,
    up_mom,
    down_mom,
    norm_m1,
    norm_m2,
):
    count = lax.axis_size("dp")
    rows = attn_w.shape[1]
    done = step_call(
        count,
        rows,
        dict(
            lengths=lengths,
            tokens=tokens,
            cotangent=cotangent,
            attn_w=attn_w,
            up_w=up_w,
            down_w=down_w.T,
            norms=norm_params,
            attn_mom=attn_mom,
            up_mom=up_mom,
            down_mom=down_mom.T,
        ),
    )
    last = finish_call(
        dict(
            attn_w=attn_w,
            up_w=up_w,
            down_w=down_w.T,
            norms=norm_params,
            norm_m1=norm_m1,
            norm_m2=norm_m2,
            **done,
        )
    )
    return (
        last["mixed_out"],
        last["input_grad_out"],
        last["attn_new"],
        last["attn_moment"],
        last["up_new"],
        last["up_moment"],
        last["down_new"].T,
        last["down_moment"].T,
        last["norm_moment1"],
        last["norm_moment2"],
        last["norm_new"],
    )


def solution(mesh):
    placed = (
        P(("dp", "tensor"), None),
        P(("dp", "tensor"), None),
        P("dp"),
        P("tensor", "dp", None),
        P("dp", "tensor"),
        P("tensor", "dp"),
        P(),
        P("tensor", "dp", None),
        P("dp", "tensor"),
        P("tensor", "dp"),
        P(),
        P(),
    )
    whole_tiles = mesh.shape["dp"] == 8 and mesh.shape["tensor"] == TENSOR
    return jax.shard_map(
        step_on_device if whole_tiles else on_device,
        mesh=mesh,
        in_specs=placed,
        out_specs=(
            P(("dp", "tensor"), None),
            P(("dp", "tensor"), None),
            P("tensor", "dp", None),
            P("tensor", "dp", None),
            P("dp", "tensor"),
            P("dp", "tensor"),
            P("tensor", "dp"),
            P("tensor", "dp"),
            P(),
            P(),
            P(),
        ),
        check_vma=False,
    )
```

```python
import functools
import math
import types

import jax
import jax.numpy as jnp
from jax import lax
from jax.experimental import pallas as pl
from jax.experimental.pallas import tpu as pltpu
from jax.sharding import PartitionSpec as P

HEADS = 12
HDIM = 64
BLOCK = 64
NS_STEPS = 5
STEP = 10


NORM_EPS = 1e-05
NS_EPS = 1e-07
COEF_A = 3.4445
COEF_B = -4.775
COEF_C = 2.0315
MUON_RATE = 0.15
MUON_DECAY = 0.1
ADAM_RATE = 0.2


def cut_along(array, dim, size):
    lengths = array.shape
    pieces = array.reshape(*lengths[:dim], size, lengths[dim] // size, *lengths[dim + 1 :])
    return jnp.moveaxis(pieces, dim, 0)


def sum_at_owner(array, axis, dim):
    size = lax.axis_size(axis)
    pieces = lax.all_to_all(cut_along(array, dim, size), axis, 0, 0, tiled=True)
    return jnp.sum(pieces.astype(jnp.float32), axis=0)


def sent_together(arrays, axis, dim, along):
    widths = [a.shape[along] for a in arrays]
    both = jnp.concatenate(arrays, axis=along)
    whole = sum_at_owner(both, axis, dim)
    return tuple(jnp.split(whole, [sum(widths[:k]) for k in range(1, len(widths))], axis=along))


def partner(array, axis, bit):
    return lax.ppermute(array, axis, [(i, i ^ 1 << bit) for i in range(lax.axis_size(axis))])


def contract_rows(left, right):
    return lax.dot_general(
        left, right, (((0,), (0,)), ((), ())), preferred_element_type=jnp.float32
    )


def contract_cols(left, right):
    return lax.dot_general(
        left, right, (((1,), (1,)), ((), ())), preferred_element_type=jnp.float32
    )


def norm_forward(resid, gain, bias):
    center = resid - jnp.mean(resid, -1, keepdims=True)
    spread = jnp.mean(center * center, -1, keepdims=True)
    scale_inv = lax.rsqrt(spread + NORM_EPS)
    normal_rows = center * scale_inv
    return (normal_rows, scale_inv, normal_rows * gain + bias)


def norm_back(normal_rows, scale_inv, grad_normed):
    return scale_inv * (
        grad_normed
        - jnp.mean(grad_normed, -1, keepdims=True)
        - normal_rows * jnp.mean(grad_normed * normal_rows, -1, keepdims=True)
    )


def smooth_gate(values):
    return jax.nn.gelu(values, approximate=True)


def features(proj, cosine, sine, weight_rows):
    count = proj.shape[0]
    soft = jax.nn.softplus(proj).reshape(count, HEADS, HDIM)
    both = jnp.concatenate([soft * cosine[:, None, None], soft * sine[:, None, None]], -1)
    return both * weight_rows[:, None, None]


def features_back(grad_feat, proj, cosine, sine, weight_rows):
    count = proj.shape[0]
    grad_soft = (
        grad_feat[..., :HDIM] * cosine[:, None, None] + grad_feat[..., HDIM:] * sine[:, None, None]
    )
    grad_soft = grad_soft * weight_rows[:, None, None]
    slope = jax.nn.sigmoid(proj).reshape(count, HEADS, HDIM)
    return (grad_soft * slope).reshape(count, HEADS * HDIM).astype(jnp.bfloat16)


def blocked(array):
    return array.reshape(array.shape[0] // BLOCK, BLOCK, array.shape[1], array.shape[2])


def attend_forward(qblock, kblock, vblock, lower):
    scores = (
        jnp.einsum("nihf,njhf->nhij", qblock, kblock, preferred_element_type=jnp.float32) * lower
    )
    scores_low = scores.astype(jnp.bfloat16)
    pairs = jnp.einsum("njhf,njhd->nhfd", kblock, vblock, preferred_element_type=jnp.float32)
    state = jnp.cumsum(pairs, 0) - pairs
    state_low = state.astype(jnp.bfloat16)
    key_sum = jnp.sum(kblock.astype(jnp.float32), 1)
    zsum = jnp.cumsum(key_sum, 0) - key_sum
    numer = jnp.einsum("nhij,njhd->nihd", scores_low, vblock, preferred_element_type=jnp.float32)
    numer = numer + jnp.einsum(
        "nihf,nhfd->nihd", qblock, state_low, preferred_element_type=jnp.float32
    )
    denom = jnp.transpose(jnp.sum(scores, -1), (0, 2, 1))
    denom = denom + jnp.einsum(
        "nihf,nhf->nih", qblock.astype(jnp.float32), zsum, precision=lax.Precision.HIGHEST
    )
    return (scores_low, state_low, zsum, denom, numer / denom[..., None])


def attend_backward(
    qblock, kblock, vblock, lower, scores_low, state_low, zsum, denom, result, grad_out
):
    grad_numer = (grad_out / denom[..., None]).astype(jnp.bfloat16)
    grad_denom = -jnp.sum(grad_out * result, -1) / denom
    grad_scores = jnp.einsum(
        "nihd,njhd->nhij", grad_numer, vblock, preferred_element_type=jnp.float32
    )
    grad_scores = ((grad_scores + jnp.transpose(grad_denom, (0, 2, 1))[..., None]) * lower).astype(
        jnp.bfloat16
    )
    grad_state = jnp.einsum(
        "nihf,nihd->nhfd", qblock, grad_numer, preferred_element_type=jnp.float32
    )
    grad_pairs = (jnp.cumsum(grad_state[::-1], 0)[::-1] - grad_state).astype(jnp.bfloat16)
    grad_z = jnp.einsum(
        "nih,nihf->nhf", grad_denom, qblock.astype(jnp.float32), precision=lax.Precision.HIGHEST
    )
    grad_ksum = jnp.cumsum(grad_z[::-1], 0)[::-1] - grad_z
    grad_qf = jnp.einsum("nhij,njhf->nihf", grad_scores, kblock, preferred_element_type=jnp.float32)
    grad_qf = grad_qf + jnp.einsum(
        "nihd,nhfd->nihf", grad_numer, state_low, preferred_element_type=jnp.float32
    )
    grad_qf = grad_qf + grad_denom[..., None] * zsum[:, None]
    grad_kf = jnp.einsum("nhij,nihf->njhf", grad_scores, qblock, preferred_element_type=jnp.float32)
    grad_kf = grad_kf + jnp.einsum(
        "njhd,nhfd->njhf", vblock, grad_pairs, preferred_element_type=jnp.float32
    )
    grad_kf = grad_kf + grad_ksum[:, None]
    grad_val = jnp.einsum(
        "nhij,nihd->njhd", scores_low, grad_numer, preferred_element_type=jnp.float32
    )
    grad_val = grad_val + jnp.einsum(
        "njhf,nhfd->njhd", kblock, grad_pairs, preferred_element_type=jnp.float32
    )
    return (grad_qf, grad_kf, grad_val.astype(jnp.bfloat16))


def newton_update(iterate, gram):
    poly = (
        COEF_B * gram.astype(jnp.float32)
        + COEF_C * jnp.dot(gram, gram, preferred_element_type=jnp.float32)
    ).astype(jnp.bfloat16)
    return (
        COEF_A * iterate.astype(jnp.float32)
        + jnp.dot(poly, iterate, preferred_element_type=jnp.float32)
    ).astype(jnp.bfloat16)


def orthogonalize(iterate):
    for step in range(NS_STEPS):
        gram = jnp.dot(iterate, iterate.T, preferred_element_type=jnp.float32).astype(jnp.bfloat16)
        iterate = newton_update(iterate, gram)
    return iterate


def on_device(
    tokens,
    cotangent,
    lengths,
    attn_w,
    up_w,
    down_w,
    norm_params,
    attn_mom,
    up_mom,
    down_mom,
    norm_m1,
    norm_m2,
):
    tensor_index = lax.axis_index("tensor")
    data_index = lax.axis_index("dp")
    tensor_count = lax.axis_size("tensor")
    length = lengths[0]
    rows_here = tokens.shape[0]
    wa_rows, up_block, down_block = (
        lax.all_gather(attn_w.astype(jnp.bfloat16), "dp", axis=1, tiled=True),
        lax.all_gather(up_w.astype(jnp.bfloat16), "dp", axis=0, tiled=True),
        lax.all_gather(down_w.astype(jnp.bfloat16), "dp", axis=1, tiled=True),
    )
    w_all = lax.all_gather(wa_rows, "tensor", axis=0, tiled=True)
    w_query = w_all[0]
    w_key = w_all[1]
    w_value = w_all[2]
    w_out = w_all[3]
    sequence = lax.all_gather(tokens, "tensor", axis=0, tiled=True)
    count = sequence.shape[0]
    width = sequence.shape[1]
    blocks = count // BLOCK
    start_row = tensor_index * rows_here

    def mine(array):
        return lax.dynamic_slice_in_dim(array, start_row, rows_here, 0)

    where = jnp.arange(count)
    live = (where < length).astype(jnp.float32)
    place = jnp.minimum(where, length - 1).astype(jnp.float32)
    theta = 0.5 * math.pi * place / length.astype(jnp.float32)
    cosine = jnp.cos(theta)
    sine = jnp.sin(theta)
    every_row = jnp.ones((count,), jnp.float32)
    query = jnp.dot(sequence, w_query, preferred_element_type=jnp.float32)
    key_proj = jnp.dot(sequence, w_key, preferred_element_type=jnp.float32)
    value = jnp.dot(sequence, w_value, preferred_element_type=jnp.float32)
    qblock = blocked(features(query, cosine, sine, every_row).astype(jnp.bfloat16))
    kblock = blocked(features(key_proj, cosine, sine, live).astype(jnp.bfloat16))
    vblock = value.astype(jnp.bfloat16).reshape(blocks, BLOCK, HEADS, HDIM)
    lower = jnp.tril(jnp.ones((BLOCK, BLOCK), jnp.float32))
    scores_low, state_low, zsum, denom, result = attend_forward(qblock, kblock, vblock, lower)
    attn_low = result.reshape(count, width).astype(jnp.bfloat16)
    branch = jnp.dot(attn_low, w_out, preferred_element_type=jnp.float32)
    normal_one, scale_one, hidden_in = norm_forward(
        sequence.astype(jnp.float32) + branch, norm_params[0], norm_params[1]
    )
    hidden_low = hidden_in.astype(jnp.bfloat16)
    pre = jnp.dot(hidden_low, up_block, preferred_element_type=jnp.float32)
    act_low = smooth_gate(pre).astype(jnp.bfloat16)
    ffn_rows = lax.psum_scatter(
        jnp.dot(act_low, down_block, preferred_element_type=jnp.float32).astype(jnp.bfloat16),
        "tensor",
        scatter_dimension=0,
        tiled=True,
    ).astype(jnp.float32)
    live_rows = mine(live)
    normal_two, scale_two, normed = norm_forward(
        mine(hidden_in) + ffn_rows, norm_params[2], norm_params[3]
    )
    mixed = (live_rows[:, None] * normed).astype(jnp.bfloat16)
    grad_y = cotangent.astype(jnp.float32) * live_rows[:, None]
    grad_g2 = jnp.sum(grad_y * normal_two, 0)
    grad_b2 = jnp.sum(grad_y, 0)
    grad_r2 = norm_back(normal_two, scale_two, grad_y * norm_params[2])
    grad_r2_all = lax.all_gather(grad_r2.astype(jnp.bfloat16), "tensor", axis=0, tiled=True)
    grad_down = contract_rows(act_low, grad_r2_all)
    grad_act = contract_cols(grad_r2_all, down_block)
    gate_out, gate_pull = jax.vjp(smooth_gate, pre)
    grad_pre = gate_pull(grad_act)[0].astype(jnp.bfloat16)
    grad_up = contract_rows(hidden_low, grad_pre)
    grad_hidden = (
        lax.psum_scatter(
            contract_cols(grad_pre, up_block).astype(jnp.bfloat16),
            "tensor",
            scatter_dimension=0,
            tiled=True,
        ).astype(jnp.float32)
        + grad_r2
    )
    normal_one_rows = mine(normal_one)
    grad_g1 = jnp.sum(grad_hidden * normal_one_rows, 0)
    grad_b1 = jnp.sum(grad_hidden, 0)
    grad_r1 = norm_back(normal_one_rows, mine(scale_one), grad_hidden * norm_params[0])
    grad_branch = lax.all_gather(grad_r1.astype(jnp.bfloat16), "tensor", axis=0, tiled=True)
    grad_attn = contract_cols(grad_branch, w_out).reshape(blocks, BLOCK, HEADS, HDIM)
    grad_qf, grad_kf, grad_val = attend_backward(
        qblock, kblock, vblock, lower, scores_low, state_low, zsum, denom, result, grad_attn
    )
    grad_query = features_back(
        grad_qf.reshape(count, HEADS, 2 * HDIM), query, cosine, sine, every_row
    )
    grad_key = features_back(grad_kf.reshape(count, HEADS, 2 * HDIM), key_proj, cosine, sine, live)
    grad_value = grad_val.reshape(count, width)
    input_grad = (
        grad_r1
        + contract_cols(mine(grad_query), w_query)
        + contract_cols(mine(grad_key), w_key)
        + contract_cols(mine(grad_value), w_value)
    )
    left_rows = jnp.where(tensor_index == 3, attn_low, sequence)
    right_all = jnp.stack((grad_query, grad_key, grad_value, grad_branch))
    right_rows = lax.dynamic_index_in_dim(right_all, tensor_index, 0, keepdims=False)
    grad_owned = contract_rows(left_rows, right_rows)
    norm_partial = jnp.stack((grad_g1, grad_b1, grad_g2, grad_b2))
    grad_a, grad_u, grad_d = (
        *sent_together((grad_owned.astype(jnp.bfloat16), grad_up.astype(jnp.bfloat16)), "dp", 0, 1),
        sum_at_owner(grad_down.astype(jnp.bfloat16), "dp", 1),
    )
    moment_a = 0.5 * attn_mom[0] + grad_a
    moment_u = 0.5 * up_mom + grad_u
    moment_d = 0.5 * down_mom + grad_d
    owner_pick = jax.nn.one_hot(tensor_index, 4, dtype=jnp.float32)
    squares = jnp.concatenate(
        (
            owner_pick * jnp.sum(moment_a * moment_a),
            jnp.stack((jnp.sum(moment_u * moment_u), jnp.sum(moment_d * moment_d))),
        )
    )
    totals, norm_grad = lax.psum((squares, norm_partial), ("dp", "tensor"))
    size_a = jnp.sqrt(jnp.sum(totals[:4] * owner_pick))
    size_u = jnp.sqrt(totals[4])
    size_d = jnp.sqrt(totals[5])
    start_a = (moment_a / (size_a + NS_EPS)).astype(jnp.bfloat16)
    start_u = (moment_u / (size_u + NS_EPS)).astype(jnp.bfloat16)
    start_d = (moment_d.T / (size_d + NS_EPS)).astype(jnp.bfloat16)
    whole_a, cols_u, cols_d = (
        lax.all_gather(start_a, "dp", axis=0, tiled=True),
        lax.all_gather(start_u, "dp", axis=0, tiled=True),
        lax.all_gather(start_d, "dp", axis=0, tiled=True),
    )
    orth_a = orthogonalize(whole_a)
    is_even = tensor_index % 2 == 0
    whole_u, whole_d = (
        lax.all_gather(cols_u, "tensor", axis=1, tiled=True),
        lax.all_gather(cols_d, "tensor", axis=1, tiled=True),
    )
    orth_whole = orthogonalize(jnp.where(is_even, whole_u, whole_d))
    block_cols = cols_u.shape[1]
    own_block = lax.dynamic_slice_in_dim(orth_whole, tensor_index * block_cols, block_cols, 1)
    partner_block = lax.dynamic_slice_in_dim(
        orth_whole, jnp.bitwise_xor(tensor_index, 1) * block_cols, block_cols, 1
    )
    fetched = partner(partner_block, "tensor", 0)
    orth_u = jnp.where(is_even, own_block, fetched)
    orth_d = jnp.where(is_even, fetched, own_block)
    span = moment_a.shape[0]

    def take_rows(array):
        return lax.dynamic_slice_in_dim(array, data_index * span, span, 0).astype(jnp.float32)

    ff_whole = up_block.shape[1] * tensor_count
    keep = 1.0 - MUON_RATE * MUON_DECAY
    new_a = attn_w[0] * keep - MUON_RATE * 0.2 * math.sqrt(width) * take_rows(orth_a)
    scale_ff = 0.2 * math.sqrt(max(width, ff_whole))
    new_u = up_w * keep - MUON_RATE * scale_ff * take_rows(orth_u)
    new_d = down_w * keep - MUON_RATE * scale_ff * take_rows(orth_d).T
    norm_moment1 = 0.5 * norm_m1 + 0.5 * norm_grad
    norm_moment2 = 0.95 * norm_m2 + 0.05 * norm_grad * norm_grad
    first_hat = norm_moment1 / (1.0 - 0.5**STEP)
    second_hat = norm_moment2 / (1.0 - 0.95**STEP)
    norm_new = norm_params - ADAM_RATE * first_hat / (jnp.sqrt(second_hat) + 1e-08)
    return (
        mixed,
        input_grad,
        new_a[None],
        moment_a[None],
        new_u,
        moment_u,
        new_d,
        moment_d,
        norm_moment1,
        norm_moment2,
        norm_new,
    )


BF = jnp.bfloat16
F32 = jnp.float32
MESH = pl.DeviceIdType.MESH
TENSOR = 4
QUARTER = 256
LANES = 128
HALF = 128
HIGH = 4
VMEM_LIMIT = 63 << 20
GELU_C = math.sqrt(2.0 / math.pi)
GELU_A = 0.044715


def nn(left, right):
    return jnp.dot(left, right, preferred_element_type=F32)


def nt(left, right):
    return lax.dot_general(left, right, (((1,), (1,)), ((), ())), preferred_element_type=F32)


def tn(left, right):
    return lax.dot_general(left, right, (((0,), (0,)), ((), ())), preferred_element_type=F32)


def lanes_of(rows, cols=LANES):
    return lax.broadcasted_iota(jnp.int32, (rows, cols), 1)


def half_roll(array):
    return pltpu.roll(array, LANES // 2, 1)


def place():
    data = lax.axis_index("dp")
    tensor = lax.axis_index("tensor")
    return data, tensor


def greet(devices):
    barrier = pltpu.get_barrier_semaphore()
    for device in devices:
        pl.semaphore_signal(barrier, inc=1, device_id=device, device_id_type=MESH)
    pl.semaphore_wait(barrier, len(devices))


def send(src, dst, send_sem, recv_sem, device):
    copy = pltpu.make_async_remote_copy(
        src_ref=src,
        dst_ref=dst,
        send_sem=send_sem,
        recv_sem=recv_sem,
        device_id=device,
        device_id_type=MESH,
    )
    copy.start()
    return copy


def kernel_call(body, name, ins, outs, scratch, collective, scalars=()):
    in_names = list(ins)
    out_names = list(outs)
    scratch_names = list(scratch)

    def kernel(*refs):
        body(types.SimpleNamespace(**dict(zip(in_names + out_names + scratch_names, refs))))

    results = pl.pallas_call(
        kernel,
        name=name,
        out_shape=[outs[n] for n in out_names],
        in_specs=[
            pl.BlockSpec(memory_space=pltpu.SMEM if n in scalars else pltpu.VMEM) for n in in_names
        ],
        out_specs=[pl.BlockSpec(memory_space=pltpu.VMEM)] * len(out_names),
        scratch_shapes=[scratch[n] for n in scratch_names],
        compiler_params=pltpu.CompilerParams(
            collective_id=collective,
            has_side_effects=collective is not None,
            vmem_limit_bytes=VMEM_LIMIT,
        ),
    )(*[ins[n] for n in in_names])
    return dict(zip(out_names, results))


def shape(*dims, dtype=BF):
    return jax.ShapeDtypeStruct(dims, dtype)


def dma(*dims):
    return pltpu.SemaphoreType.DMA(dims)


def await_bytes(ref, sem):
    pltpu.make_async_copy(ref, ref, sem).wait()


class GatherDp:
    def __init__(self, slot_of, sends, recvs, data, tensor, detour=False):
        self.slot_of, self.sends, self.recvs, self.detour = slot_of, sends, recvs, detour
        self.data, self.tensor = data, tensor
        self.high, self.low = data // 2, data % 2
        self.partner = (self.high * 2 + 1 - self.low, tensor)
        self.relays = (self.high == 1) | (self.high == 2)
        first_end, last_end = self.high == 0, self.high == HIGH - 1
        self.order = (
            jnp.where(first_end, 3, 1),
            jnp.where(first_end | last_end, 2, 3),
            jnp.where(first_end, 1, jnp.where(last_end, 3, 2)),
        )

    def source(self, step):
        return lax.rem(self.high + HIGH - step, HIGH) * 2 + self.low

    def push(self, slot, at, to, there=None):
        send(slot, slot, self.sends.at[at], self.recvs.at[at if there is None else there], to)

    def start(self):
        mine = self.slot_of(self.data)
        for step, allowed in ((1, self.high != HIGH - 1), (2, None), (3, self.high != 0)):
            to = (lax.rem(self.high + step, HIGH) * 2 + self.low, self.tensor)
            if allowed is None:
                self.push(mine, step, to)
            else:
                pl.when(allowed)(functools.partial(self.push, mine, step, to))

    def cross(self):
        self.push(self.slot_of(self.data), 0, self.partner)

    def passes(self, step):
        skip = ((self.high == 1) & (step == 1)) | ((self.high == 2) & (step == 3))
        if self.detour:
            skip = skip | ((self.high == 0) & (step == 3)) | ((self.high == 3) & (step == 1))
        return jnp.logical_not(skip)

    def forward(self, cross=True):
        beside = ((self.high ^ 1) * 2 + self.low, self.tensor)
        for position, step in enumerate(self.order):
            slot = self.slot_of(self.source(step))
            await_bytes(slot, self.recvs.at[step])
            if position == HIGH - 2:
                there = jnp.where(self.high == 2, 3, 1)
                pl.when(self.relays)(functools.partial(self.push, slot, 7, beside, there))
            if cross:
                at = HIGH - 1 + step
                pl.when(self.passes(step))(functools.partial(self.push, slot, at, self.partner))
            if cross and position == 0:
                slot = self.slot_of(self.partner_slot(0))
                await_bytes(slot, self.recvs.at[0])
                there = jnp.where((self.high == 0) | (self.high == 2), 4, 6)
                go_on = functools.partial(self.push, slot, 8, beside, there)
                if self.detour:
                    go_on()
                else:
                    pl.when(jnp.logical_not(self.relays))(go_on)

    def partner_slot(self, step):
        return self.source(step) + 1 - 2 * self.low

    def arrive(self, *steps):
        for step in steps or range(HIGH):
            if step:
                await_bytes(self.slot_of(self.partner_slot(step)), self.recvs.at[HIGH - 1 + step])

    def close(self, cross=True):
        mine = self.slot_of(self.data)

        def sent(at, allowed):
            pl.when(allowed)(functools.partial(await_bytes, mine, self.sends.at[at]))

        if cross:
            await_bytes(mine, self.sends.at[0])
            for step in range(1, HIGH):
                sent(HIGH - 1 + step, self.passes(step))
            if self.detour:
                await_bytes(mine, self.sends.at[8])
            else:
                sent(8, jnp.logical_not(self.relays))
        sent(1, self.high != HIGH - 1)
        await_bytes(mine, self.sends.at[2])
        sent(3, self.high != 0)
        sent(7, self.relays)


def softplus_and_slope(x):
    small = jnp.exp(-jnp.abs(x))
    soft = jnp.maximum(x, 0.0) + jnp.log1p(small)
    slope = jnp.where(x >= 0.0, 1.0, small) / (1.0 + small)
    return soft, slope


def spread_weights(r, tiles):
    low = lanes_of(768) < 64
    for k in tiles:
        tile = r.wp[:, k * LANES : (k + 1) * LANES].astype(F32)
        turned = half_roll(tile)
        left, right = jnp.where(low, tile, turned), jnp.where(low, turned, tile)
        if k == 0:
            parts = {0: left, 1: right}
        elif k == 1:
            parts = {3: left, 4: right}
        elif k == 2:
            parts = {2: left, 5: right}
        elif k == 3:
            parts = {6: jnp.where(low, tile, 0.0), 7: jnp.where(low, turned, 0.0)}
        else:
            parts = {8: tile}
        for at, part in parts.items():
            r.xmat[:, at * LANES : (at + 1) * LANES] = part.astype(BF)


def project(r):
    lane = lanes_of(QUARTER)

    def step(q, carry):
        both = nn(r.seq[q], r.xmat[:, : 9 * LANES])
        table, table_live = r.gp[q, :, :LANES], r.gp[q, :, LANES : 2 * LANES]
        for h in range(3):
            soft, slope = softplus_and_slope(both[:, h * LANES : (h + 1) * LANES])
            r.qf[h, q] = (soft * table).astype(BF)
            r.qg[h, q] = slope * table
            soft, slope = softplus_and_slope(both[:, (3 + h) * LANES : (4 + h) * LANES])
            r.kf[h, q] = (soft * table_live).astype(BF)
            r.kg[h, q] = slope * table_live
            value = both[:, (6 + h) * LANES : (7 + h) * LANES]
            ones = jnp.where((lane == 64) | (lane == 65), 1.0, 0.0)
            r.va[h, q] = jnp.where(lane < 64, value, ones).astype(BF)
        return carry

    lax.fori_loop(0, TENSOR, step, 0)


def attend(r, q):
    lane = lanes_of(QUARTER)
    keep = lanes_of(QUARTER, QUARTER) <= lax.broadcasted_iota(jnp.int32, (QUARTER, QUARTER), 0)

    def head(h, carry):
        qf, kf, va = r.qf[h, q], r.kf[h, q], r.va[h, q]
        scores = jnp.where(keep, nt(qf, kf), 0.0).astype(BF)
        r.sb[h, q] = scores
        total = nn(scores, va)
        if q > 0:
            state = r.state[h].astype(BF)
            r.st[h, q] = state
            total = total + nn(qf, state)
        if q < TENSOR - 1:
            pairs = tn(kf, va)
            r.state[h] = pairs if q == 0 else r.state[h] + pairs
        inverse = 1.0 / total[:, 64:65]
        r.af[h, q] = jnp.where(lane < 64, total * inverse, inverse)
        return carry

    lax.fori_loop(0, 3, head, 0)
    zero, one, two = r.af[0, q], r.af[1, q], r.af[2, q]
    r.attn[q, :, :LANES] = jnp.where(lane < 64, zero, half_roll(one)).astype(BF)
    r.attn[q, :, LANES:] = jnp.where(lane < 64, two, 0.0).astype(BF)


def norm_rows(resid):
    center = resid - jnp.mean(resid, -1, keepdims=True)
    spread = jnp.mean(center * center, -1, keepdims=True)
    scale = lax.rsqrt(spread + NORM_EPS)
    return center * scale, scale


def norm_rows_back(normal, scale, grad):
    return scale * (
        grad
        - jnp.mean(grad, -1, keepdims=True)
        - normal * jnp.mean(grad * normal, -1, keepdims=True)
    )


class Group:
    def __init__(self):
        self.data, self.tensor = place()
        self.far, self.core = self.tensor // 2, self.tensor % 2

    def device(self, k):
        return (self.data, self.tensor ^ k)


def half_of(ref, q, part):
    return ref.at[q, pl.ds(part * HALF, HALF)]


class Spread:
    def __init__(self, g, buf, sends, recvs, part):
        self.g, self.buf, self.sends, self.recvs, self.part = g, buf, sends, recvs, part
        own = half_of(buf, g.tensor, part)
        self.far = self.push(own, 0, g.device(2))
        self.near = self.push(own, 1, g.device(1))

    def push(self, ref, k, device):
        k = 3 * self.part + k
        return send(ref, ref, self.sends.at[k], self.recvs.at[k], device)

    def arrive_near(self):
        self.near.wait_recv()

    def pass_far(self):
        self.far.wait_recv()
        self.passed = self.push(half_of(self.buf, self.g.tensor ^ 2, self.part), 2, self.g.device(1))

    def arrive_far(self):
        self.passed.wait_recv()
        for copy in (self.far, self.near, self.passed):
            copy.wait_send()


class SumQuarters:
    def __init__(self, r, g, slot):
        self.r, self.g, self.slot = r, g, slot
        self.near, self.far = {}, {}

    def near_out(self, j, part, value):
        r, k = self.r, 2 * j + part
        r.near_send[k] = value.astype(BF)
        at = 4 * self.slot + k
        self.near[j, part] = send(
            r.near_send.at[k], r.near_recv.at[k], r.near_s.at[at], r.near_r.at[at], self.g.device(1)
        )

    def near_in(self, j, part, value):
        self.near[j, part].wait_recv()
        return value + self.r.near_recv[2 * j + part].astype(F32)

    def far_out(self, part, value):
        r = self.r
        r.far_send[part] = value.astype(BF)
        at = 2 * self.slot + part
        self.far[part] = send(
            r.far_send.at[part], r.far_recv.at[part], r.far_s.at[at], r.far_r.at[at], self.g.device(2)
        )

    def far_in(self, part, value):
        self.far[part].wait_recv()
        value = value + self.r.far_recv[part].astype(F32)
        for copy in (self.far[part], self.near[0, part], self.near[1, part]):
            copy.wait_send()
        return value


def pair_of(ref, quarters, part):
    return jnp.concatenate([ref[q, pl.ds(part * HALF, HALF)] for q in quarters], axis=0)


def put_pair(ref, quarters, part, value):
    for k, q in enumerate(quarters):
        ref[q, pl.ds(part * HALF, HALF)] = value[k * HALF : (k + 1) * HALF]


def feed_in(r, quarters, part):
    pre = nn(pair_of(r.hb, quarters, part), r.wu[...].reshape(768, 768))
    inner = jnp.tanh(GELU_C * (pre + GELU_A * pre * pre * pre))
    half = 0.5 * (1.0 + inner)
    slope = half + 0.5 * pre * (1.0 - inner * inner) * (GELU_C * (1.0 + 3.0 * GELU_A * pre * pre))
    put_pair(r.gp, quarters, part, slope)
    put_pair(r.hid, quarters, part, (pre * half).astype(BF))


def feed_out(r, quarters, part):
    out = nt(pair_of(r.hid, quarters, part), r.wd[...].reshape(768, 768))
    return out[:HALF], out[HALF:]


def feed_back(r, quarters, part):
    grad_act = nn(pair_of(r.dr2, quarters, part), r.wd[...].reshape(768, 768))
    grad_pre = (grad_act * pair_of(r.gp, quarters, part)).astype(BF)
    put_pair(r.du, quarters, part, grad_pre)
    out = nt(grad_pre, r.wu[...].reshape(768, 768))
    return out[:HALF], out[HALF:]


def attend_back(r, g, q):
    lane = lanes_of(QUARTER)
    keep = lanes_of(QUARTER, QUARTER) <= lax.broadcasted_iota(jnp.int32, (QUARTER, QUARTER), 0)
    dr1 = r.dr1[q]

    def head(h, carry):
        grad = nt(dr1, r.woh[h])
        af = r.af[h, q]
        inverse = af[:, 64:65]
        dden = -jnp.sum(grad * af, -1, keepdims=True) * inverse
        dden_low = dden.astype(BF).astype(F32)
        extra = jnp.where(lane == 64, dden_low, jnp.where(lane == 65, dden - dden_low, 0.0))
        dnum = jnp.where(lane < 64, grad * inverse, extra).astype(BF)
        qf, kf, va, sb = r.qf[h, q], r.kf[h, q], r.va[h, q], r.sb[h, q]
        ds = jnp.where(keep, nt(dnum, va), 0.0).astype(BF)
        dqf = nn(ds, kf)
        if q > 0:
            dqf = dqf + nt(dnum, r.st[h, q])
        dkf = tn(ds, qf)
        dv = tn(sb, dnum)
        if q < TENSOR - 1:
            dkv = r.state[h].astype(BF)
            dkf = dkf + nt(va, dkv)
            dv = dv + nn(kf, dkv)
        if q > 0:
            pairs = tn(qf, dnum)
            r.state[h] = pairs if q == TENSOR - 1 else r.state[h] + pairs
        dqf = dqf * r.qg[h, q]
        dkf = dkf * r.kg[h, q]
        r.n1[:, pl.ds(pl.multiple_of(h * LANES, LANES), LANES)] = dqf + half_roll(dqf)
        r.n1[:, pl.ds(pl.multiple_of((3 + h) * LANES, LANES), LANES)] = dkf + half_roll(dkf)
        r.h1[:, pl.ds(pl.multiple_of(h * LANES, LANES), LANES)] = dv
        return carry

    lax.fori_loop(0, 3, head, 0)
    fold = {}
    for h in range(3):
        fold[0, h] = r.n1[:, h * LANES : (h + 1) * LANES]
        fold[1, h] = r.n1[:, (3 + h) * LANES : (4 + h) * LANES]
        fold[2, h] = r.h1[:, h * LANES : (h + 1) * LANES]
    tiles = (
        jnp.where(lane < 64, fold[0, 0], fold[0, 1]),
        jnp.where(lane < 64, fold[1, 0], fold[1, 1]),
        jnp.where(lane < 64, fold[0, 2], fold[1, 2]),
        jnp.where(lane < 64, fold[2, 0], half_roll(fold[2, 1])),
        jnp.where(lane < 64, fold[2, 2], 0.0),
    )
    for k, tile in enumerate(tiles):
        r.hb[q, :, k * LANES : (k + 1) * LANES] = tile.astype(BF)
    r.gp[q] = nt(r.hb[q, :, : 5 * LANES], r.wp[...])


class ReduceDp:
    def __init__(self, src, low_buf, high_send, high_buf, sems, data, tensor):
        self.src, self.low_buf, self.high_send, self.high_buf = src, low_buf, high_send, high_buf
        self.low_s, self.low_r, self.high_s, self.high_r = sems
        self.tensor = tensor
        self.high, self.low = data // 2, data % 2

    def at(self, step):
        return lax.rem(self.high + step, HIGH)

    def start(self):
        partner = (self.high * 2 + 1 - self.low, self.tensor)
        for step in (1, 2, 3, 0):
            h = self.at(step)
            chunk = self.src.at[h * 2 + 1 - self.low]
            send(chunk, self.low_buf.at[h], self.low_s.at[step], self.low_r.at[step], partner)

    def pair(self, step):
        h = self.at(step)
        await_bytes(self.low_buf.at[h], self.low_r.at[step])
        return self.src[h * 2 + self.low].astype(F32) + self.low_buf[h].astype(F32)

    def forward(self, *steps):
        for step in steps:
            self.high_send[step - 1] = self.pair(step).astype(BF)
            to = (self.at(step) * 2 + self.low, self.tensor)
            chunk = self.high_send.at[step - 1]
            send(chunk, self.high_buf.at[step - 1], self.high_s.at[step], self.high_r.at[step], to)

    def finish(self):
        total = self.pair(0)
        for step in range(1, HIGH):
            await_bytes(self.high_buf.at[step - 1], self.high_r.at[step])
            total = total + self.high_buf[step - 1].astype(F32)
        for step in range(HIGH):
            await_bytes(self.low_buf.at[0], self.low_s.at[step])
            if step:
                await_bytes(self.high_buf.at[0], self.high_s.at[step])
        return total


def newton_scale(x):
    width = x.shape[1]

    def step(k, total):
        part = x[pl.ds(pl.multiple_of(k * 96, 96), 96)].astype(F32)
        return total + part * part

    total = lax.fori_loop(0, 8, step, jnp.zeros((96, width), F32))
    return 1.0 / (jnp.sqrt(jnp.sum(total)) + NS_EPS)


def newton_gram(x, gram, scale):
    edges = [slice(k * 256, (k + 1) * 256) for k in range(3)]
    for a in range(3):
        for b in range(a, 3):
            block = nt(x[edges[a], :], x[edges[b], :])
            block = (block if scale is None else block * (scale * scale)).astype(BF)
            gram[a, :, edges[b]] = block
            if b > a:
                gram[b, :, edges[a]] = block.T


def newton_poly(gram, poly):
    edges = [slice(k * 256, (k + 1) * 256) for k in range(3)]
    for a in range(3):
        for b in range(a, 3):
            block = COEF_C * nt(gram[a], gram[b])
            block = (block + COEF_B * gram[a, :, edges[b]].astype(F32)).astype(BF)
            poly[a, :, edges[b]] = block
            if b > a:
                poly[b, :, edges[a]] = block.T


def newton_apply(x, poly, chunk, scale):
    def columns(c, inner):
        at = pl.ds(pl.multiple_of(c * chunk, chunk), chunk)
        old = x[:, at]
        new = COEF_A * old.astype(F32) + nn(poly[:3].reshape(768, 768), old)
        if scale is not None:
            new = scale * new
        x[:, at] = new.astype(BF)
        return inner

    lax.fori_loop(0, x.shape[1] // chunk, columns, 0)


def newton(x, gram, poly, chunk, first, steps):
    def step(k, carry):
        newton_gram(x, gram, first)
        newton_poly(gram, poly)
        newton_apply(x, poly, chunk, first)
        return carry

    lax.fori_loop(0, steps, step, 0)


def newton_rows(x, gram, index, rows, out):
    own = newton_rows_gram(gram, index, rows)
    poly = (COEF_C * nn(own, gram[:3].reshape(768, 768)) + COEF_B * own.astype(F32)).astype(BF)
    here = pl.ds(pl.multiple_of(index * rows, rows), rows)
    for c in range(x.shape[1] // 768):
        at = slice(c * 768, (c + 1) * 768)
        out[c] = (COEF_A * x[here, at].astype(F32) + nn(poly, x[:, at])).astype(BF)


def newton_rows_gram(gram, index, rows):
    parts = []
    for k in range(rows // 32):
        row = index * rows + 32 * k
        parts.append(gram[row // 256, pl.ds(pl.multiple_of(lax.rem(row, 256), 32), 32), :])
    return jnp.concatenate(parts, axis=0)


def angles(r):
    rows = TENSOR * QUARTER
    length = r.lengths[0]
    where = lax.broadcasted_iota(jnp.int32, (rows, LANES), 0)
    theta = 0.5 * math.pi * jnp.minimum(where, length - 1).astype(F32) / length.astype(F32)
    table = jnp.where(lanes_of(rows) < 64, jnp.cos(theta), jnp.sin(theta))
    live = jnp.where(where < length, 1.0, 0.0)
    r.gp[:, :, :LANES] = table.reshape(TENSOR, QUARTER, LANES)
    r.gp[:, :, LANES : 2 * LANES] = (table * live).reshape(TENSOR, QUARTER, LANES)


def cut_heads(r, rows):
    low = lanes_of(rows) < 64
    tiles = [r.attn_w[0, :, k * LANES : (k + 1) * LANES] for k in range(6)]
    for pair in range(2):
        first, middle, last = tiles[3 * pair : 3 * pair + 3]
        turned, rest = half_roll(middle), half_roll(last)
        parts = [first, jnp.where(low, middle, 0.0), jnp.where(low, turned, rest), jnp.where(low, rest, 0.0)]
        for k, part in enumerate(parts):
            r.slabs[2 * pair + k // 2, :, (k % 2) * LANES : (k % 2 + 1) * LANES] = part.astype(BF)


def step_body(count, rows, r):
    g = Group()
    data, tensor, far, core = g.data, g.tensor, g.far, g.core
    high, low = data // 2, data % 2
    other = high * 2 + 1 - low
    n = count // 2
    half = rows // 2
    near_dev, far_dev = g.device(1), g.device(2)

    cut_heads(r, rows)
    r.wo_own[...] = r.attn_w[0].astype(BF).reshape(2, half, 768)
    greet(
        [g.device(k) for k in (1, 2, 3)]
        + [(lax.rem(data + k, count), tensor) for k in range(1, count)]
        + [(other, tensor ^ 1), (other, tensor ^ 2)]
    )

    def rows_of(d):
        return pl.ds(pl.multiple_of(d * rows, rows), rows)

    def cols(t):
        return pl.ds(pl.multiple_of(t * 768, 768), 768)

    here, there = rows_of(data), rows_of(other)

    for k in (1, 2, 3):
        peer = tensor ^ k

        @pl.when(tensor < 3)
        def _():
            send(r.slabs.at[peer], r.slab_in.at[tensor], r.slab_s.at[k], r.slab_r.at[tensor], g.device(k))

        @pl.when(tensor == 3)
        def _():
            send(r.wo_own.at[peer % 2], r.wo.at[data, peer % 2], r.slab_s.at[k], r.slab_r.at[3], g.device(k))

    r.seq[tensor] = r.tokens[...]
    mine = r.seq.at[tensor]
    tok_near = send(mine, mine, r.tok_s.at[0], r.tok_r.at[0], near_dev)
    tok_far = send(mine, mine, r.tok_s.at[1], r.tok_r.at[1], far_dev)

    @pl.when(tensor < 3)
    def _():
        r.slab_in[tensor] = r.slabs[tensor]

    @pl.when(tensor == 3)
    def _():
        r.wo[data, core] = r.wo_own[core]

    r.wu[data] = r.up_w[...].astype(BF)
    r.wd[data] = r.down_w[...].astype(BF)

    def gather(slot_of, key, detour=False):
        return GatherDp(slot_of, r.gather_s.at[key], r.gather_r.at[key], data, tensor, detour)

    spans = ((0, 2), (2, 5))
    heads = [
        gather(lambda d, a=a, b=b: r.wp.at[rows_of(d), a * LANES : b * LANES], k, k == 1)
        for k, (a, b) in enumerate(spans)
    ]
    outs = gather(lambda d: r.wo.at[d, core], 2)
    ups = [gather(lambda d, k=k: r.wu.at[d, pl.ds(k * half, half)], 3 + k, k == 1) for k in range(2)]
    downs = [gather(lambda d, k=k: r.wd.at[d, pl.ds(k * half, half)], 5 + k, k == 1) for k in range(2)]
    first_half = lanes_of(rows) < 64

    def slab(m):
        @pl.when(tensor != m)
        def _():
            await_bytes(r.slab_in.at[m], r.slab_r.at[m])

        return r.slab_in[m, :, :LANES], r.slab_in[m, :, LANES:]

    query, query_last = slab(0)
    key, key_last = slab(1)
    r.wp[here, :LANES] = query
    r.wp[here, LANES : 2 * LANES] = key
    heads[0].start()
    heads[0].cross()
    both = jnp.where(first_half, query_last.astype(F32), half_roll(key_last.astype(F32)))
    r.wp[here, 2 * LANES : 3 * LANES] = both.astype(BF)
    value, value_last = slab(2)
    r.wp[here, 3 * LANES : 4 * LANES] = value
    r.wp[here, 4 * LANES :] = value_last
    heads[1].start()
    heads[1].cross()

    @pl.when(tensor != 3)
    def _():
        await_bytes(r.wo.at[data, core], r.slab_r.at[3])

    outs.start()
    outs.cross()
    angles(r)
    heads[0].forward()
    ups[0].start()
    tok_far.wait_recv()
    slot = r.seq.at[tensor ^ 2]
    tok_pass = send(slot, slot, r.tok_s.at[2], r.tok_r.at[2], near_dev)
    heads[1].forward()
    ups[1].start()
    for part in ups + downs:
        part.cross()
    outs.forward()
    downs[0].start()
    heads[0].arrive()
    spread_weights(r, (0, 1))
    heads[1].arrive()
    spread_weights(r, (2, 3, 4))
    tok_near.wait_recv()
    tok_pass.wait_recv()
    project(r)
    ups[0].forward()
    downs[1].start()

    copies = [[], []]
    for j in range(2):
        attend(r, 2 * j)
        attend(r, 2 * j + 1)
        mine, rest = 2 * j + core, 2 * j + 1 - core
        for k in (2, 1, 3):
            quarter = mine if k == 2 else rest
            copies[j].append(
                send(r.attn.at[quarter], r.aall.at[tensor, j], r.attn_s.at[j, k], r.attn_r.at[j, k], g.device(k))
            )
        r.aall[tensor, j] = r.attn[mine]
        if j == 0:
            ups[1].forward()

    outs.arrive()
    share = []
    for d in range(count):
        part = r.wo.at[d, core]
        share.append(send(part, part, r.share_s.at[d], r.share_r.at[d], near_dev))
    for part in downs:
        part.forward()
    for d in range(count):
        part = r.wo.at[d, 1 - core]
        await_bytes(part, r.share_r.at[d])
    whole_out = r.wo[...].reshape(768, 768)
    wop = [r.xmat.at[256 * t : 256 * (t + 1), 1536:2304] for t in range(3)] + [r.xmat.at[0:256, 2304:3072]]
    for t in range(TENSOR):
        wop[t][:192, :] = whole_out[192 * t : 192 * (t + 1)]
        wop[t][192:, :] = jnp.zeros((64, 768), BF)
    for t in range(TENSOR):

        @pl.when(tensor == t)
        def _():
            for h in range(3):
                r.woh[h, :64] = wop[t][64 * h : 64 * (h + 1), :]
                r.woh[h, 64:] = jnp.zeros((64, 768), BF)

    gain1, bias1, gain2, bias2 = (r.norms[k : k + 1] for k in range(4))
    hs = []
    for group_copies in copies:
        for copy in group_copies:
            copy.wait_recv()
    for own in (False, True):
        j = far if own else 1 - far
        q = 2 * j + core
        branch = nn(r.aall[0, j], wop[0][...])
        for t in range(1, TENSOR):
            branch = branch + nn(r.aall[t, j], wop[t][...])
        normal, scale = norm_rows(r.seq[q].astype(F32) + branch)
        hidden = normal * gain1 + bias1
        r.hb[q] = hidden.astype(BF)
        if own:
            r.n1[...] = normal
            r.s1[...] = jnp.broadcast_to(scale, (QUARTER, LANES))
            r.h1[...] = hidden
        hs.append(send(r.hb.at[q], r.hb.at[q], r.h_s.at[int(own)], r.h_r.at[int(own)], near_dev))
    for part in ups:
        part.arrive()

    theirs, ours = (tensor ^ 2, tensor ^ 3), (tensor, tensor ^ 1)
    halves = (0, 1)
    total = SumQuarters(r, g, 0)
    hs[0].wait_recv()
    for part in halves:
        feed_in(r, theirs, part)
    hs[1].wait_recv()
    for part in downs:
        part.arrive()
    for part in halves:
        kept, other_half = feed_out(r, theirs, part)
        total.near_out(0, part, other_half)
        r.kept[part] = kept
    for part in halves:
        total.far_out(part, total.near_in(0, part, r.kept[part]))
    for part in halves:
        feed_in(r, ours, part)
        kept, other_half = feed_out(r, ours, part)
        total.near_out(1, part, other_half)
        r.kept[part] = kept
    for part in heads + [outs] + ups + downs:
        part.close()
    for group_copies in copies:
        for copy in group_copies:
            copy.wait_send()
    for copy in hs + share + [tok_near, tok_far, tok_pass]:
        copy.wait_send()
    for k in (1, 2, 3):

        @pl.when(tensor < 3)
        def _():
            await_bytes(r.slabs.at[0], r.slab_s.at[k])

        @pl.when(tensor == 3)
        def _():
            await_bytes(r.wo_own.at[0], r.slab_s.at[k])

    back = SumQuarters(r, g, 1)
    spread = []

    def second_norm(part):
        at = pl.ds(part * HALF, HALF)
        ffn = total.far_in(part, total.near_in(1, part, r.kept[part]))
        n2, s2 = norm_rows(r.h1[at] + ffn)
        row = lax.broadcasted_iota(jnp.int32, (HALF, 1), 0) + (tensor * QUARTER + part * HALF)
        live = jnp.where(row < r.lengths[0], 1.0, 0.0)
        r.mixed[at] = (live * (n2 * gain2 + bias2)).astype(BF)
        dy = live * r.cotangent[at].astype(F32)
        gain_grad, bias_grad = jnp.sum(dy * n2, 0, keepdims=True), jnp.sum(dy, 0, keepdims=True)
        r.partial[2:3] = gain_grad if part == 0 else r.partial[2:3] + gain_grad
        r.partial[3:4] = bias_grad if part == 0 else r.partial[3:4] + bias_grad
        dr2 = norm_rows_back(n2, s2, dy * gain2)
        r.drf[at] = dr2
        r.dr2[tensor, at] = dr2.astype(BF)
        spread.append(Spread(g, r.dr2, r.dr2_s, r.dr2_r, part))

    def own_back(part):
        spread[part].arrive_near()
        kept, other_half = feed_back(r, ours, part)
        back.near_out(0, part, other_half)
        r.kept[part] = kept

    def their_back(part):
        spread[part].arrive_far()
        kept, other_half = feed_back(r, theirs, part)
        back.near_out(1, part, other_half)
        back.far_out(part, back.near_in(1, part, kept))

    works = core == 1

    @pl.when(works & (low == 1))
    def _():
        r.mrows[1] = r.attn_mom[0]

    @pl.when((core == 0) | (low == 0))
    def _():
        send(r.attn_mom.at[0], r.mrows.at[low], r.m_s, r.m_r.at[low], (high * 2 + core, far * 2 + 1))

    second_norm(0)
    own_back(0)
    second_norm(1)
    spread[0].pass_far()
    own_back(1)
    their_back(0)
    spread[1].pass_far()
    their_back(1)

    sums = {}
    for key in "dua":
        sums[key] = ReduceDp(
            *(getattr(r, name + key) for name in ("g", "low", "hs", "hb")),
            [getattr(r, name + key) for name in ("ls_", "lr_", "hs_", "hr_")],
            data,
            tensor,
        )
    spread = []

    def first_norm_back(part):
        at = pl.ds(part * HALF, HALF)
        dh = back.far_in(part, back.near_in(0, part, r.kept[part])) + r.drf[at]
        n1 = r.n1[at]
        gain_grad, bias_grad = jnp.sum(dh * n1, 0, keepdims=True), jnp.sum(dh, 0, keepdims=True)
        r.partial[0:1] = gain_grad if part == 0 else r.partial[0:1] + gain_grad
        r.partial[1:2] = bias_grad if part == 0 else r.partial[1:2] + bias_grad
        dr1 = norm_rows_back(n1, r.s1[at, :1], dh * gain1)
        r.drf[at] = dr1
        r.dr1[tensor, at] = dr1.astype(BF)
        spread.append(Spread(g, r.dr1, r.dr1_s, r.dr1_r, part))

    grad = tn(r.dr2[...].reshape(1024, 768), r.hid[...].reshape(1024, 768))
    r.gd[...] = grad.astype(BF).reshape(r.gd.shape)
    sums["d"].start()
    first_norm_back(0)
    grad = tn(r.hb[...].reshape(1024, 768), r.du[...].reshape(1024, 768))
    r.gu[...] = grad.astype(BF).reshape(r.gu.shape)
    sums["u"].start()
    first_norm_back(1)
    r.pbuf[tensor] = r.partial[...]
    parts = []
    for k in (1, 2, 3):
        parts.append(send(r.partial, r.pbuf.at[tensor], r.pt_s.at[k], r.pt_r.at[k], g.device(k)))
    sums["d"].forward(1, 2)
    spread[0].pass_far()
    sums["d"].forward(3)
    spread[1].pass_far()
    for part in halves:
        spread[part].arrive_near()
        spread[part].arrive_far()

    attend_back(r, g, 3)
    sums["u"].forward(1)
    for copy in parts:
        copy.wait()
    r.psum[...] = ((r.pbuf[0] + r.pbuf[1]) + r.pbuf[2]) + r.pbuf[3]
    r.qbuf[data] = r.psum[...]
    parts = []
    for k in range(1, count):
        to = (lax.rem(data + k, count), tensor)
        parts.append(send(r.psum, r.qbuf.at[data], r.pd_s.at[k], r.pd_r.at[k], to))
    attend_back(r, g, 2)
    sums["u"].forward(2, 3)
    moment = 0.5 * r.down_mom[...] + sums["d"].finish()
    r.mom_d[...] = moment
    r.xsd[...] = moment.astype(BF)
    attend_back(r, g, 1)
    moment = 0.5 * r.up_mom[...] + sums["u"].finish()
    r.mom_u[...] = moment
    r.xsu[...] = moment.astype(BF)
    own = r.xmat.at[here, cols(tensor)]

    @pl.when(far == 0)
    def _():
        r.xmat[here, cols(tensor)] = r.xsu[...]
        send(r.xsd, own, r.swap_s, r.swap_r, far_dev)

    @pl.when(far == 1)
    def _():
        r.xmat[here, cols(tensor)] = r.xsd[...]
        send(r.xsu, own, r.swap_s, r.swap_r, far_dev)

    blocks = [
        GatherDp(lambda d: r.xmat.at[rows_of(d), cols(tensor)], r.x_s.at[0], r.x_r.at[0], data, tensor),
        GatherDp(lambda d: r.xmat.at[rows_of(d), cols(tensor ^ 2)], r.x_s.at[1], r.x_r.at[1], data, tensor, True),
    ]

    def pass_on(b, d):
        @pl.when(core == 1)
        def _():
            slot = blocks[b].slot_of(d)
            send(slot, slot, r.j_s.at[b, d], r.j_r.at[b, d], near_dev)

    blocks[0].start()
    blocks[0].cross()
    attend_back(r, g, 0)
    await_bytes(r.xmat.at[here, cols(tensor ^ 2)], r.swap_r)
    blocks[1].start()
    blocks[1].cross()

    grad = tn(r.seq[...].reshape(1024, 768), r.hb[:, :, : 5 * LANES].reshape(1024, 5 * LANES)).astype(BF)

    def put(at, k):
        r.ga[:, :, at * LANES : (at + 1) * LANES] = grad[:, k * LANES : (k + 1) * LANES].reshape(count, rows, LANES)

    grad_out = tn(r.attn[...].reshape(1024, 256), r.dr1[...].reshape(1024, 768)).astype(BF)
    r.gos[core] = grad_out[:192].reshape(2, rows, 768)

    @pl.when(core == 0)
    def _():
        for at, k in enumerate((0, 1, 3, 2, 4)):
            put(at, k)

    @pl.when(works)
    def _():
        for at, k in zip((3, 4, 5, 6, 7), (0, 1, 3, 2, 4)):
            put(at, k)

    total = SumQuarters(r, g, 2)
    for part in halves:
        total.near_out(0, part, half_of(r.gp, tensor ^ 3, part)[...])
        total.near_out(1, part, half_of(r.gp, tensor ^ 1, part)[...])
    for part in halves:
        total.far_out(part, total.near_in(0, part, half_of(r.gp, tensor ^ 2, part)[...]))

    extra_in = r.gd.at[:, :, : 2 * LANES]

    @pl.when(core == 0)
    def _():
        wide, rest = r.ga.at[:, :, : 3 * LANES], r.ga.at[:, :, 3 * LANES : 5 * LANES]
        send(wide, wide, r.t_s.at[0], r.t_r.at[0], near_dev)
        send(rest, extra_in, r.t_s.at[1], r.t_r.at[1], near_dev)
        send(r.gos.at[0], r.gos.at[0], r.t_s.at[2], r.t_r.at[2], near_dev)

    def pass_far_rows(b):
        blocks[b].forward()
        for step in range(n):
            pass_on(b, blocks[b].source(step))

    pass_far_rows(0)
    for part in halves:
        at = pl.ds(part * HALF, HALF)
        value = total.near_in(1, part, half_of(r.gp, tensor, part)[...])
        r.input_grad[at] = total.far_in(part, value) + r.drf[at]

    @pl.when(works)
    def _():
        await_bytes(extra_in, r.t_r.at[1])
        first = lanes_of(768) < 64
        extra, own_last = [r.gd[:, :, k * LANES : (k + 1) * LANES].reshape(768, LANES).astype(F32) for k in range(2)], [
            r.ga[:, :, (6 + k) * LANES : (7 + k) * LANES].reshape(768, LANES).astype(F32) for k in range(2)
        ]
        tiles = (
            jnp.where(first, extra[0], half_roll(own_last[0])),
            jnp.where(first, half_roll(extra[0]), own_last[0]),
            jnp.where(first, extra[1], half_roll(own_last[1])),
        )
        for k, tile in enumerate(tiles):
            r.ga[:, :, (6 + k) * LANES : (7 + k) * LANES] = tile.astype(BF).reshape(count, rows, LANES)
        await_bytes(r.ga.at[:, :, : 3 * LANES], r.t_r.at[0])
        await_bytes(r.gos.at[0], r.t_r.at[2])

    pass_far_rows(1)

    @pl.when(works)
    def _():
        sums["a"].start()
        for k in range(2):
            send(r.gos.at[k, 1 - low], r.olow.at[k], r.o_s.at[0, k], r.o_r.at[k], (other, tensor))

    for b in range(2):
        for step in range(n):
            blocks[b].arrive(step)
            pass_on(b, blocks[b].partner_slot(step))
        blocks[b].close()

    sides = [
        GatherDp(lambda d, side=side: r.xa.at[rows_of(d // 2 * 2 + side)], r.f_s.at[side], r.f_r.at[side], data, tensor)
        for side in range(2)
    ]
    role = 2 * far + low
    homes = ((high * 2, 1), (high * 2 + 1, 1), (high * 2, 3))
    out_home = (high * 2 + 1, 3)

    @pl.when(works)
    def _():
        sums["a"].forward(1, 2, 3)

        for k in range(2):
            t = 2 * far + k
            await_bytes(r.olow.at[k], r.o_r.at[k])
            r.osend[k] = (r.gos[k, low].astype(F32) + r.olow[k].astype(F32)).astype(BF)
            for step in range(1, n):

                @pl.when(lax.rem(high + step, n) == t)
                def _():
                    send(r.osend.at[k], r.ohigh.at[step - 1], r.o_s.at[1, k], r.oh_r.at[step], (t * 2 + low, tensor))

        summed = sums["a"].finish()
        for m in range(3):
            for k in range(3):
                tile = summed[:, (m + 3 * k) * LANES : (m + 3 * k + 1) * LANES]
                r.asend[m, :, k * LANES : (k + 1) * LANES] = tile.astype(BF)

            @pl.when(role == m)
            def _():
                r.gin[low, far] = r.asend[m]

            @pl.when(role != m)
            def _():
                send(r.asend.at[m], r.gin.at[low, far], r.g_s.at[m], r.g_r.at[low, far], homes[m])

        for k in range(2):

            @pl.when(high == 2 * far + k)
            def _():
                whole = r.gos[k, low].astype(F32) + r.olow[k].astype(F32)
                for step in range(1, n):
                    await_bytes(r.ohigh.at[step - 1], r.oh_r.at[step])
                    whole = whole + r.ohigh[step - 1].astype(F32)
                r.oout[...] = whole.astype(BF)

                @pl.when(role == 3)
                def _():
                    r.gown[low] = r.oout[...]

                @pl.when(role != 3)
                def _():
                    send(r.oout, r.gown.at[low], r.o_s.at[2, 0], r.go_r.at[low], out_home)

        for side in range(2):
            row_block = rows_of(high * 2 + side)

            @pl.when(role == 3)
            def _():
                @pl.when((high // 2 == 0) | (side == 0))
                def _():
                    await_bytes(r.gown.at[side], r.go_r.at[side])

            @pl.when(role != 3)
            def _():
                first = lanes_of(rows) < 64
                for x in range(2):

                    @pl.when((low != side) | (far != x))
                    def _():
                        await_bytes(r.gin.at[side, x], r.g_r.at[side, x])

                    piece = [r.gin[side, x, :, k * LANES : (k + 1) * LANES] for k in range(3)]
                    turned, last = half_roll(piece[1].astype(F32)), piece[2].astype(F32)
                    base = 3 * LANES * x
                    r.gown[side, :, base : base + LANES] = piece[0]
                    r.gown[side, :, base + LANES : base + 2 * LANES] = jnp.where(first, last, turned).astype(BF)
                    r.gown[side, :, base + 2 * LANES : base + 3 * LANES] = jnp.where(first, turned, last).astype(BF)

            if side == 0:
                await_bytes(r.mrows.at[0], r.m_r.at[0])
            else:

                @pl.when(low == 0)
                def _():
                    await_bytes(r.mrows.at[1], r.m_r.at[1])

            r.xa[row_block] = (0.5 * r.mrows[side] + r.gown[side].astype(F32)).astype(BF)
            sides[side].start()

        @pl.when(low == 1)
        def _():
            r.gback[...] = r.gown[1]
            send(r.gown.at[0], r.gback, r.b_s.at[0], r.b_r, (other, tensor))

        @pl.when(low == 0)
        def _():
            send(r.gown.at[0], r.gback, r.b_s.at[0], r.b_r, (data, tensor ^ 1))
            send(r.gown.at[1], r.gback, r.b_s.at[1], r.b_r, (other, tensor ^ 1))

    for copy in parts:
        copy.wait()
    r.norm_grad[...] = sum((r.qbuf[d] for d in range(1, count)), r.qbuf[0])

    @pl.when(core == 0)
    def _():
        for b in range(2):
            for d in range(count):
                await_bytes(own, r.j_r.at[b, d])
        newton(r.xmat, r.du, r.hid, 1536, newton_scale(r.xmat), 1)
        newton(r.xmat, r.du, r.hid, 3072, None, NS_STEPS - 2)
        newton_gram(r.xmat, r.du, None)
        newton_rows(r.xmat, r.du, data, rows, r.lowd)

    for m, out in enumerate((r.o_u, r.o_d)):

        @pl.when((core == 0) & (far == m))
        def _():
            for k in (1, 2, 3):
                send(r.lowd.at[tensor ^ k], out, r.w_s.at[k], r.w_r.at[m], g.device(k))
            out[...] = r.lowd[tensor]

    owner = far * 2 + low

    @pl.when(core == 1)
    def _():
        for side in range(2):
            sides[side].forward(cross=False)
        for side in range(2):
            sides[side].close(cross=False)
        newton(r.xa, r.du, r.hid, 768, newton_scale(r.xa), 1)
        newton(r.xa, r.du, r.hid, 768, None, NS_STEPS - 2)
        newton_gram(r.xa, r.du, None)
        newton_rows(r.xa, r.du, other, rows, r.lowd.at[1:2])
        send(r.lowd.at[1], r.o_a, r.v_s.at[0], r.v_r, (other, owner))
        newton_rows(r.xa, r.du, data, rows, r.lowd.at[0:1])

    @pl.when((core == 1) & (low == 1))
    def _():
        r.o_a[...] = r.lowd[0]

    @pl.when((core == 1) & (low == 0))
    def _():
        send(r.lowd.at[0], r.o_a, r.v_s.at[1], r.v_r, (data, owner))

    @pl.when((core == 0) | (low == 0))
    def _():
        await_bytes(r.o_a, r.v_r)

    for m, out in enumerate((r.o_u, r.o_d)):

        @pl.when((core == 1) | (far != m))
        def _():
            await_bytes(out, r.w_r.at[m])

    @pl.when((core == 0) | (low == 0))
    def _():
        await_bytes(r.gback, r.b_r)

    r.mom_a[...] = 0.5 * r.attn_mom[0] + r.gback[...].astype(F32)

    await_bytes(r.xsd, r.swap_s)

    @pl.when((core == 0) | (low == 0))
    def _():
        await_bytes(r.mrows.at[0], r.m_s)

    @pl.when(core == 0)
    def _():
        await_bytes(r.ga.at[:, :, : 3 * LANES], r.t_s.at[0])
        await_bytes(extra_in, r.t_s.at[1])
        await_bytes(r.gos.at[0], r.t_s.at[2])

    @pl.when(works)
    def _():
        for k in range(2):
            await_bytes(r.olow.at[k], r.o_s.at[0, k])
            pl.when(high != 2 * far + k)(functools.partial(await_bytes, r.osend.at[k], r.o_s.at[1, k]))
        for m in range(3):
            pl.when(role != m)(functools.partial(await_bytes, r.asend.at[m], r.g_s.at[m]))
        pl.when((high // 2 == far) & (role != 3))(functools.partial(await_bytes, r.oout, r.o_s.at[2, 0]))
        await_bytes(r.gback, r.b_s.at[0])
        pl.when(low == 0)(functools.partial(await_bytes, r.gback, r.b_s.at[1]))

    @pl.when(core == 0)
    def _():
        for k in (1, 2, 3):
            await_bytes(r.o_u, r.w_s.at[k])

    @pl.when(core == 1)
    def _():
        for b in range(2):
            for d in range(count):
                await_bytes(own, r.j_s.at[b, d])
        await_bytes(r.o_a, r.v_s.at[0])

    @pl.when((core == 1) & (low == 0))
    def _():
        await_bytes(r.o_a, r.v_s.at[1])


def step_call(count, rows, ins):
    v = pltpu.VMEM
    n = count // 2
    one = pltpu.SemaphoreType.DMA
    outs = dict(
        mixed=shape(QUARTER, 768),
        input_grad=shape(QUARTER, 768, dtype=F32),
        mom_a=shape(rows, 768, dtype=F32),
        mom_u=shape(rows, 768, dtype=F32),
        mom_d=shape(rows, 768, dtype=F32),
        norm_grad=shape(4, 768, dtype=F32),
        o_u=shape(rows, 768),
        o_d=shape(rows, 768),
        o_a=shape(rows, 768),
    )
    per_head = (3, TENSOR, QUARTER, LANES)
    quarters = (TENSOR, QUARTER, 768)
    scratch = dict(
        slabs=v((TENSOR, rows, 256), BF),
        wo_own=v((2, rows // 2, 768), BF),
        seq=v(quarters, BF),
        slab_in=v((3, rows, 256), BF),
        wp=v((768, 5 * LANES), BF),
        wo=v((count, 2, rows // 2, 768), BF),
        wu=v((count, rows, 768), BF),
        wd=v((count, rows, 768), BF),
        woh=v((3, LANES, 768), BF),
        slab_s=dma(4),
        slab_r=dma(4),
        tok_s=dma(3),
        tok_r=dma(3),
        share_s=dma(count),
        share_r=dma(count),
        gather_s=dma(7, 9),
        gather_r=dma(7, 9),
        qf=v(per_head, BF),
        kf=v(per_head, BF),
        va=v(per_head, BF),
        qg=v(per_head, F32),
        kg=v(per_head, F32),
        af=v(per_head, F32),
        sb=v((3, TENSOR, QUARTER, QUARTER), BF),
        st=v((3, TENSOR, LANES, LANES), BF),
        state=v((3, LANES, LANES), F32),
        attn=v((TENSOR, QUARTER, 256), BF),
        aall=v((TENSOR, 2, QUARTER, 256), BF),
        attn_s=dma(2, 4),
        attn_r=dma(2, 4),
        hb=v(quarters, BF),
        n1=v((QUARTER, 768), F32),
        s1=v((QUARTER, LANES), F32),
        h1=v((QUARTER, 768), F32),
        hid=v(quarters, BF),
        gp=v(quarters, F32),
        du=v(quarters, BF),
        dr2=v(quarters, BF),
        drf=v((QUARTER, 768), F32),
        dr1=v(quarters, BF),
        kept=v((2, HALF, 768), F32),
        near_send=v((4, HALF, 768), BF),
        near_recv=v((4, HALF, 768), BF),
        far_send=v((2, HALF, 768), BF),
        far_recv=v((2, HALF, 768), BF),
        near_s=dma(12),
        near_r=dma(12),
        far_s=dma(6),
        far_r=dma(6),
        h_s=dma(2),
        h_r=dma(2),
        dr2_s=dma(6),
        dr2_r=dma(6),
        dr1_s=dma(6),
        dr1_r=dma(6),
        gu=v((count, rows, 768), BF),
        gd=v((count, rows, 768), BF),
        ga=v((count, rows, 9 * LANES), BF),
        gos=v((2, 2, rows, 768), BF),
        t_s=dma(3),
        t_r=dma(3),
        olow=v((2, rows, 768), BF),
        osend=v((2, rows, 768), BF),
        ohigh=v((n - 1, rows, 768), BF),
        o_s=dma(3, 2),
        o_r=dma(2),
        oh_r=dma(n),
        asend=v((3, rows, 3 * LANES), BF),
        gin=v((2, 2, rows, 3 * LANES), BF),
        g_s=dma(3),
        g_r=dma(2, 2),
        gown=v((2, rows, 768), BF),
        go_r=dma(2),
        gback=v((rows, 768), BF),
        b_s=dma(2),
        b_r=one,
        mrows=v((2, rows, 768), F32),
        m_s=one,
        m_r=dma(2),
        partial=v((4, 768), F32),
        pbuf=v((TENSOR, 4, 768), F32),
        psum=v((4, 768), F32),
        qbuf=v((count, 4, 768), F32),
        pt_s=dma(4),
        pt_r=dma(4),
        pd_s=dma(count),
        pd_r=dma(count),
        oout=v((rows, 768), BF),
        xsd=v((rows, 768), BF),
        xsu=v((rows, 768), BF),
        xmat=v((768, TENSOR * 768), BF),
        xa=v((768, 768), BF),
        swap_s=one,
        swap_r=one,
        x_s=dma(2, 9),
        x_r=dma(2, 9),
        f_s=dma(2, 8),
        f_r=dma(2, 8),
        j_s=dma(2, count),
        j_r=dma(2, count),
        w_s=dma(4),
        w_r=dma(2),
        v_s=dma(2),
        v_r=one,
    )
    for key in "dua":
        part = (rows, 9 * LANES if key == "a" else 768)
        for name, slots in (("low", n), ("hs", n - 1), ("hb", n - 1)):
            scratch[name + key] = v((slots,) + part, BF)
        for name in ("ls_", "lr_", "hs_", "hr_"):
            scratch[name + key] = dma(n)
    body = functools.partial(step_body, count, rows)
    return kernel_call(body, "layer_step", ins, outs, scratch, 0, ("lengths",))


def finish_body(r):
    keep = 1.0 - MUON_RATE * MUON_DECAY
    rate_a = MUON_RATE * 0.2 * math.sqrt(768)
    rate_ff = MUON_RATE * 0.2 * math.sqrt(TENSOR * 768)
    r.attn_new[0] = r.attn_w[0] * keep - rate_a * r.o_a[...].astype(F32)
    r.up_new[...] = r.up_w[...] * keep - rate_ff * r.o_u[...].astype(F32)
    r.down_new[...] = r.down_w[...] * keep - rate_ff * r.o_d[...].astype(F32)
    r.attn_moment[0] = r.mom_a[...]
    r.up_moment[...] = r.mom_u[...]
    r.down_moment[...] = r.mom_d[...]
    r.mixed_out[...] = r.mixed[...]
    r.input_grad_out[...] = r.input_grad[...]
    grad = r.norm_grad[...]
    moment1 = 0.5 * r.norm_m1[...] + 0.5 * grad
    moment2 = 0.95 * r.norm_m2[...] + 0.05 * grad * grad
    first_hat = moment1 / (1.0 - 0.5**STEP)
    second_hat = moment2 / (1.0 - 0.95**STEP)
    r.norm_moment1[...] = moment1
    r.norm_moment2[...] = moment2
    r.norm_new[...] = r.norms[...] - ADAM_RATE * first_hat / (jnp.sqrt(second_hat) + 1e-08)


def finish_call(ins):
    rows = ins["up_w"].shape[0]
    block = shape(rows, 768, dtype=F32)
    small = shape(4, 768, dtype=F32)
    outs = dict(
        mixed_out=shape(QUARTER, 768),
        input_grad_out=shape(QUARTER, 768, dtype=F32),
        attn_new=shape(1, rows, 768, dtype=F32),
        attn_moment=shape(1, rows, 768, dtype=F32),
        up_new=block,
        up_moment=block,
        down_new=block,
        down_moment=block,
        norm_moment1=small,
        norm_moment2=small,
        norm_new=small,
    )
    return kernel_call(finish_body, "finish", ins, outs, {}, None)


def step_on_device(
    tokens,
    cotangent,
    lengths,
    attn_w,
    up_w,
    down_w,
    norm_params,
    attn_mom,
    up_mom,
    down_mom,
    norm_m1,
    norm_m2,
):
    count = lax.axis_size("dp")
    rows = attn_w.shape[1]
    done = step_call(
        count,
        rows,
        dict(
            lengths=lengths,
            tokens=tokens,
            cotangent=cotangent,
            attn_w=attn_w,
            up_w=up_w,
            down_w=down_w.T,
            norms=norm_params,
            attn_mom=attn_mom,
            up_mom=up_mom,
            down_mom=down_mom.T,
        ),
    )
    last = finish_call(
        dict(
            attn_w=attn_w,
            up_w=up_w,
            down_w=down_w.T,
            norms=norm_params,
            norm_m1=norm_m1,
            norm_m2=norm_m2,
            **done,
        )
    )
    return (
        last["mixed_out"],
        last["input_grad_out"],
        last["attn_new"],
        last["attn_moment"],
        last["up_new"],
        last["up_moment"],
        last["down_new"].T,
        last["down_moment"].T,
        last["norm_moment1"],
        last["norm_moment2"],
        last["norm_new"],
    )


def solution(mesh):
    placed = (
        P(("dp", "tensor"), None),
        P(("dp", "tensor"), None),
        P("dp"),
        P("tensor", "dp", None),
        P("dp", "tensor"),
        P("tensor", "dp"),
        P(),
        P("tensor", "dp", None),
        P("dp", "tensor"),
        P("tensor", "dp"),
        P(),
        P(),
    )
    whole_tiles = mesh.shape["dp"] == 8 and mesh.shape["tensor"] == TENSOR
    return jax.shard_map(
        step_on_device if whole_tiles else on_device,
        mesh=mesh,
        in_specs=placed,
        out_specs=(
            P(("dp", "tensor"), None),
            P(("dp", "tensor"), None),
            P("tensor", "dp", None),
            P("tensor", "dp", None),
            P("dp", "tensor"),
            P("dp", "tensor"),
            P("tensor", "dp"),
            P("tensor", "dp"),
            P(),
            P(),
            P(),
        ),
        check_vma=False,
    )
```

```python
import functools
import math
import types

import jax
import jax.numpy as jnp
from jax import lax
from jax.experimental import pallas as pl
from jax.experimental.pallas import tpu as pltpu
from jax.sharding import PartitionSpec as P

HEADS = 12
HDIM = 64
BLOCK = 64
NS_STEPS = 5
STEP = 10


NORM_EPS = 1e-05
NS_EPS = 1e-07
COEF_A = 3.4445
COEF_B = -4.775
COEF_C = 2.0315
MUON_RATE = 0.15
MUON_DECAY = 0.1
ADAM_RATE = 0.2


def cut_along(array, dim, size):
    lengths = array.shape
    pieces = array.reshape(*lengths[:dim], size, lengths[dim] // size, *lengths[dim + 1 :])
    return jnp.moveaxis(pieces, dim, 0)


def sum_at_owner(array, axis, dim):
    size = lax.axis_size(axis)
    pieces = lax.all_to_all(cut_along(array, dim, size), axis, 0, 0, tiled=True)
    return jnp.sum(pieces.astype(jnp.float32), axis=0)


def sent_together(arrays, axis, dim, along):
    widths = [a.shape[along] for a in arrays]
    both = jnp.concatenate(arrays, axis=along)
    whole = sum_at_owner(both, axis, dim)
    return tuple(jnp.split(whole, [sum(widths[:k]) for k in range(1, len(widths))], axis=along))


def partner(array, axis, bit):
    return lax.ppermute(array, axis, [(i, i ^ 1 << bit) for i in range(lax.axis_size(axis))])


def contract_rows(left, right):
    return lax.dot_general(
        left, right, (((0,), (0,)), ((), ())), preferred_element_type=jnp.float32
    )


def contract_cols(left, right):
    return lax.dot_general(
        left, right, (((1,), (1,)), ((), ())), preferred_element_type=jnp.float32
    )


def norm_forward(resid, gain, bias):
    center = resid - jnp.mean(resid, -1, keepdims=True)
    spread = jnp.mean(center * center, -1, keepdims=True)
    scale_inv = lax.rsqrt(spread + NORM_EPS)
    normal_rows = center * scale_inv
    return (normal_rows, scale_inv, normal_rows * gain + bias)


def norm_back(normal_rows, scale_inv, grad_normed):
    return scale_inv * (
        grad_normed
        - jnp.mean(grad_normed, -1, keepdims=True)
        - normal_rows * jnp.mean(grad_normed * normal_rows, -1, keepdims=True)
    )


def smooth_gate(values):
    return jax.nn.gelu(values, approximate=True)


def features(proj, cosine, sine, weight_rows):
    count = proj.shape[0]
    soft = jax.nn.softplus(proj).reshape(count, HEADS, HDIM)
    both = jnp.concatenate([soft * cosine[:, None, None], soft * sine[:, None, None]], -1)
    return both * weight_rows[:, None, None]


def features_back(grad_feat, proj, cosine, sine, weight_rows):
    count = proj.shape[0]
    grad_soft = (
        grad_feat[..., :HDIM] * cosine[:, None, None] + grad_feat[..., HDIM:] * sine[:, None, None]
    )
    grad_soft = grad_soft * weight_rows[:, None, None]
    slope = jax.nn.sigmoid(proj).reshape(count, HEADS, HDIM)
    return (grad_soft * slope).reshape(count, HEADS * HDIM).astype(jnp.bfloat16)


def blocked(array):
    return array.reshape(array.shape[0] // BLOCK, BLOCK, array.shape[1], array.shape[2])


def attend_forward(qblock, kblock, vblock, lower):
    scores = (
        jnp.einsum("nihf,njhf->nhij", qblock, kblock, preferred_element_type=jnp.float32) * lower
    )
    scores_low = scores.astype(jnp.bfloat16)
    pairs = jnp.einsum("njhf,njhd->nhfd", kblock, vblock, preferred_element_type=jnp.float32)
    state = jnp.cumsum(pairs, 0) - pairs
    state_low = state.astype(jnp.bfloat16)
    key_sum = jnp.sum(kblock.astype(jnp.float32), 1)
    zsum = jnp.cumsum(key_sum, 0) - key_sum
    numer = jnp.einsum("nhij,njhd->nihd", scores_low, vblock, preferred_element_type=jnp.float32)
    numer = numer + jnp.einsum(
        "nihf,nhfd->nihd", qblock, state_low, preferred_element_type=jnp.float32
    )
    denom = jnp.transpose(jnp.sum(scores, -1), (0, 2, 1))
    denom = denom + jnp.einsum(
        "nihf,nhf->nih", qblock.astype(jnp.float32), zsum, precision=lax.Precision.HIGHEST
    )
    return (scores_low, state_low, zsum, denom, numer / denom[..., None])


def attend_backward(
    qblock, kblock, vblock, lower, scores_low, state_low, zsum, denom, result, grad_out
):
    grad_numer = (grad_out / denom[..., None]).astype(jnp.bfloat16)
    grad_denom = -jnp.sum(grad_out * result, -1) / denom
    grad_scores = jnp.einsum(
        "nihd,njhd->nhij", grad_numer, vblock, preferred_element_type=jnp.float32
    )
    grad_scores = ((grad_scores + jnp.transpose(grad_denom, (0, 2, 1))[..., None]) * lower).astype(
        jnp.bfloat16
    )
    grad_state = jnp.einsum(
        "nihf,nihd->nhfd", qblock, grad_numer, preferred_element_type=jnp.float32
    )
    grad_pairs = (jnp.cumsum(grad_state[::-1], 0)[::-1] - grad_state).astype(jnp.bfloat16)
    grad_z = jnp.einsum(
        "nih,nihf->nhf", grad_denom, qblock.astype(jnp.float32), precision=lax.Precision.HIGHEST
    )
    grad_ksum = jnp.cumsum(grad_z[::-1], 0)[::-1] - grad_z
    grad_qf = jnp.einsum("nhij,njhf->nihf", grad_scores, kblock, preferred_element_type=jnp.float32)
    grad_qf = grad_qf + jnp.einsum(
        "nihd,nhfd->nihf", grad_numer, state_low, preferred_element_type=jnp.float32
    )
    grad_qf = grad_qf + grad_denom[..., None] * zsum[:, None]
    grad_kf = jnp.einsum("nhij,nihf->njhf", grad_scores, qblock, preferred_element_type=jnp.float32)
    grad_kf = grad_kf + jnp.einsum(
        "njhd,nhfd->njhf", vblock, grad_pairs, preferred_element_type=jnp.float32
    )
    grad_kf = grad_kf + grad_ksum[:, None]
    grad_val = jnp.einsum(
        "nhij,nihd->njhd", scores_low, grad_numer, preferred_element_type=jnp.float32
    )
    grad_val = grad_val + jnp.einsum(
        "njhf,nhfd->njhd", kblock, grad_pairs, preferred_element_type=jnp.float32
    )
    return (grad_qf, grad_kf, grad_val.astype(jnp.bfloat16))


def newton_update(iterate, gram):
    poly = (
        COEF_B * gram.astype(jnp.float32)
        + COEF_C * jnp.dot(gram, gram, preferred_element_type=jnp.float32)
    ).astype(jnp.bfloat16)
    return (
        COEF_A * iterate.astype(jnp.float32)
        + jnp.dot(poly, iterate, preferred_element_type=jnp.float32)
    ).astype(jnp.bfloat16)


def orthogonalize(iterate):
    for step in range(NS_STEPS):
        gram = jnp.dot(iterate, iterate.T, preferred_element_type=jnp.float32).astype(jnp.bfloat16)
        iterate = newton_update(iterate, gram)
    return iterate


def on_device(
    tokens,
    cotangent,
    lengths,
    attn_w,
    up_w,
    down_w,
    norm_params,
    attn_mom,
    up_mom,
    down_mom,
    norm_m1,
    norm_m2,
):
    tensor_index = lax.axis_index("tensor")
    data_index = lax.axis_index("dp")
    tensor_count = lax.axis_size("tensor")
    length = lengths[0]
    rows_here = tokens.shape[0]
    wa_rows, up_block, down_block = (
        lax.all_gather(attn_w.astype(jnp.bfloat16), "dp", axis=1, tiled=True),
        lax.all_gather(up_w.astype(jnp.bfloat16), "dp", axis=0, tiled=True),
        lax.all_gather(down_w.astype(jnp.bfloat16), "dp", axis=1, tiled=True),
    )
    w_all = lax.all_gather(wa_rows, "tensor", axis=0, tiled=True)
    w_query = w_all[0]
    w_key = w_all[1]
    w_value = w_all[2]
    w_out = w_all[3]
    sequence = lax.all_gather(tokens, "tensor", axis=0, tiled=True)
    count = sequence.shape[0]
    width = sequence.shape[1]
    blocks = count // BLOCK
    start_row = tensor_index * rows_here

    def mine(array):
        return lax.dynamic_slice_in_dim(array, start_row, rows_here, 0)

    where = jnp.arange(count)
    live = (where < length).astype(jnp.float32)
    place = jnp.minimum(where, length - 1).astype(jnp.float32)
    theta = 0.5 * math.pi * place / length.astype(jnp.float32)
    cosine = jnp.cos(theta)
    sine = jnp.sin(theta)
    every_row = jnp.ones((count,), jnp.float32)
    query = jnp.dot(sequence, w_query, preferred_element_type=jnp.float32)
    key_proj = jnp.dot(sequence, w_key, preferred_element_type=jnp.float32)
    value = jnp.dot(sequence, w_value, preferred_element_type=jnp.float32)
    qblock = blocked(features(query, cosine, sine, every_row).astype(jnp.bfloat16))
    kblock = blocked(features(key_proj, cosine, sine, live).astype(jnp.bfloat16))
    vblock = value.astype(jnp.bfloat16).reshape(blocks, BLOCK, HEADS, HDIM)
    lower = jnp.tril(jnp.ones((BLOCK, BLOCK), jnp.float32))
    scores_low, state_low, zsum, denom, result = attend_forward(qblock, kblock, vblock, lower)
    attn_low = result.reshape(count, width).astype(jnp.bfloat16)
    branch = jnp.dot(attn_low, w_out, preferred_element_type=jnp.float32)
    normal_one, scale_one, hidden_in = norm_forward(
        sequence.astype(jnp.float32) + branch, norm_params[0], norm_params[1]
    )
    hidden_low = hidden_in.astype(jnp.bfloat16)
    pre = jnp.dot(hidden_low, up_block, preferred_element_type=jnp.float32)
    act_low = smooth_gate(pre).astype(jnp.bfloat16)
    ffn_rows = lax.psum_scatter(
        jnp.dot(act_low, down_block, preferred_element_type=jnp.float32).astype(jnp.bfloat16),
        "tensor",
        scatter_dimension=0,
        tiled=True,
    ).astype(jnp.float32)
    live_rows = mine(live)
    normal_two, scale_two, normed = norm_forward(
        mine(hidden_in) + ffn_rows, norm_params[2], norm_params[3]
    )
    mixed = (live_rows[:, None] * normed).astype(jnp.bfloat16)
    grad_y = cotangent.astype(jnp.float32) * live_rows[:, None]
    grad_g2 = jnp.sum(grad_y * normal_two, 0)
    grad_b2 = jnp.sum(grad_y, 0)
    grad_r2 = norm_back(normal_two, scale_two, grad_y * norm_params[2])
    grad_r2_all = lax.all_gather(grad_r2.astype(jnp.bfloat16), "tensor", axis=0, tiled=True)
    grad_down = contract_rows(act_low, grad_r2_all)
    grad_act = contract_cols(grad_r2_all, down_block)
    gate_out, gate_pull = jax.vjp(smooth_gate, pre)
    grad_pre = gate_pull(grad_act)[0].astype(jnp.bfloat16)
    grad_up = contract_rows(hidden_low, grad_pre)
    grad_hidden = (
        lax.psum_scatter(
            contract_cols(grad_pre, up_block).astype(jnp.bfloat16),
            "tensor",
            scatter_dimension=0,
            tiled=True,
        ).astype(jnp.float32)
        + grad_r2
    )
    normal_one_rows = mine(normal_one)
    grad_g1 = jnp.sum(grad_hidden * normal_one_rows, 0)
    grad_b1 = jnp.sum(grad_hidden, 0)
    grad_r1 = norm_back(normal_one_rows, mine(scale_one), grad_hidden * norm_params[0])
    grad_branch = lax.all_gather(grad_r1.astype(jnp.bfloat16), "tensor", axis=0, tiled=True)
    grad_attn = contract_cols(grad_branch, w_out).reshape(blocks, BLOCK, HEADS, HDIM)
    grad_qf, grad_kf, grad_val = attend_backward(
        qblock, kblock, vblock, lower, scores_low, state_low, zsum, denom, result, grad_attn
    )
    grad_query = features_back(
        grad_qf.reshape(count, HEADS, 2 * HDIM), query, cosine, sine, every_row
    )
    grad_key = features_back(grad_kf.reshape(count, HEADS, 2 * HDIM), key_proj, cosine, sine, live)
    grad_value = grad_val.reshape(count, width)
    input_grad = (
        grad_r1
        + contract_cols(mine(grad_query), w_query)
        + contract_cols(mine(grad_key), w_key)
        + contract_cols(mine(grad_value), w_value)
    )
    left_rows = jnp.where(tensor_index == 3, attn_low, sequence)
    right_all = jnp.stack((grad_query, grad_key, grad_value, grad_branch))
    right_rows = lax.dynamic_index_in_dim(right_all, tensor_index, 0, keepdims=False)
    grad_owned = contract_rows(left_rows, right_rows)
    norm_partial = jnp.stack((grad_g1, grad_b1, grad_g2, grad_b2))
    grad_a, grad_u, grad_d = (
        *sent_together((grad_owned.astype(jnp.bfloat16), grad_up.astype(jnp.bfloat16)), "dp", 0, 1),
        sum_at_owner(grad_down.astype(jnp.bfloat16), "dp", 1),
    )
    moment_a = 0.5 * attn_mom[0] + grad_a
    moment_u = 0.5 * up_mom + grad_u
    moment_d = 0.5 * down_mom + grad_d
    owner_pick = jax.nn.one_hot(tensor_index, 4, dtype=jnp.float32)
    squares = jnp.concatenate(
        (
            owner_pick * jnp.sum(moment_a * moment_a),
            jnp.stack((jnp.sum(moment_u * moment_u), jnp.sum(moment_d * moment_d))),
        )
    )
    totals, norm_grad = lax.psum((squares, norm_partial), ("dp", "tensor"))
    size_a = jnp.sqrt(jnp.sum(totals[:4] * owner_pick))
    size_u = jnp.sqrt(totals[4])
    size_d = jnp.sqrt(totals[5])
    start_a = (moment_a / (size_a + NS_EPS)).astype(jnp.bfloat16)
    start_u = (moment_u / (size_u + NS_EPS)).astype(jnp.bfloat16)
    start_d = (moment_d.T / (size_d + NS_EPS)).astype(jnp.bfloat16)
    whole_a, cols_u, cols_d = (
        lax.all_gather(start_a, "dp", axis=0, tiled=True),
        lax.all_gather(start_u, "dp", axis=0, tiled=True),
        lax.all_gather(start_d, "dp", axis=0, tiled=True),
    )
    orth_a = orthogonalize(whole_a)
    is_even = tensor_index % 2 == 0
    whole_u, whole_d = (
        lax.all_gather(cols_u, "tensor", axis=1, tiled=True),
        lax.all_gather(cols_d, "tensor", axis=1, tiled=True),
    )
    orth_whole = orthogonalize(jnp.where(is_even, whole_u, whole_d))
    block_cols = cols_u.shape[1]
    own_block = lax.dynamic_slice_in_dim(orth_whole, tensor_index * block_cols, block_cols, 1)
    partner_block = lax.dynamic_slice_in_dim(
        orth_whole, jnp.bitwise_xor(tensor_index, 1) * block_cols, block_cols, 1
    )
    fetched = partner(partner_block, "tensor", 0)
    orth_u = jnp.where(is_even, own_block, fetched)
    orth_d = jnp.where(is_even, fetched, own_block)
    span = moment_a.shape[0]

    def take_rows(array):
        return lax.dynamic_slice_in_dim(array, data_index * span, span, 0).astype(jnp.float32)

    ff_whole = up_block.shape[1] * tensor_count
    keep = 1.0 - MUON_RATE * MUON_DECAY
    new_a = attn_w[0] * keep - MUON_RATE * 0.2 * math.sqrt(width) * take_rows(orth_a)
    scale_ff = 0.2 * math.sqrt(max(width, ff_whole))
    new_u = up_w * keep - MUON_RATE * scale_ff * take_rows(orth_u)
    new_d = down_w * keep - MUON_RATE * scale_ff * take_rows(orth_d).T
    norm_moment1 = 0.5 * norm_m1 + 0.5 * norm_grad
    norm_moment2 = 0.95 * norm_m2 + 0.05 * norm_grad * norm_grad
    first_hat = norm_moment1 / (1.0 - 0.5**STEP)
    second_hat = norm_moment2 / (1.0 - 0.95**STEP)
    norm_new = norm_params - ADAM_RATE * first_hat / (jnp.sqrt(second_hat) + 1e-08)
    return (
        mixed,
        input_grad,
        new_a[None],
        moment_a[None],
        new_u,
        moment_u,
        new_d,
        moment_d,
        norm_moment1,
        norm_moment2,
        norm_new,
    )


BF = jnp.bfloat16
F32 = jnp.float32
MESH = pl.DeviceIdType.MESH
TENSOR = 4
QUARTER = 256
LANES = 128
HALF = 128
HIGH = 4
VMEM_LIMIT = (63 << 20) + (640 << 10)
GELU_C = math.sqrt(2.0 / math.pi)
GELU_A = 0.044715


def nn(left, right):
    return jnp.dot(left, right, preferred_element_type=F32)


def nt(left, right):
    return lax.dot_general(left, right, (((1,), (1,)), ((), ())), preferred_element_type=F32)


def tn(left, right):
    return lax.dot_general(left, right, (((0,), (0,)), ((), ())), preferred_element_type=F32)


def lanes_of(rows, cols=LANES):
    return lax.broadcasted_iota(jnp.int32, (rows, cols), 1)


def half_roll(array):
    return pltpu.roll(array, LANES // 2, 1)


def place():
    data = lax.axis_index("dp")
    tensor = lax.axis_index("tensor")
    return data, tensor


def greet(devices):
    barrier = pltpu.get_barrier_semaphore()
    for device in devices:
        pl.semaphore_signal(barrier, inc=1, device_id=device, device_id_type=MESH)
    pl.semaphore_wait(barrier, len(devices))


def send(src, dst, send_sem, recv_sem, device):
    copy = pltpu.make_async_remote_copy(
        src_ref=src,
        dst_ref=dst,
        send_sem=send_sem,
        recv_sem=recv_sem,
        device_id=device,
        device_id_type=MESH,
    )
    copy.start()
    return copy


def kernel_call(body, name, ins, outs, scratch, collective, scalars=(), anywhere=()):
    in_names = list(ins)
    out_names = list(outs)
    scratch_names = list(scratch)

    def space_of(n):
        return pltpu.SMEM if n in scalars else pl.ANY if n in anywhere else pltpu.VMEM

    def kernel(*refs):
        body(types.SimpleNamespace(**dict(zip(in_names + out_names + scratch_names, refs))))

    results = pl.pallas_call(
        kernel,
        name=name,
        out_shape=[outs[n] for n in out_names],
        in_specs=[
            pl.BlockSpec(memory_space=space_of(n)) for n in in_names
        ],
        out_specs=[pl.BlockSpec(memory_space=space_of(n)) for n in out_names],
        scratch_shapes=[scratch[n] for n in scratch_names],
        compiler_params=pltpu.CompilerParams(
            collective_id=collective,
            has_side_effects=collective is not None,
            vmem_limit_bytes=VMEM_LIMIT,
        ),
    )(*[ins[n] for n in in_names])
    return dict(zip(out_names, results))


def shape(*dims, dtype=BF):
    return jax.ShapeDtypeStruct(dims, dtype)


def dma(*dims):
    return pltpu.SemaphoreType.DMA(dims)


def await_bytes(ref, sem):
    pltpu.make_async_copy(ref, ref, sem).wait()


class GatherDp:
    def __init__(self, slot_of, sends, recvs, data, tensor, detour=False):
        self.slot_of, self.sends, self.recvs, self.detour = slot_of, sends, recvs, detour
        self.data, self.tensor = data, tensor
        self.high, self.low = data // 2, data % 2
        self.partner = (self.high * 2 + 1 - self.low, tensor)
        self.relays = (self.high == 1) | (self.high == 2)
        first_end, last_end = self.high == 0, self.high == HIGH - 1
        self.order = (
            jnp.where(first_end, 3, 1),
            jnp.where(first_end | last_end, 2, 3),
            jnp.where(first_end, 1, jnp.where(last_end, 3, 2)),
        )

    def source(self, step):
        return lax.rem(self.high + HIGH - step, HIGH) * 2 + self.low

    def push(self, slot, at, to, there=None):
        send(slot, slot, self.sends.at[at], self.recvs.at[at if there is None else there], to)

    def start(self):
        mine = self.slot_of(self.data)
        for step, allowed in ((1, self.high != HIGH - 1), (2, None), (3, self.high != 0)):
            to = (lax.rem(self.high + step, HIGH) * 2 + self.low, self.tensor)
            if allowed is None:
                self.push(mine, step, to)
            else:
                pl.when(allowed)(functools.partial(self.push, mine, step, to))

    def cross(self):
        self.push(self.slot_of(self.data), 0, self.partner)

    def passes(self, step):
        skip = ((self.high == 1) & (step == 1)) | ((self.high == 2) & (step == 3))
        if self.detour:
            skip = skip | ((self.high == 0) & (step == 3)) | ((self.high == 3) & (step == 1))
        return jnp.logical_not(skip)

    def forward(self, cross=True):
        beside = ((self.high ^ 1) * 2 + self.low, self.tensor)
        for position, step in enumerate(self.order):
            slot = self.slot_of(self.source(step))
            await_bytes(slot, self.recvs.at[step])
            if position == HIGH - 2:
                there = jnp.where(self.high == 2, 3, 1)
                pl.when(self.relays)(functools.partial(self.push, slot, 7, beside, there))
            if cross:
                at = HIGH - 1 + step
                pl.when(self.passes(step))(functools.partial(self.push, slot, at, self.partner))
            if cross and position == 0:
                slot = self.slot_of(self.partner_slot(0))
                await_bytes(slot, self.recvs.at[0])
                there = jnp.where((self.high == 0) | (self.high == 2), 4, 6)
                go_on = functools.partial(self.push, slot, 8, beside, there)
                if self.detour:
                    go_on()
                else:
                    pl.when(jnp.logical_not(self.relays))(go_on)

    def partner_slot(self, step):
        return self.source(step) + 1 - 2 * self.low

    def arrive(self, *steps):
        for step in steps or range(HIGH):
            if step:
                await_bytes(self.slot_of(self.partner_slot(step)), self.recvs.at[HIGH - 1 + step])

    def close(self, cross=True):
        mine = self.slot_of(self.data)

        def sent(at, allowed):
            pl.when(allowed)(functools.partial(await_bytes, mine, self.sends.at[at]))

        if cross:
            await_bytes(mine, self.sends.at[0])
            for step in range(1, HIGH):
                sent(HIGH - 1 + step, self.passes(step))
            if self.detour:
                await_bytes(mine, self.sends.at[8])
            else:
                sent(8, jnp.logical_not(self.relays))
        sent(1, self.high != HIGH - 1)
        await_bytes(mine, self.sends.at[2])
        sent(3, self.high != 0)
        sent(7, self.relays)


def softplus_and_slope(x):
    small = jnp.exp(-jnp.abs(x))
    soft = jnp.maximum(x, 0.0) + jnp.log1p(small)
    slope = jnp.where(x >= 0.0, 1.0, small) / (1.0 + small)
    return soft, slope


def spread_weights(r, tiles):
    low = lanes_of(768) < 64
    for k in tiles:
        tile = r.wp[:, k * LANES : (k + 1) * LANES].astype(F32)
        turned = half_roll(tile)
        left, right = jnp.where(low, tile, turned), jnp.where(low, turned, tile)
        if k == 0:
            parts = {0: left, 1: right}
        elif k == 1:
            parts = {3: left, 4: right}
        elif k == 2:
            parts = {2: left, 5: right}
        elif k == 3:
            parts = {6: jnp.where(low, tile, 0.0), 7: jnp.where(low, turned, 0.0)}
        else:
            parts = {8: tile}
        for at, part in parts.items():
            r.xmat[:, at * LANES : (at + 1) * LANES] = part.astype(BF)


def project(r):
    lane = lanes_of(QUARTER)

    def step(q, carry):
        both = nn(r.seq[q], r.xmat[:, : 9 * LANES])
        table, table_live = r.gp[q, :, :LANES], r.gp[q, :, LANES : 2 * LANES]
        for h in range(3):
            soft, slope = softplus_and_slope(both[:, h * LANES : (h + 1) * LANES])
            r.qf[h, q] = (soft * table).astype(BF)
            r.qg[h, q] = slope * table
            soft, slope = softplus_and_slope(both[:, (3 + h) * LANES : (4 + h) * LANES])
            r.kf[h, q] = (soft * table_live).astype(BF)
            r.kg[h, q] = slope * table_live
            value = both[:, (6 + h) * LANES : (7 + h) * LANES]
            ones = jnp.where((lane == 64) | (lane == 65), 1.0, 0.0)
            r.va[h, q] = jnp.where(lane < 64, value, ones).astype(BF)
        return carry

    lax.fori_loop(0, TENSOR, step, 0)


def attend(r, q):
    heads = range(3)
    lane = lanes_of(QUARTER)
    keep = lanes_of(QUARTER, QUARTER) <= lax.broadcasted_iota(jnp.int32, (QUARTER, QUARTER), 0)
    scores = [jnp.where(keep, nt(r.qf[h, q], r.kf[h, q]), 0.0).astype(BF) for h in heads]
    total = [None] * 3
    if q > 0:
        states = [r.state[h].astype(BF) for h in heads]
        total = [nn(r.qf[h, q], states[h]) for h in heads]
        for h in heads:
            r.st[h, q] = states[h]
    if q < TENSOR - 1:
        pairs = [tn(r.kf[h, q], r.va[h, q]) for h in heads]
        for h in heads:
            r.state[h] = pairs[h] if q == 0 else r.state[h] + pairs[h]
    outs = []
    for h in heads:
        r.sb[h, q] = scores[h]
        part = nn(scores[h], r.va[h, q])
        outs.append(part if total[h] is None else total[h] + part)
    for h in heads:
        inverse = 1.0 / outs[h][:, 64:65]
        outs[h] = jnp.where(lane < 64, outs[h] * inverse, inverse)
        r.af[h, q] = outs[h]
    r.attn[q, :, :LANES] = jnp.where(lane < 64, outs[0], half_roll(outs[1])).astype(BF)
    r.attn[q, :, LANES:] = jnp.where(lane < 64, outs[2], 0.0).astype(BF)


def norm_rows(resid):
    center = resid - jnp.mean(resid, -1, keepdims=True)
    spread = jnp.mean(center * center, -1, keepdims=True)
    scale = lax.rsqrt(spread + NORM_EPS)
    return center * scale, scale


def norm_rows_back(normal, scale, grad):
    return scale * (
        grad
        - jnp.mean(grad, -1, keepdims=True)
        - normal * jnp.mean(grad * normal, -1, keepdims=True)
    )


class Group:
    def __init__(self):
        self.data, self.tensor = place()
        self.far, self.core = self.tensor // 2, self.tensor % 2

    def device(self, k):
        return (self.data, self.tensor ^ k)


def half_of(ref, q, part):
    return ref.at[q, pl.ds(part * HALF, HALF)]


class Spread:
    def __init__(self, g, buf, sends, recvs, part):
        self.g, self.buf, self.sends, self.recvs, self.part = g, buf, sends, recvs, part
        own = half_of(buf, g.tensor, part)
        self.far = self.push(own, 0, g.device(2))
        self.near = self.push(own, 1, g.device(1))

    def push(self, ref, k, device):
        k = 3 * self.part + k
        return send(ref, ref, self.sends.at[k], self.recvs.at[k], device)

    def arrive_near(self):
        self.near.wait_recv()

    def pass_far(self):
        self.far.wait_recv()
        self.passed = self.push(half_of(self.buf, self.g.tensor ^ 2, self.part), 2, self.g.device(1))

    def arrive_far(self):
        self.passed.wait_recv()
        for copy in (self.far, self.near, self.passed):
            copy.wait_send()


class SumQuarters:
    def __init__(self, r, g, slot):
        self.r, self.g, self.slot = r, g, slot
        self.near, self.far = {}, {}

    def near_out(self, j, part, value):
        r, k = self.r, 2 * j + part
        r.near_send[k] = value.astype(BF)
        at = 4 * self.slot + k
        self.near[j, part] = send(
            r.near_send.at[k], r.near_recv.at[k], r.near_s.at[at], r.near_r.at[at], self.g.device(1)
        )

    def near_in(self, j, part, value):
        self.near[j, part].wait_recv()
        return value + self.r.near_recv[2 * j + part].astype(F32)

    def far_out(self, part, value):
        r = self.r
        r.far_send[part] = value.astype(BF)
        at = 2 * self.slot + part
        self.far[part] = send(
            r.far_send.at[part], r.far_recv.at[part], r.far_s.at[at], r.far_r.at[at], self.g.device(2)
        )

    def far_in(self, part, value):
        self.far[part].wait_recv()
        value = value + self.r.far_recv[part].astype(F32)
        for copy in (self.far[part], self.near[0, part], self.near[1, part]):
            copy.wait_send()
        return value


def pair_of(ref, quarters, part):
    return jnp.concatenate([ref[q, pl.ds(part * HALF, HALF)] for q in quarters], axis=0)


def put_pair(ref, quarters, part, value):
    for k, q in enumerate(quarters):
        ref[q, pl.ds(part * HALF, HALF)] = value[k * HALF : (k + 1) * HALF]


def feed_in(r, quarters, part):
    pre = nn(pair_of(r.hb, quarters, part), r.wu[...].reshape(768, 768))
    inner = jnp.tanh(GELU_C * (pre + GELU_A * pre * pre * pre))
    half = 0.5 * (1.0 + inner)
    slope = half + 0.5 * pre * (1.0 - inner * inner) * (GELU_C * (1.0 + 3.0 * GELU_A * pre * pre))
    put_pair(r.gp, quarters, part, slope)
    put_pair(r.hid, quarters, part, (pre * half).astype(BF))


def feed_out(r, quarters, part):
    out = nt(pair_of(r.hid, quarters, part), r.wd[...].reshape(768, 768))
    return out[:HALF], out[HALF:]


def feed_back(r, quarters, part):
    grad_act = nn(pair_of(r.dr2, quarters, part), r.wd[...].reshape(768, 768))
    grad_pre = (grad_act * pair_of(r.gp, quarters, part)).astype(BF)
    put_pair(r.du, quarters, part, grad_pre)
    out = nt(grad_pre, r.wu[...].reshape(768, 768))
    return out[:HALF], out[HALF:]


def attend_back(r, g, q):
    heads = range(3)
    lane = lanes_of(QUARTER)
    keep = lanes_of(QUARTER, QUARTER) <= lax.broadcasted_iota(jnp.int32, (QUARTER, QUARTER), 0)
    grads = nt(r.dr1[q], r.woh[...].reshape(3 * LANES, 768))
    dnum = []
    for h in heads:
        grad, af = grads[:, h * LANES : (h + 1) * LANES], r.af[h, q]
        inverse = af[:, 64:65]
        dden = -jnp.sum(grad * af, -1, keepdims=True) * inverse
        dden_low = dden.astype(BF).astype(F32)
        extra = jnp.where(lane == 64, dden_low, jnp.where(lane == 65, dden - dden_low, 0.0))
        dnum.append(jnp.where(lane < 64, grad * inverse, extra).astype(BF))
    ds = [jnp.where(keep, nt(dnum[h], r.va[h, q]), 0.0).astype(BF) for h in heads]
    dv = [tn(r.sb[h, q], dnum[h]) for h in heads]
    dqf = [nn(ds[h], r.kf[h, q]) for h in heads]
    dkf = [tn(ds[h], r.qf[h, q]) for h in heads]
    if q > 0:
        dqf = [dqf[h] + nt(dnum[h], r.st[h, q]) for h in heads]
    if q < TENSOR - 1:
        dkv = [r.state[h].astype(BF) for h in heads]
        dkf = [dkf[h] + nt(r.va[h, q], dkv[h]) for h in heads]
        dv = [dv[h] + nn(r.kf[h, q], dkv[h]) for h in heads]
    if q > 0:
        pairs = [tn(r.qf[h, q], dnum[h]) for h in heads]
        for h in heads:
            r.state[h] = pairs[h] if q == TENSOR - 1 else r.state[h] + pairs[h]
    fold = {}
    for h in heads:
        back = dqf[h] * r.qg[h, q]
        fold[0, h] = back + half_roll(back)
        back = dkf[h] * r.kg[h, q]
        fold[1, h] = back + half_roll(back)
        fold[2, h] = dv[h]
    tiles = (
        jnp.where(lane < 64, fold[0, 0], fold[0, 1]),
        jnp.where(lane < 64, fold[1, 0], fold[1, 1]),
        jnp.where(lane < 64, fold[0, 2], fold[1, 2]),
        jnp.where(lane < 64, fold[2, 0], half_roll(fold[2, 1])),
        jnp.where(lane < 64, fold[2, 2], 0.0),
    )
    for k, tile in enumerate(tiles):
        r.hb[q, :, k * LANES : (k + 1) * LANES] = tile.astype(BF)


def back_to_input(r, q):
    r.gp[q] = nt(r.hb[q, :, : 5 * LANES], r.wp[...])


class ReduceDp:
    def __init__(self, src, low_buf, high_send, high_buf, merge_buf, sems, data, tensor):
        self.src, self.low_buf, self.high_send, self.high_buf = src, low_buf, high_send, high_buf
        self.merge_buf = merge_buf
        self.low_s, self.low_r, self.high_s, self.high_r = sems
        self.tensor = tensor
        self.high, self.low = data // 2, data % 2
        self.first_end, self.last_end = self.high == 0, self.high == HIGH - 1
        self.inner = (self.high == 1) | (self.high == 2)
        self.order = (
            jnp.where(self.first_end, 3, 1),
            jnp.where(self.inner, 3, 2),
            jnp.where(self.first_end, 1, jnp.where(self.last_end, 3, 2)),
        )

    def at(self, step):
        return lax.rem(self.high + step, HIGH)

    def start(self, *positions):
        partner = (self.high * 2 + 1 - self.low, self.tensor)
        for position in positions or range(HIGH):
            step = (self.order + (0,))[position]
            h = self.at(step)
            chunk = self.src.at[h * 2 + 1 - self.low]
            send(chunk, self.low_buf.at[h], self.low_s.at[step], self.low_r.at[step], partner)

    def pair(self, step):
        h = self.at(step)
        await_bytes(self.low_buf.at[h], self.low_r.at[step])
        return self.src[h * 2 + self.low].astype(F32) + self.low_buf[h].astype(F32)

    def forward(self, *positions):
        for position in positions:
            step = self.order[position]
            value = self.pair(step)
            chunk = self.high_send.at[step - 1]
            if position == HIGH - 2 and self.merge_buf is not None:
                pl.when(self.inner)(functools.partial(await_bytes, self.merge_buf, self.high_r.at[0]))
                value = value + jnp.where(self.inner, self.merge_buf[...].astype(F32), 0.0)
            self.high_send[step - 1] = value.astype(BF)

            def straight():
                to = (self.at(step) * 2 + self.low, self.tensor)
                send(chunk, self.high_buf.at[step - 1], self.high_s.at[step], self.high_r.at[step], to)

            def beside():
                to = ((self.high ^ 1) * 2 + self.low, self.tensor)
                send(chunk, self.merge_buf, self.high_s.at[step], self.high_r.at[0], to)

            if position == 0 and self.merge_buf is not None:
                pl.when(self.inner)(straight)
                pl.when(jnp.logical_not(self.inner))(beside)
            else:
                straight()

    def finish(self):
        total = self.pair(0)
        for step in range(1, HIGH):
            chunk = self.high_buf.at[step - 1]
            if self.merge_buf is None:
                await_bytes(chunk, self.high_r.at[step])
                total = total + self.high_buf[step - 1].astype(F32)
                continue
            merged = (self.last_end & (step == 3)) | (self.first_end & (step == 1))
            pl.when(jnp.logical_not(merged))(functools.partial(await_bytes, chunk, self.high_r.at[step]))
            total = total + jnp.where(merged, 0.0, self.high_buf[step - 1].astype(F32))
        for step in range(HIGH):
            await_bytes(self.low_buf.at[0], self.low_s.at[step])
            if step:
                await_bytes(self.high_buf.at[0], self.high_s.at[step])
        return total


EDGES = tuple(slice(k * 256, (k + 1) * 256) for k in range(3))
PAIRS = tuple((a, b) for a in range(3) for b in range(a, 3))


def first_gram(x, spans, acc, add):
    for k, (a, b) in enumerate(PAIRS):
        block = sum(nt(x[EDGES[a], at], x[EDGES[b], at]) for at in spans)
        for side in range(2):
            piece = block[:, side * LANES : (side + 1) * LANES]
            at = (k // 2, 2 * (k % 2) + side)
            acc[at] = acc[at] + piece if add else piece


def first_scale(acc, gram):
    def block_of(k):
        return jnp.concatenate([acc[k // 2, 2 * (k % 2) + side] for side in range(2)], axis=1)

    diagonal = lanes_of(256, 256) == lax.broadcasted_iota(jnp.int32, (256, 256), 0)
    trace = sum(jnp.where(diagonal, block_of(k), 0.0) for k, (a, b) in enumerate(PAIRS) if a == b)
    scale = 1.0 / (jnp.sqrt(jnp.sum(trace)) + NS_EPS)
    for k, (a, b) in enumerate(PAIRS):
        block = (block_of(k) * (scale * scale)).astype(BF)
        gram[a, :, EDGES[b]] = block
        if b > a:
            gram[b, :, EDGES[a]] = block.T
    return scale


def newton_gram(x, gram):
    for a, b in PAIRS:
        block = nt(x[EDGES[a], :], x[EDGES[b], :]).astype(BF)
        gram[a, :, EDGES[b]] = block
        if b > a:
            gram[b, :, EDGES[a]] = block.T


def newton_poly(gram, poly):
    for a, b in PAIRS:
        block = COEF_C * nt(gram[a], gram[b])
        block = (block + COEF_B * gram[a, :, EDGES[b]].astype(F32)).astype(BF)
        poly[a, :, EDGES[b]] = block
        if b > a:
            poly[b, :, EDGES[a]] = block.T


def newton_apply(x, poly, chunk, scale):
    def columns(c, inner):
        at = pl.ds(pl.multiple_of(c * chunk, chunk), chunk)
        old = x[:, at]
        new = COEF_A * old.astype(F32) + nn(poly[:3].reshape(768, 768), old)
        if scale is not None:
            new = scale * new
        x[:, at] = new.astype(BF)
        return inner

    lax.fori_loop(0, x.shape[1] // chunk, columns, 0)


def newton(x, gram, poly, chunk, steps):
    def step(k, carry):
        newton_gram(x, gram)
        newton_poly(gram, poly)
        newton_apply(x, poly, chunk, None)
        return carry

    lax.fori_loop(0, steps, step, 0)


def last_poly(gram, index, rows):
    own = newton_rows_gram(gram, index, rows)
    return (COEF_C * nn(own, gram[:3].reshape(768, 768)) + COEF_B * own.astype(F32)).astype(BF)


def last_rows(x, poly, here, at):
    return (COEF_A * x[here, at].astype(F32) + nn(poly, x[:, at])).astype(BF)


def newton_rows_gram(gram, index, rows):
    parts = []
    for k in range(rows // 32):
        row = index * rows + 32 * k
        parts.append(gram[row // 256, pl.ds(pl.multiple_of(lax.rem(row, 256), 32), 32), :])
    return jnp.concatenate(parts, axis=0)


LOADED = ("cotangent", "attn_mom", "up_mom", "down_mom")


def angles(r):
    rows = TENSOR * QUARTER
    length = r.lengths[0]
    where = lax.broadcasted_iota(jnp.int32, (rows, LANES), 0)
    theta = 0.5 * math.pi * jnp.minimum(where, length - 1).astype(F32) / length.astype(F32)
    table = jnp.where(lanes_of(rows) < 64, jnp.cos(theta), jnp.sin(theta))
    live = jnp.where(where < length, 1.0, 0.0)
    r.gp[:, :, :LANES] = table.reshape(TENSOR, QUARTER, LANES)
    r.gp[:, :, LANES : 2 * LANES] = (table * live).reshape(TENSOR, QUARTER, LANES)


def cut_heads(r, rows):
    low = lanes_of(rows) < 64
    tiles = [r.attn_w[0, :, k * LANES : (k + 1) * LANES] for k in range(6)]
    for pair in range(2):
        first, middle, last = tiles[3 * pair : 3 * pair + 3]
        turned, rest = half_roll(middle), half_roll(last)
        parts = [first, jnp.where(low, middle, 0.0), jnp.where(low, turned, rest), jnp.where(low, rest, 0.0)]
        for k, part in enumerate(parts):
            r.slabs[2 * pair + k // 2, :, (k % 2) * LANES : (k % 2 + 1) * LANES] = part.astype(BF)


def step_body(count, rows, r):
    g = Group()
    data, tensor, far, core = g.data, g.tensor, g.far, g.core
    high, low = data // 2, data % 2
    other = high * 2 + 1 - low
    n = count // 2
    half = rows // 2
    near_dev, far_dev = g.device(1), g.device(2)

    loads = {}
    for k, name in enumerate(LOADED):
        loads[name] = pltpu.make_async_copy(getattr(r, name + "_in"), getattr(r, name), r.load_sem.at[k])
        loads[name].start()
    stores = []

    def store(name):
        k = len(stores)
        stores.append(pltpu.make_async_copy(getattr(r, name), getattr(r, name + "_hbm"), r.store_sem.at[k]))
        stores[-1].start()

    cut_heads(r, rows)
    r.wo_own[...] = r.attn_w[0].astype(BF).reshape(2, half, 768)
    greet(
        [g.device(k) for k in (1, 2, 3)]
        + [(lax.rem(data + k, count), tensor) for k in range(1, count)]
        + [(other, tensor ^ 1), (other, tensor ^ 2)]
    )

    def rows_of(d):
        return pl.ds(pl.multiple_of(d * rows, rows), rows)

    def cols(t):
        return pl.ds(pl.multiple_of(t * 768, 768), 768)

    here, there = rows_of(data), rows_of(other)

    for k in (1, 2, 3):
        peer = tensor ^ k

        @pl.when(tensor < 3)
        def _():
            send(r.slabs.at[peer], r.slab_in.at[tensor], r.slab_s.at[k], r.slab_r.at[tensor], g.device(k))

        @pl.when(tensor == 3)
        def _():
            send(r.wo_own.at[peer % 2], r.wo.at[data, peer % 2], r.slab_s.at[k], r.slab_r.at[3], g.device(k))

    r.seq[tensor] = r.tokens[...]
    mine = r.seq.at[tensor]
    tok_near = send(mine, mine, r.tok_s.at[0], r.tok_r.at[0], near_dev)
    tok_far = send(mine, mine, r.tok_s.at[1], r.tok_r.at[1], far_dev)

    @pl.when(tensor < 3)
    def _():
        r.slab_in[tensor] = r.slabs[tensor]

    @pl.when(tensor == 3)
    def _():
        r.wo[data, core] = r.wo_own[core]

    r.wu[data] = r.up_w[...].astype(BF)
    r.wd[data] = r.down_w[...].astype(BF)

    def gather(slot_of, key, detour=False):
        return GatherDp(slot_of, r.gather_s.at[key], r.gather_r.at[key], data, tensor, detour)

    spans = ((0, 2), (2, 5))
    heads = [
        gather(lambda d, a=a, b=b: r.wp.at[rows_of(d), a * LANES : b * LANES], k, k == 1)
        for k, (a, b) in enumerate(spans)
    ]
    outs = gather(lambda d: r.wo.at[d, core], 2)
    ups = [gather(lambda d, k=k: r.wu.at[d, pl.ds(k * half, half)], 3 + k, k == 1) for k in range(2)]
    downs = [gather(lambda d, k=k: r.wd.at[d, pl.ds(k * half, half)], 5 + k, k == 1) for k in range(2)]
    first_half = lanes_of(rows) < 64

    def slab(m):
        @pl.when(tensor != m)
        def _():
            await_bytes(r.slab_in.at[m], r.slab_r.at[m])

        return r.slab_in[m, :, :LANES], r.slab_in[m, :, LANES:]

    query, query_last = slab(0)
    key, key_last = slab(1)
    r.wp[here, :LANES] = query
    r.wp[here, LANES : 2 * LANES] = key
    heads[0].start()
    heads[0].cross()
    both = jnp.where(first_half, query_last.astype(F32), half_roll(key_last.astype(F32)))
    r.wp[here, 2 * LANES : 3 * LANES] = both.astype(BF)
    value, value_last = slab(2)
    r.wp[here, 3 * LANES : 4 * LANES] = value
    r.wp[here, 4 * LANES :] = value_last
    heads[1].start()
    heads[1].cross()

    @pl.when(tensor != 3)
    def _():
        await_bytes(r.wo.at[data, core], r.slab_r.at[3])

    outs.start()
    outs.cross()
    angles(r)
    heads[0].forward()
    ups[0].start()
    tok_far.wait_recv()
    slot = r.seq.at[tensor ^ 2]
    tok_pass = send(slot, slot, r.tok_s.at[2], r.tok_r.at[2], near_dev)
    heads[1].forward()
    ups[1].start()
    for part in ups + downs:
        part.cross()
    outs.forward()
    downs[0].start()
    heads[0].arrive()
    spread_weights(r, (0, 1))
    heads[1].arrive()
    spread_weights(r, (2, 3, 4))
    tok_near.wait_recv()
    tok_pass.wait_recv()
    project(r)
    ups[0].forward()
    downs[1].start()

    copies = [[], []]
    for j in range(2):
        attend(r, 2 * j)
        attend(r, 2 * j + 1)
        mine, rest = 2 * j + core, 2 * j + 1 - core
        for k in (2, 1, 3):
            quarter = mine if k == 2 else rest
            copies[j].append(
                send(r.attn.at[quarter], r.aall.at[tensor, j], r.attn_s.at[j, k], r.attn_r.at[j, k], g.device(k))
            )
        r.aall[tensor, j] = r.attn[mine]
        if j == 0:
            ups[1].forward()

    outs.arrive()
    share = []
    for d in range(count):
        part = r.wo.at[d, core]
        share.append(send(part, part, r.share_s.at[d], r.share_r.at[d], near_dev))
    for part in downs:
        part.forward()
    for d in range(count):
        part = r.wo.at[d, 1 - core]
        await_bytes(part, r.share_r.at[d])
    whole_out = r.wo[...].reshape(768, 768)
    wop = [r.xmat.at[256 * t : 256 * (t + 1), 1536:2304] for t in range(3)] + [r.xmat.at[0:256, 2304:3072]]
    for t in range(TENSOR):
        wop[t][:192, :] = whole_out[192 * t : 192 * (t + 1)]
        wop[t][192:, :] = jnp.zeros((64, 768), BF)
    for t in range(TENSOR):

        @pl.when(tensor == t)
        def _():
            for h in range(3):
                r.woh[h, :64] = wop[t][64 * h : 64 * (h + 1), :]
                r.woh[h, 64:] = jnp.zeros((64, 768), BF)

    gain1, bias1, gain2, bias2 = (r.norms[k : k + 1] for k in range(4))
    hs = []
    for group_copies in copies:
        for copy in group_copies:
            copy.wait_recv()
    for own in (False, True):
        j = far if own else 1 - far
        q = 2 * j + core
        branch = nn(r.aall[0, j], wop[0][...])
        for t in range(1, TENSOR):
            branch = branch + nn(r.aall[t, j], wop[t][...])
        normal, scale = norm_rows(r.seq[q].astype(F32) + branch)
        hidden = normal * gain1 + bias1
        r.hb[q] = hidden.astype(BF)
        if own:
            r.n1[...] = normal
            r.s1[...] = jnp.broadcast_to(scale, (QUARTER, LANES))
            r.h1[...] = hidden
        hs.append(send(r.hb.at[q], r.hb.at[q], r.h_s.at[int(own)], r.h_r.at[int(own)], near_dev))
    for part in ups:
        part.arrive()

    theirs, ours = (tensor ^ 2, tensor ^ 3), (tensor, tensor ^ 1)
    halves = (0, 1)
    total = SumQuarters(r, g, 0)
    hs[0].wait_recv()
    for part in halves:
        feed_in(r, theirs, part)
    hs[1].wait_recv()
    for part in downs:
        part.arrive()
    for part in halves:
        kept, other_half = feed_out(r, theirs, part)
        total.near_out(0, part, other_half)
        r.kept[part] = kept
    for part in halves:
        total.far_out(part, total.near_in(0, part, r.kept[part]))
    for part in halves:
        feed_in(r, ours, part)
        kept, other_half = feed_out(r, ours, part)
        total.near_out(1, part, other_half)
        r.kept[part] = kept
    for part in heads + [outs] + ups + downs:
        part.close()
    for group_copies in copies:
        for copy in group_copies:
            copy.wait_send()
    for copy in hs + share + [tok_near, tok_far, tok_pass]:
        copy.wait_send()
    for k in (1, 2, 3):

        @pl.when(tensor < 3)
        def _():
            await_bytes(r.slabs.at[0], r.slab_s.at[k])

        @pl.when(tensor == 3)
        def _():
            await_bytes(r.wo_own.at[0], r.slab_s.at[k])

    back = SumQuarters(r, g, 1)
    spread = []

    def second_norm(part):
        at = pl.ds(part * HALF, HALF)
        ffn = total.far_in(part, total.near_in(1, part, r.kept[part]))
        n2, s2 = norm_rows(r.h1[at] + ffn)
        row = lax.broadcasted_iota(jnp.int32, (HALF, 1), 0) + (tensor * QUARTER + part * HALF)
        live = jnp.where(row < r.lengths[0], 1.0, 0.0)
        r.mixed[at] = (live * (n2 * gain2 + bias2)).astype(BF)
        dy = live * r.cotangent[at].astype(F32)
        gain_grad, bias_grad = jnp.sum(dy * n2, 0, keepdims=True), jnp.sum(dy, 0, keepdims=True)
        r.partial[2:3] = gain_grad if part == 0 else r.partial[2:3] + gain_grad
        r.partial[3:4] = bias_grad if part == 0 else r.partial[3:4] + bias_grad
        dr2 = norm_rows_back(n2, s2, dy * gain2)
        r.drf[at] = dr2
        r.dr2[tensor, at] = dr2.astype(BF)
        spread.append(Spread(g, r.dr2, r.dr2_s, r.dr2_r, part))

    def own_back(part):
        spread[part].arrive_near()
        kept, other_half = feed_back(r, ours, part)
        back.near_out(0, part, other_half)
        r.kept[part] = kept

    def their_back(part):
        spread[part].arrive_far()
        kept, other_half = feed_back(r, theirs, part)
        back.near_out(1, part, other_half)
        back.far_out(part, back.near_in(1, part, kept))

    for name in LOADED:
        loads[name].wait()

    works = core == 1

    @pl.when(works & (low == 1))
    def _():
        r.mrows[1] = r.attn_mom[0]

    @pl.when((core == 0) | (low == 0))
    def _():
        send(r.attn_mom.at[0], r.mrows.at[low], r.m_s, r.m_r.at[low], (high * 2 + core, far * 2 + 1))

    second_norm(0)
    own_back(0)
    second_norm(1)
    store("mixed")
    spread[0].pass_far()
    own_back(1)
    their_back(0)
    spread[1].pass_far()
    their_back(1)

    sums = {}
    for key in "dua":
        sums[key] = ReduceDp(
            *(getattr(r, name + key) for name in ("g", "low", "hs", "hb")),
            getattr(r, "mb" + key, None),
            [getattr(r, name + key) for name in ("ls_", "lr_", "hs_", "hr_")],
            data,
            tensor,
        )
    spread = []

    def first_norm_back(part):
        at = pl.ds(part * HALF, HALF)
        dh = back.far_in(part, back.near_in(0, part, r.kept[part])) + r.drf[at]
        n1 = r.n1[at]
        gain_grad, bias_grad = jnp.sum(dh * n1, 0, keepdims=True), jnp.sum(dh, 0, keepdims=True)
        r.partial[0:1] = gain_grad if part == 0 else r.partial[0:1] + gain_grad
        r.partial[1:2] = bias_grad if part == 0 else r.partial[1:2] + bias_grad
        dr1 = norm_rows_back(n1, r.s1[at, :1], dh * gain1)
        r.drf[at] = dr1
        r.dr1[tensor, at] = dr1.astype(BF)
        spread.append(Spread(g, r.dr1, r.dr1_s, r.dr1_r, part))

    grad = tn(r.dr2[...].reshape(1024, 768), r.hid[...].reshape(1024, 768))
    r.gd[...] = grad.astype(BF).reshape(r.gd.shape)
    sums["d"].start()
    first_norm_back(0)
    sums["d"].forward(0)
    grad = tn(r.hb[...].reshape(1024, 768), r.du[...].reshape(1024, 768))
    r.gu[...] = grad.astype(BF).reshape(r.gu.shape)
    sums["u"].start()
    sums["d"].forward(1)
    first_norm_back(1)
    r.pbuf[tensor] = r.partial[...]
    parts = []
    for k in (1, 2, 3):
        parts.append(send(r.partial, r.pbuf.at[tensor], r.pt_s.at[k], r.pt_r.at[k], g.device(k)))
    spread[0].pass_far()
    sums["d"].forward(2)
    spread[1].pass_far()
    for part in halves:
        spread[part].arrive_near()
        spread[part].arrive_far()

    sums["u"].forward(0)
    attend_back(r, g, 3)
    sums["u"].forward(1)
    for copy in parts:
        copy.wait()
    r.psum[...] = ((r.pbuf[0] + r.pbuf[1]) + r.pbuf[2]) + r.pbuf[3]
    r.qbuf[data] = r.psum[...]
    parts = []
    for k in range(1, count):
        to = (lax.rem(data + k, count), tensor)
        parts.append(send(r.psum, r.qbuf.at[data], r.pd_s.at[k], r.pd_r.at[k], to))
    attend_back(r, g, 2)
    sums["u"].forward(2)
    attend_back(r, g, 1)
    moment = 0.5 * r.down_mom[...] + sums["d"].finish()
    r.mom_d[...] = moment
    r.xsd[...] = moment.astype(BF)
    attend_back(r, g, 0)
    moment = 0.5 * r.up_mom[...] + sums["u"].finish()
    r.mom_u[...] = moment
    store("mom_d")
    store("mom_u")
    r.xsu[...] = moment.astype(BF)
    own = r.xmat.at[here, cols(tensor)]

    @pl.when(far == 0)
    def _():
        r.xmat[here, cols(tensor)] = r.xsu[...]
        send(r.xsd, own, r.swap_s, r.swap_r, far_dev)

    @pl.when(far == 1)
    def _():
        r.xmat[here, cols(tensor)] = r.xsd[...]
        send(r.xsu, own, r.swap_s, r.swap_r, far_dev)

    blocks = [
        GatherDp(lambda d: r.xmat.at[rows_of(d), cols(tensor)], r.x_s.at[0], r.x_r.at[0], data, tensor),
        GatherDp(lambda d: r.xmat.at[rows_of(d), cols(tensor ^ 2)], r.x_s.at[1], r.x_r.at[1], data, tensor, True),
    ]

    def pass_on(b, d):
        @pl.when(core == 1)
        def _():
            slot = blocks[b].slot_of(d)
            send(slot, slot, r.j_s.at[b, d], r.j_r.at[b, d], near_dev)

    blocks[0].start()
    blocks[0].cross()
    grad = tn(r.seq[...].reshape(1024, 768), r.hb[:, :, : 5 * LANES].reshape(1024, 5 * LANES)).astype(BF)

    def put(at, k):
        r.ga[:, :, at * LANES : (at + 1) * LANES] = grad[:, k * LANES : (k + 1) * LANES].reshape(count, rows, LANES)

    grad_out = tn(r.attn[...].reshape(1024, 256), r.dr1[...].reshape(1024, 768)).astype(BF)
    r.gos[core] = grad_out[:192].reshape(2, rows, 768)

    @pl.when(core == 0)
    def _():
        for at, k in enumerate((0, 1, 3, 2, 4)):
            put(at, k)

    @pl.when(works)
    def _():
        for at, k in zip((3, 4, 5, 6, 7), (0, 1, 3, 2, 4)):
            put(at, k)

    await_bytes(r.xmat.at[here, cols(tensor ^ 2)], r.swap_r)
    blocks[1].start()
    blocks[1].cross()

    def pass_far_rows(b):
        blocks[b].forward()
        for step in range(n):
            pass_on(b, blocks[b].source(step))

    pass_far_rows(0)

    for q in (3, 2, 1, 0):
        back_to_input(r, q)
    total = SumQuarters(r, g, 2)
    for part in halves:
        total.near_out(0, part, half_of(r.gp, tensor ^ 3, part)[...])
        total.near_out(1, part, half_of(r.gp, tensor ^ 1, part)[...])
    for part in halves:
        total.far_out(part, total.near_in(0, part, half_of(r.gp, tensor ^ 2, part)[...]))

    extra_in = r.gd.at[:, :, : 2 * LANES]

    @pl.when(core == 0)
    def _():
        wide, rest = r.ga.at[:, :, : 3 * LANES], r.ga.at[:, :, 3 * LANES : 5 * LANES]
        send(wide, wide, r.t_s.at[0], r.t_r.at[0], near_dev)
        send(rest, extra_in, r.t_s.at[1], r.t_r.at[1], near_dev)
        send(r.gos.at[0], r.gos.at[0], r.t_s.at[2], r.t_r.at[2], near_dev)

    @pl.when(works)
    def _():
        await_bytes(extra_in, r.t_r.at[1])
        first = lanes_of(768) < 64
        extra, own_last = [r.gd[:, :, k * LANES : (k + 1) * LANES].reshape(768, LANES).astype(F32) for k in range(2)], [
            r.ga[:, :, (6 + k) * LANES : (7 + k) * LANES].reshape(768, LANES).astype(F32) for k in range(2)
        ]
        tiles = (
            jnp.where(first, extra[0], half_roll(own_last[0])),
            jnp.where(first, half_roll(extra[0]), own_last[0]),
            jnp.where(first, extra[1], half_roll(own_last[1])),
        )
        for k, tile in enumerate(tiles):
            r.ga[:, :, (6 + k) * LANES : (7 + k) * LANES] = tile.astype(BF).reshape(count, rows, LANES)
        await_bytes(r.ga.at[:, :, : 3 * LANES], r.t_r.at[0])
        await_bytes(r.gos.at[0], r.t_r.at[2])

    @pl.when(works)
    def _():
        sums["a"].start(0)

    pass_far_rows(1)

    @pl.when(works)
    def _():
        sums["a"].start(1, 2, 3)
        for k in range(2):
            send(r.gos.at[k, 1 - low], r.olow.at[k], r.o_s.at[0, k], r.o_r.at[k], (other, tensor))

    for part in halves:
        at = pl.ds(part * HALF, HALF)
        value = total.near_in(1, part, half_of(r.gp, tensor, part)[...])
        r.input_grad[at] = total.far_in(part, value) + r.drf[at]
    store("input_grad")

    for b in range(2):
        for step in range(n):
            blocks[b].arrive(step)
            pass_on(b, blocks[b].partner_slot(step))
        blocks[b].close()

    sides = [
        GatherDp(lambda d, side=side: r.xa.at[rows_of(d // 2 * 2 + side)], r.f_s.at[side], r.f_r.at[side], data, tensor)
        for side in range(2)
    ]
    role = 2 * far + low
    homes = ((high * 2, 1), (high * 2 + 1, 1), (high * 2, 3))
    out_home = (high * 2 + 1, 3)

    @pl.when(works)
    def _():
        sums["a"].forward(0, 1, 2)

        for k in range(2):
            t = 2 * far + k
            await_bytes(r.olow.at[k], r.o_r.at[k])
            r.osend[k] = (r.gos[k, low].astype(F32) + r.olow[k].astype(F32)).astype(BF)
            for step in range(1, n):

                @pl.when(lax.rem(high + step, n) == t)
                def _():
                    send(r.osend.at[k], r.ohigh.at[step - 1], r.o_s.at[1, k], r.oh_r.at[step], (t * 2 + low, tensor))

        summed = sums["a"].finish()
        for m in range(3):
            for k in range(3):
                tile = summed[:, (m + 3 * k) * LANES : (m + 3 * k + 1) * LANES]
                r.asend[m, :, k * LANES : (k + 1) * LANES] = tile.astype(BF)

            @pl.when(role == m)
            def _():
                r.gin[low, far] = r.asend[m]

            @pl.when(role != m)
            def _():
                send(r.asend.at[m], r.gin.at[low, far], r.g_s.at[m], r.g_r.at[low, far], homes[m])

        for k in range(2):

            @pl.when(high == 2 * far + k)
            def _():
                whole = r.gos[k, low].astype(F32) + r.olow[k].astype(F32)
                for step in range(1, n):
                    await_bytes(r.ohigh.at[step - 1], r.oh_r.at[step])
                    whole = whole + r.ohigh[step - 1].astype(F32)
                r.oout[...] = whole.astype(BF)

                @pl.when(role == 3)
                def _():
                    r.gown[low] = r.oout[...]

                @pl.when(role != 3)
                def _():
                    send(r.oout, r.gown.at[low], r.o_s.at[2, 0], r.go_r.at[low], out_home)

        for side in range(2):
            row_block = rows_of(high * 2 + side)

            @pl.when(role == 3)
            def _():
                @pl.when((high // 2 == 0) | (side == 0))
                def _():
                    await_bytes(r.gown.at[side], r.go_r.at[side])

            @pl.when(role != 3)
            def _():
                first = lanes_of(rows) < 64
                for x in range(2):

                    @pl.when((low != side) | (far != x))
                    def _():
                        await_bytes(r.gin.at[side, x], r.g_r.at[side, x])

                    piece = [r.gin[side, x, :, k * LANES : (k + 1) * LANES] for k in range(3)]
                    turned, last = half_roll(piece[1].astype(F32)), piece[2].astype(F32)
                    base = 3 * LANES * x
                    r.gown[side, :, base : base + LANES] = piece[0]
                    r.gown[side, :, base + LANES : base + 2 * LANES] = jnp.where(first, last, turned).astype(BF)
                    r.gown[side, :, base + 2 * LANES : base + 3 * LANES] = jnp.where(first, turned, last).astype(BF)

            if side == 0:
                await_bytes(r.mrows.at[0], r.m_r.at[0])
            else:

                @pl.when(low == 0)
                def _():
                    await_bytes(r.mrows.at[1], r.m_r.at[1])

            r.xa[row_block] = (0.5 * r.mrows[side] + r.gown[side].astype(F32)).astype(BF)
            sides[side].start()

        @pl.when(low == 1)
        def _():
            r.gback[...] = r.gown[1]
            send(r.gown.at[0], r.gback, r.b_s.at[0], r.b_r, (other, tensor))

        @pl.when(low == 0)
        def _():
            send(r.gown.at[0], r.gback, r.b_s.at[0], r.b_r, (data, tensor ^ 1))
            send(r.gown.at[1], r.gback, r.b_s.at[1], r.b_r, (other, tensor ^ 1))

    for copy in parts:
        copy.wait()
    r.norm_grad[...] = sum((r.qbuf[d] for d in range(1, count)), r.qbuf[0])

    @pl.when(core == 0)
    def _():
        for b in range(2):
            for d in range(count):
                await_bytes(own, r.j_r.at[b, d])
            first_gram(r.xmat, [cols(tensor ^ (2 * b)), cols(tensor ^ (2 * b + 1))], r.kg, b > 0)
        scale = first_scale(r.kg, r.du)
        newton_poly(r.du, r.hid)
        newton_apply(r.xmat, r.hid, 1536, scale)
        newton(r.xmat, r.du, r.hid, 3072, NS_STEPS - 2)
        newton_gram(r.xmat, r.du)
        poly = last_poly(r.du, data, rows)
        for k in (2, 3, 1, 0):
            r.lowd[tensor ^ k] = last_rows(r.xmat, poly, here, cols(tensor ^ k))
            for m, out in enumerate((r.o_u, r.o_d)):

                @pl.when(far == m)
                def _():
                    if k:
                        send(r.lowd.at[tensor ^ k], out, r.w_s.at[k], r.w_r.at[m], g.device(k))
                    else:
                        out[...] = r.lowd[tensor]

    owner = far * 2 + low

    @pl.when(core == 1)
    def _():
        for side in range(2):
            sides[side].forward(cross=False)
        for side in range(2):
            sides[side].close(cross=False)
        whole = slice(0, 768)
        first_gram(r.xa, [whole], r.kg, False)
        scale = first_scale(r.kg, r.du)
        newton_poly(r.du, r.hid)
        newton_apply(r.xa, r.hid, 768, scale)
        newton(r.xa, r.du, r.hid, 768, NS_STEPS - 2)
        newton_gram(r.xa, r.du)
        r.lowd[1] = last_rows(r.xa, last_poly(r.du, other, rows), there, whole)
        send(r.lowd.at[1], r.o_a, r.v_s.at[0], r.v_r, (other, owner))
        r.lowd[0] = last_rows(r.xa, last_poly(r.du, data, rows), here, whole)

    @pl.when((core == 1) & (low == 1))
    def _():
        r.o_a[...] = r.lowd[0]

    @pl.when((core == 1) & (low == 0))
    def _():
        send(r.lowd.at[0], r.o_a, r.v_s.at[1], r.v_r, (data, owner))

    @pl.when((core == 0) | (low == 0))
    def _():
        await_bytes(r.o_a, r.v_r)

    for m, out in enumerate((r.o_u, r.o_d)):

        @pl.when((core == 1) | (far != m))
        def _():
            await_bytes(out, r.w_r.at[m])

    @pl.when((core == 0) | (low == 0))
    def _():
        await_bytes(r.gback, r.b_r)

    r.mom_a[...] = 0.5 * r.attn_mom[0] + r.gback[...].astype(F32)

    for copy in stores:
        copy.wait()
    await_bytes(r.xsd, r.swap_s)

    @pl.when((core == 0) | (low == 0))
    def _():
        await_bytes(r.mrows.at[0], r.m_s)

    @pl.when(core == 0)
    def _():
        await_bytes(r.ga.at[:, :, : 3 * LANES], r.t_s.at[0])
        await_bytes(extra_in, r.t_s.at[1])
        await_bytes(r.gos.at[0], r.t_s.at[2])

    @pl.when(works)
    def _():
        for k in range(2):
            await_bytes(r.olow.at[k], r.o_s.at[0, k])
            pl.when(high != 2 * far + k)(functools.partial(await_bytes, r.osend.at[k], r.o_s.at[1, k]))
        for m in range(3):
            pl.when(role != m)(functools.partial(await_bytes, r.asend.at[m], r.g_s.at[m]))
        pl.when((high // 2 == far) & (role != 3))(functools.partial(await_bytes, r.oout, r.o_s.at[2, 0]))
        await_bytes(r.gback, r.b_s.at[0])
        pl.when(low == 0)(functools.partial(await_bytes, r.gback, r.b_s.at[1]))

    @pl.when(core == 0)
    def _():
        for k in (1, 2, 3):
            await_bytes(r.o_u, r.w_s.at[k])

    @pl.when(core == 1)
    def _():
        for b in range(2):
            for d in range(count):
                await_bytes(own, r.j_s.at[b, d])
        await_bytes(r.o_a, r.v_s.at[0])

    @pl.when((core == 1) & (low == 0))
    def _():
        await_bytes(r.o_a, r.v_s.at[1])


def step_call(count, rows, ins):
    v = pltpu.VMEM
    n = count // 2
    one = pltpu.SemaphoreType.DMA
    outs = dict(
        mixed_hbm=shape(QUARTER, 768),
        input_grad_hbm=shape(QUARTER, 768, dtype=F32),
        mom_a=shape(rows, 768, dtype=F32),
        mom_u_hbm=shape(rows, 768, dtype=F32),
        mom_d_hbm=shape(rows, 768, dtype=F32),
        norm_grad=shape(4, 768, dtype=F32),
        o_u=shape(rows, 768),
        o_d=shape(rows, 768),
        o_a=shape(rows, 768),
    )
    per_head = (3, TENSOR, QUARTER, LANES)
    quarters = (TENSOR, QUARTER, 768)
    scratch = dict(
        cotangent=v((QUARTER, 768), BF),
        attn_mom=v((1, rows, 768), F32),
        up_mom=v((rows, 768), F32),
        down_mom=v((rows, 768), F32),
        mixed=v((QUARTER, 768), BF),
        input_grad=v((QUARTER, 768), F32),
        mom_u=v((rows, 768), F32),
        mom_d=v((rows, 768), F32),
        load_sem=dma(len(LOADED)),
        store_sem=dma(4),
        slabs=v((TENSOR, rows, 256), BF),
        wo_own=v((2, rows // 2, 768), BF),
        seq=v(quarters, BF),
        slab_in=v((3, rows, 256), BF),
        wp=v((768, 5 * LANES), BF),
        wo=v((count, 2, rows // 2, 768), BF),
        wu=v((count, rows, 768), BF),
        wd=v((count, rows, 768), BF),
        woh=v((3, LANES, 768), BF),
        slab_s=dma(4),
        slab_r=dma(4),
        tok_s=dma(3),
        tok_r=dma(3),
        share_s=dma(count),
        share_r=dma(count),
        gather_s=dma(7, 9),
        gather_r=dma(7, 9),
        qf=v(per_head, BF),
        kf=v(per_head, BF),
        va=v(per_head, BF),
        qg=v(per_head, F32),
        kg=v(per_head, F32),
        af=v(per_head, F32),
        sb=v((3, TENSOR, QUARTER, QUARTER), BF),
        st=v((3, TENSOR, LANES, LANES), BF),
        state=v((3, LANES, LANES), F32),
        attn=v((TENSOR, QUARTER, 256), BF),
        aall=v((TENSOR, 2, QUARTER, 256), BF),
        attn_s=dma(2, 4),
        attn_r=dma(2, 4),
        hb=v(quarters, BF),
        n1=v((QUARTER, 768), F32),
        s1=v((QUARTER, LANES), F32),
        h1=v((QUARTER, 768), F32),
        hid=v(quarters, BF),
        gp=v(quarters, F32),
        du=v(quarters, BF),
        dr2=v(quarters, BF),
        drf=v((QUARTER, 768), F32),
        dr1=v(quarters, BF),
        kept=v((2, HALF, 768), F32),
        near_send=v((4, HALF, 768), BF),
        near_recv=v((4, HALF, 768), BF),
        far_send=v((2, HALF, 768), BF),
        far_recv=v((2, HALF, 768), BF),
        near_s=dma(12),
        near_r=dma(12),
        far_s=dma(6),
        far_r=dma(6),
        h_s=dma(2),
        h_r=dma(2),
        dr2_s=dma(6),
        dr2_r=dma(6),
        dr1_s=dma(6),
        dr1_r=dma(6),
        gu=v((count, rows, 768), BF),
        gd=v((count, rows, 768), BF),
        ga=v((count, rows, 9 * LANES), BF),
        gos=v((2, 2, rows, 768), BF),
        t_s=dma(3),
        t_r=dma(3),
        olow=v((2, rows, 768), BF),
        osend=v((2, rows, 768), BF),
        ohigh=v((n - 1, rows, 768), BF),
        o_s=dma(3, 2),
        o_r=dma(2),
        oh_r=dma(n),
        asend=v((3, rows, 3 * LANES), BF),
        gin=v((2, 2, rows, 3 * LANES), BF),
        g_s=dma(3),
        g_r=dma(2, 2),
        gown=v((2, rows, 768), BF),
        go_r=dma(2),
        gback=v((rows, 768), BF),
        b_s=dma(2),
        b_r=one,
        mrows=v((2, rows, 768), F32),
        m_s=one,
        m_r=dma(2),
        partial=v((4, 768), F32),
        pbuf=v((TENSOR, 4, 768), F32),
        psum=v((4, 768), F32),
        qbuf=v((count, 4, 768), F32),
        pt_s=dma(4),
        pt_r=dma(4),
        pd_s=dma(count),
        pd_r=dma(count),
        oout=v((rows, 768), BF),
        xsd=v((rows, 768), BF),
        xsu=v((rows, 768), BF),
        xmat=v((768, TENSOR * 768), BF),
        xa=v((768, 768), BF),
        swap_s=one,
        swap_r=one,
        x_s=dma(2, 9),
        x_r=dma(2, 9),
        f_s=dma(2, 8),
        f_r=dma(2, 8),
        j_s=dma(2, count),
        j_r=dma(2, count),
        w_s=dma(4),
        w_r=dma(2),
        v_s=dma(2),
        v_r=one,
    )
    for key in "dua":
        part = (rows, 9 * LANES if key == "a" else 768)
        for name, slots in (("low", n), ("hs", n - 1), ("hb", n - 1)):
            scratch[name + key] = v((slots,) + part, BF)
        if key != "a":
            scratch["mb" + key] = v(part, BF)
        for name in ("ls_", "lr_", "hs_", "hr_"):
            scratch[name + key] = dma(n)
    body = functools.partial(step_body, count, rows)
    anywhere = [n + "_in" for n in LOADED] + [n for n in outs if n.endswith("_hbm")]
    return kernel_call(body, "layer_step", ins, outs, scratch, 0, ("lengths",), anywhere)


def finish_body(r):
    keep = 1.0 - MUON_RATE * MUON_DECAY
    rate_a = MUON_RATE * 0.2 * math.sqrt(768)
    rate_ff = MUON_RATE * 0.2 * math.sqrt(TENSOR * 768)
    r.attn_new[0] = r.attn_w[0] * keep - rate_a * r.o_a[...].astype(F32)
    r.up_new[...] = r.up_w[...] * keep - rate_ff * r.o_u[...].astype(F32)
    r.down_new[...] = r.down_w[...] * keep - rate_ff * r.o_d[...].astype(F32)
    r.attn_moment[0] = r.mom_a[...]
    r.up_moment[...] = r.mom_u[...]
    r.down_moment[...] = r.mom_d[...]
    r.mixed_out[...] = r.mixed[...]
    r.input_grad_out[...] = r.input_grad[...]
    grad = r.norm_grad[...]
    moment1 = 0.5 * r.norm_m1[...] + 0.5 * grad
    moment2 = 0.95 * r.norm_m2[...] + 0.05 * grad * grad
    first_hat = moment1 / (1.0 - 0.5**STEP)
    second_hat = moment2 / (1.0 - 0.95**STEP)
    r.norm_moment1[...] = moment1
    r.norm_moment2[...] = moment2
    r.norm_new[...] = r.norms[...] - ADAM_RATE * first_hat / (jnp.sqrt(second_hat) + 1e-08)


def finish_call(ins):
    rows = ins["up_w"].shape[0]
    block = shape(rows, 768, dtype=F32)
    small = shape(4, 768, dtype=F32)
    outs = dict(
        mixed_out=shape(QUARTER, 768),
        input_grad_out=shape(QUARTER, 768, dtype=F32),
        attn_new=shape(1, rows, 768, dtype=F32),
        attn_moment=shape(1, rows, 768, dtype=F32),
        up_new=block,
        up_moment=block,
        down_new=block,
        down_moment=block,
        norm_moment1=small,
        norm_moment2=small,
        norm_new=small,
    )
    return kernel_call(finish_body, "finish", ins, outs, {}, None)


def step_on_device(
    tokens,
    cotangent,
    lengths,
    attn_w,
    up_w,
    down_w,
    norm_params,
    attn_mom,
    up_mom,
    down_mom,
    norm_m1,
    norm_m2,
):
    count = lax.axis_size("dp")
    rows = attn_w.shape[1]
    done = step_call(
        count,
        rows,
        dict(
            lengths=lengths,
            tokens=tokens,
            cotangent_in=cotangent,
            attn_w=attn_w,
            up_w=up_w,
            down_w=down_w.T,
            norms=norm_params,
            attn_mom_in=attn_mom,
            up_mom_in=up_mom,
            down_mom_in=down_mom.T,
        ),
    )
    last = finish_call(
        dict(
            attn_w=attn_w,
            up_w=up_w,
            down_w=down_w.T,
            norms=norm_params,
            norm_m1=norm_m1,
            norm_m2=norm_m2,
            **{n.removesuffix("_hbm"): a for n, a in done.items()},
        )
    )
    return (
        last["mixed_out"],
        last["input_grad_out"],
        last["attn_new"],
        last["attn_moment"],
        last["up_new"],
        last["up_moment"],
        last["down_new"].T,
        last["down_moment"].T,
        last["norm_moment1"],
        last["norm_moment2"],
        last["norm_new"],
    )


def solution(mesh):
    placed = (
        P(("dp", "tensor"), None),
        P(("dp", "tensor"), None),
        P("dp"),
        P("tensor", "dp", None),
        P("dp", "tensor"),
        P("tensor", "dp"),
        P(),
        P("tensor", "dp", None),
        P("dp", "tensor"),
        P("tensor", "dp"),
        P(),
        P(),
    )
    whole_tiles = mesh.shape["dp"] == 8 and mesh.shape["tensor"] == TENSOR
    return jax.shard_map(
        step_on_device if whole_tiles else on_device,
        mesh=mesh,
        in_specs=placed,
        out_specs=(
            P(("dp", "tensor"), None),
            P(("dp", "tensor"), None),
            P("tensor", "dp", None),
            P("tensor", "dp", None),
            P("dp", "tensor"),
            P("dp", "tensor"),
            P("tensor", "dp"),
            P("tensor", "dp"),
            P(),
            P(),
            P(),
        ),
        check_vma=False,
    )
```

```python
import functools
import math
import types

import jax
import jax.numpy as jnp
from jax import lax
from jax.experimental import pallas as pl
from jax.experimental.pallas import tpu as pltpu
from jax.sharding import PartitionSpec as P

HEADS = 12
HDIM = 64
BLOCK = 64
NS_STEPS = 5
STEP = 10


NORM_EPS = 1e-05
NS_EPS = 1e-07
COEF_A = 3.4445
COEF_B = -4.775
COEF_C = 2.0315
MUON_RATE = 0.15
MUON_DECAY = 0.1
ADAM_RATE = 0.2


def cut_along(array, dim, size):
    lengths = array.shape
    pieces = array.reshape(*lengths[:dim], size, lengths[dim] // size, *lengths[dim + 1 :])
    return jnp.moveaxis(pieces, dim, 0)


def sum_at_owner(array, axis, dim):
    size = lax.axis_size(axis)
    pieces = lax.all_to_all(cut_along(array, dim, size), axis, 0, 0, tiled=True)
    return jnp.sum(pieces.astype(jnp.float32), axis=0)


def sent_together(arrays, axis, dim, along):
    widths = [a.shape[along] for a in arrays]
    both = jnp.concatenate(arrays, axis=along)
    whole = sum_at_owner(both, axis, dim)
    return tuple(jnp.split(whole, [sum(widths[:k]) for k in range(1, len(widths))], axis=along))


def partner(array, axis, bit):
    return lax.ppermute(array, axis, [(i, i ^ 1 << bit) for i in range(lax.axis_size(axis))])


def contract_rows(left, right):
    return lax.dot_general(
        left, right, (((0,), (0,)), ((), ())), preferred_element_type=jnp.float32
    )


def contract_cols(left, right):
    return lax.dot_general(
        left, right, (((1,), (1,)), ((), ())), preferred_element_type=jnp.float32
    )


def norm_forward(resid, gain, bias):
    center = resid - jnp.mean(resid, -1, keepdims=True)
    spread = jnp.mean(center * center, -1, keepdims=True)
    scale_inv = lax.rsqrt(spread + NORM_EPS)
    normal_rows = center * scale_inv
    return (normal_rows, scale_inv, normal_rows * gain + bias)


def norm_back(normal_rows, scale_inv, grad_normed):
    return scale_inv * (
        grad_normed
        - jnp.mean(grad_normed, -1, keepdims=True)
        - normal_rows * jnp.mean(grad_normed * normal_rows, -1, keepdims=True)
    )


def smooth_gate(values):
    return jax.nn.gelu(values, approximate=True)


def features(proj, cosine, sine, weight_rows):
    count = proj.shape[0]
    soft = jax.nn.softplus(proj).reshape(count, HEADS, HDIM)
    both = jnp.concatenate([soft * cosine[:, None, None], soft * sine[:, None, None]], -1)
    return both * weight_rows[:, None, None]


def features_back(grad_feat, proj, cosine, sine, weight_rows):
    count = proj.shape[0]
    grad_soft = (
        grad_feat[..., :HDIM] * cosine[:, None, None] + grad_feat[..., HDIM:] * sine[:, None, None]
    )
    grad_soft = grad_soft * weight_rows[:, None, None]
    slope = jax.nn.sigmoid(proj).reshape(count, HEADS, HDIM)
    return (grad_soft * slope).reshape(count, HEADS * HDIM).astype(jnp.bfloat16)


def blocked(array):
    return array.reshape(array.shape[0] // BLOCK, BLOCK, array.shape[1], array.shape[2])


def attend_forward(qblock, kblock, vblock, lower):
    scores = (
        jnp.einsum("nihf,njhf->nhij", qblock, kblock, preferred_element_type=jnp.float32) * lower
    )
    scores_low = scores.astype(jnp.bfloat16)
    pairs = jnp.einsum("njhf,njhd->nhfd", kblock, vblock, preferred_element_type=jnp.float32)
    state = jnp.cumsum(pairs, 0) - pairs
    state_low = state.astype(jnp.bfloat16)
    key_sum = jnp.sum(kblock.astype(jnp.float32), 1)
    zsum = jnp.cumsum(key_sum, 0) - key_sum
    numer = jnp.einsum("nhij,njhd->nihd", scores_low, vblock, preferred_element_type=jnp.float32)
    numer = numer + jnp.einsum(
        "nihf,nhfd->nihd", qblock, state_low, preferred_element_type=jnp.float32
    )
    denom = jnp.transpose(jnp.sum(scores, -1), (0, 2, 1))
    denom = denom + jnp.einsum(
        "nihf,nhf->nih", qblock.astype(jnp.float32), zsum, precision=lax.Precision.HIGHEST
    )
    return (scores_low, state_low, zsum, denom, numer / denom[..., None])


def attend_backward(
    qblock, kblock, vblock, lower, scores_low, state_low, zsum, denom, result, grad_out
):
    grad_numer = (grad_out / denom[..., None]).astype(jnp.bfloat16)
    grad_denom = -jnp.sum(grad_out * result, -1) / denom
    grad_scores = jnp.einsum(
        "nihd,njhd->nhij", grad_numer, vblock, preferred_element_type=jnp.float32
    )
    grad_scores = ((grad_scores + jnp.transpose(grad_denom, (0, 2, 1))[..., None]) * lower).astype(
        jnp.bfloat16
    )
    grad_state = jnp.einsum(
        "nihf,nihd->nhfd", qblock, grad_numer, preferred_element_type=jnp.float32
    )
    grad_pairs = (jnp.cumsum(grad_state[::-1], 0)[::-1] - grad_state).astype(jnp.bfloat16)
    grad_z = jnp.einsum(
        "nih,nihf->nhf", grad_denom, qblock.astype(jnp.float32), precision=lax.Precision.HIGHEST
    )
    grad_ksum = jnp.cumsum(grad_z[::-1], 0)[::-1] - grad_z
    grad_qf = jnp.einsum("nhij,njhf->nihf", grad_scores, kblock, preferred_element_type=jnp.float32)
    grad_qf = grad_qf + jnp.einsum(
        "nihd,nhfd->nihf", grad_numer, state_low, preferred_element_type=jnp.float32
    )
    grad_qf = grad_qf + grad_denom[..., None] * zsum[:, None]
    grad_kf = jnp.einsum("nhij,nihf->njhf", grad_scores, qblock, preferred_element_type=jnp.float32)
    grad_kf = grad_kf + jnp.einsum(
        "njhd,nhfd->njhf", vblock, grad_pairs, preferred_element_type=jnp.float32
    )
    grad_kf = grad_kf + grad_ksum[:, None]
    grad_val = jnp.einsum(
        "nhij,nihd->njhd", scores_low, grad_numer, preferred_element_type=jnp.float32
    )
    grad_val = grad_val + jnp.einsum(
        "njhf,nhfd->njhd", kblock, grad_pairs, preferred_element_type=jnp.float32
    )
    return (grad_qf, grad_kf, grad_val.astype(jnp.bfloat16))


def newton_update(iterate, gram):
    poly = (
        COEF_B * gram.astype(jnp.float32)
        + COEF_C * jnp.dot(gram, gram, preferred_element_type=jnp.float32)
    ).astype(jnp.bfloat16)
    return (
        COEF_A * iterate.astype(jnp.float32)
        + jnp.dot(poly, iterate, preferred_element_type=jnp.float32)
    ).astype(jnp.bfloat16)


def orthogonalize(iterate):
    for step in range(NS_STEPS):
        gram = jnp.dot(iterate, iterate.T, preferred_element_type=jnp.float32).astype(jnp.bfloat16)
        iterate = newton_update(iterate, gram)
    return iterate


def on_device(
    tokens,
    cotangent,
    lengths,
    attn_w,
    up_w,
    down_w,
    norm_params,
    attn_mom,
    up_mom,
    down_mom,
    norm_m1,
    norm_m2,
):
    tensor_index = lax.axis_index("tensor")
    data_index = lax.axis_index("dp")
    tensor_count = lax.axis_size("tensor")
    length = lengths[0]
    rows_here = tokens.shape[0]
    wa_rows, up_block, down_block = (
        lax.all_gather(attn_w.astype(jnp.bfloat16), "dp", axis=1, tiled=True),
        lax.all_gather(up_w.astype(jnp.bfloat16), "dp", axis=0, tiled=True),
        lax.all_gather(down_w.astype(jnp.bfloat16), "dp", axis=1, tiled=True),
    )
    w_all = lax.all_gather(wa_rows, "tensor", axis=0, tiled=True)
    w_query = w_all[0]
    w_key = w_all[1]
    w_value = w_all[2]
    w_out = w_all[3]
    sequence = lax.all_gather(tokens, "tensor", axis=0, tiled=True)
    count = sequence.shape[0]
    width = sequence.shape[1]
    blocks = count // BLOCK
    start_row = tensor_index * rows_here

    def mine(array):
        return lax.dynamic_slice_in_dim(array, start_row, rows_here, 0)

    where = jnp.arange(count)
    live = (where < length).astype(jnp.float32)
    place = jnp.minimum(where, length - 1).astype(jnp.float32)
    theta = 0.5 * math.pi * place / length.astype(jnp.float32)
    cosine = jnp.cos(theta)
    sine = jnp.sin(theta)
    every_row = jnp.ones((count,), jnp.float32)
    query = jnp.dot(sequence, w_query, preferred_element_type=jnp.float32)
    key_proj = jnp.dot(sequence, w_key, preferred_element_type=jnp.float32)
    value = jnp.dot(sequence, w_value, preferred_element_type=jnp.float32)
    qblock = blocked(features(query, cosine, sine, every_row).astype(jnp.bfloat16))
    kblock = blocked(features(key_proj, cosine, sine, live).astype(jnp.bfloat16))
    vblock = value.astype(jnp.bfloat16).reshape(blocks, BLOCK, HEADS, HDIM)
    lower = jnp.tril(jnp.ones((BLOCK, BLOCK), jnp.float32))
    scores_low, state_low, zsum, denom, result = attend_forward(qblock, kblock, vblock, lower)
    attn_low = result.reshape(count, width).astype(jnp.bfloat16)
    branch = jnp.dot(attn_low, w_out, preferred_element_type=jnp.float32)
    normal_one, scale_one, hidden_in = norm_forward(
        sequence.astype(jnp.float32) + branch, norm_params[0], norm_params[1]
    )
    hidden_low = hidden_in.astype(jnp.bfloat16)
    pre = jnp.dot(hidden_low, up_block, preferred_element_type=jnp.float32)
    act_low = smooth_gate(pre).astype(jnp.bfloat16)
    ffn_rows = lax.psum_scatter(
        jnp.dot(act_low, down_block, preferred_element_type=jnp.float32).astype(jnp.bfloat16),
        "tensor",
        scatter_dimension=0,
        tiled=True,
    ).astype(jnp.float32)
    live_rows = mine(live)
    normal_two, scale_two, normed = norm_forward(
        mine(hidden_in) + ffn_rows, norm_params[2], norm_params[3]
    )
    mixed = (live_rows[:, None] * normed).astype(jnp.bfloat16)
    grad_y = cotangent.astype(jnp.float32) * live_rows[:, None]
    grad_g2 = jnp.sum(grad_y * normal_two, 0)
    grad_b2 = jnp.sum(grad_y, 0)
    grad_r2 = norm_back(normal_two, scale_two, grad_y * norm_params[2])
    grad_r2_all = lax.all_gather(grad_r2.astype(jnp.bfloat16), "tensor", axis=0, tiled=True)
    grad_down = contract_rows(act_low, grad_r2_all)
    grad_act = contract_cols(grad_r2_all, down_block)
    gate_out, gate_pull = jax.vjp(smooth_gate, pre)
    grad_pre = gate_pull(grad_act)[0].astype(jnp.bfloat16)
    grad_up = contract_rows(hidden_low, grad_pre)
    grad_hidden = (
        lax.psum_scatter(
            contract_cols(grad_pre, up_block).astype(jnp.bfloat16),
            "tensor",
            scatter_dimension=0,
            tiled=True,
        ).astype(jnp.float32)
        + grad_r2
    )
    normal_one_rows = mine(normal_one)
    grad_g1 = jnp.sum(grad_hidden * normal_one_rows, 0)
    grad_b1 = jnp.sum(grad_hidden, 0)
    grad_r1 = norm_back(normal_one_rows, mine(scale_one), grad_hidden * norm_params[0])
    grad_branch = lax.all_gather(grad_r1.astype(jnp.bfloat16), "tensor", axis=0, tiled=True)
    grad_attn = contract_cols(grad_branch, w_out).reshape(blocks, BLOCK, HEADS, HDIM)
    grad_qf, grad_kf, grad_val = attend_backward(
        qblock, kblock, vblock, lower, scores_low, state_low, zsum, denom, result, grad_attn
    )
    grad_query = features_back(
        grad_qf.reshape(count, HEADS, 2 * HDIM), query, cosine, sine, every_row
    )
    grad_key = features_back(grad_kf.reshape(count, HEADS, 2 * HDIM), key_proj, cosine, sine, live)
    grad_value = grad_val.reshape(count, width)
    input_grad = (
        grad_r1
        + contract_cols(mine(grad_query), w_query)
        + contract_cols(mine(grad_key), w_key)
        + contract_cols(mine(grad_value), w_value)
    )
    left_rows = jnp.where(tensor_index == 3, attn_low, sequence)
    right_all = jnp.stack((grad_query, grad_key, grad_value, grad_branch))
    right_rows = lax.dynamic_index_in_dim(right_all, tensor_index, 0, keepdims=False)
    grad_owned = contract_rows(left_rows, right_rows)
    norm_partial = jnp.stack((grad_g1, grad_b1, grad_g2, grad_b2))
    grad_a, grad_u, grad_d = (
        *sent_together((grad_owned.astype(jnp.bfloat16), grad_up.astype(jnp.bfloat16)), "dp", 0, 1),
        sum_at_owner(grad_down.astype(jnp.bfloat16), "dp", 1),
    )
    moment_a = 0.5 * attn_mom[0] + grad_a
    moment_u = 0.5 * up_mom + grad_u
    moment_d = 0.5 * down_mom + grad_d
    owner_pick = jax.nn.one_hot(tensor_index, 4, dtype=jnp.float32)
    squares = jnp.concatenate(
        (
            owner_pick * jnp.sum(moment_a * moment_a),
            jnp.stack((jnp.sum(moment_u * moment_u), jnp.sum(moment_d * moment_d))),
        )
    )
    totals, norm_grad = lax.psum((squares, norm_partial), ("dp", "tensor"))
    size_a = jnp.sqrt(jnp.sum(totals[:4] * owner_pick))
    size_u = jnp.sqrt(totals[4])
    size_d = jnp.sqrt(totals[5])
    start_a = (moment_a / (size_a + NS_EPS)).astype(jnp.bfloat16)
    start_u = (moment_u / (size_u + NS_EPS)).astype(jnp.bfloat16)
    start_d = (moment_d.T / (size_d + NS_EPS)).astype(jnp.bfloat16)
    whole_a, cols_u, cols_d = (
        lax.all_gather(start_a, "dp", axis=0, tiled=True),
        lax.all_gather(start_u, "dp", axis=0, tiled=True),
        lax.all_gather(start_d, "dp", axis=0, tiled=True),
    )
    orth_a = orthogonalize(whole_a)
    is_even = tensor_index % 2 == 0
    whole_u, whole_d = (
        lax.all_gather(cols_u, "tensor", axis=1, tiled=True),
        lax.all_gather(cols_d, "tensor", axis=1, tiled=True),
    )
    orth_whole = orthogonalize(jnp.where(is_even, whole_u, whole_d))
    block_cols = cols_u.shape[1]
    own_block = lax.dynamic_slice_in_dim(orth_whole, tensor_index * block_cols, block_cols, 1)
    partner_block = lax.dynamic_slice_in_dim(
        orth_whole, jnp.bitwise_xor(tensor_index, 1) * block_cols, block_cols, 1
    )
    fetched = partner(partner_block, "tensor", 0)
    orth_u = jnp.where(is_even, own_block, fetched)
    orth_d = jnp.where(is_even, fetched, own_block)
    span = moment_a.shape[0]

    def take_rows(array):
        return lax.dynamic_slice_in_dim(array, data_index * span, span, 0).astype(jnp.float32)

    ff_whole = up_block.shape[1] * tensor_count
    keep = 1.0 - MUON_RATE * MUON_DECAY
    new_a = attn_w[0] * keep - MUON_RATE * 0.2 * math.sqrt(width) * take_rows(orth_a)
    scale_ff = 0.2 * math.sqrt(max(width, ff_whole))
    new_u = up_w * keep - MUON_RATE * scale_ff * take_rows(orth_u)
    new_d = down_w * keep - MUON_RATE * scale_ff * take_rows(orth_d).T
    norm_moment1 = 0.5 * norm_m1 + 0.5 * norm_grad
    norm_moment2 = 0.95 * norm_m2 + 0.05 * norm_grad * norm_grad
    first_hat = norm_moment1 / (1.0 - 0.5**STEP)
    second_hat = norm_moment2 / (1.0 - 0.95**STEP)
    norm_new = norm_params - ADAM_RATE * first_hat / (jnp.sqrt(second_hat) + 1e-08)
    return (
        mixed,
        input_grad,
        new_a[None],
        moment_a[None],
        new_u,
        moment_u,
        new_d,
        moment_d,
        norm_moment1,
        norm_moment2,
        norm_new,
    )


BF = jnp.bfloat16
F32 = jnp.float32
MESH = pl.DeviceIdType.MESH
TENSOR = 4
QUARTER = 256
LANES = 128
HALF = 128
HIGH = 4
VMEM_LIMIT = (63 << 20) + (640 << 10)
GELU_C = math.sqrt(2.0 / math.pi)
GELU_A = 0.044715


def nn(left, right):
    return jnp.dot(left, right, preferred_element_type=F32)


def nt(left, right):
    return lax.dot_general(left, right, (((1,), (1,)), ((), ())), preferred_element_type=F32)


def tn(left, right):
    return lax.dot_general(left, right, (((0,), (0,)), ((), ())), preferred_element_type=F32)


def lanes_of(rows, cols=LANES):
    return lax.broadcasted_iota(jnp.int32, (rows, cols), 1)


def half_roll(array):
    return pltpu.roll(array, LANES // 2, 1)


def place():
    data = lax.axis_index("dp")
    tensor = lax.axis_index("tensor")
    return data, tensor


def greet(devices):
    barrier = pltpu.get_barrier_semaphore()
    for device in devices:
        pl.semaphore_signal(barrier, inc=1, device_id=device, device_id_type=MESH)
    pl.semaphore_wait(barrier, len(devices))


def send(src, dst, send_sem, recv_sem, device):
    copy = pltpu.make_async_remote_copy(
        src_ref=src,
        dst_ref=dst,
        send_sem=send_sem,
        recv_sem=recv_sem,
        device_id=device,
        device_id_type=MESH,
    )
    copy.start()
    return copy


def kernel_call(body, name, ins, outs, scratch, collective, scalars=(), anywhere=()):
    in_names = list(ins)
    out_names = list(outs)
    scratch_names = list(scratch)

    def space_of(n):
        return pltpu.SMEM if n in scalars else pl.ANY if n in anywhere else pltpu.VMEM

    def kernel(*refs):
        body(types.SimpleNamespace(**dict(zip(in_names + out_names + scratch_names, refs))))

    results = pl.pallas_call(
        kernel,
        name=name,
        out_shape=[outs[n] for n in out_names],
        in_specs=[
            pl.BlockSpec(memory_space=space_of(n)) for n in in_names
        ],
        out_specs=[pl.BlockSpec(memory_space=space_of(n)) for n in out_names],
        scratch_shapes=[scratch[n] for n in scratch_names],
        compiler_params=pltpu.CompilerParams(
            collective_id=collective,
            has_side_effects=collective is not None,
            vmem_limit_bytes=VMEM_LIMIT,
        ),
    )(*[ins[n] for n in in_names])
    return dict(zip(out_names, results))


def shape(*dims, dtype=BF):
    return jax.ShapeDtypeStruct(dims, dtype)


def dma(*dims):
    return pltpu.SemaphoreType.DMA(dims)


def await_bytes(ref, sem):
    pltpu.make_async_copy(ref, ref, sem).wait()


class GatherDp:
    def __init__(self, slot_of, sends, recvs, data, tensor, detour=False):
        self.slot_of, self.sends, self.recvs, self.detour = slot_of, sends, recvs, detour
        self.data, self.tensor = data, tensor
        self.high, self.low = data // 2, data % 2
        self.partner = (self.high * 2 + 1 - self.low, tensor)
        self.relays = (self.high == 1) | (self.high == 2)
        first_end, last_end = self.high == 0, self.high == HIGH - 1
        self.order = (
            jnp.where(first_end, 3, 1),
            jnp.where(first_end | last_end, 2, 3),
            jnp.where(first_end, 1, jnp.where(last_end, 3, 2)),
        )

    def source(self, step):
        return lax.rem(self.high + HIGH - step, HIGH) * 2 + self.low

    def push(self, slot, at, to, there=None):
        send(slot, slot, self.sends.at[at], self.recvs.at[at if there is None else there], to)

    def start(self):
        mine = self.slot_of(self.data)
        for step, allowed in ((1, self.high != HIGH - 1), (2, None), (3, self.high != 0)):
            to = (lax.rem(self.high + step, HIGH) * 2 + self.low, self.tensor)
            if allowed is None:
                self.push(mine, step, to)
            else:
                pl.when(allowed)(functools.partial(self.push, mine, step, to))

    def cross(self):
        self.push(self.slot_of(self.data), 0, self.partner)

    def passes(self, step):
        skip = ((self.high == 1) & (step == 1)) | ((self.high == 2) & (step == 3))
        if self.detour:
            skip = skip | ((self.high == 0) & (step == 3)) | ((self.high == 3) & (step == 1))
        return jnp.logical_not(skip)

    def forward(self, *positions, cross=True):
        beside = ((self.high ^ 1) * 2 + self.low, self.tensor)
        for position in positions or range(HIGH - 1):
            step = self.order[position]
            slot = self.slot_of(self.source(step))
            await_bytes(slot, self.recvs.at[step])
            if position == HIGH - 2:
                there = jnp.where(self.high == 2, 3, 1)
                pl.when(self.relays)(functools.partial(self.push, slot, 7, beside, there))
            if cross:
                at = HIGH - 1 + step
                pl.when(self.passes(step))(functools.partial(self.push, slot, at, self.partner))
            if cross and position == 0:
                slot = self.slot_of(self.partner_slot(0))
                await_bytes(slot, self.recvs.at[0])
                there = jnp.where((self.high == 0) | (self.high == 2), 4, 6)
                go_on = functools.partial(self.push, slot, 8, beside, there)
                if self.detour:
                    go_on()
                else:
                    pl.when(jnp.logical_not(self.relays))(go_on)

    def partner_slot(self, step):
        return self.source(step) + 1 - 2 * self.low

    def arrive(self, *steps):
        for step in steps or range(HIGH):
            if step:
                await_bytes(self.slot_of(self.partner_slot(step)), self.recvs.at[HIGH - 1 + step])

    def close(self, cross=True):
        mine = self.slot_of(self.data)

        def sent(at, allowed):
            pl.when(allowed)(functools.partial(await_bytes, mine, self.sends.at[at]))

        if cross:
            await_bytes(mine, self.sends.at[0])
            for step in range(1, HIGH):
                sent(HIGH - 1 + step, self.passes(step))
            if self.detour:
                await_bytes(mine, self.sends.at[8])
            else:
                sent(8, jnp.logical_not(self.relays))
        sent(1, self.high != HIGH - 1)
        await_bytes(mine, self.sends.at[2])
        sent(3, self.high != 0)
        sent(7, self.relays)


def softplus_and_slope(x):
    small = jnp.exp(-jnp.abs(x))
    soft = jnp.maximum(x, 0.0) + jnp.log1p(small)
    slope = jnp.where(x >= 0.0, 1.0, small) / (1.0 + small)
    return soft, slope


def spread_weights(r, tiles):
    low = lanes_of(768) < 64
    for k in tiles:
        tile = r.wp[:, k * LANES : (k + 1) * LANES].astype(F32)
        turned = half_roll(tile)
        left, right = jnp.where(low, tile, turned), jnp.where(low, turned, tile)
        if k == 0:
            parts = {0: left, 1: right}
        elif k == 1:
            parts = {3: left, 4: right}
        elif k == 2:
            parts = {2: left, 5: right}
        elif k == 3:
            parts = {6: jnp.where(low, tile, 0.0), 7: jnp.where(low, turned, 0.0)}
        else:
            parts = {8: tile}
        for at, part in parts.items():
            r.xmat[:, at * LANES : (at + 1) * LANES] = part.astype(BF)


def project(r):
    lane = lanes_of(QUARTER)

    def step(q, carry):
        both = nn(r.seq[q], r.xmat[:, : 9 * LANES])
        table, table_live = r.gp[q, :, :LANES], r.gp[q, :, LANES : 2 * LANES]
        for h in range(3):
            soft, slope = softplus_and_slope(both[:, h * LANES : (h + 1) * LANES])
            r.qf[h, q] = (soft * table).astype(BF)
            r.qg[h, q] = slope * table
            soft, slope = softplus_and_slope(both[:, (3 + h) * LANES : (4 + h) * LANES])
            r.kf[h, q] = (soft * table_live).astype(BF)
            r.kg[h, q] = slope * table_live
            value = both[:, (6 + h) * LANES : (7 + h) * LANES]
            ones = jnp.where((lane == 64) | (lane == 65), 1.0, 0.0)
            r.va[h, q] = jnp.where(lane < 64, value, ones).astype(BF)
        return carry

    lax.fori_loop(0, TENSOR, step, 0)


def attend(r, q):
    heads = range(3)
    lane = lanes_of(QUARTER)
    keep = lanes_of(QUARTER, QUARTER) <= lax.broadcasted_iota(jnp.int32, (QUARTER, QUARTER), 0)
    scores = [jnp.where(keep, nt(r.qf[h, q], r.kf[h, q]), 0.0).astype(BF) for h in heads]
    total = [None] * 3
    if q > 0:
        states = [r.state[h].astype(BF) for h in heads]
        total = [nn(r.qf[h, q], states[h]) for h in heads]
        for h in heads:
            r.st[h, q] = states[h]
    if q < TENSOR - 1:
        pairs = [tn(r.kf[h, q], r.va[h, q]) for h in heads]
        for h in heads:
            r.state[h] = pairs[h] if q == 0 else r.state[h] + pairs[h]
    outs = []
    for h in heads:
        r.sb[h, q] = scores[h]
        part = nn(scores[h], r.va[h, q])
        outs.append(part if total[h] is None else total[h] + part)
    for h in heads:
        inverse = 1.0 / outs[h][:, 64:65]
        outs[h] = jnp.where(lane < 64, outs[h] * inverse, inverse)
        r.af[h, q] = outs[h]
    r.attn[q, :, :LANES] = jnp.where(lane < 64, outs[0], half_roll(outs[1])).astype(BF)
    r.attn[q, :, LANES:] = jnp.where(lane < 64, outs[2], 0.0).astype(BF)


def norm_rows(resid):
    center = resid - jnp.mean(resid, -1, keepdims=True)
    spread = jnp.mean(center * center, -1, keepdims=True)
    scale = lax.rsqrt(spread + NORM_EPS)
    return center * scale, scale


def norm_rows_back(normal, scale, grad):
    return scale * (
        grad
        - jnp.mean(grad, -1, keepdims=True)
        - normal * jnp.mean(grad * normal, -1, keepdims=True)
    )


class Group:
    def __init__(self):
        self.data, self.tensor = place()
        self.far, self.core = self.tensor // 2, self.tensor % 2

    def device(self, k):
        return (self.data, self.tensor ^ k)


def half_of(ref, q, part):
    return ref.at[q, pl.ds(part * HALF, HALF)]


class Spread:
    def __init__(self, g, buf, sends, recvs, part):
        self.g, self.buf, self.sends, self.recvs, self.part = g, buf, sends, recvs, part
        own = half_of(buf, g.tensor, part)
        self.far = self.push(own, 0, g.device(2))
        self.near = self.push(own, 1, g.device(1))

    def push(self, ref, k, device):
        k = 3 * self.part + k
        return send(ref, ref, self.sends.at[k], self.recvs.at[k], device)

    def arrive_near(self):
        self.near.wait_recv()

    def pass_far(self):
        self.far.wait_recv()
        self.passed = self.push(half_of(self.buf, self.g.tensor ^ 2, self.part), 2, self.g.device(1))

    def arrive_far(self):
        self.passed.wait_recv()
        for copy in (self.far, self.near, self.passed):
            copy.wait_send()


class SumQuarters:
    def __init__(self, r, g, slot):
        self.r, self.g, self.slot = r, g, slot
        self.near, self.far = {}, {}

    def near_out(self, j, part, value):
        r, k = self.r, 2 * j + part
        r.near_send[k] = value.astype(BF)
        at = 4 * self.slot + k
        self.near[j, part] = send(
            r.near_send.at[k], r.near_recv.at[k], r.near_s.at[at], r.near_r.at[at], self.g.device(1)
        )

    def near_in(self, j, part, value):
        self.near[j, part].wait_recv()
        return value + self.r.near_recv[2 * j + part].astype(F32)

    def far_out(self, part, value):
        r = self.r
        r.far_send[part] = value.astype(BF)
        at = 2 * self.slot + part
        self.far[part] = send(
            r.far_send.at[part], r.far_recv.at[part], r.far_s.at[at], r.far_r.at[at], self.g.device(2)
        )

    def far_in(self, part, value):
        self.far[part].wait_recv()
        value = value + self.r.far_recv[part].astype(F32)
        for copy in (self.far[part], self.near[0, part], self.near[1, part]):
            copy.wait_send()
        return value


def pair_of(ref, quarters, part):
    return jnp.concatenate([ref[q, pl.ds(part * HALF, HALF)] for q in quarters], axis=0)


def put_pair(ref, quarters, part, value):
    for k, q in enumerate(quarters):
        ref[q, pl.ds(part * HALF, HALF)] = value[k * HALF : (k + 1) * HALF]


def feed_in(r, quarters, part):
    pre = nn(pair_of(r.hb, quarters, part), r.wu[...].reshape(768, 768))
    inner = jnp.tanh(GELU_C * (pre + GELU_A * pre * pre * pre))
    half = 0.5 * (1.0 + inner)
    slope = half + 0.5 * pre * (1.0 - inner * inner) * (GELU_C * (1.0 + 3.0 * GELU_A * pre * pre))
    put_pair(r.gp, quarters, part, slope)
    put_pair(r.hid, quarters, part, (pre * half).astype(BF))


def feed_out(r, quarters, part):
    out = nt(pair_of(r.hid, quarters, part), r.wd[...].reshape(768, 768))
    return out[:HALF], out[HALF:]


def feed_back(r, quarters, part):
    grad_act = nn(pair_of(r.dr2, quarters, part), r.wd[...].reshape(768, 768))
    grad_pre = (grad_act * pair_of(r.gp, quarters, part)).astype(BF)
    put_pair(r.du, quarters, part, grad_pre)
    out = nt(grad_pre, r.wu[...].reshape(768, 768))
    return out[:HALF], out[HALF:]


def attend_back(r, g, q):
    heads = range(3)
    lane = lanes_of(QUARTER)
    keep = lanes_of(QUARTER, QUARTER) <= lax.broadcasted_iota(jnp.int32, (QUARTER, QUARTER), 0)
    grads = nt(r.dr1[q], r.woh[...].reshape(3 * LANES, 768))
    dnum = []
    for h in heads:
        grad, af = grads[:, h * LANES : (h + 1) * LANES], r.af[h, q]
        inverse = af[:, 64:65]
        dden = -jnp.sum(grad * af, -1, keepdims=True) * inverse
        dden_low = dden.astype(BF).astype(F32)
        extra = jnp.where(lane == 64, dden_low, jnp.where(lane == 65, dden - dden_low, 0.0))
        dnum.append(jnp.where(lane < 64, grad * inverse, extra).astype(BF))
    ds = [jnp.where(keep, nt(dnum[h], r.va[h, q]), 0.0).astype(BF) for h in heads]
    dv = [tn(r.sb[h, q], dnum[h]) for h in heads]
    dqf = [nn(ds[h], r.kf[h, q]) for h in heads]
    dkf = [tn(ds[h], r.qf[h, q]) for h in heads]
    if q > 0:
        dqf = [dqf[h] + nt(dnum[h], r.st[h, q]) for h in heads]
    if q < TENSOR - 1:
        dkv = [r.state[h].astype(BF) for h in heads]
        dkf = [dkf[h] + nt(r.va[h, q], dkv[h]) for h in heads]
        dv = [dv[h] + nn(r.kf[h, q], dkv[h]) for h in heads]
    if q > 0:
        pairs = [tn(r.qf[h, q], dnum[h]) for h in heads]
        for h in heads:
            r.state[h] = pairs[h] if q == TENSOR - 1 else r.state[h] + pairs[h]
    fold = {}
    for h in heads:
        back = dqf[h] * r.qg[h, q]
        fold[0, h] = back + half_roll(back)
        back = dkf[h] * r.kg[h, q]
        fold[1, h] = back + half_roll(back)
        fold[2, h] = dv[h]
    tiles = (
        jnp.where(lane < 64, fold[0, 0], fold[0, 1]),
        jnp.where(lane < 64, fold[1, 0], fold[1, 1]),
        jnp.where(lane < 64, fold[0, 2], fold[1, 2]),
        jnp.where(lane < 64, fold[2, 0], half_roll(fold[2, 1])),
        jnp.where(lane < 64, fold[2, 2], 0.0),
    )
    for k, tile in enumerate(tiles):
        r.hb[q, :, k * LANES : (k + 1) * LANES] = tile.astype(BF)


def back_to_input(r, q):
    r.gp[q] = nt(r.hb[q, :, : 5 * LANES], r.wp[...])


class ReduceDp:
    def __init__(self, src, low_buf, high_send, high_buf, merge_buf, sems, data, tensor):
        self.src, self.low_buf, self.high_send, self.high_buf = src, low_buf, high_send, high_buf
        self.merge_buf = merge_buf
        self.low_s, self.low_r, self.high_s, self.high_r = sems
        self.tensor = tensor
        self.high, self.low = data // 2, data % 2
        self.first_end, self.last_end = self.high == 0, self.high == HIGH - 1
        self.inner = (self.high == 1) | (self.high == 2)
        self.order = (
            jnp.where(self.first_end, 3, 1),
            jnp.where(self.inner, 3, 2),
            jnp.where(self.first_end, 1, jnp.where(self.last_end, 3, 2)),
        )

    def at(self, step):
        return lax.rem(self.high + step, HIGH)

    def start(self, *positions):
        partner = (self.high * 2 + 1 - self.low, self.tensor)
        for position in positions or range(HIGH):
            step = (self.order + (0,))[position]
            h = self.at(step)
            chunk = self.src.at[h * 2 + 1 - self.low]
            send(chunk, self.low_buf.at[h], self.low_s.at[step], self.low_r.at[step], partner)

    def pair(self, step):
        h = self.at(step)
        await_bytes(self.low_buf.at[h], self.low_r.at[step])
        return self.src[h * 2 + self.low].astype(F32) + self.low_buf[h].astype(F32)

    def forward(self, *positions):
        for position in positions:
            step = self.order[position]
            value = self.pair(step)
            chunk = self.high_send.at[step - 1]
            if position == HIGH - 2 and self.merge_buf is not None:
                pl.when(self.inner)(functools.partial(await_bytes, self.merge_buf, self.high_r.at[0]))
                value = value + jnp.where(self.inner, self.merge_buf[...].astype(F32), 0.0)
            self.high_send[step - 1] = value.astype(BF)

            def straight():
                to = (self.at(step) * 2 + self.low, self.tensor)
                send(chunk, self.high_buf.at[step - 1], self.high_s.at[step], self.high_r.at[step], to)

            def beside():
                to = ((self.high ^ 1) * 2 + self.low, self.tensor)
                send(chunk, self.merge_buf, self.high_s.at[step], self.high_r.at[0], to)

            if position == 0 and self.merge_buf is not None:
                pl.when(self.inner)(straight)
                pl.when(jnp.logical_not(self.inner))(beside)
            else:
                straight()

    def finish(self):
        total = self.pair(0)
        for step in range(1, HIGH):
            chunk = self.high_buf.at[step - 1]
            if self.merge_buf is None:
                await_bytes(chunk, self.high_r.at[step])
                total = total + self.high_buf[step - 1].astype(F32)
                continue
            merged = (self.last_end & (step == 3)) | (self.first_end & (step == 1))
            pl.when(jnp.logical_not(merged))(functools.partial(await_bytes, chunk, self.high_r.at[step]))
            total = total + jnp.where(merged, 0.0, self.high_buf[step - 1].astype(F32))
        for step in range(HIGH):
            await_bytes(self.low_buf.at[0], self.low_s.at[step])
            if step:
                await_bytes(self.high_buf.at[0], self.high_s.at[step])
        return total


EDGES = tuple(slice(k * 256, (k + 1) * 256) for k in range(3))
PAIRS = tuple((a, b) for a in range(3) for b in range(a, 3))


def first_gram(x, spans, acc, add):
    for k, (a, b) in enumerate(PAIRS):
        block = sum(nt(x[EDGES[a], at], x[EDGES[b], at]) for at in spans)
        for side in range(2):
            piece = block[:, side * LANES : (side + 1) * LANES]
            at = (k // 2, 2 * (k % 2) + side)
            acc[at] = acc[at] + piece if add else piece


def first_scale(acc, gram):
    def block_of(k):
        return jnp.concatenate([acc[k // 2, 2 * (k % 2) + side] for side in range(2)], axis=1)

    diagonal = lanes_of(256, 256) == lax.broadcasted_iota(jnp.int32, (256, 256), 0)
    trace = sum(jnp.where(diagonal, block_of(k), 0.0) for k, (a, b) in enumerate(PAIRS) if a == b)
    scale = 1.0 / (jnp.sqrt(jnp.sum(trace)) + NS_EPS)
    for k, (a, b) in enumerate(PAIRS):
        block = (block_of(k) * (scale * scale)).astype(BF)
        gram[a, :, EDGES[b]] = block
        if b > a:
            gram[b, :, EDGES[a]] = block.T
    return scale


def newton_gram(x, gram):
    for a, b in PAIRS:
        block = nt(x[EDGES[a], :], x[EDGES[b], :]).astype(BF)
        gram[a, :, EDGES[b]] = block
        if b > a:
            gram[b, :, EDGES[a]] = block.T


def newton_poly(gram, poly):
    for a, b in PAIRS:
        block = COEF_C * nt(gram[a], gram[b])
        block = (block + COEF_B * gram[a, :, EDGES[b]].astype(F32)).astype(BF)
        poly[a, :, EDGES[b]] = block
        if b > a:
            poly[b, :, EDGES[a]] = block.T


def newton_apply(x, poly, chunk, scale):
    def columns(c, inner):
        at = pl.ds(pl.multiple_of(c * chunk, chunk), chunk)
        old = x[:, at]
        new = COEF_A * old.astype(F32) + nn(poly[:3].reshape(768, 768), old)
        if scale is not None:
            new = scale * new
        x[:, at] = new.astype(BF)
        return inner

    lax.fori_loop(0, x.shape[1] // chunk, columns, 0)


def newton(x, gram, poly, chunk, steps):
    def step(k, carry):
        newton_gram(x, gram)
        newton_poly(gram, poly)
        newton_apply(x, poly, chunk, None)
        return carry

    lax.fori_loop(0, steps, step, 0)


def last_poly(gram, index, rows):
    own = newton_rows_gram(gram, index, rows)
    return (COEF_C * nn(own, gram[:3].reshape(768, 768)) + COEF_B * own.astype(F32)).astype(BF)


def last_rows(x, poly, here, at):
    return (COEF_A * x[here, at].astype(F32) + nn(poly, x[:, at])).astype(BF)


def newton_rows_gram(gram, index, rows):
    parts = []
    for k in range(rows // 32):
        row = index * rows + 32 * k
        parts.append(gram[row // 256, pl.ds(pl.multiple_of(lax.rem(row, 256), 32), 32), :])
    return jnp.concatenate(parts, axis=0)


LOADED = ("cotangent", "attn_mom", "up_mom", "down_mom")


def angles(r):
    rows = TENSOR * QUARTER
    length = r.lengths[0]
    where = lax.broadcasted_iota(jnp.int32, (rows, LANES), 0)
    theta = 0.5 * math.pi * jnp.minimum(where, length - 1).astype(F32) / length.astype(F32)
    table = jnp.where(lanes_of(rows) < 64, jnp.cos(theta), jnp.sin(theta))
    live = jnp.where(where < length, 1.0, 0.0)
    r.gp[:, :, :LANES] = table.reshape(TENSOR, QUARTER, LANES)
    r.gp[:, :, LANES : 2 * LANES] = (table * live).reshape(TENSOR, QUARTER, LANES)


def cut_heads(r, rows):
    low = lanes_of(rows) < 64
    tiles = [r.attn_w[0, :, k * LANES : (k + 1) * LANES] for k in range(6)]
    for pair in range(2):
        first, middle, last = tiles[3 * pair : 3 * pair + 3]
        turned, rest = half_roll(middle), half_roll(last)
        parts = [first, jnp.where(low, middle, 0.0), jnp.where(low, turned, rest), jnp.where(low, rest, 0.0)]
        for k, part in enumerate(parts):
            r.slabs[2 * pair + k // 2, :, (k % 2) * LANES : (k % 2 + 1) * LANES] = part.astype(BF)


def step_body(count, rows, r):
    g = Group()
    data, tensor, far, core = g.data, g.tensor, g.far, g.core
    high, low = data // 2, data % 2
    other = high * 2 + 1 - low
    n = count // 2
    half = rows // 2
    near_dev, far_dev = g.device(1), g.device(2)

    loads = {}
    for k, name in enumerate(LOADED):
        loads[name] = pltpu.make_async_copy(getattr(r, name + "_in"), getattr(r, name), r.load_sem.at[k])
        loads[name].start()
    stores = []

    def store(name):
        k = len(stores)
        stores.append(pltpu.make_async_copy(getattr(r, name), getattr(r, name + "_hbm"), r.store_sem.at[k]))
        stores[-1].start()

    cut_heads(r, rows)
    r.wo_own[...] = r.attn_w[0].astype(BF).reshape(2, half, 768)
    greet(
        [g.device(k) for k in (1, 2, 3)]
        + [(lax.rem(data + k, count), tensor) for k in range(1, count)]
        + [(other, tensor ^ 1), (other, tensor ^ 2)]
    )

    def rows_of(d):
        return pl.ds(pl.multiple_of(d * rows, rows), rows)

    def cols(t):
        return pl.ds(pl.multiple_of(t * 768, 768), 768)

    here, there = rows_of(data), rows_of(other)

    for k in (1, 2, 3):
        peer = tensor ^ k

        @pl.when(tensor < 3)
        def _():
            send(r.slabs.at[peer], r.slab_in.at[tensor], r.slab_s.at[k], r.slab_r.at[tensor], g.device(k))

        @pl.when(tensor == 3)
        def _():
            send(r.wo_own.at[peer % 2], r.wo.at[data, peer % 2], r.slab_s.at[k], r.slab_r.at[3], g.device(k))

    r.seq[tensor] = r.tokens[...]
    mine = r.seq.at[tensor]
    tok_near = send(mine, mine, r.tok_s.at[0], r.tok_r.at[0], near_dev)
    tok_far = send(mine, mine, r.tok_s.at[1], r.tok_r.at[1], far_dev)

    @pl.when(tensor < 3)
    def _():
        r.slab_in[tensor] = r.slabs[tensor]

    @pl.when(tensor == 3)
    def _():
        r.wo[data, core] = r.wo_own[core]

    r.wu[data] = r.up_w[...].astype(BF)
    r.wd[data] = r.down_w[...].astype(BF)

    def gather(slot_of, key, detour=False):
        return GatherDp(slot_of, r.gather_s.at[key], r.gather_r.at[key], data, tensor, detour)

    spans = ((0, 2), (2, 5))
    heads = [
        gather(lambda d, a=a, b=b: r.wp.at[rows_of(d), a * LANES : b * LANES], k, k == 1)
        for k, (a, b) in enumerate(spans)
    ]
    outs = gather(lambda d: r.wo.at[d, core], 2)
    ups = [gather(lambda d, k=k: r.wu.at[d, pl.ds(k * half, half)], 3 + k, k == 1) for k in range(2)]
    downs = [gather(lambda d, k=k: r.wd.at[d, pl.ds(k * half, half)], 5 + k, k == 1) for k in range(2)]
    first_half = lanes_of(rows) < 64

    def slab(m):
        @pl.when(tensor != m)
        def _():
            await_bytes(r.slab_in.at[m], r.slab_r.at[m])

        return r.slab_in[m, :, :LANES], r.slab_in[m, :, LANES:]

    query, query_last = slab(0)
    key, key_last = slab(1)
    r.wp[here, :LANES] = query
    r.wp[here, LANES : 2 * LANES] = key
    heads[0].start()
    heads[0].cross()
    both = jnp.where(first_half, query_last.astype(F32), half_roll(key_last.astype(F32)))
    r.wp[here, 2 * LANES : 3 * LANES] = both.astype(BF)
    value, value_last = slab(2)
    r.wp[here, 3 * LANES : 4 * LANES] = value
    r.wp[here, 4 * LANES :] = value_last
    heads[1].start()
    heads[1].cross()

    @pl.when(tensor != 3)
    def _():
        await_bytes(r.wo.at[data, core], r.slab_r.at[3])

    outs.start()
    outs.cross()
    angles(r)
    heads[0].forward()
    ups[0].start()
    tok_far.wait_recv()
    slot = r.seq.at[tensor ^ 2]
    tok_pass = send(slot, slot, r.tok_s.at[2], r.tok_r.at[2], near_dev)
    heads[1].forward()
    ups[1].start()
    for part in ups + downs:
        part.cross()
    outs.forward()
    downs[0].start()
    heads[0].arrive()
    spread_weights(r, (0, 1))
    heads[1].arrive()
    spread_weights(r, (2, 3, 4))
    tok_near.wait_recv()
    tok_pass.wait_recv()
    project(r)
    ups[0].forward()
    downs[1].start()

    copies = [[], []]
    for j in range(2):
        attend(r, 2 * j)
        attend(r, 2 * j + 1)
        mine, rest = 2 * j + core, 2 * j + 1 - core
        for k in (2, 1, 3):
            quarter = mine if k == 2 else rest
            copies[j].append(
                send(r.attn.at[quarter], r.aall.at[tensor, j], r.attn_s.at[j, k], r.attn_r.at[j, k], g.device(k))
            )
        r.aall[tensor, j] = r.attn[mine]
        if j == 0:
            ups[1].forward()

    outs.arrive()
    share = []
    for d in range(count):
        part = r.wo.at[d, core]
        share.append(send(part, part, r.share_s.at[d], r.share_r.at[d], near_dev))
    for part in downs:
        part.forward()
    for d in range(count):
        part = r.wo.at[d, 1 - core]
        await_bytes(part, r.share_r.at[d])
    whole_out = r.wo[...].reshape(768, 768)
    wop = [r.xmat.at[256 * t : 256 * (t + 1), 1536:2304] for t in range(3)] + [r.xmat.at[0:256, 2304:3072]]
    for t in range(TENSOR):
        wop[t][:192, :] = whole_out[192 * t : 192 * (t + 1)]
        wop[t][192:, :] = jnp.zeros((64, 768), BF)
    for t in range(TENSOR):

        @pl.when(tensor == t)
        def _():
            for h in range(3):
                r.woh[h, :64] = wop[t][64 * h : 64 * (h + 1), :]
                r.woh[h, 64:] = jnp.zeros((64, 768), BF)

    gain1, bias1, gain2, bias2 = (r.norms[k : k + 1] for k in range(4))
    hs = []
    for group_copies in copies:
        for copy in group_copies:
            copy.wait_recv()
    for own in (False, True):
        j = far if own else 1 - far
        q = 2 * j + core
        branch = nn(r.aall[0, j], wop[0][...])
        for t in range(1, TENSOR):
            branch = branch + nn(r.aall[t, j], wop[t][...])
        normal, scale = norm_rows(r.seq[q].astype(F32) + branch)
        hidden = normal * gain1 + bias1
        r.hb[q] = hidden.astype(BF)
        if own:
            r.n1[...] = normal
            r.s1[...] = jnp.broadcast_to(scale, (QUARTER, LANES))
            r.h1[...] = hidden
        hs.append(send(r.hb.at[q], r.hb.at[q], r.h_s.at[int(own)], r.h_r.at[int(own)], near_dev))
    for part in ups:
        part.arrive()

    theirs, ours = (tensor ^ 2, tensor ^ 3), (tensor, tensor ^ 1)
    halves = (0, 1)
    total = SumQuarters(r, g, 0)
    hs[0].wait_recv()
    for part in halves:
        feed_in(r, theirs, part)
    hs[1].wait_recv()
    for part in downs:
        part.arrive()
    for part in halves:
        kept, other_half = feed_out(r, theirs, part)
        total.near_out(0, part, other_half)
        r.kept[part] = kept
    for part in halves:
        total.far_out(part, total.near_in(0, part, r.kept[part]))
    for part in halves:
        feed_in(r, ours, part)
        kept, other_half = feed_out(r, ours, part)
        total.near_out(1, part, other_half)
        r.kept[part] = kept
    for part in heads + [outs] + ups + downs:
        part.close()
    for group_copies in copies:
        for copy in group_copies:
            copy.wait_send()
    for copy in hs + share + [tok_near, tok_far, tok_pass]:
        copy.wait_send()
    for k in (1, 2, 3):

        @pl.when(tensor < 3)
        def _():
            await_bytes(r.slabs.at[0], r.slab_s.at[k])

        @pl.when(tensor == 3)
        def _():
            await_bytes(r.wo_own.at[0], r.slab_s.at[k])

    back = SumQuarters(r, g, 1)
    spread = []

    def second_norm(part):
        at = pl.ds(part * HALF, HALF)
        ffn = total.far_in(part, total.near_in(1, part, r.kept[part]))
        n2, s2 = norm_rows(r.h1[at] + ffn)
        row = lax.broadcasted_iota(jnp.int32, (HALF, 1), 0) + (tensor * QUARTER + part * HALF)
        live = jnp.where(row < r.lengths[0], 1.0, 0.0)
        r.mixed[at] = (live * (n2 * gain2 + bias2)).astype(BF)
        dy = live * r.cotangent[at].astype(F32)
        gain_grad, bias_grad = jnp.sum(dy * n2, 0, keepdims=True), jnp.sum(dy, 0, keepdims=True)
        r.partial[2:3] = gain_grad if part == 0 else r.partial[2:3] + gain_grad
        r.partial[3:4] = bias_grad if part == 0 else r.partial[3:4] + bias_grad
        dr2 = norm_rows_back(n2, s2, dy * gain2)
        r.drf[at] = dr2
        r.dr2[tensor, at] = dr2.astype(BF)
        spread.append(Spread(g, r.dr2, r.dr2_s, r.dr2_r, part))

    def own_back(part):
        spread[part].arrive_near()
        kept, other_half = feed_back(r, ours, part)
        back.near_out(0, part, other_half)
        r.kept[part] = kept

    def their_back(part):
        spread[part].arrive_far()
        kept, other_half = feed_back(r, theirs, part)
        back.near_out(1, part, other_half)
        back.far_out(part, back.near_in(1, part, kept))

    for name in LOADED:
        loads[name].wait()

    works = core == 1

    @pl.when(works & (low == 1))
    def _():
        r.mrows[1] = r.attn_mom[0]

    @pl.when((core == 0) | (low == 0))
    def _():
        send(r.attn_mom.at[0], r.mrows.at[low], r.m_s, r.m_r.at[low], (high * 2 + core, far * 2 + 1))

    second_norm(0)
    own_back(0)
    second_norm(1)
    store("mixed")
    spread[0].pass_far()
    own_back(1)
    their_back(0)
    spread[1].pass_far()
    their_back(1)

    sums = {}
    for key in "fsa":
        sums[key] = ReduceDp(
            *(getattr(r, name + key) for name in ("g", "low", "hs", "hb")),
            getattr(r, "mb" + key, None),
            [getattr(r, name + key) for name in ("ls_", "lr_", "hs_", "hr_")],
            data,
            tensor,
        )
    spread = []

    def first_norm_back(part):
        at = pl.ds(part * HALF, HALF)
        dh = back.far_in(part, back.near_in(0, part, r.kept[part])) + r.drf[at]
        n1 = r.n1[at]
        gain_grad, bias_grad = jnp.sum(dh * n1, 0, keepdims=True), jnp.sum(dh, 0, keepdims=True)
        r.partial[0:1] = gain_grad if part == 0 else r.partial[0:1] + gain_grad
        r.partial[1:2] = bias_grad if part == 0 else r.partial[1:2] + bias_grad
        dr1 = norm_rows_back(n1, r.s1[at, :1], dh * gain1)
        r.drf[at] = dr1
        r.dr1[tensor, at] = dr1.astype(BF)
        spread.append(Spread(g, r.dr1, r.dr1_s, r.dr1_r, part))

    def up_grad(buf):
        grad = tn(r.hb[...].reshape(1024, 768), r.du[...].reshape(1024, 768))
        buf[...] = grad.astype(BF).reshape(buf.shape)

    def down_grad(buf):
        grad = tn(r.dr2[...].reshape(1024, 768), r.hid[...].reshape(1024, 768))
        buf[...] = grad.astype(BF).reshape(buf.shape)

    pl.when(far == 0)(functools.partial(up_grad, r.gf))
    pl.when(far == 1)(functools.partial(down_grad, r.gf))
    sums["f"].start()
    first_norm_back(0)
    sums["f"].forward(0)
    pl.when(far == 0)(functools.partial(down_grad, r.gs))
    pl.when(far == 1)(functools.partial(up_grad, r.gs))
    sums["s"].start()
    sums["f"].forward(1)
    first_norm_back(1)
    r.pbuf[tensor] = r.partial[...]
    parts = []
    for k in (1, 2, 3):
        parts.append(send(r.partial, r.pbuf.at[tensor], r.pt_s.at[k], r.pt_r.at[k], g.device(k)))
    spread[0].pass_far()
    sums["f"].forward(2)
    spread[1].pass_far()
    for part in halves:
        spread[part].arrive_near()
        spread[part].arrive_far()

    attend_back(r, g, 3)
    sums["s"].forward(0)
    for copy in parts:
        copy.wait()
    r.psum[...] = ((r.pbuf[0] + r.pbuf[1]) + r.pbuf[2]) + r.pbuf[3]
    r.qbuf[data] = r.psum[...]
    parts = []
    for k in range(1, count):
        to = (lax.rem(data + k, count), tensor)
        parts.append(send(r.psum, r.qbuf.at[data], r.pd_s.at[k], r.pd_r.at[k], to))
    attend_back(r, g, 2)
    sums["s"].forward(1)

    def new_moment(up_here, key):
        moment = 0.5 * jnp.where(up_here, r.up_mom[...], r.down_mom[...]) + sums[key].finish()

        @pl.when(up_here)
        def _():
            r.mom_u[...] = moment

        @pl.when(jnp.logical_not(up_here))
        def _():
            r.mom_d[...] = moment

        return moment.astype(BF)

    r.xmat[here, cols(tensor)] = new_moment(far == 0, "f")
    attend_back(r, g, 1)
    sums["s"].forward(2)
    own = r.xmat.at[here, cols(tensor)]
    blocks = [
        GatherDp(lambda d: r.xmat.at[rows_of(d), cols(tensor)], r.x_s.at[0], r.x_r.at[0], data, tensor),
        GatherDp(lambda d: r.xmat.at[rows_of(d), cols(tensor ^ 2)], r.x_s.at[1], r.x_r.at[1], data, tensor, True),
    ]

    def pass_on(b, d):
        @pl.when(core == 1)
        def _():
            slot = blocks[b].slot_of(d)
            send(slot, slot, r.j_s.at[b, d], r.j_r.at[b, d], near_dev)

    blocks[0].start()
    blocks[0].cross()
    attend_back(r, g, 0)
    r.xs[...] = new_moment(far == 1, "s")
    send(r.xs, own, r.swap_s, r.swap_r, far_dev)
    store("mom_d")
    store("mom_u")
    blocks[0].forward(0)

    grad = tn(r.seq[...].reshape(1024, 768), r.hb[:, :, : 5 * LANES].reshape(1024, 5 * LANES)).astype(BF)

    def put(at, k):
        r.ga[:, :, at * LANES : (at + 1) * LANES] = grad[:, k * LANES : (k + 1) * LANES].reshape(count, rows, LANES)

    @pl.when(core == 0)
    def _():
        for at, k in enumerate((0, 1, 3, 2, 4)):
            put(at, k)

    @pl.when(works)
    def _():
        for at, k in zip((3, 4, 5, 6, 7), (0, 1, 3, 2, 4)):
            put(at, k)

    blocks[0].forward(1)
    await_bytes(r.xmat.at[here, cols(tensor ^ 2)], r.swap_r)
    blocks[1].start()
    blocks[1].cross()
    grad_out = tn(r.attn[...].reshape(1024, 256), r.dr1[...].reshape(1024, 768)).astype(BF)
    r.gos[core] = grad_out[:192].reshape(2, rows, 768)
    blocks[0].forward(2)

    for step in range(n):
        pass_on(0, blocks[0].source(step))

    for q in (3, 2, 1, 0):
        back_to_input(r, q)
    total = SumQuarters(r, g, 2)
    for part in halves:
        total.near_out(0, part, half_of(r.gp, tensor ^ 3, part)[...])
        total.near_out(1, part, half_of(r.gp, tensor ^ 1, part)[...])
    for part in halves:
        total.far_out(part, total.near_in(0, part, half_of(r.gp, tensor ^ 2, part)[...]))

    extra_in = r.gf.at[:, :, : 2 * LANES]

    @pl.when(core == 0)
    def _():
        wide, rest = r.ga.at[:, :, : 3 * LANES], r.ga.at[:, :, 3 * LANES : 5 * LANES]
        send(wide, wide, r.t_s.at[0], r.t_r.at[0], near_dev)
        send(rest, extra_in, r.t_s.at[1], r.t_r.at[1], near_dev)
        send(r.gos.at[0], r.gos.at[0], r.t_s.at[2], r.t_r.at[2], near_dev)

    @pl.when(works)
    def _():
        await_bytes(extra_in, r.t_r.at[1])
        first = lanes_of(768) < 64
        extra, own_last = [r.gf[:, :, k * LANES : (k + 1) * LANES].reshape(768, LANES).astype(F32) for k in range(2)], [
            r.ga[:, :, (6 + k) * LANES : (7 + k) * LANES].reshape(768, LANES).astype(F32) for k in range(2)
        ]
        tiles = (
            jnp.where(first, extra[0], half_roll(own_last[0])),
            jnp.where(first, half_roll(extra[0]), own_last[0]),
            jnp.where(first, extra[1], half_roll(own_last[1])),
        )
        for k, tile in enumerate(tiles):
            r.ga[:, :, (6 + k) * LANES : (7 + k) * LANES] = tile.astype(BF).reshape(count, rows, LANES)
        await_bytes(r.ga.at[:, :, : 3 * LANES], r.t_r.at[0])
        await_bytes(r.gos.at[0], r.t_r.at[2])

    @pl.when(works)
    def _():
        sums["a"].start(0, 1)

    blocks[1].forward()
    for step in range(n):
        pass_on(1, blocks[1].source(step))

    @pl.when(works)
    def _():
        for k in range(2):
            send(r.gos.at[k, 1 - low], r.olow.at[k], r.o_s.at[0, k], r.o_r.at[k], (other, tensor))
        sums["a"].start(2, 3)
        sums["a"].forward(0, 1)

    for b in range(2):
        for step in range(n):
            blocks[b].arrive(step)
            pass_on(b, blocks[b].partner_slot(step))
        blocks[b].close()

    for part in halves:
        at = pl.ds(part * HALF, HALF)
        value = total.near_in(1, part, half_of(r.gp, tensor, part)[...])
        r.input_grad[at] = total.far_in(part, value) + r.drf[at]
    store("input_grad")

    sides = [
        GatherDp(lambda d, side=side: r.xa.at[rows_of(d // 2 * 2 + side)], r.f_s.at[side], r.f_r.at[side], data, tensor)
        for side in range(2)
    ]
    role = 2 * far + low
    homes = ((high * 2, 1), (high * 2 + 1, 1), (high * 2, 3))
    out_home = (high * 2 + 1, 3)

    @pl.when(works)
    def _():
        for k in range(2):
            t = 2 * far + k
            await_bytes(r.olow.at[k], r.o_r.at[k])
            r.osend[k] = (r.gos[k, low].astype(F32) + r.olow[k].astype(F32)).astype(BF)
            for step in range(1, n):

                @pl.when(lax.rem(high + step, n) == t)
                def _():
                    send(r.osend.at[k], r.ohigh.at[step - 1], r.o_s.at[1, k], r.oh_r.at[step], (t * 2 + low, tensor))

        sums["a"].forward(2)
        summed = sums["a"].finish()
        for m in range(3):
            for k in range(3):
                tile = summed[:, (m + 3 * k) * LANES : (m + 3 * k + 1) * LANES]
                r.asend[m, :, k * LANES : (k + 1) * LANES] = tile.astype(BF)

            @pl.when(role == m)
            def _():
                r.gin[low, far] = r.asend[m]

            @pl.when(role != m)
            def _():
                send(r.asend.at[m], r.gin.at[low, far], r.g_s.at[m], r.g_r.at[low, far], homes[m])

        for k in range(2):

            @pl.when(high == 2 * far + k)
            def _():
                whole = r.gos[k, low].astype(F32) + r.olow[k].astype(F32)
                for step in range(1, n):
                    await_bytes(r.ohigh.at[step - 1], r.oh_r.at[step])
                    whole = whole + r.ohigh[step - 1].astype(F32)
                r.oout[...] = whole.astype(BF)

                @pl.when(role == 3)
                def _():
                    r.gown[low] = r.oout[...]

                @pl.when(role != 3)
                def _():
                    send(r.oout, r.gown.at[low], r.o_s.at[2, 0], r.go_r.at[low], out_home)

        for side in range(2):
            row_block = rows_of(high * 2 + side)

            @pl.when(role == 3)
            def _():
                @pl.when((high // 2 == 0) | (side == 0))
                def _():
                    await_bytes(r.gown.at[side], r.go_r.at[side])

            @pl.when(role != 3)
            def _():
                first = lanes_of(rows) < 64
                for x in range(2):

                    @pl.when((low != side) | (far != x))
                    def _():
                        await_bytes(r.gin.at[side, x], r.g_r.at[side, x])

                    piece = [r.gin[side, x, :, k * LANES : (k + 1) * LANES] for k in range(3)]
                    turned, last = half_roll(piece[1].astype(F32)), piece[2].astype(F32)
                    base = 3 * LANES * x
                    r.gown[side, :, base : base + LANES] = piece[0]
                    r.gown[side, :, base + LANES : base + 2 * LANES] = jnp.where(first, last, turned).astype(BF)
                    r.gown[side, :, base + 2 * LANES : base + 3 * LANES] = jnp.where(first, turned, last).astype(BF)

            if side == 0:
                await_bytes(r.mrows.at[0], r.m_r.at[0])
            else:

                @pl.when(low == 0)
                def _():
                    await_bytes(r.mrows.at[1], r.m_r.at[1])

            r.xa[row_block] = (0.5 * r.mrows[side] + r.gown[side].astype(F32)).astype(BF)
            sides[side].start()

        @pl.when(low == 1)
        def _():
            r.gback[...] = r.gown[1]
            send(r.gown.at[0], r.gback, r.b_s.at[0], r.b_r, (other, tensor))

        @pl.when(low == 0)
        def _():
            send(r.gown.at[0], r.gback, r.b_s.at[0], r.b_r, (data, tensor ^ 1))
            send(r.gown.at[1], r.gback, r.b_s.at[1], r.b_r, (other, tensor ^ 1))

    for copy in parts:
        copy.wait()
    r.norm_grad[...] = sum((r.qbuf[d] for d in range(1, count)), r.qbuf[0])

    @pl.when(core == 0)
    def _():
        for b in range(2):
            for d in range(count):
                await_bytes(own, r.j_r.at[b, d])
            first_gram(r.xmat, [cols(tensor ^ (2 * b)), cols(tensor ^ (2 * b + 1))], r.kg, b > 0)
        scale = first_scale(r.kg, r.du)
        newton_poly(r.du, r.hid)
        newton_apply(r.xmat, r.hid, 1536, scale)
        newton(r.xmat, r.du, r.hid, 3072, NS_STEPS - 2)
        newton_gram(r.xmat, r.du)
        poly = last_poly(r.du, data, rows)
        for k in (2, 3, 1, 0):
            r.lowf[tensor ^ k] = last_rows(r.xmat, poly, here, cols(tensor ^ k))
            for m, out in enumerate((r.o_u, r.o_d)):

                @pl.when(far == m)
                def _():
                    if k:
                        send(r.lowf.at[tensor ^ k], out, r.w_s.at[k], r.w_r.at[m], g.device(k))
                    else:
                        out[...] = r.lowf[tensor]

    owner = far * 2 + low

    @pl.when(core == 1)
    def _():
        for side in range(2):
            sides[side].forward(cross=False)
        for side in range(2):
            sides[side].close(cross=False)
        whole = slice(0, 768)
        first_gram(r.xa, [whole], r.kg, False)
        scale = first_scale(r.kg, r.du)
        newton_poly(r.du, r.hid)
        newton_apply(r.xa, r.hid, 768, scale)
        newton(r.xa, r.du, r.hid, 768, NS_STEPS - 2)
        newton_gram(r.xa, r.du)
        r.lowf[1] = last_rows(r.xa, last_poly(r.du, other, rows), there, whole)
        send(r.lowf.at[1], r.o_a, r.v_s.at[0], r.v_r, (other, owner))
        r.lowf[0] = last_rows(r.xa, last_poly(r.du, data, rows), here, whole)

    @pl.when((core == 1) & (low == 1))
    def _():
        r.o_a[...] = r.lowf[0]

    @pl.when((core == 1) & (low == 0))
    def _():
        send(r.lowf.at[0], r.o_a, r.v_s.at[1], r.v_r, (data, owner))

    @pl.when((core == 0) | (low == 0))
    def _():
        await_bytes(r.o_a, r.v_r)

    for m, out in enumerate((r.o_u, r.o_d)):

        @pl.when((core == 1) | (far != m))
        def _():
            await_bytes(out, r.w_r.at[m])

    @pl.when((core == 0) | (low == 0))
    def _():
        await_bytes(r.gback, r.b_r)

    r.mom_a[...] = 0.5 * r.attn_mom[0] + r.gback[...].astype(F32)

    for copy in stores:
        copy.wait()
    await_bytes(r.xs, r.swap_s)

    @pl.when((core == 0) | (low == 0))
    def _():
        await_bytes(r.mrows.at[0], r.m_s)

    @pl.when(core == 0)
    def _():
        await_bytes(r.ga.at[:, :, : 3 * LANES], r.t_s.at[0])
        await_bytes(extra_in, r.t_s.at[1])
        await_bytes(r.gos.at[0], r.t_s.at[2])

    @pl.when(works)
    def _():
        for k in range(2):
            await_bytes(r.olow.at[k], r.o_s.at[0, k])
            pl.when(high != 2 * far + k)(functools.partial(await_bytes, r.osend.at[k], r.o_s.at[1, k]))
        for m in range(3):
            pl.when(role != m)(functools.partial(await_bytes, r.asend.at[m], r.g_s.at[m]))
        pl.when((high // 2 == far) & (role != 3))(functools.partial(await_bytes, r.oout, r.o_s.at[2, 0]))
        await_bytes(r.gback, r.b_s.at[0])
        pl.when(low == 0)(functools.partial(await_bytes, r.gback, r.b_s.at[1]))

    @pl.when(core == 0)
    def _():
        for k in (1, 2, 3):
            await_bytes(r.o_u, r.w_s.at[k])

    @pl.when(core == 1)
    def _():
        for b in range(2):
            for d in range(count):
                await_bytes(own, r.j_s.at[b, d])
        await_bytes(r.o_a, r.v_s.at[0])

    @pl.when((core == 1) & (low == 0))
    def _():
        await_bytes(r.o_a, r.v_s.at[1])


def step_call(count, rows, ins):
    v = pltpu.VMEM
    n = count // 2
    one = pltpu.SemaphoreType.DMA
    outs = dict(
        mixed_hbm=shape(QUARTER, 768),
        input_grad_hbm=shape(QUARTER, 768, dtype=F32),
        mom_a=shape(rows, 768, dtype=F32),
        mom_u_hbm=shape(rows, 768, dtype=F32),
        mom_d_hbm=shape(rows, 768, dtype=F32),
        norm_grad=shape(4, 768, dtype=F32),
        o_u=shape(rows, 768),
        o_d=shape(rows, 768),
        o_a=shape(rows, 768),
    )
    per_head = (3, TENSOR, QUARTER, LANES)
    quarters = (TENSOR, QUARTER, 768)
    scratch = dict(
        cotangent=v((QUARTER, 768), BF),
        attn_mom=v((1, rows, 768), F32),
        up_mom=v((rows, 768), F32),
        down_mom=v((rows, 768), F32),
        mixed=v((QUARTER, 768), BF),
        input_grad=v((QUARTER, 768), F32),
        mom_u=v((rows, 768), F32),
        mom_d=v((rows, 768), F32),
        load_sem=dma(len(LOADED)),
        store_sem=dma(4),
        slabs=v((TENSOR, rows, 256), BF),
        wo_own=v((2, rows // 2, 768), BF),
        seq=v(quarters, BF),
        slab_in=v((3, rows, 256), BF),
        wp=v((768, 5 * LANES), BF),
        wo=v((count, 2, rows // 2, 768), BF),
        wu=v((count, rows, 768), BF),
        wd=v((count, rows, 768), BF),
        woh=v((3, LANES, 768), BF),
        slab_s=dma(4),
        slab_r=dma(4),
        tok_s=dma(3),
        tok_r=dma(3),
        share_s=dma(count),
        share_r=dma(count),
        gather_s=dma(7, 9),
        gather_r=dma(7, 9),
        qf=v(per_head, BF),
        kf=v(per_head, BF),
        va=v(per_head, BF),
        qg=v(per_head, F32),
        kg=v(per_head, F32),
        af=v(per_head, F32),
        sb=v((3, TENSOR, QUARTER, QUARTER), BF),
        st=v((3, TENSOR, LANES, LANES), BF),
        state=v((3, LANES, LANES), F32),
        attn=v((TENSOR, QUARTER, 256), BF),
        aall=v((TENSOR, 2, QUARTER, 256), BF),
        attn_s=dma(2, 4),
        attn_r=dma(2, 4),
        hb=v(quarters, BF),
        n1=v((QUARTER, 768), F32),
        s1=v((QUARTER, LANES), F32),
        h1=v((QUARTER, 768), F32),
        hid=v(quarters, BF),
        gp=v(quarters, F32),
        du=v(quarters, BF),
        dr2=v(quarters, BF),
        drf=v((QUARTER, 768), F32),
        dr1=v(quarters, BF),
        kept=v((2, HALF, 768), F32),
        near_send=v((4, HALF, 768), BF),
        near_recv=v((4, HALF, 768), BF),
        far_send=v((2, HALF, 768), BF),
        far_recv=v((2, HALF, 768), BF),
        near_s=dma(12),
        near_r=dma(12),
        far_s=dma(6),
        far_r=dma(6),
        h_s=dma(2),
        h_r=dma(2),
        dr2_s=dma(6),
        dr2_r=dma(6),
        dr1_s=dma(6),
        dr1_r=dma(6),
        gf=v((count, rows, 768), BF),
        gs=v((count, rows, 768), BF),
        ga=v((count, rows, 9 * LANES), BF),
        gos=v((2, 2, rows, 768), BF),
        t_s=dma(3),
        t_r=dma(3),
        olow=v((2, rows, 768), BF),
        osend=v((2, rows, 768), BF),
        ohigh=v((n - 1, rows, 768), BF),
        o_s=dma(3, 2),
        o_r=dma(2),
        oh_r=dma(n),
        asend=v((3, rows, 3 * LANES), BF),
        gin=v((2, 2, rows, 3 * LANES), BF),
        g_s=dma(3),
        g_r=dma(2, 2),
        gown=v((2, rows, 768), BF),
        go_r=dma(2),
        gback=v((rows, 768), BF),
        b_s=dma(2),
        b_r=one,
        mrows=v((2, rows, 768), F32),
        m_s=one,
        m_r=dma(2),
        partial=v((4, 768), F32),
        pbuf=v((TENSOR, 4, 768), F32),
        psum=v((4, 768), F32),
        qbuf=v((count, 4, 768), F32),
        pt_s=dma(4),
        pt_r=dma(4),
        pd_s=dma(count),
        pd_r=dma(count),
        oout=v((rows, 768), BF),
        xs=v((rows, 768), BF),
        xmat=v((768, TENSOR * 768), BF),
        xa=v((768, 768), BF),
        swap_s=one,
        swap_r=one,
        x_s=dma(2, 9),
        x_r=dma(2, 9),
        f_s=dma(2, 8),
        f_r=dma(2, 8),
        j_s=dma(2, count),
        j_r=dma(2, count),
        w_s=dma(4),
        w_r=dma(2),
        v_s=dma(2),
        v_r=one,
    )
    for key in "fsa":
        part = (rows, 9 * LANES if key == "a" else 768)
        for name, slots in (("low", n), ("hs", n - 1), ("hb", n - 1)):
            scratch[name + key] = v((slots,) + part, BF)
        if key != "a":
            scratch["mb" + key] = v(part, BF)
        for name in ("ls_", "lr_", "hs_", "hr_"):
            scratch[name + key] = dma(n)
    body = functools.partial(step_body, count, rows)
    anywhere = [n + "_in" for n in LOADED] + [n for n in outs if n.endswith("_hbm")]
    return kernel_call(body, "layer_step", ins, outs, scratch, 0, ("lengths",), anywhere)


def finish_body(r):
    keep = 1.0 - MUON_RATE * MUON_DECAY
    rate_a = MUON_RATE * 0.2 * math.sqrt(768)
    rate_ff = MUON_RATE * 0.2 * math.sqrt(TENSOR * 768)
    r.attn_new[0] = r.attn_w[0] * keep - rate_a * r.o_a[...].astype(F32)
    r.up_new[...] = r.up_w[...] * keep - rate_ff * r.o_u[...].astype(F32)
    r.down_new[...] = r.down_w[...] * keep - rate_ff * r.o_d[...].astype(F32)
    r.attn_moment[0] = r.mom_a[...]
    r.up_moment[...] = r.mom_u[...]
    r.down_moment[...] = r.mom_d[...]
    r.mixed_out[...] = r.mixed[...]
    r.input_grad_out[...] = r.input_grad[...]
    grad = r.norm_grad[...]
    moment1 = 0.5 * r.norm_m1[...] + 0.5 * grad
    moment2 = 0.95 * r.norm_m2[...] + 0.05 * grad * grad
    first_hat = moment1 / (1.0 - 0.5**STEP)
    second_hat = moment2 / (1.0 - 0.95**STEP)
    r.norm_moment1[...] = moment1
    r.norm_moment2[...] = moment2
    r.norm_new[...] = r.norms[...] - ADAM_RATE * first_hat / (jnp.sqrt(second_hat) + 1e-08)


def finish_call(ins):
    rows = ins["up_w"].shape[0]
    block = shape(rows, 768, dtype=F32)
    small = shape(4, 768, dtype=F32)
    outs = dict(
        mixed_out=shape(QUARTER, 768),
        input_grad_out=shape(QUARTER, 768, dtype=F32),
        attn_new=shape(1, rows, 768, dtype=F32),
        attn_moment=shape(1, rows, 768, dtype=F32),
        up_new=block,
        up_moment=block,
        down_new=block,
        down_moment=block,
        norm_moment1=small,
        norm_moment2=small,
        norm_new=small,
    )
    return kernel_call(finish_body, "finish", ins, outs, {}, None)


def step_on_device(
    tokens,
    cotangent,
    lengths,
    attn_w,
    up_w,
    down_w,
    norm_params,
    attn_mom,
    up_mom,
    down_mom,
    norm_m1,
    norm_m2,
):
    count = lax.axis_size("dp")
    rows = attn_w.shape[1]
    done = step_call(
        count,
        rows,
        dict(
            lengths=lengths,
            tokens=tokens,
            cotangent_in=cotangent,
            attn_w=attn_w,
            up_w=up_w,
            down_w=down_w.T,
            norms=norm_params,
            attn_mom_in=attn_mom,
            up_mom_in=up_mom,
            down_mom_in=down_mom.T,
        ),
    )
    last = finish_call(
        dict(
            attn_w=attn_w,
            up_w=up_w,
            down_w=down_w.T,
            norms=norm_params,
            norm_m1=norm_m1,
            norm_m2=norm_m2,
            **{n.removesuffix("_hbm"): a for n, a in done.items()},
        )
    )
    return (
        last["mixed_out"],
        last["input_grad_out"],
        last["attn_new"],
        last["attn_moment"],
        last["up_new"],
        last["up_moment"],
        last["down_new"].T,
        last["down_moment"].T,
        last["norm_moment1"],
        last["norm_moment2"],
        last["norm_new"],
    )


def solution(mesh):
    placed = (
        P(("dp", "tensor"), None),
        P(("dp", "tensor"), None),
        P("dp"),
        P("tensor", "dp", None),
        P("dp", "tensor"),
        P("tensor", "dp"),
        P(),
        P("tensor", "dp", None),
        P("dp", "tensor"),
        P("tensor", "dp"),
        P(),
        P(),
    )
    whole_tiles = mesh.shape["dp"] == 8 and mesh.shape["tensor"] == TENSOR
    return jax.shard_map(
        step_on_device if whole_tiles else on_device,
        mesh=mesh,
        in_specs=placed,
        out_specs=(
            P(("dp", "tensor"), None),
            P(("dp", "tensor"), None),
            P("tensor", "dp", None),
            P("tensor", "dp", None),
            P("dp", "tensor"),
            P("dp", "tensor"),
            P("tensor", "dp"),
            P("tensor", "dp"),
            P(),
            P(),
            P(),
        ),
        check_vma=False,
    )
```

```python
import functools
import math
import types

import jax
import jax.numpy as jnp
from jax import lax
from jax.experimental import pallas as pl
from jax.experimental.pallas import tpu as pltpu
from jax.sharding import PartitionSpec as P

HEADS = 12
HDIM = 64
BLOCK = 64
NS_STEPS = 5
STEP = 10


NORM_EPS = 1e-05
NS_EPS = 1e-07
COEF_A = 3.4445
COEF_B = -4.775
COEF_C = 2.0315
MUON_RATE = 0.15
MUON_DECAY = 0.1
ADAM_RATE = 0.2


def cut_along(array, dim, size):
    lengths = array.shape
    pieces = array.reshape(*lengths[:dim], size, lengths[dim] // size, *lengths[dim + 1 :])
    return jnp.moveaxis(pieces, dim, 0)


def sum_at_owner(array, axis, dim):
    size = lax.axis_size(axis)
    pieces = lax.all_to_all(cut_along(array, dim, size), axis, 0, 0, tiled=True)
    return jnp.sum(pieces.astype(jnp.float32), axis=0)


def sent_together(arrays, axis, dim, along):
    widths = [a.shape[along] for a in arrays]
    both = jnp.concatenate(arrays, axis=along)
    whole = sum_at_owner(both, axis, dim)
    return tuple(jnp.split(whole, [sum(widths[:k]) for k in range(1, len(widths))], axis=along))


def partner(array, axis, bit):
    return lax.ppermute(array, axis, [(i, i ^ 1 << bit) for i in range(lax.axis_size(axis))])


def contract_rows(left, right):
    return lax.dot_general(
        left, right, (((0,), (0,)), ((), ())), preferred_element_type=jnp.float32
    )


def contract_cols(left, right):
    return lax.dot_general(
        left, right, (((1,), (1,)), ((), ())), preferred_element_type=jnp.float32
    )


def norm_forward(resid, gain, bias):
    center = resid - jnp.mean(resid, -1, keepdims=True)
    spread = jnp.mean(center * center, -1, keepdims=True)
    scale_inv = lax.rsqrt(spread + NORM_EPS)
    normal_rows = center * scale_inv
    return (normal_rows, scale_inv, normal_rows * gain + bias)


def norm_back(normal_rows, scale_inv, grad_normed):
    return scale_inv * (
        grad_normed
        - jnp.mean(grad_normed, -1, keepdims=True)
        - normal_rows * jnp.mean(grad_normed * normal_rows, -1, keepdims=True)
    )


def smooth_gate(values):
    return jax.nn.gelu(values, approximate=True)


def features(proj, cosine, sine, weight_rows):
    count = proj.shape[0]
    soft = jax.nn.softplus(proj).reshape(count, HEADS, HDIM)
    both = jnp.concatenate([soft * cosine[:, None, None], soft * sine[:, None, None]], -1)
    return both * weight_rows[:, None, None]


def features_back(grad_feat, proj, cosine, sine, weight_rows):
    count = proj.shape[0]
    grad_soft = (
        grad_feat[..., :HDIM] * cosine[:, None, None] + grad_feat[..., HDIM:] * sine[:, None, None]
    )
    grad_soft = grad_soft * weight_rows[:, None, None]
    slope = jax.nn.sigmoid(proj).reshape(count, HEADS, HDIM)
    return (grad_soft * slope).reshape(count, HEADS * HDIM).astype(jnp.bfloat16)


def blocked(array):
    return array.reshape(array.shape[0] // BLOCK, BLOCK, array.shape[1], array.shape[2])


def attend_forward(qblock, kblock, vblock, lower):
    scores = (
        jnp.einsum("nihf,njhf->nhij", qblock, kblock, preferred_element_type=jnp.float32) * lower
    )
    scores_low = scores.astype(jnp.bfloat16)
    pairs = jnp.einsum("njhf,njhd->nhfd", kblock, vblock, preferred_element_type=jnp.float32)
    state = jnp.cumsum(pairs, 0) - pairs
    state_low = state.astype(jnp.bfloat16)
    key_sum = jnp.sum(kblock.astype(jnp.float32), 1)
    zsum = jnp.cumsum(key_sum, 0) - key_sum
    numer = jnp.einsum("nhij,njhd->nihd", scores_low, vblock, preferred_element_type=jnp.float32)
    numer = numer + jnp.einsum(
        "nihf,nhfd->nihd", qblock, state_low, preferred_element_type=jnp.float32
    )
    denom = jnp.transpose(jnp.sum(scores, -1), (0, 2, 1))
    denom = denom + jnp.einsum(
        "nihf,nhf->nih", qblock.astype(jnp.float32), zsum, precision=lax.Precision.HIGHEST
    )
    return (scores_low, state_low, zsum, denom, numer / denom[..., None])


def attend_backward(
    qblock, kblock, vblock, lower, scores_low, state_low, zsum, denom, result, grad_out
):
    grad_numer = (grad_out / denom[..., None]).astype(jnp.bfloat16)
    grad_denom = -jnp.sum(grad_out * result, -1) / denom
    grad_scores = jnp.einsum(
        "nihd,njhd->nhij", grad_numer, vblock, preferred_element_type=jnp.float32
    )
    grad_scores = ((grad_scores + jnp.transpose(grad_denom, (0, 2, 1))[..., None]) * lower).astype(
        jnp.bfloat16
    )
    grad_state = jnp.einsum(
        "nihf,nihd->nhfd", qblock, grad_numer, preferred_element_type=jnp.float32
    )
    grad_pairs = (jnp.cumsum(grad_state[::-1], 0)[::-1] - grad_state).astype(jnp.bfloat16)
    grad_z = jnp.einsum(
        "nih,nihf->nhf", grad_denom, qblock.astype(jnp.float32), precision=lax.Precision.HIGHEST
    )
    grad_ksum = jnp.cumsum(grad_z[::-1], 0)[::-1] - grad_z
    grad_qf = jnp.einsum("nhij,njhf->nihf", grad_scores, kblock, preferred_element_type=jnp.float32)
    grad_qf = grad_qf + jnp.einsum(
        "nihd,nhfd->nihf", grad_numer, state_low, preferred_element_type=jnp.float32
    )
    grad_qf = grad_qf + grad_denom[..., None] * zsum[:, None]
    grad_kf = jnp.einsum("nhij,nihf->njhf", grad_scores, qblock, preferred_element_type=jnp.float32)
    grad_kf = grad_kf + jnp.einsum(
        "njhd,nhfd->njhf", vblock, grad_pairs, preferred_element_type=jnp.float32
    )
    grad_kf = grad_kf + grad_ksum[:, None]
    grad_val = jnp.einsum(
        "nhij,nihd->njhd", scores_low, grad_numer, preferred_element_type=jnp.float32
    )
    grad_val = grad_val + jnp.einsum(
        "njhf,nhfd->njhd", kblock, grad_pairs, preferred_element_type=jnp.float32
    )
    return (grad_qf, grad_kf, grad_val.astype(jnp.bfloat16))


def newton_update(iterate, gram):
    poly = (
        COEF_B * gram.astype(jnp.float32)
        + COEF_C * jnp.dot(gram, gram, preferred_element_type=jnp.float32)
    ).astype(jnp.bfloat16)
    return (
        COEF_A * iterate.astype(jnp.float32)
        + jnp.dot(poly, iterate, preferred_element_type=jnp.float32)
    ).astype(jnp.bfloat16)


def orthogonalize(iterate):
    for step in range(NS_STEPS):
        gram = jnp.dot(iterate, iterate.T, preferred_element_type=jnp.float32).astype(jnp.bfloat16)
        iterate = newton_update(iterate, gram)
    return iterate


def on_device(
    tokens,
    cotangent,
    lengths,
    attn_w,
    up_w,
    down_w,
    norm_params,
    attn_mom,
    up_mom,
    down_mom,
    norm_m1,
    norm_m2,
):
    tensor_index = lax.axis_index("tensor")
    data_index = lax.axis_index("dp")
    tensor_count = lax.axis_size("tensor")
    length = lengths[0]
    rows_here = tokens.shape[0]
    wa_rows, up_block, down_block = (
        lax.all_gather(attn_w.astype(jnp.bfloat16), "dp", axis=1, tiled=True),
        lax.all_gather(up_w.astype(jnp.bfloat16), "dp", axis=0, tiled=True),
        lax.all_gather(down_w.astype(jnp.bfloat16), "dp", axis=1, tiled=True),
    )
    w_all = lax.all_gather(wa_rows, "tensor", axis=0, tiled=True)
    w_query = w_all[0]
    w_key = w_all[1]
    w_value = w_all[2]
    w_out = w_all[3]
    sequence = lax.all_gather(tokens, "tensor", axis=0, tiled=True)
    count = sequence.shape[0]
    width = sequence.shape[1]
    blocks = count // BLOCK
    start_row = tensor_index * rows_here

    def mine(array):
        return lax.dynamic_slice_in_dim(array, start_row, rows_here, 0)

    where = jnp.arange(count)
    live = (where < length).astype(jnp.float32)
    place = jnp.minimum(where, length - 1).astype(jnp.float32)
    theta = 0.5 * math.pi * place / length.astype(jnp.float32)
    cosine = jnp.cos(theta)
    sine = jnp.sin(theta)
    every_row = jnp.ones((count,), jnp.float32)
    query = jnp.dot(sequence, w_query, preferred_element_type=jnp.float32)
    key_proj = jnp.dot(sequence, w_key, preferred_element_type=jnp.float32)
    value = jnp.dot(sequence, w_value, preferred_element_type=jnp.float32)
    qblock = blocked(features(query, cosine, sine, every_row).astype(jnp.bfloat16))
    kblock = blocked(features(key_proj, cosine, sine, live).astype(jnp.bfloat16))
    vblock = value.astype(jnp.bfloat16).reshape(blocks, BLOCK, HEADS, HDIM)
    lower = jnp.tril(jnp.ones((BLOCK, BLOCK), jnp.float32))
    scores_low, state_low, zsum, denom, result = attend_forward(qblock, kblock, vblock, lower)
    attn_low = result.reshape(count, width).astype(jnp.bfloat16)
    branch = jnp.dot(attn_low, w_out, preferred_element_type=jnp.float32)
    normal_one, scale_one, hidden_in = norm_forward(
        sequence.astype(jnp.float32) + branch, norm_params[0], norm_params[1]
    )
    hidden_low = hidden_in.astype(jnp.bfloat16)
    pre = jnp.dot(hidden_low, up_block, preferred_element_type=jnp.float32)
    act_low = smooth_gate(pre).astype(jnp.bfloat16)
    ffn_rows = lax.psum_scatter(
        jnp.dot(act_low, down_block, preferred_element_type=jnp.float32).astype(jnp.bfloat16),
        "tensor",
        scatter_dimension=0,
        tiled=True,
    ).astype(jnp.float32)
    live_rows = mine(live)
    normal_two, scale_two, normed = norm_forward(
        mine(hidden_in) + ffn_rows, norm_params[2], norm_params[3]
    )
    mixed = (live_rows[:, None] * normed).astype(jnp.bfloat16)
    grad_y = cotangent.astype(jnp.float32) * live_rows[:, None]
    grad_g2 = jnp.sum(grad_y * normal_two, 0)
    grad_b2 = jnp.sum(grad_y, 0)
    grad_r2 = norm_back(normal_two, scale_two, grad_y * norm_params[2])
    grad_r2_all = lax.all_gather(grad_r2.astype(jnp.bfloat16), "tensor", axis=0, tiled=True)
    grad_down = contract_rows(act_low, grad_r2_all)
    grad_act = contract_cols(grad_r2_all, down_block)
    gate_out, gate_pull = jax.vjp(smooth_gate, pre)
    grad_pre = gate_pull(grad_act)[0].astype(jnp.bfloat16)
    grad_up = contract_rows(hidden_low, grad_pre)
    grad_hidden = (
        lax.psum_scatter(
            contract_cols(grad_pre, up_block).astype(jnp.bfloat16),
            "tensor",
            scatter_dimension=0,
            tiled=True,
        ).astype(jnp.float32)
        + grad_r2
    )
    normal_one_rows = mine(normal_one)
    grad_g1 = jnp.sum(grad_hidden * normal_one_rows, 0)
    grad_b1 = jnp.sum(grad_hidden, 0)
    grad_r1 = norm_back(normal_one_rows, mine(scale_one), grad_hidden * norm_params[0])
    grad_branch = lax.all_gather(grad_r1.astype(jnp.bfloat16), "tensor", axis=0, tiled=True)
    grad_attn = contract_cols(grad_branch, w_out).reshape(blocks, BLOCK, HEADS, HDIM)
    grad_qf, grad_kf, grad_val = attend_backward(
        qblock, kblock, vblock, lower, scores_low, state_low, zsum, denom, result, grad_attn
    )
    grad_query = features_back(
        grad_qf.reshape(count, HEADS, 2 * HDIM), query, cosine, sine, every_row
    )
    grad_key = features_back(grad_kf.reshape(count, HEADS, 2 * HDIM), key_proj, cosine, sine, live)
    grad_value = grad_val.reshape(count, width)
    input_grad = (
        grad_r1
        + contract_cols(mine(grad_query), w_query)
        + contract_cols(mine(grad_key), w_key)
        + contract_cols(mine(grad_value), w_value)
    )
    left_rows = jnp.where(tensor_index == 3, attn_low, sequence)
    right_all = jnp.stack((grad_query, grad_key, grad_value, grad_branch))
    right_rows = lax.dynamic_index_in_dim(right_all, tensor_index, 0, keepdims=False)
    grad_owned = contract_rows(left_rows, right_rows)
    norm_partial = jnp.stack((grad_g1, grad_b1, grad_g2, grad_b2))
    grad_a, grad_u, grad_d = (
        *sent_together((grad_owned.astype(jnp.bfloat16), grad_up.astype(jnp.bfloat16)), "dp", 0, 1),
        sum_at_owner(grad_down.astype(jnp.bfloat16), "dp", 1),
    )
    moment_a = 0.5 * attn_mom[0] + grad_a
    moment_u = 0.5 * up_mom + grad_u
    moment_d = 0.5 * down_mom + grad_d
    owner_pick = jax.nn.one_hot(tensor_index, 4, dtype=jnp.float32)
    squares = jnp.concatenate(
        (
            owner_pick * jnp.sum(moment_a * moment_a),
            jnp.stack((jnp.sum(moment_u * moment_u), jnp.sum(moment_d * moment_d))),
        )
    )
    totals, norm_grad = lax.psum((squares, norm_partial), ("dp", "tensor"))
    size_a = jnp.sqrt(jnp.sum(totals[:4] * owner_pick))
    size_u = jnp.sqrt(totals[4])
    size_d = jnp.sqrt(totals[5])
    start_a = (moment_a / (size_a + NS_EPS)).astype(jnp.bfloat16)
    start_u = (moment_u / (size_u + NS_EPS)).astype(jnp.bfloat16)
    start_d = (moment_d.T / (size_d + NS_EPS)).astype(jnp.bfloat16)
    whole_a, cols_u, cols_d = (
        lax.all_gather(start_a, "dp", axis=0, tiled=True),
        lax.all_gather(start_u, "dp", axis=0, tiled=True),
        lax.all_gather(start_d, "dp", axis=0, tiled=True),
    )
    orth_a = orthogonalize(whole_a)
    is_even = tensor_index % 2 == 0
    whole_u, whole_d = (
        lax.all_gather(cols_u, "tensor", axis=1, tiled=True),
        lax.all_gather(cols_d, "tensor", axis=1, tiled=True),
    )
    orth_whole = orthogonalize(jnp.where(is_even, whole_u, whole_d))
    block_cols = cols_u.shape[1]
    own_block = lax.dynamic_slice_in_dim(orth_whole, tensor_index * block_cols, block_cols, 1)
    partner_block = lax.dynamic_slice_in_dim(
        orth_whole, jnp.bitwise_xor(tensor_index, 1) * block_cols, block_cols, 1
    )
    fetched = partner(partner_block, "tensor", 0)
    orth_u = jnp.where(is_even, own_block, fetched)
    orth_d = jnp.where(is_even, fetched, own_block)
    span = moment_a.shape[0]

    def take_rows(array):
        return lax.dynamic_slice_in_dim(array, data_index * span, span, 0).astype(jnp.float32)

    ff_whole = up_block.shape[1] * tensor_count
    keep = 1.0 - MUON_RATE * MUON_DECAY
    new_a = attn_w[0] * keep - MUON_RATE * 0.2 * math.sqrt(width) * take_rows(orth_a)
    scale_ff = 0.2 * math.sqrt(max(width, ff_whole))
    new_u = up_w * keep - MUON_RATE * scale_ff * take_rows(orth_u)
    new_d = down_w * keep - MUON_RATE * scale_ff * take_rows(orth_d).T
    norm_moment1 = 0.5 * norm_m1 + 0.5 * norm_grad
    norm_moment2 = 0.95 * norm_m2 + 0.05 * norm_grad * norm_grad
    first_hat = norm_moment1 / (1.0 - 0.5**STEP)
    second_hat = norm_moment2 / (1.0 - 0.95**STEP)
    norm_new = norm_params - ADAM_RATE * first_hat / (jnp.sqrt(second_hat) + 1e-08)
    return (
        mixed,
        input_grad,
        new_a[None],
        moment_a[None],
        new_u,
        moment_u,
        new_d,
        moment_d,
        norm_moment1,
        norm_moment2,
        norm_new,
    )


BF = jnp.bfloat16
F32 = jnp.float32
MESH = pl.DeviceIdType.MESH
TENSOR = 4
QUARTER = 256
LANES = 128
HALF = 128
HIGH = 4
VMEM_LIMIT = (63 << 20) + (640 << 10)
GELU_C = math.sqrt(2.0 / math.pi)
GELU_A = 0.044715


def nn(left, right):
    return jnp.dot(left, right, preferred_element_type=F32)


def nt(left, right):
    return lax.dot_general(left, right, (((1,), (1,)), ((), ())), preferred_element_type=F32)


def tn(left, right):
    return lax.dot_general(left, right, (((0,), (0,)), ((), ())), preferred_element_type=F32)


def lanes_of(rows, cols=LANES):
    return lax.broadcasted_iota(jnp.int32, (rows, cols), 1)


def half_roll(array):
    return pltpu.roll(array, LANES // 2, 1)


def place():
    data = lax.axis_index("dp")
    tensor = lax.axis_index("tensor")
    return data, tensor


def greet(devices):
    barrier = pltpu.get_barrier_semaphore()
    for device in devices:
        pl.semaphore_signal(barrier, inc=1, device_id=device, device_id_type=MESH)
    pl.semaphore_wait(barrier, len(devices))


def send(src, dst, send_sem, recv_sem, device):
    copy = pltpu.make_async_remote_copy(
        src_ref=src,
        dst_ref=dst,
        send_sem=send_sem,
        recv_sem=recv_sem,
        device_id=device,
        device_id_type=MESH,
    )
    copy.start()
    return copy


def kernel_call(body, name, ins, outs, scratch, collective, scalars=(), anywhere=()):
    in_names = list(ins)
    out_names = list(outs)
    scratch_names = list(scratch)

    def space_of(n):
        return pltpu.SMEM if n in scalars else pl.ANY if n in anywhere else pltpu.VMEM

    def kernel(*refs):
        body(types.SimpleNamespace(**dict(zip(in_names + out_names + scratch_names, refs))))

    results = pl.pallas_call(
        kernel,
        name=name,
        out_shape=[outs[n] for n in out_names],
        in_specs=[
            pl.BlockSpec(memory_space=space_of(n)) for n in in_names
        ],
        out_specs=[pl.BlockSpec(memory_space=space_of(n)) for n in out_names],
        scratch_shapes=[scratch[n] for n in scratch_names],
        compiler_params=pltpu.CompilerParams(
            collective_id=collective,
            has_side_effects=collective is not None,
            vmem_limit_bytes=VMEM_LIMIT,
        ),
    )(*[ins[n] for n in in_names])
    return dict(zip(out_names, results))


def shape(*dims, dtype=BF):
    return jax.ShapeDtypeStruct(dims, dtype)


def dma(*dims):
    return pltpu.SemaphoreType.DMA(dims)


def await_bytes(ref, sem):
    pltpu.make_async_copy(ref, ref, sem).wait()


class GatherDp:
    def __init__(self, slot_of, sends, recvs, data, tensor, detour=False):
        self.slot_of, self.sends, self.recvs, self.detour = slot_of, sends, recvs, detour
        self.data, self.tensor = data, tensor
        self.high, self.low = data // 2, data % 2
        self.partner = (self.high * 2 + 1 - self.low, tensor)
        self.relays = (self.high == 1) | (self.high == 2)
        first_end, last_end = self.high == 0, self.high == HIGH - 1
        self.order = (
            jnp.where(first_end, 3, 1),
            jnp.where(first_end | last_end, 2, 3),
            jnp.where(first_end, 1, jnp.where(last_end, 3, 2)),
        )

    def source(self, step):
        return lax.rem(self.high + HIGH - step, HIGH) * 2 + self.low

    def push(self, slot, at, to, there=None):
        send(slot, slot, self.sends.at[at], self.recvs.at[at if there is None else there], to)

    def start(self):
        mine = self.slot_of(self.data)
        for step, allowed in ((1, self.high != HIGH - 1), (2, None), (3, self.high != 0)):
            to = (lax.rem(self.high + step, HIGH) * 2 + self.low, self.tensor)
            if allowed is None:
                self.push(mine, step, to)
            else:
                pl.when(allowed)(functools.partial(self.push, mine, step, to))

    def cross(self):
        self.push(self.slot_of(self.data), 0, self.partner)

    def passes(self, step):
        skip = ((self.high == 1) & (step == 1)) | ((self.high == 2) & (step == 3))
        if self.detour:
            skip = skip | ((self.high == 0) & (step == 3)) | ((self.high == 3) & (step == 1))
        return jnp.logical_not(skip)

    def forward(self, *positions, cross=True):
        beside = ((self.high ^ 1) * 2 + self.low, self.tensor)
        for position in positions or range(HIGH - 1):
            step = self.order[position]
            slot = self.slot_of(self.source(step))
            await_bytes(slot, self.recvs.at[step])
            if position == HIGH - 2:
                there = jnp.where(self.high == 2, 3, 1)
                pl.when(self.relays)(functools.partial(self.push, slot, 7, beside, there))
            if cross:
                at = HIGH - 1 + step
                pl.when(self.passes(step))(functools.partial(self.push, slot, at, self.partner))
            if cross and position == 0:
                slot = self.slot_of(self.partner_slot(0))
                await_bytes(slot, self.recvs.at[0])
                there = jnp.where((self.high == 0) | (self.high == 2), 4, 6)
                go_on = functools.partial(self.push, slot, 8, beside, there)
                if self.detour:
                    go_on()
                else:
                    pl.when(jnp.logical_not(self.relays))(go_on)

    def partner_slot(self, step):
        return self.source(step) + 1 - 2 * self.low

    def arrive(self, *steps):
        for step in steps or range(HIGH):
            if step:
                await_bytes(self.slot_of(self.partner_slot(step)), self.recvs.at[HIGH - 1 + step])

    def close(self, cross=True):
        mine = self.slot_of(self.data)

        def sent(at, allowed):
            pl.when(allowed)(functools.partial(await_bytes, mine, self.sends.at[at]))

        if cross:
            await_bytes(mine, self.sends.at[0])
            for step in range(1, HIGH):
                sent(HIGH - 1 + step, self.passes(step))
            if self.detour:
                await_bytes(mine, self.sends.at[8])
            else:
                sent(8, jnp.logical_not(self.relays))
        sent(1, self.high != HIGH - 1)
        await_bytes(mine, self.sends.at[2])
        sent(3, self.high != 0)
        sent(7, self.relays)


def softplus_and_slope(x):
    small = jnp.exp(-jnp.abs(x))
    soft = jnp.maximum(x, 0.0) + jnp.log1p(small)
    slope = jnp.where(x >= 0.0, 1.0, small) / (1.0 + small)
    return soft, slope


def spread_weights(r, tiles):
    low = lanes_of(768) < 64
    for k in tiles:
        tile = r.wp[:, k * LANES : (k + 1) * LANES].astype(F32)
        turned = half_roll(tile)
        left, right = jnp.where(low, tile, turned), jnp.where(low, turned, tile)
        if k == 0:
            parts = {0: left, 1: right}
        elif k == 1:
            parts = {3: left, 4: right}
        elif k == 2:
            parts = {2: left, 5: right}
        elif k == 3:
            parts = {6: jnp.where(low, tile, 0.0), 7: jnp.where(low, turned, 0.0)}
        else:
            parts = {8: tile}
        for at, part in parts.items():
            r.xmat[:, at * LANES : (at + 1) * LANES] = part.astype(BF)


def project(r):
    lane = lanes_of(QUARTER)

    def step(q, carry):
        both = nn(r.seq[q], r.xmat[:, : 9 * LANES])
        table, table_live = r.gp[q, :, :LANES], r.gp[q, :, LANES : 2 * LANES]
        for h in range(3):
            soft, slope = softplus_and_slope(both[:, h * LANES : (h + 1) * LANES])
            r.qf[h, q] = (soft * table).astype(BF)
            r.qg[h, q] = slope * table
            soft, slope = softplus_and_slope(both[:, (3 + h) * LANES : (4 + h) * LANES])
            r.kf[h, q] = (soft * table_live).astype(BF)
            r.kg[h, q] = slope * table_live
            value = both[:, (6 + h) * LANES : (7 + h) * LANES]
            ones = jnp.where((lane == 64) | (lane == 65), 1.0, 0.0)
            r.va[h, q] = jnp.where(lane < 64, value, ones).astype(BF)
        return carry

    lax.fori_loop(0, TENSOR, step, 0)


def attend(r, q):
    heads = range(3)
    lane = lanes_of(QUARTER)
    keep = lanes_of(QUARTER, QUARTER) <= lax.broadcasted_iota(jnp.int32, (QUARTER, QUARTER), 0)
    scores = [jnp.where(keep, nt(r.qf[h, q], r.kf[h, q]), 0.0).astype(BF) for h in heads]
    total = [None] * 3
    if q > 0:
        states = [r.state[h].astype(BF) for h in heads]
        total = [nn(r.qf[h, q], states[h]) for h in heads]
        for h in heads:
            r.st[h, q] = states[h]
    if q < TENSOR - 1:
        pairs = [tn(r.kf[h, q], r.va[h, q]) for h in heads]
        for h in heads:
            r.state[h] = pairs[h] if q == 0 else r.state[h] + pairs[h]
    outs = []
    for h in heads:
        r.sb[h, q] = scores[h]
        part = nn(scores[h], r.va[h, q])
        outs.append(part if total[h] is None else total[h] + part)
    for h in heads:
        inverse = 1.0 / outs[h][:, 64:65]
        outs[h] = jnp.where(lane < 64, outs[h] * inverse, inverse)
        r.af[h, q] = outs[h]
    r.attn[q, :, :LANES] = jnp.where(lane < 64, outs[0], half_roll(outs[1])).astype(BF)
    r.attn[q, :, LANES:] = jnp.where(lane < 64, outs[2], 0.0).astype(BF)


def norm_rows(resid):
    center = resid - jnp.mean(resid, -1, keepdims=True)
    spread = jnp.mean(center * center, -1, keepdims=True)
    scale = lax.rsqrt(spread + NORM_EPS)
    return center * scale, scale


def norm_rows_back(normal, scale, grad):
    return scale * (
        grad
        - jnp.mean(grad, -1, keepdims=True)
        - normal * jnp.mean(grad * normal, -1, keepdims=True)
    )


class Group:
    def __init__(self):
        self.data, self.tensor = place()
        self.far, self.core = self.tensor // 2, self.tensor % 2

    def device(self, k):
        return (self.data, self.tensor ^ k)


def half_of(ref, q, part):
    return ref.at[q, pl.ds(part * HALF, HALF)]


class Spread:
    def __init__(self, g, buf, sends, recvs, part):
        self.g, self.buf, self.sends, self.recvs, self.part = g, buf, sends, recvs, part
        own = half_of(buf, g.tensor, part)
        self.far = self.push(own, 0, g.device(2))
        self.near = self.push(own, 1, g.device(1))

    def push(self, ref, k, device):
        k = 3 * self.part + k
        return send(ref, ref, self.sends.at[k], self.recvs.at[k], device)

    def arrive_near(self):
        self.near.wait_recv()

    def pass_far(self):
        self.far.wait_recv()
        self.passed = self.push(half_of(self.buf, self.g.tensor ^ 2, self.part), 2, self.g.device(1))

    def arrive_far(self):
        self.passed.wait_recv()
        for copy in (self.far, self.near, self.passed):
            copy.wait_send()


class SumQuarters:
    def __init__(self, r, g, slot):
        self.r, self.g, self.slot = r, g, slot
        self.near, self.far = {}, {}

    def near_out(self, j, part, value):
        r, k = self.r, 2 * j + part
        r.near_send[k] = value.astype(BF)
        at = 4 * self.slot + k
        self.near[j, part] = send(
            r.near_send.at[k], r.near_recv.at[k], r.near_s.at[at], r.near_r.at[at], self.g.device(1)
        )

    def near_in(self, j, part, value):
        self.near[j, part].wait_recv()
        return value + self.r.near_recv[2 * j + part].astype(F32)

    def far_out(self, part, value):
        r = self.r
        r.far_send[part] = value.astype(BF)
        at = 2 * self.slot + part
        self.far[part] = send(
            r.far_send.at[part], r.far_recv.at[part], r.far_s.at[at], r.far_r.at[at], self.g.device(2)
        )

    def far_in(self, part, value):
        self.far[part].wait_recv()
        value = value + self.r.far_recv[part].astype(F32)
        for copy in (self.far[part], self.near[0, part], self.near[1, part]):
            copy.wait_send()
        return value


def pair_of(ref, quarters, part):
    return jnp.concatenate([ref[q, pl.ds(part * HALF, HALF)] for q in quarters], axis=0)


def put_pair(ref, quarters, part, value):
    for k, q in enumerate(quarters):
        ref[q, pl.ds(part * HALF, HALF)] = value[k * HALF : (k + 1) * HALF]


def feed_in(r, quarters, part):
    pre = nn(pair_of(r.hb, quarters, part), r.wu[...].reshape(768, 768))
    inner = jnp.tanh(GELU_C * (pre + GELU_A * pre * pre * pre))
    half = 0.5 * (1.0 + inner)
    slope = half + 0.5 * pre * (1.0 - inner * inner) * (GELU_C * (1.0 + 3.0 * GELU_A * pre * pre))
    put_pair(r.gp, quarters, part, slope)
    put_pair(r.hid, quarters, part, (pre * half).astype(BF))


def feed_out(r, quarters, part):
    out = nt(pair_of(r.hid, quarters, part), r.wd[...].reshape(768, 768))
    return out[:HALF], out[HALF:]


def feed_back(r, quarters, part):
    grad_act = nn(pair_of(r.dr2, quarters, part), r.wd[...].reshape(768, 768))
    grad_pre = (grad_act * pair_of(r.gp, quarters, part)).astype(BF)
    put_pair(r.du, quarters, part, grad_pre)
    out = nt(grad_pre, r.wu[...].reshape(768, 768))
    return out[:HALF], out[HALF:]


def attend_back(r, g, q):
    heads = range(3)
    lane = lanes_of(QUARTER)
    keep = lanes_of(QUARTER, QUARTER) <= lax.broadcasted_iota(jnp.int32, (QUARTER, QUARTER), 0)
    grads = nt(r.dr1[q], r.woh[...].reshape(3 * LANES, 768))
    dnum = []
    for h in heads:
        grad, af = grads[:, h * LANES : (h + 1) * LANES], r.af[h, q]
        inverse = af[:, 64:65]
        dden = -jnp.sum(grad * af, -1, keepdims=True) * inverse
        dden_low = dden.astype(BF).astype(F32)
        extra = jnp.where(lane == 64, dden_low, jnp.where(lane == 65, dden - dden_low, 0.0))
        dnum.append(jnp.where(lane < 64, grad * inverse, extra).astype(BF))
    ds = [jnp.where(keep, nt(dnum[h], r.va[h, q]), 0.0).astype(BF) for h in heads]
    dv = [tn(r.sb[h, q], dnum[h]) for h in heads]
    dqf = [nn(ds[h], r.kf[h, q]) for h in heads]
    dkf = [tn(ds[h], r.qf[h, q]) for h in heads]
    if q > 0:
        dqf = [dqf[h] + nt(dnum[h], r.st[h, q]) for h in heads]
    if q < TENSOR - 1:
        dkv = [r.state[h].astype(BF) for h in heads]
        dkf = [dkf[h] + nt(r.va[h, q], dkv[h]) for h in heads]
        dv = [dv[h] + nn(r.kf[h, q], dkv[h]) for h in heads]
    if q > 0:
        pairs = [tn(r.qf[h, q], dnum[h]) for h in heads]
        for h in heads:
            r.state[h] = pairs[h] if q == TENSOR - 1 else r.state[h] + pairs[h]
    fold = {}
    for h in heads:
        back = dqf[h] * r.qg[h, q]
        fold[0, h] = back + half_roll(back)
        back = dkf[h] * r.kg[h, q]
        fold[1, h] = back + half_roll(back)
        fold[2, h] = dv[h]
    tiles = (
        jnp.where(lane < 64, fold[0, 0], fold[0, 1]),
        jnp.where(lane < 64, fold[1, 0], fold[1, 1]),
        jnp.where(lane < 64, fold[0, 2], fold[1, 2]),
        jnp.where(lane < 64, fold[2, 0], half_roll(fold[2, 1])),
        jnp.where(lane < 64, fold[2, 2], 0.0),
    )
    for k, tile in enumerate(tiles):
        r.hb[q, :, k * LANES : (k + 1) * LANES] = tile.astype(BF)


def back_to_input(r, q):
    r.gp[q] = nt(r.hb[q, :, : 5 * LANES], r.wp[...])


class ReduceDp:
    def __init__(self, src, low_buf, high_send, high_buf, merge_buf, sems, data, tensor):
        self.src, self.low_buf, self.high_send, self.high_buf = src, low_buf, high_send, high_buf
        self.merge_buf = merge_buf
        self.low_s, self.low_r, self.high_s, self.high_r = sems
        self.tensor = tensor
        self.high, self.low = data // 2, data % 2
        self.first_end, self.last_end = self.high == 0, self.high == HIGH - 1
        self.inner = (self.high == 1) | (self.high == 2)
        self.order = (
            jnp.where(self.first_end, 3, 1),
            jnp.where(self.inner, 3, 2),
            jnp.where(self.first_end, 1, jnp.where(self.last_end, 3, 2)),
        )

    def at(self, step):
        return lax.rem(self.high + step, HIGH)

    def start(self, *positions):
        partner = (self.high * 2 + 1 - self.low, self.tensor)
        for position in positions or range(HIGH):
            step = (self.order + (0,))[position]
            h = self.at(step)
            chunk = self.src.at[h * 2 + 1 - self.low]
            send(chunk, self.low_buf.at[h], self.low_s.at[step], self.low_r.at[step], partner)

    def pair(self, step):
        h = self.at(step)
        await_bytes(self.low_buf.at[h], self.low_r.at[step])
        return self.src[h * 2 + self.low].astype(F32) + self.low_buf[h].astype(F32)

    def forward(self, *positions):
        for position in positions:
            step = self.order[position]
            value = self.pair(step)
            chunk = self.high_send.at[step - 1]
            if position == HIGH - 2 and self.merge_buf is not None:
                pl.when(self.inner)(functools.partial(await_bytes, self.merge_buf, self.high_r.at[0]))
                value = value + jnp.where(self.inner, self.merge_buf[...].astype(F32), 0.0)
            self.high_send[step - 1] = value.astype(BF)

            def straight():
                to = (self.at(step) * 2 + self.low, self.tensor)
                send(chunk, self.high_buf.at[step - 1], self.high_s.at[step], self.high_r.at[step], to)

            def beside():
                to = ((self.high ^ 1) * 2 + self.low, self.tensor)
                send(chunk, self.merge_buf, self.high_s.at[step], self.high_r.at[0], to)

            if position == 0 and self.merge_buf is not None:
                pl.when(self.inner)(straight)
                pl.when(jnp.logical_not(self.inner))(beside)
            else:
                straight()

    def finish(self):
        total = self.pair(0)
        for step in range(1, HIGH):
            chunk = self.high_buf.at[step - 1]
            if self.merge_buf is None:
                await_bytes(chunk, self.high_r.at[step])
                total = total + self.high_buf[step - 1].astype(F32)
                continue
            merged = (self.last_end & (step == 3)) | (self.first_end & (step == 1))
            pl.when(jnp.logical_not(merged))(functools.partial(await_bytes, chunk, self.high_r.at[step]))
            total = total + jnp.where(merged, 0.0, self.high_buf[step - 1].astype(F32))
        for step in range(HIGH):
            await_bytes(self.low_buf.at[0], self.low_s.at[step])
            if step:
                await_bytes(self.high_buf.at[0], self.high_s.at[step])
        return total


EDGES = tuple(slice(k * 256, (k + 1) * 256) for k in range(3))
PAIRS = tuple((a, b) for a in range(3) for b in range(a, 3))


def first_gram(x, spans, acc, add):
    for k, (a, b) in enumerate(PAIRS):
        block = sum(nt(x[EDGES[a], at], x[EDGES[b], at]) for at in spans)
        for side in range(2):
            piece = block[:, side * LANES : (side + 1) * LANES]
            at = (k // 2, 2 * (k % 2) + side)
            acc[at] = acc[at] + piece if add else piece


def first_scale(acc, gram):
    def block_of(k):
        return jnp.concatenate([acc[k // 2, 2 * (k % 2) + side] for side in range(2)], axis=1)

    diagonal = lanes_of(256, 256) == lax.broadcasted_iota(jnp.int32, (256, 256), 0)
    trace = sum(jnp.where(diagonal, block_of(k), 0.0) for k, (a, b) in enumerate(PAIRS) if a == b)
    scale = 1.0 / (jnp.sqrt(jnp.sum(trace)) + NS_EPS)
    for k, (a, b) in enumerate(PAIRS):
        block = (block_of(k) * (scale * scale)).astype(BF)
        gram[a, :, EDGES[b]] = block
        if b > a:
            gram[b, :, EDGES[a]] = block.T
    return scale


def newton_gram(x, gram):
    for a, b in PAIRS:
        block = nt(x[EDGES[a], :], x[EDGES[b], :]).astype(BF)
        gram[a, :, EDGES[b]] = block
        if b > a:
            gram[b, :, EDGES[a]] = block.T


def newton_poly(gram, poly):
    for a, b in PAIRS:
        block = COEF_C * nt(gram[a], gram[b])
        block = (block + COEF_B * gram[a, :, EDGES[b]].astype(F32)).astype(BF)
        poly[a, :, EDGES[b]] = block
        if b > a:
            poly[b, :, EDGES[a]] = block.T


def newton_apply(x, poly, chunk, scale):
    def columns(c, inner):
        at = pl.ds(pl.multiple_of(c * chunk, chunk), chunk)
        old = x[:, at]
        new = COEF_A * old.astype(F32) + nn(poly[:3].reshape(768, 768), old)
        if scale is not None:
            new = scale * new
        x[:, at] = new.astype(BF)
        return inner

    lax.fori_loop(0, x.shape[1] // chunk, columns, 0)


def newton(x, gram, poly, chunk, steps):
    def step(k, carry):
        newton_gram(x, gram)
        newton_poly(gram, poly)
        newton_apply(x, poly, chunk, None)
        return carry

    lax.fori_loop(0, steps, step, 0)


def last_poly(gram, index, rows):
    own = newton_rows_gram(gram, index, rows)
    return (COEF_C * nn(own, gram[:3].reshape(768, 768)) + COEF_B * own.astype(F32)).astype(BF)


def last_rows(x, poly, here, at):
    return (COEF_A * x[here, at].astype(F32) + nn(poly, x[:, at])).astype(BF)


def newton_rows_gram(gram, index, rows):
    parts = []
    for k in range(rows // 32):
        row = index * rows + 32 * k
        parts.append(gram[row // 256, pl.ds(pl.multiple_of(lax.rem(row, 256), 32), 32), :])
    return jnp.concatenate(parts, axis=0)


LOADED = ("cotangent", "attn_mom", "up_mom", "down_mom")


def angles(r):
    rows = TENSOR * QUARTER
    length = r.lengths[0]
    where = lax.broadcasted_iota(jnp.int32, (rows, LANES), 0)
    theta = 0.5 * math.pi * jnp.minimum(where, length - 1).astype(F32) / length.astype(F32)
    table = jnp.where(lanes_of(rows) < 64, jnp.cos(theta), jnp.sin(theta))
    live = jnp.where(where < length, 1.0, 0.0)
    r.gp[:, :, :LANES] = table.reshape(TENSOR, QUARTER, LANES)
    r.gp[:, :, LANES : 2 * LANES] = (table * live).reshape(TENSOR, QUARTER, LANES)


def cut_heads(r, rows):
    low = lanes_of(rows) < 64
    tiles = [r.attn_w[0, :, k * LANES : (k + 1) * LANES] for k in range(6)]
    for pair in range(2):
        first, middle, last = tiles[3 * pair : 3 * pair + 3]
        turned, rest = half_roll(middle), half_roll(last)
        parts = [first, jnp.where(low, middle, 0.0), jnp.where(low, turned, rest), jnp.where(low, rest, 0.0)]
        for k, part in enumerate(parts):
            r.slabs[2 * pair + k // 2, :, (k % 2) * LANES : (k % 2 + 1) * LANES] = part.astype(BF)


def step_body(count, rows, r):
    g = Group()
    data, tensor, far, core = g.data, g.tensor, g.far, g.core
    high, low = data // 2, data % 2
    other = high * 2 + 1 - low
    n = count // 2
    half = rows // 2
    near_dev, far_dev = g.device(1), g.device(2)

    loads = {}
    for k, name in enumerate(LOADED):
        loads[name] = pltpu.make_async_copy(getattr(r, name + "_in"), getattr(r, name), r.load_sem.at[k])
        loads[name].start()
    stores = []

    def store(name):
        k = len(stores)
        stores.append(pltpu.make_async_copy(getattr(r, name), getattr(r, name + "_hbm"), r.store_sem.at[k]))
        stores[-1].start()

    cut_heads(r, rows)
    r.wo_own[...] = r.attn_w[0].astype(BF).reshape(2, half, 768)
    greet(
        [g.device(k) for k in (1, 2, 3)]
        + [(lax.rem(data + k, count), tensor) for k in range(1, count)]
        + [(other, tensor ^ 1), (other, tensor ^ 2)]
    )

    def rows_of(d):
        return pl.ds(pl.multiple_of(d * rows, rows), rows)

    def cols(t):
        return pl.ds(pl.multiple_of(t * 768, 768), 768)

    here, there = rows_of(data), rows_of(other)

    for k in (1, 2, 3):
        peer = tensor ^ k

        @pl.when(tensor < 3)
        def _():
            send(r.slabs.at[peer], r.slab_in.at[tensor], r.slab_s.at[k], r.slab_r.at[tensor], g.device(k))

        @pl.when(tensor == 3)
        def _():
            send(r.wo_own.at[peer % 2], r.wo.at[data, peer % 2], r.slab_s.at[k], r.slab_r.at[3], g.device(k))

    r.seq[tensor] = r.tokens[...]
    mine = r.seq.at[tensor]
    tok_near = send(mine, mine, r.tok_s.at[0], r.tok_r.at[0], near_dev)
    tok_far = send(mine, mine, r.tok_s.at[1], r.tok_r.at[1], far_dev)

    @pl.when(tensor < 3)
    def _():
        r.slab_in[tensor] = r.slabs[tensor]

    @pl.when(tensor == 3)
    def _():
        r.wo[data, core] = r.wo_own[core]

    r.wu[data] = r.up_w[...].astype(BF)
    r.wd[data] = r.down_w[...].astype(BF)

    def gather(slot_of, key, detour=False):
        return GatherDp(slot_of, r.gather_s.at[key], r.gather_r.at[key], data, tensor, detour)

    spans = ((0, 2), (2, 5))
    heads = [
        gather(lambda d, a=a, b=b: r.wp.at[rows_of(d), a * LANES : b * LANES], k, k == 1)
        for k, (a, b) in enumerate(spans)
    ]
    outs = gather(lambda d: r.wo.at[d, core], 2)
    ups = [gather(lambda d, k=k: r.wu.at[d, pl.ds(k * half, half)], 3 + k, k == 1) for k in range(2)]
    downs = [gather(lambda d, k=k: r.wd.at[d, pl.ds(k * half, half)], 5 + k, k == 1) for k in range(2)]
    first_half = lanes_of(rows) < 64

    def slab(m):
        @pl.when(tensor != m)
        def _():
            await_bytes(r.slab_in.at[m], r.slab_r.at[m])

        return r.slab_in[m, :, :LANES], r.slab_in[m, :, LANES:]

    query, query_last = slab(0)
    key, key_last = slab(1)
    r.wp[here, :LANES] = query
    r.wp[here, LANES : 2 * LANES] = key
    heads[0].start()
    heads[0].cross()
    both = jnp.where(first_half, query_last.astype(F32), half_roll(key_last.astype(F32)))
    r.wp[here, 2 * LANES : 3 * LANES] = both.astype(BF)
    value, value_last = slab(2)
    r.wp[here, 3 * LANES : 4 * LANES] = value
    r.wp[here, 4 * LANES :] = value_last
    heads[1].start()
    heads[1].cross()

    @pl.when(tensor != 3)
    def _():
        await_bytes(r.wo.at[data, core], r.slab_r.at[3])

    outs.start()
    outs.cross()
    angles(r)
    heads[0].forward()
    ups[0].start()
    tok_far.wait_recv()
    slot = r.seq.at[tensor ^ 2]
    tok_pass = send(slot, slot, r.tok_s.at[2], r.tok_r.at[2], near_dev)
    heads[1].forward()
    ups[1].start()
    for part in ups + downs:
        part.cross()
    outs.forward()
    downs[0].start()
    heads[0].arrive()
    spread_weights(r, (0, 1))
    heads[1].arrive()
    spread_weights(r, (2, 3, 4))
    tok_near.wait_recv()
    tok_pass.wait_recv()
    project(r)
    ups[0].forward()
    downs[1].start()

    copies = [[], []]
    for j in range(2):
        attend(r, 2 * j)
        attend(r, 2 * j + 1)
        mine, rest = 2 * j + core, 2 * j + 1 - core
        for k in (2, 1, 3):
            quarter = mine if k == 2 else rest
            copies[j].append(
                send(r.attn.at[quarter], r.aall.at[tensor, j], r.attn_s.at[j, k], r.attn_r.at[j, k], g.device(k))
            )
        r.aall[tensor, j] = r.attn[mine]
        if j == 0:
            ups[1].forward()

    outs.arrive()
    share = []
    for d in range(count):
        part = r.wo.at[d, core]
        share.append(send(part, part, r.share_s.at[d], r.share_r.at[d], near_dev))
    for part in downs:
        part.forward()
    for d in range(count):
        part = r.wo.at[d, 1 - core]
        await_bytes(part, r.share_r.at[d])
    whole_out = r.wo[...].reshape(768, 768)
    wop = [r.xmat.at[256 * t : 256 * (t + 1), 1536:2304] for t in range(3)] + [r.xmat.at[0:256, 2304:3072]]
    for t in range(TENSOR):
        wop[t][:192, :] = whole_out[192 * t : 192 * (t + 1)]
        wop[t][192:, :] = jnp.zeros((64, 768), BF)
    for t in range(TENSOR):

        @pl.when(tensor == t)
        def _():
            for h in range(3):
                r.woh[h, :64] = wop[t][64 * h : 64 * (h + 1), :]
                r.woh[h, 64:] = jnp.zeros((64, 768), BF)

    gain1, bias1, gain2, bias2 = (r.norms[k : k + 1] for k in range(4))
    hs = []
    for group_copies in copies:
        for copy in group_copies:
            copy.wait_recv()
    for own in (False, True):
        j = far if own else 1 - far
        q = 2 * j + core
        branch = nn(r.aall[0, j], wop[0][...])
        for t in range(1, TENSOR):
            branch = branch + nn(r.aall[t, j], wop[t][...])
        normal, scale = norm_rows(r.seq[q].astype(F32) + branch)
        hidden = normal * gain1 + bias1
        r.hb[q] = hidden.astype(BF)
        if own:
            r.n1[...] = normal
            r.s1[...] = jnp.broadcast_to(scale, (QUARTER, LANES))
            r.h1[...] = hidden
        hs.append(send(r.hb.at[q], r.hb.at[q], r.h_s.at[int(own)], r.h_r.at[int(own)], near_dev))
    for part in ups:
        part.arrive()

    theirs, ours = (tensor ^ 2, tensor ^ 3), (tensor, tensor ^ 1)
    halves = (0, 1)
    total = SumQuarters(r, g, 0)
    hs[0].wait_recv()
    for part in halves:
        feed_in(r, theirs, part)
    hs[1].wait_recv()
    for part in downs:
        part.arrive()
    for part in halves:
        kept, other_half = feed_out(r, theirs, part)
        total.near_out(0, part, other_half)
        r.kept[part] = kept
    for part in halves:
        total.far_out(part, total.near_in(0, part, r.kept[part]))
    for part in halves:
        feed_in(r, ours, part)
        kept, other_half = feed_out(r, ours, part)
        total.near_out(1, part, other_half)
        r.kept[part] = kept
    for part in heads + [outs] + ups + downs:
        part.close()
    for group_copies in copies:
        for copy in group_copies:
            copy.wait_send()
    for copy in hs + share + [tok_near, tok_far, tok_pass]:
        copy.wait_send()
    for k in (1, 2, 3):

        @pl.when(tensor < 3)
        def _():
            await_bytes(r.slabs.at[0], r.slab_s.at[k])

        @pl.when(tensor == 3)
        def _():
            await_bytes(r.wo_own.at[0], r.slab_s.at[k])

    back = SumQuarters(r, g, 1)
    spread = []

    def second_norm(part):
        at = pl.ds(part * HALF, HALF)
        ffn = total.far_in(part, total.near_in(1, part, r.kept[part]))
        n2, s2 = norm_rows(r.h1[at] + ffn)
        row = lax.broadcasted_iota(jnp.int32, (HALF, 1), 0) + (tensor * QUARTER + part * HALF)
        live = jnp.where(row < r.lengths[0], 1.0, 0.0)
        r.mixed[at] = (live * (n2 * gain2 + bias2)).astype(BF)
        dy = live * r.cotangent[at].astype(F32)
        gain_grad, bias_grad = jnp.sum(dy * n2, 0, keepdims=True), jnp.sum(dy, 0, keepdims=True)
        r.partial[2:3] = gain_grad if part == 0 else r.partial[2:3] + gain_grad
        r.partial[3:4] = bias_grad if part == 0 else r.partial[3:4] + bias_grad
        dr2 = norm_rows_back(n2, s2, dy * gain2)
        r.drf[at] = dr2
        r.dr2[tensor, at] = dr2.astype(BF)
        spread.append(Spread(g, r.dr2, r.dr2_s, r.dr2_r, part))

    def own_back(part):
        spread[part].arrive_near()
        kept, other_half = feed_back(r, ours, part)
        back.near_out(0, part, other_half)
        r.kept[part] = kept

    def their_back(part):
        spread[part].arrive_far()
        kept, other_half = feed_back(r, theirs, part)
        back.near_out(1, part, other_half)
        back.far_out(part, back.near_in(1, part, kept))

    for name in LOADED:
        loads[name].wait()

    works = core == 1

    @pl.when(works & (low == 1))
    def _():
        r.mrows[1] = r.attn_mom[0]

    @pl.when((core == 0) | (low == 0))
    def _():
        send(r.attn_mom.at[0], r.mrows.at[low], r.m_s, r.m_r.at[low], (high * 2 + core, far * 2 + 1))

    second_norm(0)
    own_back(0)
    second_norm(1)
    store("mixed")
    spread[0].pass_far()
    own_back(1)
    their_back(0)
    spread[1].pass_far()
    their_back(1)

    sums = {}
    for key in "fsa":
        sums[key] = ReduceDp(
            *(getattr(r, name + key) for name in ("g", "low", "hs", "hb")),
            getattr(r, "mb" + key, None),
            [getattr(r, name + key) for name in ("ls_", "lr_", "hs_", "hr_")],
            data,
            tensor,
        )
    spread = []

    def first_norm_back(part):
        at = pl.ds(part * HALF, HALF)
        dh = back.far_in(part, back.near_in(0, part, r.kept[part])) + r.drf[at]
        n1 = r.n1[at]
        gain_grad, bias_grad = jnp.sum(dh * n1, 0, keepdims=True), jnp.sum(dh, 0, keepdims=True)
        r.partial[0:1] = gain_grad if part == 0 else r.partial[0:1] + gain_grad
        r.partial[1:2] = bias_grad if part == 0 else r.partial[1:2] + bias_grad
        dr1 = norm_rows_back(n1, r.s1[at, :1], dh * gain1)
        r.drf[at] = dr1
        r.dr1[tensor, at] = dr1.astype(BF)
        spread.append(Spread(g, r.dr1, r.dr1_s, r.dr1_r, part))

    def up_grad(buf):
        grad = tn(r.hb[...].reshape(1024, 768), r.du[...].reshape(1024, 768))
        buf[...] = grad.astype(BF).reshape(buf.shape)

    def down_grad(buf):
        grad = tn(r.dr2[...].reshape(1024, 768), r.hid[...].reshape(1024, 768))
        buf[...] = grad.astype(BF).reshape(buf.shape)

    pl.when(far == 0)(functools.partial(up_grad, r.gf))
    pl.when(far == 1)(functools.partial(down_grad, r.gf))
    sums["f"].start()
    first_norm_back(0)
    sums["f"].forward(0)
    pl.when(far == 0)(functools.partial(down_grad, r.gs))
    pl.when(far == 1)(functools.partial(up_grad, r.gs))
    sums["s"].start()
    sums["f"].forward(1)
    first_norm_back(1)
    r.pbuf[tensor] = r.partial[...]
    parts = []
    for k in (1, 2, 3):
        parts.append(send(r.partial, r.pbuf.at[tensor], r.pt_s.at[k], r.pt_r.at[k], g.device(k)))
    spread[0].pass_far()
    sums["f"].forward(2)
    spread[1].pass_far()
    for part in halves:
        spread[part].arrive_near()
        spread[part].arrive_far()

    attend_back(r, g, 3)
    sums["s"].forward(0)
    for copy in parts:
        copy.wait()
    r.psum[...] = ((r.pbuf[0] + r.pbuf[1]) + r.pbuf[2]) + r.pbuf[3]
    r.qbuf[data] = r.psum[...]
    parts = []
    for k in range(1, count):
        to = (lax.rem(data + k, count), tensor)
        parts.append(send(r.psum, r.qbuf.at[data], r.pd_s.at[k], r.pd_r.at[k], to))
    attend_back(r, g, 2)
    sums["s"].forward(1)

    def new_moment(up_here, key):
        moment = 0.5 * jnp.where(up_here, r.up_mom[...], r.down_mom[...]) + sums[key].finish()

        @pl.when(up_here)
        def _():
            r.mom_u[...] = moment

        @pl.when(jnp.logical_not(up_here))
        def _():
            r.mom_d[...] = moment

        return moment.astype(BF)

    r.xmat[here, cols(tensor)] = new_moment(far == 0, "f")
    attend_back(r, g, 1)
    sums["s"].forward(2)
    own = r.xmat.at[here, cols(tensor)]
    blocks = [
        GatherDp(lambda d: r.xmat.at[rows_of(d), cols(tensor)], r.x_s.at[0], r.x_r.at[0], data, tensor),
        GatherDp(lambda d: r.xmat.at[rows_of(d), cols(tensor ^ 2)], r.x_s.at[1], r.x_r.at[1], data, tensor, True),
    ]

    def pass_on(b, d):
        @pl.when(core == 1)
        def _():
            slot = blocks[b].slot_of(d)
            send(slot, slot, r.j_s.at[b, d], r.j_r.at[b, d], near_dev)

    blocks[0].start()
    blocks[0].cross()
    attend_back(r, g, 0)
    r.xs[...] = new_moment(far == 1, "s")
    send(r.xs, own, r.swap_s, r.swap_r, far_dev)
    store("mom_d")
    store("mom_u")
    blocks[0].forward(0)

    grad = tn(r.seq[...].reshape(1024, 768), r.hb[:, :, : 5 * LANES].reshape(1024, 5 * LANES)).astype(BF)

    def put(at, k):
        r.ga[:, :, at * LANES : (at + 1) * LANES] = grad[:, k * LANES : (k + 1) * LANES].reshape(count, rows, LANES)

    @pl.when(core == 0)
    def _():
        for at, k in enumerate((0, 1, 3, 2, 4)):
            put(at, k)

    @pl.when(works)
    def _():
        for at, k in zip((3, 4, 5, 6, 7), (0, 1, 3, 2, 4)):
            put(at, k)

    blocks[0].forward(1)
    await_bytes(r.xmat.at[here, cols(tensor ^ 2)], r.swap_r)
    blocks[1].start()
    blocks[1].cross()
    grad_out = tn(r.attn[...].reshape(1024, 256), r.dr1[...].reshape(1024, 768)).astype(BF)
    r.gos[core] = grad_out[:192].reshape(2, rows, 768)
    extra_in = r.wd.at[:, :, : 2 * LANES]

    @pl.when(core == 0)
    def _():
        wide, rest = r.ga.at[:, :, : 3 * LANES], r.ga.at[:, :, 3 * LANES : 5 * LANES]
        send(wide, wide, r.t_s.at[0], r.t_r.at[0], near_dev)
        send(rest, extra_in, r.t_s.at[1], r.t_r.at[1], near_dev)
        send(r.gos.at[0], r.gos.at[0], r.t_s.at[2], r.t_r.at[2], near_dev)

    blocks[0].forward(2)

    for step in range(n):
        pass_on(0, blocks[0].source(step))

    @pl.when(works)
    def _():
        await_bytes(extra_in, r.t_r.at[1])
        first = lanes_of(768) < 64
        extra, own_last = [r.wd[:, :, k * LANES : (k + 1) * LANES].reshape(768, LANES).astype(F32) for k in range(2)], [
            r.ga[:, :, (6 + k) * LANES : (7 + k) * LANES].reshape(768, LANES).astype(F32) for k in range(2)
        ]
        tiles = (
            jnp.where(first, extra[0], half_roll(own_last[0])),
            jnp.where(first, half_roll(extra[0]), own_last[0]),
            jnp.where(first, extra[1], half_roll(own_last[1])),
        )
        for k, tile in enumerate(tiles):
            r.ga[:, :, (6 + k) * LANES : (7 + k) * LANES] = tile.astype(BF).reshape(count, rows, LANES)
        await_bytes(r.ga.at[:, :, : 3 * LANES], r.t_r.at[0])
        await_bytes(r.gos.at[0], r.t_r.at[2])

    @pl.when(works)
    def _():
        sums["a"].start(0, 1)

    for q in (3, 2, 1, 0):
        back_to_input(r, q)
    total = SumQuarters(r, g, 2)
    for part in halves:
        total.near_out(0, part, half_of(r.gp, tensor ^ 3, part)[...])
        total.near_out(1, part, half_of(r.gp, tensor ^ 1, part)[...])
    for part in halves:
        total.far_out(part, total.near_in(0, part, half_of(r.gp, tensor ^ 2, part)[...]))

    blocks[1].forward()
    for step in range(n):
        pass_on(1, blocks[1].source(step))

    @pl.when(works)
    def _():
        for k in range(2):
            send(r.gos.at[k, 1 - low], r.olow.at[k], r.o_s.at[0, k], r.o_r.at[k], (other, tensor))
        sums["a"].start(2, 3)
        sums["a"].forward(0, 1)

    for b in range(2):
        for step in range(n):
            blocks[b].arrive(step)
            pass_on(b, blocks[b].partner_slot(step))
        blocks[b].close()

    for part in halves:
        at = pl.ds(part * HALF, HALF)
        value = total.near_in(1, part, half_of(r.gp, tensor, part)[...])
        r.input_grad[at] = total.far_in(part, value) + r.drf[at]
    store("input_grad")

    sides = [
        GatherDp(lambda d, side=side: r.xa.at[rows_of(d // 2 * 2 + side)], r.f_s.at[side], r.f_r.at[side], data, tensor)
        for side in range(2)
    ]
    role = 2 * far + low
    homes = ((high * 2, 1), (high * 2 + 1, 1), (high * 2, 3))
    out_home = (high * 2 + 1, 3)

    @pl.when(works)
    def _():
        for k in range(2):
            t = 2 * far + k
            await_bytes(r.olow.at[k], r.o_r.at[k])
            r.osend[k] = (r.gos[k, low].astype(F32) + r.olow[k].astype(F32)).astype(BF)
            for step in range(1, n):

                @pl.when(lax.rem(high + step, n) == t)
                def _():
                    send(r.osend.at[k], r.ohigh.at[step - 1], r.o_s.at[1, k], r.oh_r.at[step], (t * 2 + low, tensor))

        sums["a"].forward(2)
        summed = sums["a"].finish()
        for m in range(3):
            for k in range(3):
                tile = summed[:, (m + 3 * k) * LANES : (m + 3 * k + 1) * LANES]
                r.asend[m, :, k * LANES : (k + 1) * LANES] = tile.astype(BF)

            @pl.when(role == m)
            def _():
                r.gin[low, far] = r.asend[m]

            @pl.when(role != m)
            def _():
                send(r.asend.at[m], r.gin.at[low, far], r.g_s.at[m], r.g_r.at[low, far], homes[m])

        for k in range(2):

            @pl.when(high == 2 * far + k)
            def _():
                whole = r.gos[k, low].astype(F32) + r.olow[k].astype(F32)
                for step in range(1, n):
                    await_bytes(r.ohigh.at[step - 1], r.oh_r.at[step])
                    whole = whole + r.ohigh[step - 1].astype(F32)
                r.oout[...] = whole.astype(BF)

                @pl.when(role == 3)
                def _():
                    r.gown[low] = r.oout[...]

                @pl.when(role != 3)
                def _():
                    send(r.oout, r.gown.at[low], r.o_s.at[2, 0], r.go_r.at[low], out_home)

        for side in range(2):
            row_block = rows_of(high * 2 + side)

            @pl.when(role == 3)
            def _():
                @pl.when((high // 2 == 0) | (side == 0))
                def _():
                    await_bytes(r.gown.at[side], r.go_r.at[side])

            @pl.when(role != 3)
            def _():
                first = lanes_of(rows) < 64
                for x in range(2):

                    @pl.when((low != side) | (far != x))
                    def _():
                        await_bytes(r.gin.at[side, x], r.g_r.at[side, x])

                    piece = [r.gin[side, x, :, k * LANES : (k + 1) * LANES] for k in range(3)]
                    turned, last = half_roll(piece[1].astype(F32)), piece[2].astype(F32)
                    base = 3 * LANES * x
                    r.gown[side, :, base : base + LANES] = piece[0]
                    r.gown[side, :, base + LANES : base + 2 * LANES] = jnp.where(first, last, turned).astype(BF)
                    r.gown[side, :, base + 2 * LANES : base + 3 * LANES] = jnp.where(first, turned, last).astype(BF)

            if side == 0:
                await_bytes(r.mrows.at[0], r.m_r.at[0])
            else:

                @pl.when(low == 0)
                def _():
                    await_bytes(r.mrows.at[1], r.m_r.at[1])

            r.xa[row_block] = (0.5 * r.mrows[side] + r.gown[side].astype(F32)).astype(BF)
            sides[side].start()

        @pl.when(low == 1)
        def _():
            r.gback[...] = r.gown[1]
            send(r.gown.at[0], r.gback, r.b_s.at[0], r.b_r, (other, tensor))

        @pl.when(low == 0)
        def _():
            send(r.gown.at[0], r.gback, r.b_s.at[0], r.b_r, (data, tensor ^ 1))
            send(r.gown.at[1], r.gback, r.b_s.at[1], r.b_r, (other, tensor ^ 1))

    for copy in parts:
        copy.wait()
    r.norm_grad[...] = sum((r.qbuf[d] for d in range(1, count)), r.qbuf[0])

    @pl.when(core == 0)
    def _():
        for b in range(2):
            for d in range(count):
                await_bytes(own, r.j_r.at[b, d])
            first_gram(r.xmat, [cols(tensor ^ (2 * b)), cols(tensor ^ (2 * b + 1))], r.kg, b > 0)
        scale = first_scale(r.kg, r.du)
        newton_poly(r.du, r.hid)
        newton_apply(r.xmat, r.hid, 1536, scale)
        newton(r.xmat, r.du, r.hid, 3072, NS_STEPS - 2)
        newton_gram(r.xmat, r.du)
        poly = last_poly(r.du, data, rows)
        for k in (2, 3, 1, 0):
            r.lowf[tensor ^ k] = last_rows(r.xmat, poly, here, cols(tensor ^ k))
            for m, out in enumerate((r.o_u, r.o_d)):

                @pl.when(far == m)
                def _():
                    if k:
                        send(r.lowf.at[tensor ^ k], out, r.w_s.at[k], r.w_r.at[m], g.device(k))
                    else:
                        out[...] = r.lowf[tensor]

    owner = far * 2 + low

    @pl.when(core == 1)
    def _():
        for side in range(2):
            sides[side].forward(cross=False)
        for side in range(2):
            sides[side].close(cross=False)
        whole = slice(0, 768)
        first_gram(r.xa, [whole], r.kg, False)
        scale = first_scale(r.kg, r.du)
        newton_poly(r.du, r.hid)
        newton_apply(r.xa, r.hid, 768, scale)
        newton(r.xa, r.du, r.hid, 768, NS_STEPS - 2)
        newton_gram(r.xa, r.du)
        r.lowf[1] = last_rows(r.xa, last_poly(r.du, other, rows), there, whole)
        send(r.lowf.at[1], r.o_a, r.v_s.at[0], r.v_r, (other, owner))
        r.lowf[0] = last_rows(r.xa, last_poly(r.du, data, rows), here, whole)

    @pl.when((core == 1) & (low == 1))
    def _():
        r.o_a[...] = r.lowf[0]

    @pl.when((core == 1) & (low == 0))
    def _():
        send(r.lowf.at[0], r.o_a, r.v_s.at[1], r.v_r, (data, owner))

    @pl.when((core == 0) | (low == 0))
    def _():
        await_bytes(r.o_a, r.v_r)

    for m, out in enumerate((r.o_u, r.o_d)):

        @pl.when((core == 1) | (far != m))
        def _():
            await_bytes(out, r.w_r.at[m])

    @pl.when((core == 0) | (low == 0))
    def _():
        await_bytes(r.gback, r.b_r)

    r.mom_a[...] = 0.5 * r.attn_mom[0] + r.gback[...].astype(F32)

    for copy in stores:
        copy.wait()
    await_bytes(r.xs, r.swap_s)

    @pl.when((core == 0) | (low == 0))
    def _():
        await_bytes(r.mrows.at[0], r.m_s)

    @pl.when(core == 0)
    def _():
        await_bytes(r.ga.at[:, :, : 3 * LANES], r.t_s.at[0])
        await_bytes(extra_in, r.t_s.at[1])
        await_bytes(r.gos.at[0], r.t_s.at[2])

    @pl.when(works)
    def _():
        for k in range(2):
            await_bytes(r.olow.at[k], r.o_s.at[0, k])
            pl.when(high != 2 * far + k)(functools.partial(await_bytes, r.osend.at[k], r.o_s.at[1, k]))
        for m in range(3):
            pl.when(role != m)(functools.partial(await_bytes, r.asend.at[m], r.g_s.at[m]))
        pl.when((high // 2 == far) & (role != 3))(functools.partial(await_bytes, r.oout, r.o_s.at[2, 0]))
        await_bytes(r.gback, r.b_s.at[0])
        pl.when(low == 0)(functools.partial(await_bytes, r.gback, r.b_s.at[1]))

    @pl.when(core == 0)
    def _():
        for k in (1, 2, 3):
            await_bytes(r.o_u, r.w_s.at[k])

    @pl.when(core == 1)
    def _():
        for b in range(2):
            for d in range(count):
                await_bytes(own, r.j_s.at[b, d])
        await_bytes(r.o_a, r.v_s.at[0])

    @pl.when((core == 1) & (low == 0))
    def _():
        await_bytes(r.o_a, r.v_s.at[1])


def step_call(count, rows, ins):
    v = pltpu.VMEM
    n = count // 2
    one = pltpu.SemaphoreType.DMA
    outs = dict(
        mixed_hbm=shape(QUARTER, 768),
        input_grad_hbm=shape(QUARTER, 768, dtype=F32),
        mom_a=shape(rows, 768, dtype=F32),
        mom_u_hbm=shape(rows, 768, dtype=F32),
        mom_d_hbm=shape(rows, 768, dtype=F32),
        norm_grad=shape(4, 768, dtype=F32),
        o_u=shape(rows, 768),
        o_d=shape(rows, 768),
        o_a=shape(rows, 768),
    )
    per_head = (3, TENSOR, QUARTER, LANES)
    quarters = (TENSOR, QUARTER, 768)
    scratch = dict(
        cotangent=v((QUARTER, 768), BF),
        attn_mom=v((1, rows, 768), F32),
        up_mom=v((rows, 768), F32),
        down_mom=v((rows, 768), F32),
        mixed=v((QUARTER, 768), BF),
        input_grad=v((QUARTER, 768), F32),
        mom_u=v((rows, 768), F32),
        mom_d=v((rows, 768), F32),
        load_sem=dma(len(LOADED)),
        store_sem=dma(4),
        slabs=v((TENSOR, rows, 256), BF),
        wo_own=v((2, rows // 2, 768), BF),
        seq=v(quarters, BF),
        slab_in=v((3, rows, 256), BF),
        wp=v((768, 5 * LANES), BF),
        wo=v((count, 2, rows // 2, 768), BF),
        wu=v((count, rows, 768), BF),
        wd=v((count, rows, 768), BF),
        woh=v((3, LANES, 768), BF),
        slab_s=dma(4),
        slab_r=dma(4),
        tok_s=dma(3),
        tok_r=dma(3),
        share_s=dma(count),
        share_r=dma(count),
        gather_s=dma(7, 9),
        gather_r=dma(7, 9),
        qf=v(per_head, BF),
        kf=v(per_head, BF),
        va=v(per_head, BF),
        qg=v(per_head, F32),
        kg=v(per_head, F32),
        af=v(per_head, F32),
        sb=v((3, TENSOR, QUARTER, QUARTER), BF),
        st=v((3, TENSOR, LANES, LANES), BF),
        state=v((3, LANES, LANES), F32),
        attn=v((TENSOR, QUARTER, 256), BF),
        aall=v((TENSOR, 2, QUARTER, 256), BF),
        attn_s=dma(2, 4),
        attn_r=dma(2, 4),
        hb=v(quarters, BF),
        n1=v((QUARTER, 768), F32),
        s1=v((QUARTER, LANES), F32),
        h1=v((QUARTER, 768), F32),
        hid=v(quarters, BF),
        gp=v(quarters, F32),
        du=v(quarters, BF),
        dr2=v(quarters, BF),
        drf=v((QUARTER, 768), F32),
        dr1=v(quarters, BF),
        kept=v((2, HALF, 768), F32),
        near_send=v((4, HALF, 768), BF),
        near_recv=v((4, HALF, 768), BF),
        far_send=v((2, HALF, 768), BF),
        far_recv=v((2, HALF, 768), BF),
        near_s=dma(12),
        near_r=dma(12),
        far_s=dma(6),
        far_r=dma(6),
        h_s=dma(2),
        h_r=dma(2),
        dr2_s=dma(6),
        dr2_r=dma(6),
        dr1_s=dma(6),
        dr1_r=dma(6),
        gf=v((count, rows, 768), BF),
        gs=v((count, rows, 768), BF),
        ga=v((count, rows, 9 * LANES), BF),
        gos=v((2, 2, rows, 768), BF),
        t_s=dma(3),
        t_r=dma(3),
        olow=v((2, rows, 768), BF),
        osend=v((2, rows, 768), BF),
        ohigh=v((n - 1, rows, 768), BF),
        o_s=dma(3, 2),
        o_r=dma(2),
        oh_r=dma(n),
        asend=v((3, rows, 3 * LANES), BF),
        gin=v((2, 2, rows, 3 * LANES), BF),
        g_s=dma(3),
        g_r=dma(2, 2),
        gown=v((2, rows, 768), BF),
        go_r=dma(2),
        gback=v((rows, 768), BF),
        b_s=dma(2),
        b_r=one,
        mrows=v((2, rows, 768), F32),
        m_s=one,
        m_r=dma(2),
        partial=v((4, 768), F32),
        pbuf=v((TENSOR, 4, 768), F32),
        psum=v((4, 768), F32),
        qbuf=v((count, 4, 768), F32),
        pt_s=dma(4),
        pt_r=dma(4),
        pd_s=dma(count),
        pd_r=dma(count),
        oout=v((rows, 768), BF),
        xs=v((rows, 768), BF),
        xmat=v((768, TENSOR * 768), BF),
        xa=v((768, 768), BF),
        swap_s=one,
        swap_r=one,
        x_s=dma(2, 9),
        x_r=dma(2, 9),
        f_s=dma(2, 8),
        f_r=dma(2, 8),
        j_s=dma(2, count),
        j_r=dma(2, count),
        w_s=dma(4),
        w_r=dma(2),
        v_s=dma(2),
        v_r=one,
    )
    for key in "fsa":
        part = (rows, 9 * LANES if key == "a" else 768)
        for name, slots in (("low", n), ("hs", n - 1), ("hb", n - 1)):
            scratch[name + key] = v((slots,) + part, BF)
        if key != "a":
            scratch["mb" + key] = v(part, BF)
        for name in ("ls_", "lr_", "hs_", "hr_"):
            scratch[name + key] = dma(n)
    body = functools.partial(step_body, count, rows)
    anywhere = [n + "_in" for n in LOADED] + [n for n in outs if n.endswith("_hbm")]
    return kernel_call(body, "layer_step", ins, outs, scratch, 0, ("lengths",), anywhere)


def finish_body(r):
    keep = 1.0 - MUON_RATE * MUON_DECAY
    rate_a = MUON_RATE * 0.2 * math.sqrt(768)
    rate_ff = MUON_RATE * 0.2 * math.sqrt(TENSOR * 768)
    r.attn_new[0] = r.attn_w[0] * keep - rate_a * r.o_a[...].astype(F32)
    r.up_new[...] = r.up_w[...] * keep - rate_ff * r.o_u[...].astype(F32)
    r.down_new[...] = r.down_w[...] * keep - rate_ff * r.o_d[...].astype(F32)
    r.attn_moment[0] = r.mom_a[...]
    r.up_moment[...] = r.mom_u[...]
    r.down_moment[...] = r.mom_d[...]
    r.mixed_out[...] = r.mixed[...]
    r.input_grad_out[...] = r.input_grad[...]
    grad = r.norm_grad[...]
    moment1 = 0.5 * r.norm_m1[...] + 0.5 * grad
    moment2 = 0.95 * r.norm_m2[...] + 0.05 * grad * grad
    first_hat = moment1 / (1.0 - 0.5**STEP)
    second_hat = moment2 / (1.0 - 0.95**STEP)
    r.norm_moment1[...] = moment1
    r.norm_moment2[...] = moment2
    r.norm_new[...] = r.norms[...] - ADAM_RATE * first_hat / (jnp.sqrt(second_hat) + 1e-08)


def finish_call(ins):
    rows = ins["up_w"].shape[0]
    block = shape(rows, 768, dtype=F32)
    small = shape(4, 768, dtype=F32)
    outs = dict(
        mixed_out=shape(QUARTER, 768),
        input_grad_out=shape(QUARTER, 768, dtype=F32),
        attn_new=shape(1, rows, 768, dtype=F32),
        attn_moment=shape(1, rows, 768, dtype=F32),
        up_new=block,
        up_moment=block,
        down_new=block,
        down_moment=block,
        norm_moment1=small,
        norm_moment2=small,
        norm_new=small,
    )
    return kernel_call(finish_body, "finish", ins, outs, {}, None)


def step_on_device(
    tokens,
    cotangent,
    lengths,
    attn_w,
    up_w,
    down_w,
    norm_params,
    attn_mom,
    up_mom,
    down_mom,
    norm_m1,
    norm_m2,
):
    count = lax.axis_size("dp")
    rows = attn_w.shape[1]
    done = step_call(
        count,
        rows,
        dict(
            lengths=lengths,
            tokens=tokens,
            cotangent_in=cotangent,
            attn_w=attn_w,
            up_w=up_w,
            down_w=down_w.T,
            norms=norm_params,
            attn_mom_in=attn_mom,
            up_mom_in=up_mom,
            down_mom_in=down_mom.T,
        ),
    )
    last = finish_call(
        dict(
            attn_w=attn_w,
            up_w=up_w,
            down_w=down_w.T,
            norms=norm_params,
            norm_m1=norm_m1,
            norm_m2=norm_m2,
            **{n.removesuffix("_hbm"): a for n, a in done.items()},
        )
    )
    return (
        last["mixed_out"],
        last["input_grad_out"],
        last["attn_new"],
        last["attn_moment"],
        last["up_new"],
        last["up_moment"],
        last["down_new"].T,
        last["down_moment"].T,
        last["norm_moment1"],
        last["norm_moment2"],
        last["norm_new"],
    )


def solution(mesh):
    placed = (
        P(("dp", "tensor"), None),
        P(("dp", "tensor"), None),
        P("dp"),
        P("tensor", "dp", None),
        P("dp", "tensor"),
        P("tensor", "dp"),
        P(),
        P("tensor", "dp", None),
        P("dp", "tensor"),
        P("tensor", "dp"),
        P(),
        P(),
    )
    whole_tiles = mesh.shape["dp"] == 8 and mesh.shape["tensor"] == TENSOR
    return jax.shard_map(
        step_on_device if whole_tiles else on_device,
        mesh=mesh,
        in_specs=placed,
        out_specs=(
            P(("dp", "tensor"), None),
            P(("dp", "tensor"), None),
            P("tensor", "dp", None),
            P("tensor", "dp", None),
            P("dp", "tensor"),
            P("dp", "tensor"),
            P("tensor", "dp"),
            P("tensor", "dp"),
            P(),
            P(),
            P(),
        ),
        check_vma=False,
    )
```
